512 devices in a mesh: gx: 16 (over z), gy: 8 (over x, core), gz: 4 (over y).
Axes of the slice: x: 4, y: 4, z: 16, core: 2. Of those that a mesh axis runs over, the one named last changes fastest.
Arguments:
- global_now: float32 [32, 6, 128, 128], P('gy', None, 'gx'), may hold values from -6 to 6
- global_prev: float32 [32, 6, 128, 128], P('gy', None, 'gx'), may hold values from -6 to 6
- cycle_modes: int32 [128], P('gx'), may hold values from 1 to 32
- wave_speed: float32 [128, 128], P('gx'), may hold values from 1 to 3
- inv_radius: float32 [128, 128], P('gx'), may hold values from 0.0005 to 0.005
- theta_second: float32 [128, 128], replicated, may hold values from -0.5 to 0.5
- theta_first: float32 [128, 128], replicated, may hold values from -0.5 to 0.5
- point_dest: int32 [4, 8192, 1], P('gz', 'gx'), may hold values from 0 to 127; in each aligned block of 512 rows (0 to 511, 512 to 1023, ..., all dimensions but the last counted through in order) at most 8 rows name the same one
- point_target: int32 [4, 8192], P('gz', 'gx'), may hold values from 0 to 4095
- point_source: int32 [4, 8192], P('gz', 'gx'), may hold values from 0 to 1023
- point_azimuth: float32 [4, 8192], P('gz', 'gx'), may hold values from -3.140625 to 3.140625
- regional_now: float32 [3, 64, 64, 512], P(None, 'gx', 'gy', 'gz'), may hold values from -6 to 6
- regional_prev: float32 [3, 64, 64, 512], P(None, 'gx', 'gy', 'gz'), may hold values from -6 to 6
- moduli: float32 [64, 64, 512], P('gx', 'gy', 'gz'), may hold values from 0.5 to 2
- inv_mass: float32 [64, 64, 512], P('gx', 'gy', 'gz'), may hold values from 0.5 to 2
Outputs:
- global_next: float32 [32, 6, 128, 128], P('gy', None, 'gx')
- regional_next: float32 [3, 64, 64, 512], P(None, 'gx', 'gy', 'gz')
- injected_force: float32 [3, 64, 64, 512], P(None, 'gx', 'gy', 'gz')
The draws below stay inside these ranges and needn't reach their ends.
Inputs may be any that keep to these rules, and one draw needn't show every extreme that they name: `point_dest`: among the 512 points of one device (one aligned block of rows) at most 8 name one owner; in some block an owner is named exactly 8 times.
All inputs are finite; a program needn't handle non-finite values.
Results may differ from the reference program's by a relative error of at most 0.0003.
Values sent between devices are 32-bit elements; how exact they have to be, the bound alone decides.
A program may use at most 64 MiB of HBM per device.

```python
import math
import jax
import jax.numpy as jnp
import numpy as np
from jax import lax

MODES = 32
R_DEV = 8
CYCLES = 128
TH = 128
P_ROW = 512
C = 8
EX = 1
EY = 2
EZ = 32
PTS_DEV = 4096
NX = 64
NY = 64
NZ = 512
N_GX = 16
N_GY = 8
N_GZ = 4


def plant(entries, stream_key, low, top_value):
    index_at = [jax.random.randint(jax.random.fold_in(stream_key, axis), (), 0, length) for axis, length in enumerate(entries.shape)]
    longest = entries.shape.index(max(entries.shape))
    next_to = index_at[:longest] + [(index_at[longest] + 1) % entries.shape[longest]] + index_at[longest + 1:]
    return entries.at[tuple(index_at)].set(low).at[tuple(next_to)].set(top_value)


def level_of(rng, extent, cuts, smallest, top_value):
    factor_of, own = 1.0, jax.random.fold_in(rng, 6)
    for dim, blocks in cuts:
        draws = jnp.exp(jax.random.uniform(jax.random.fold_in(own, dim), (blocks,), jnp.float32, smallest / len(cuts), top_value / len(cuts)))
        factor_of = factor_of * jnp.repeat(draws, extent[dim] // blocks).reshape([-1 if axis == dim else 1 for axis in range(len(extent))])
    return factor_of


def deal_out(rng, own, number, rows, count, top, bound, skew):
    sequence = jax.random.permutation(rng, count)
    heavy_load, usual = load_shares(count, rows * top, bound, skew, True), load_shares(count, rows * top, bound, skew, False)
    places = jnp.arange(count)

    def named(sizes, rotation):
        used = int((sizes > 0).sum())
        fixed = max(1, used // 4)
        passed = fixed + (places - fixed + rotation * (used - fixed)) % max(1, count - fixed)
        return jnp.zeros((count,), jnp.int32).at[sequence[jnp.where(places < fixed, places, passed)]].set(jnp.asarray(sizes, jnp.int32))

    sizes = jnp.where(number % 4 == 0, named(heavy_load, number // 4), named(usual, number - number // 4 - 1))
    mixed = jax.random.permutation(jax.random.fold_in(own, 3), count)
    giver, receiver = mixed[0:count // 2 * 2:2], mixed[1:count // 2 * 2:2]
    slack = jnp.minimum(sizes[giver] - 1, bound - sizes[receiver]) // 2
    slack = jnp.where((giver == sequence[0]) | (receiver == sequence[0]) | (sizes[receiver] == 0), 0, jnp.maximum(slack, 0))
    passed = jax.random.randint(jax.random.fold_in(own, 4), (count // 2,), 0, 1 << 20) % (slack + 1)
    sizes = sizes.at[giver].add(-passed).at[receiver].add(passed)
    members = jnp.searchsorted(jnp.cumsum(sizes), jnp.arange(rows * top), side="right").astype(jnp.int32)
    table = members.reshape(top, rows).T
    table = table[jax.random.permutation(jax.random.fold_in(own, 1), rows)]
    rotation = jax.random.randint(jax.random.fold_in(own, 2), (rows, 1), 0, top)
    return jnp.take_along_axis(table, (jnp.arange(top)[None, :] + rotation) % top, axis=1)


def load_shares(number_of, total, most, lean, full):
    portions = [(1 << 20) // math.isqrt(rank ** lean) + 1 for rank in range(1, number_of + 1)]
    largest = most if full else min(most, max(-(-total // number_of), total * portions[0] // sum(portions)))
    least = 1 if total - largest >= number_of - 1 else 0
    counts, rest = [largest] + [least] * (number_of - 1), total - largest - least * (number_of - 1)
    while rest > 0:
        free = [i for i in range(1, number_of) if counts[i] < largest] or [i for i in range(1, number_of) if counts[i] < most]
        pool, left = sum([portions[i] for i in free]), rest
        for i in free:
            extra = min(most - counts[i], max(1, left * portions[i] // pool), rest)
            counts[i] = counts[i] + extra
            rest = rest - extra
    return np.array(counts)


def normal_values(rng, extent, deviation, limit, cuts=(), held_as=jnp.bfloat16):
    values = deviation * jax.random.normal(rng, extent, jnp.float32)
    if cuts:
        values = values * level_of(rng, extent, cuts, -0.22, 0.18)
    return jnp.clip(values, -limit, limit).astype(held_as)


def setup_inputs(seed: int = 0) -> dict:
    arg_keys = jax.random.split(jax.random.key(seed), 16)
    global_now = normal_values(arg_keys[0], (MODES, 6, CYCLES, TH), 1.0, 6.0, ((0, 8), (2, 16)), jnp.float32)
    global_prev = normal_values(arg_keys[1], (MODES, 6, CYCLES, TH), 1.0, 6.0, ((0, 8), (2, 16)), jnp.float32)
    cycle_modes = plant(jax.random.randint(arg_keys[2], (CYCLES,), 1, MODES + 1), jax.random.fold_in(arg_keys[2], 1), 1, MODES).astype(jnp.int32)
    wave_speed = jnp.clip(1.0 + 2.0 * jax.random.uniform(arg_keys[3], (CYCLES, TH), jnp.float32) ** level_of(arg_keys[3], (CYCLES, TH), ((0, 16),), -0.2, 0.2), 1.0, 3.0)
    inv_radius = jnp.clip(jnp.exp(math.log(0.005) - 2.30258502 * jax.random.uniform(arg_keys[4], (CYCLES, TH), jnp.float32) ** level_of(arg_keys[4], (CYCLES, TH), ((0, 16),), -0.2, 0.2)), 0.0005, 0.005)
    theta_second = normal_values(arg_keys[5], (TH, TH), TH ** -0.5, 0.5, (), jnp.float32)
    theta_first = normal_values(arg_keys[6], (TH, TH), TH ** -0.5, 0.5, (), jnp.float32)
    point_dest_keys = jax.random.split(jax.random.fold_in(arg_keys[7], 1), N_GZ * (N_GX * P_ROW) // P_ROW)
    point_dest_turns = jax.random.permutation(jax.random.fold_in(arg_keys[7], 3), N_GZ * (N_GX * P_ROW) // P_ROW)
    point_dest = jax.vmap(lambda own, number: deal_out(jax.random.fold_in(arg_keys[7], 2), own, number, P_ROW, N_GX * N_GY, 1, C, 2))(point_dest_keys, point_dest_turns).reshape((N_GZ, N_GX * P_ROW, 1))
    point_target = plant(jax.random.randint(arg_keys[8], (N_GZ, N_GX * P_ROW), 0, PTS_DEV), jax.random.fold_in(arg_keys[8], 1), 0, PTS_DEV - 1).astype(jnp.int32)
    point_source = plant(jax.random.randint(arg_keys[9], (N_GZ, N_GX * P_ROW), 0, R_DEV * TH), jax.random.fold_in(arg_keys[9], 1), 0, (R_DEV * TH) - 1).astype(jnp.int32)
    point_azimuth = jnp.clip(jax.random.uniform(arg_keys[10], (N_GZ, N_GX * P_ROW), jnp.float32, -3.140625, 3.140625), -3.140625, 3.140625)
    regional_now = normal_values(arg_keys[11], (3, NX, NY, NZ), 1.0, 6.0, ((1, 16), (2, 8), (3, 4)), jnp.float32)
    regional_prev = normal_values(arg_keys[12], (3, NX, NY, NZ), 1.0, 6.0, ((1, 16), (2, 8), (3, 4)), jnp.float32)
    moduli = jnp.clip(jnp.exp(math.log(2.0) - 1.3862944 * jax.random.uniform(arg_keys[13], (NX, NY, NZ), jnp.float32) ** level_of(arg_keys[13], (NX, NY, NZ), ((0, 16), (1, 8), (2, 4)), -0.2, 0.2)), 0.5, 2.0)
    inv_mass = jnp.clip(jnp.exp(math.log(2.0) - 1.3862944 * jax.random.uniform(arg_keys[14], (NX, NY, NZ), jnp.float32) ** level_of(arg_keys[14], (NX, NY, NZ), ((0, 16), (1, 8), (2, 4)), -0.2, 0.2)), 0.5, 2.0)
    return dict(global_now=global_now, global_prev=global_prev, cycle_modes=cycle_modes, wave_speed=wave_speed, inv_radius=inv_radius, theta_second=theta_second, theta_first=theta_first, point_dest=point_dest, point_target=point_target, point_source=point_source, point_azimuth=point_azimuth, regional_now=regional_now, regional_prev=regional_prev, moduli=moduli, inv_mass=inv_mass)


time_step = 0.3
time_sq = 0.09
impedance = 0.5
coupling = 0.05
slab_factor = 0.04

def gll_tables():
    nodes = np.array([-1.0, -math.sqrt(3.0 / 7.0), 0.0, math.sqrt(3.0 / 7.0), 1.0])
    weights = np.array([0.1, 49.0 / 90.0, 32.0 / 45.0, 49.0 / 90.0, 0.1])
    factor = np.array([np.prod([nodes[i] - nodes[k] for k in range(5) if k != i]) for i in range(5)])
    deriv = np.zeros((5, 5))
    for i in range(5):
        for j in range(5):
            if i != j:
                deriv[i, j] = factor[i] / factor[j] / (nodes[i] - nodes[j])
            else:
                deriv[i, j] = sum((1.0 / (nodes[i] - nodes[k]) for k in range(5) if k != i))
    cube = weights[:, None, None] * weights[None, :, None] * weights[None, None, :]
    return (jnp.asarray(deriv, jnp.float32), jnp.asarray(cube, jnp.float32))

def split_axis(grid, axis, count):
    lead = lax.slice_in_dim(grid, 0, 4 * count, axis=axis)
    lead = lead.reshape(lead.shape[:axis] + (count, 4) + lead.shape[axis + 1:])
    tail = lax.slice_in_dim(grid, 4, 4 * count + 1, stride=4, axis=axis)
    return jnp.concatenate([lead, jnp.expand_dims(tail, axis + 1)], axis=axis + 1)

def join_axis(parts, axis, count):
    shape = parts.shape
    merged = shape[:axis] + (4 * count,) + shape[axis + 2:]
    lead = lax.slice_in_dim(parts, 0, 4, axis=axis + 1).reshape(merged)
    tail = lax.slice_in_dim(parts, 4, 5, axis=axis + 1)
    widths = [(0, 0)] * len(shape)
    widths[axis + 1] = (0, 3)
    tail = jnp.pad(tail, widths).reshape(merged)
    ends = [(0, 0)] * len(merged)
    ends[axis] = (4, 0)
    tail = lax.slice_in_dim(jnp.pad(tail, ends), 0, 4 * count + 1, axis=axis)
    ends[axis] = (0, 1)
    return jnp.pad(lead, ends) + tail

def element_forces(window, count_x, count_y, count_z, keep):
    deriv, cube = gll_tables()
    hp = lax.Precision.HIGHEST
    parts = split_axis(window, 1, count_x)
    parts = split_axis(parts, 3, count_y)
    parts = split_axis(parts, 5, count_z)
    parts = jnp.transpose(parts, (2, 4, 6, 0, 1, 3, 5)).reshape(5, 5, 5, window.shape[0], -1)
    field = parts[:, :, :, :3]
    scale = cube[:, :, :, None, None] * parts[:, :, :, 3:] * keep.reshape(1, 1, 1, 1, -1)
    along_a = jnp.einsum('ai,ijklE->ajklE', deriv, field, precision=hp)
    along_b = jnp.einsum('bj,ijklE->ibklE', deriv, field, precision=hp)
    along_c = jnp.einsum('ck,ijklE->ijclE', deriv, field, precision=hp)
    total = jnp.einsum('ai,ajklE->ijklE', deriv, scale * along_a, precision=hp)
    total = total + jnp.einsum('bj,ibklE->ijklE', deriv, scale * along_b, precision=hp)
    total = total + jnp.einsum('ck,ijclE->ijklE', deriv, scale * along_c, precision=hp)
    total = total.reshape(5, 5, 5, 3, count_x, count_y, count_z).transpose(3, 4, 0, 5, 1, 6, 2)
    total = join_axis(total, 5, count_z)
    total = join_axis(total, 3, count_y)
    return join_axis(total, 1, count_x)

def reference(global_now, global_prev, cycle_modes, wave_speed, inv_radius, theta_second, theta_first, point_dest, point_target, point_source, point_azimuth, regional_now, regional_prev, moduli, inv_mass):
    hp = lax.Precision.HIGHEST
    mode_ids = jnp.arange(MODES, dtype=jnp.int32)
    orders = mode_ids.astype(jnp.float32)
    mask = (mode_ids[:, None] < cycle_modes[None, :]).astype(jnp.float32)[:, None, :, None]
    squares = (orders * orders)[:, None, None, None]

    def advance(now, prev):
        padded = jnp.pad(now, ((0, 0), (0, 0), (1, 1), (0, 0)))
        lap = padded[:, :, 2:] - 2.0 * now + padded[:, :, :-2]
        bend = jnp.einsum('mcrt,ts->mcrs', now, theta_second, precision=hp)
        return mask * (2.0 * now - prev + time_sq * (wave_speed * lap + bend - squares * inv_radius * now))
    g_one = advance(global_now, global_prev)
    g_two = advance(g_one, global_now)
    coef = coupling * (jnp.einsum('mcrt,ts->mcrs', g_two, theta_first, precision=hp) + impedance * (g_two - g_one) / time_step)
    flat = coef.reshape(MODES, 6, CYCLES * TH)
    sender = (jnp.arange(N_GX * P_ROW, dtype=jnp.int32) // P_ROW)[None, :]
    cycle_index = (sender * (R_DEV * TH) + point_source).reshape(-1)
    azimuth = point_azimuth.reshape(-1)
    picked = jnp.take(flat, cycle_index, axis=2).reshape(MODES, 3, 2, -1)
    angles = orders[:, None] * azimuth[None, :]
    injected = lax.optimization_barrier(jnp.sum(picked[:, :, 0] * jnp.cos(angles)[:, None] + picked[:, :, 1] * jnp.sin(angles)[:, None], axis=0))
    size_x, size_y, size_z = (4 * EX, 4 * EY, 4 * EZ)
    dest = point_dest[:, :, 0]
    owner_x = dest // N_GY
    owner_y = dest % N_GY
    owner_z = jnp.broadcast_to(jnp.arange(N_GZ, dtype=jnp.int32)[:, None], dest.shape)
    local_x = point_target // (size_y * size_z)
    local_y = point_target // size_z % size_y
    local_z = point_target % size_z
    spot = ((owner_x * size_x + local_x) * NY + owner_y * size_y + local_y) * NZ + owner_z * size_z + local_z
    injected_force = jnp.zeros((3, NX * NY * NZ), jnp.float32).at[:, spot.reshape(-1)].add(injected)
    injected_force = injected_force.reshape(3, NX, NY, NZ)
    moduli_pad = jnp.pad(moduli, 4)[None]
    keep_y = (jnp.arange(NY // 4 + 1, dtype=jnp.int32) >= 1).astype(jnp.float32)
    keep_z = (jnp.arange(NZ // 4 + 1, dtype=jnp.int32) >= 1).astype(jnp.float32)

    def stiffness(field):
        both = jnp.concatenate([jnp.pad(field, ((0, 0), (4, 4), (4, 4), (4, 4))), moduli_pad], axis=0)

        def slab(block):
            zero = jnp.int32(0)
            window = lax.dynamic_slice(both, (zero, block * size_x, zero, zero), (4, size_x + 5, NY + 5, NZ + 5))
            starts = block * size_x - 4 + 4 * jnp.arange(EX + 1, dtype=jnp.int32)
            keep_x = (starts >= 0).astype(jnp.float32)
            keep = keep_x[:, None, None] * keep_y[None, :, None] * keep_z[None, None, :]
            out = element_forces(window, EX + 1, NY // 4 + 1, NZ // 4 + 1, keep)
            return out[:, 4:4 + size_x, 4:4 + NY, 4:4 + NZ]
        pieces = lax.map(slab, jnp.arange(N_GX, dtype=jnp.int32))
        return jnp.transpose(pieces, (1, 0, 2, 3, 4)).reshape(3, NX, NY, NZ)
    u_one = 2.0 * regional_now - regional_prev + slab_factor * inv_mass * (injected_force - stiffness(regional_now))
    u_two = 2.0 * u_one - regional_now + slab_factor * inv_mass * (injected_force - stiffness(u_one))
    return (g_two, u_two, injected_force)
```

```python
import functools
import math

import jax
import jax.numpy as jnp
import numpy as np
from jax import lax
from jax.experimental import pallas as pl
from jax.experimental.pallas import tpu as pltpu
from jax.sharding import PartitionSpec as P

F32 = jnp.float32
BF16 = jnp.bfloat16
MESH = pl.DeviceIdType.MESH

time_step = 0.3
time_sq = 0.09
impedance = 0.5
coupling = 0.05
slab_factor = 0.04

LANES = 128
RANKS = 8


def gll_products():
    nodes = np.array([-1.0, -math.sqrt(3.0 / 7.0), 0.0, math.sqrt(3.0 / 7.0), 1.0])
    weights = np.array([0.1, 49.0 / 90.0, 32.0 / 45.0, 49.0 / 90.0, 0.1])
    factor = np.array(
        [np.prod([nodes[i] - nodes[k] for k in range(5) if k != i]) for i in range(5)]
    )
    deriv = np.zeros((5, 5))
    for i in range(5):
        for j in range(5):
            if i != j:
                deriv[i, j] = factor[i] / factor[j] / (nodes[i] - nodes[j])
            else:
                deriv[i, j] = sum((1.0 / (nodes[i] - nodes[k]) for k in range(5) if k != i))
    return weights, np.einsum("ki,k,kj->kij", deriv, weights, deriv)


WEIGHTS, GRAM = gll_products()


def cosine_series():
    f = np.cos(np.linspace(0.0, np.pi / 2, 2001)) * 0.5
    fit = np.polynomial.chebyshev.Chebyshev.fit(f * f, np.cos(2 * np.pi * f), 8, domain=[0, 0.25])
    return [float(v) for v in fit.convert(kind=np.polynomial.Polynomial).coef]


COSINE = cosine_series()


def halves(x):
    high = x.astype(BF16)
    return high, (x - high.astype(F32)).astype(BF16)


def dot(a, b):
    return lax.dot_general(a, b, (((1,), (0,)), ((), ())), preferred_element_type=F32)


def dot_rows(a, b):
    return lax.dot_general(a, b, (((1,), (1,)), ((), ())), preferred_element_type=F32)


def operator_pair(t):
    high, low = halves(t)
    top = jnp.concatenate([high, low], axis=1)
    bottom = jnp.concatenate([high, jnp.zeros_like(low)], axis=1)
    return jnp.concatenate([top, bottom], axis=0)


def times_operator(x, pair_ref):
    high, low = halves(x)
    both = dot(jnp.concatenate([high, low], axis=1), pair_ref[...])
    return both[:, :LANES] + both[:, LANES:]


def iota(shape, axis):
    return lax.broadcasted_iota(jnp.int32, shape, axis)


def by_four(phase, values):
    out = jnp.full(phase.shape, values[3], F32)
    for i in (2, 1, 0):
        out = jnp.where(phase == i, F32(values[i]), out)
    return out


def kernel(
    sizes,
    modes_ref,
    now_in,
    prev_in,
    speed_in,
    radius_in,
    second_in,
    first_in,
    dest_in,
    target_in,
    source_in,
    azimuth_in,
    slab_in,
    before_in,
    moduli_in,
    mass_in,
    g_out,
    slab_out,
    force_out,
    now_ref,
    prev_ref,
    speed_ref,
    radius_ref,
    second_ref,
    first_ref,
    dest_ref,
    target_ref,
    source_ref,
    azimuth_ref,
    slab_ref,
    before_ref,
    moduli_ref,
    mass_ref,
    one_ref,
    two_ref,
    edge_ref,
    pair_second,
    pair_first,
    pick_ref,
    trig_ref,
    slot_ref,
    mark_ref,
    base_ref,
    force_ref,
    step_ref,
    last_ref,
    band_z,
    band_y,
    band_x,
    over_z,
    over_y,
    spread_ref,
    part_ref,
    cycle_send,
    cycle_recv,
    x_send,
    x_recv,
    y_send,
    y_recv,
    z_send,
    z_recv,
    group_send,
    group_recv,
    owner_send,
    owner_recv,
    in_sem,
    out_sem,
    cycle_sems,
    face_sems,
    group_sems,
    owner_sems,
):
    n_gx, n_gy, n_gz = sizes
    gx, gy, gz = lax.axis_index("gx"), lax.axis_index("gy"), lax.axis_index("gz")
    points = dest_ref.shape[1]

    loads = {}
    for number, (name, src, dst) in enumerate(
        (
            ("now", now_in, now_ref),
            ("prev", prev_in, prev_ref),
            ("speed", speed_in, speed_ref),
            ("radius", radius_in, radius_ref),
            ("moduli", moduli_in, moduli_ref),
            ("second", second_in, second_ref),
            ("dest", dest_in, dest_ref),
            ("target", target_in, target_ref),
            ("source", source_in, source_ref),
            ("azimuth", azimuth_in, azimuth_ref),
            ("first", first_in, first_ref),
            ("slab", slab_in, slab_ref),
            ("before", before_in, before_ref),
            ("mass", mass_in, mass_ref),
        )
    ):
        loads[name] = pltpu.make_async_copy(src, dst, in_sem.at[number])
        loads[name].start()

    def away(axis, step):
        index, count = {"gx": (gx, n_gx), "gy": (gy, n_gy), "gz": (gz, n_gz)}[axis]
        return {axis: lax.rem(index + step + count, count)}

    barrier = pltpu.get_barrier_semaphore()
    for axis, steps in (
        ("gx", range(1, n_gx)),
        ("gy", range(1, n_gy)),
        ("gz", sorted({1, n_gz - 1})),
    ):
        for step in steps:
            pl.semaphore_signal(
                barrier, inc=1, device_id=away(axis, step), device_id_type=MESH
            )
    greeted = n_gx - 1 + n_gy - 1 + len({1, n_gz - 1})

    def push(src, dst, sems, index, device):
        copy = pltpu.make_async_remote_copy(
            src_ref=src,
            dst_ref=dst,
            send_sem=sems.at[(0, *index)],
            recv_sem=sems.at[(1, *index)],
            device_id=device,
            device_id_type=MESH,
        )
        copy.start()
        return copy

    sub = iota((8, LANES), 0)
    lane = iota((8, LANES), 1)

    mode_base = (4 * gy).astype(F32)
    row24 = iota((24, LANES), 0)
    order24 = mode_base + (
        (row24 >= 6).astype(F32) + (row24 >= 12).astype(F32) + (row24 >= 18).astype(F32)
    )
    square24 = order24 * order24
    for name in ("now", "prev", "speed", "radius"):
        loads[name].wait()
    for side, (edge, inner) in enumerate(((0, 1), (7, 6))):
        count = modes_ref[edge].astype(F32)
        mask = jnp.where(order24 < count, F32(1.0), F32(0.0))
        speed = speed_ref[edge : edge + 1, :]
        radius = radius_ref[edge : edge + 1, :]
        at_edge = now_ref[pl.ds(edge, 24, stride=8), :]
        cycle_send[side, 0:24, :] = at_edge
        cycle_send[side, 24:48, :] = mask * (
            (2.0 - 2.0 * time_sq * speed - time_sq * square24 * radius) * at_edge
            - prev_ref[pl.ds(edge, 24, stride=8), :]
            + time_sq * speed * now_ref[pl.ds(inner, 24, stride=8), :]
        )
        cycle_send[side, 48:56, :] = jnp.where(
            sub == 0, jnp.broadcast_to(speed, (8, LANES)), jnp.full((8, LANES), count, F32)
        )

    pl.semaphore_wait(barrier, greeted)

    sent = []
    cycle_in = []
    for side, step in ((0, -1), (1, 1)):
        copy = push(
            cycle_send.at[side], cycle_recv.at[side], cycle_sems, (side,), away("gx", step)
        )
        sent.append(copy)
        cycle_in.append(copy)

    last_x = jnp.where(gx < n_gx - 1, F32(1.0), F32(0.0))
    last_y = jnp.where(gy < n_gy - 1, F32(1.0), F32(0.0))
    last_z = jnp.where(gz < n_gz - 1, F32(1.0), F32(0.0))
    has_x = jnp.where(gx > 0, F32(1.0), F32(0.0))
    has_y = jnp.where(gy > 0, F32(1.0), F32(0.0))
    has_z = jnp.where(gz > 0, F32(1.0), F32(0.0))

    def send_faces(number, x_count, y_count):
        copies = []
        for side, step in ((0, -1), (1, 1)):
            for place, (axis, src, dst) in enumerate(
                (
                    ("gx", x_send.at[number, side, 0:x_count], x_recv.at[number, side, 0:x_count]),
                    ("gy", y_send.at[number, side, 0:y_count], y_recv.at[number, side, 0:y_count]),
                    ("gz", z_send.at[number, side], z_recv.at[number, side]),
                )
            ):
                copies.append(
                    push(src, dst, face_sems, (number, 2 * place + side), away(axis, step))
                )
        sent.extend(copies)
        return copies

    def columns_to_lanes(columns):
        out = jnp.zeros((8, LANES), F32)
        for number, column in enumerate(columns):
            out = jnp.where(lane == number, jnp.broadcast_to(column, (8, LANES)), out)
        return out

    loads["moduli"].wait()
    inner = [float(GRAM[k, 4, 4]) for k in range(5)]
    mu = moduli_ref[...].reshape(4, 8, LANES)
    x_send[0, 0, 0] = mu[0]
    x_send[0, 1, 0] = last_x * (
        inner[0] * mu[0] + inner[1] * mu[1] + inner[2] * mu[2] + inner[3] * mu[3]
    )
    y_send[0, 0, 0:8] = jnp.zeros((8, LANES), F32)
    y_send[0, 1, 0:8] = jnp.zeros((8, LANES), F32)
    y_send[0, 0, 0:4] = moduli_ref[pl.ds(0, 4, stride=8), :]
    y_send[0, 1, 0:4] = last_y * sum(
        inner[k] * moduli_ref[pl.ds(4 + k, 4, stride=8), :] for k in range(4)
    )
    tail = by_four(lane & 3, inner[:4]) * jnp.where(lane >= LANES - 4, last_z, F32(0.0))
    z_send[0, 0] = columns_to_lanes([mu[x][:, 0:1] for x in range(4)])
    z_send[0, 1] = columns_to_lanes(
        [jnp.sum(tail * mu[x], axis=1, keepdims=True) for x in range(4)]
    )
    moduli_copies = send_faces(0, 1, 8)

    loads["second"].wait()
    pair_second[...] = operator_pair(second_ref[...])
    counts = jnp.zeros((8, LANES), F32)
    for row in range(8):
        counts = jnp.where(sub == row, modes_ref[row].astype(F32), counts)
    order = mode_base + iota((4, 8, LANES), 0).astype(F32)
    mask = jnp.where(order < counts[None], F32(1.0), F32(0.0))
    speed, radius = speed_ref[...][None], radius_ref[...][None]
    hold = (mask * (2.0 - 2.0 * time_sq * speed - time_sq * (order * order) * radius))[:, None]
    side_weight = (mask * (time_sq * speed))[:, None]
    bend_weight = (mask * time_sq)[:, None]
    mask = mask[:, None]

    def section_sum(now, prev):
        cells = now.reshape(24, 8, LANES)
        rows = iota((24, 8, LANES), 1)
        near = jnp.where(rows == 0, F32(0.0), pltpu.roll(cells, 1, 1)) + jnp.where(
            rows == 7, F32(0.0), pltpu.roll(cells, 7, 1)
        )
        return (
            hold * now.reshape(4, 6, 8, LANES)
            - mask * prev.reshape(4, 6, 8, LANES)
            + side_weight * near.reshape(4, 6, 8, LANES)
            + bend_weight * times_operator(now, pair_second).reshape(4, 6, 8, LANES)
        )

    one_ref[...] = section_sum(now_ref[...], prev_ref[...]).reshape(192, LANES)
    edge_ref[...] = jnp.zeros((192, LANES), F32)

    for name in ("dest", "target", "source", "azimuth"):
        loads[name].wait()
    owner = dest_ref[...]
    blocks = points // LANES
    named = (iota((LANES, points), 0) == owner).astype(F32)
    named_rows = jnp.concatenate(
        [named[:, b * LANES : (b + 1) * LANES] for b in range(blocks)], axis=0
    ).astype(BF16)
    before = (iota((LANES, LANES), 0) < iota((LANES, LANES), 1)).astype(F32)
    counted = dot(
        named_rows, jnp.concatenate([before, jnp.ones_like(before)], axis=1).astype(BF16)
    )
    ranks, offset = [], None
    for b in range(blocks):
        piece = counted[b * LANES : (b + 1) * LANES]
        place = piece[:, :LANES] if offset is None else piece[:, :LANES] + offset
        ranks.append(
            jnp.sum(named[:, b * LANES : (b + 1) * LANES] * place, axis=0, keepdims=True)
        )
        offset = piece[:, LANES:] if offset is None else offset + piece[:, LANES:]
    rank = jnp.concatenate(ranks, axis=1).astype(jnp.int32)
    if n_gy == 8:
        owner_x, owner_y = owner >> 3, owner & 7
    else:
        owner_x, owner_y = owner >> 1, owner & 1
    slot = owner_x * RANKS + rank
    slot_ref[...] = (iota((LANES, points), 0) == slot).astype(F32).astype(BF16)
    target = target_ref[...]
    mine = jnp.where(owner_y == gy, F32(1.0), F32(0.0))
    sub_p = iota((8, points), 0)
    marks = jnp.where(
        sub_p == 0,
        (target >> 7).astype(F32) * mine,
        jnp.where(sub_p == 1, (target & 127).astype(F32) * mine, F32(0.0)),
    )
    marked = dot_rows(marks.astype(BF16), slot_ref[...])
    mark_ref[...] = jnp.broadcast_to(128.0 * marked[0:1] + marked[1:2], (8, LANES))
    source = source_ref[...]
    picked = (iota((LANES, points), 0) == (source & 127)).astype(F32).astype(BF16)
    pick_ref[0:LANES, :] = picked
    pick_ref[LANES:, :] = picked
    turns = (mode_base + (sub_p & 3).astype(F32)) * (azimuth_ref[...] * (0.5 / math.pi))
    turns = turns - jnp.where(sub_p >= 4, F32(0.25), F32(0.0))
    turns = turns - jnp.floor(turns + 0.5)
    square = turns * turns
    wave = jnp.full(square.shape, COSINE[-1], F32)
    for value in COSINE[-2::-1]:
        wave = wave * square + value
    in_cycle = sub_p == (source >> 7)
    for row in range(8):
        trig_ref[row] = jnp.where(
            in_cycle, jnp.broadcast_to(wave[row : row + 1], (8, points)), F32(0.0)
        )
    loads["first"].wait()
    pair_first[...] = operator_pair(first_ref[...])

    for copy in cycle_in:
        copy.wait_recv()
    flags = (last_x, has_x)
    near_edges = [cycle_recv[side, 0:24, :] for side in range(2)]
    bends = times_operator(jnp.concatenate(near_edges, axis=0), pair_second)
    beyond = []
    for side, edge in ((0, 7), (1, 0)):
        tail_rows = cycle_recv[side, 48:56, :]
        speed24 = tail_rows[0:1]
        mask24 = jnp.where(order24 < tail_rows[1:2], F32(1.0), F32(0.0))
        edge_ref[pl.ds(edge, 24, stride=8), :] = flags[side] * near_edges[side]
        value = cycle_recv[side, 24:48, :] + mask24 * time_sq * (
            speed24 * now_ref[pl.ds(edge, 24, stride=8), :] + bends[24 * side : 24 * side + 24]
        )
        beyond.append(flags[side] * value)
    one = one_ref[...].reshape(4, 6, 8, LANES) + side_weight * edge_ref[...].reshape(
        4, 6, 8, LANES
    )
    one = one.reshape(192, LANES)
    for side, edge in ((0, 7), (1, 0)):
        edge_ref[pl.ds(edge, 24, stride=8), :] = beyond[side]
    two = section_sum(one, now_ref[...]) + side_weight * edge_ref[...].reshape(4, 6, 8, LANES)
    two = two.reshape(192, LANES)
    two_ref[...] = two
    outs = [pltpu.make_async_copy(two_ref, g_out, out_sem.at[0])]
    outs[0].start()

    coef = coupling * times_operator(two, pair_first) + (coupling * impedance / time_step) * (
        two - one
    )
    high, low = halves(coef)
    at_points = dot(jnp.concatenate([high, low], axis=1), pick_ref[...]).reshape(
        4, 6, 8, points
    )
    values = jnp.zeros((8, points), F32)
    for c in range(3):
        total = jnp.zeros((8, points), F32)
        for m in range(4):
            total = total + at_points[m, 2 * c] * trig_ref[m]
            total = total + at_points[m, 2 * c + 1] * trig_ref[4 + m]
        values = jnp.where(
            (sub_p & 3) == c,
            jnp.broadcast_to(jnp.sum(total, axis=0, keepdims=True), (8, points)),
            values,
        )
    by_group = jnp.concatenate(
        [
            jnp.where(owner_y == 2 * t + (sub_p >> 2), values, F32(0.0))
            for t in range(n_gy // 2)
        ],
        axis=0,
    )
    high, low = halves(by_group)
    packed = dot_rows(jnp.concatenate([high, low], axis=0), slot_ref[...])
    packed = packed[: 4 * n_gy] + packed[4 * n_gy :]
    for group in range(n_gy):
        group_send[group] = packed[4 * group : 4 * group + 4]
    for step in range(1, n_gy):
        peer = away("gy", step)
        sent.append(
            push(
                group_send.at[peer["gy"]],
                group_recv.at[step],
                group_sems,
                (step,),
                peer,
            )
        )
    group_in = sent[-(n_gy - 1) :]

    for copy in moduli_copies:
        copy.wait_recv()
    mu_next_x = last_x * x_recv[0, 0, 0]
    sum_prev_x = x_recv[0, 1, 0]
    lane4 = iota((4, 8, LANES), 2)
    sub4 = iota((4, 8, LANES), 1)
    side_w = [0.2] + [float(v) for v in WEIGHTS[1:4]]
    first_weight = -float(WEIGHTS[4])
    weight_y = by_four(sub & 3, side_w) + jnp.where(
        sub == 0, (1.0 - has_y) * first_weight, F32(0.0)
    )
    weight_z = by_four(lane & 3, side_w) + jnp.where(
        lane == 0, (1.0 - has_z) * first_weight, F32(0.0)
    )
    weight_x = [side_w[0] + (1.0 - has_x) * first_weight] + side_w[1:]

    def make_band(axis, position, count, following, preceding, weights, has, last, band, over):
        shifted = {0: mu}
        for t in range(-4, 5):
            if t:
                rolled = pltpu.roll(mu, (-t) % count, axis)
                if t > 0:
                    rolled = jnp.where(position == count - t, following, rolled)
                shifted[t] = rolled
        pos2 = position[0]
        phase = pos2 & 3
        later = pos2 > 3
        band_values = []
        for s in range(5):
            total = None
            for t in range(s - 4, 5):
                row = [
                    GRAM[i + t, i, i + s] if 0 <= i + t <= 4 and i + s <= 4 else 0.0
                    for i in range(4)
                ]
                pattern = by_four(phase, row)
                if s == 0 and t <= 0:
                    pattern = pattern + jnp.where(
                        (phase == 0) & later, F32(GRAM[4 + t, 4, 4]), F32(0.0)
                    )
                term = pattern[None] * shifted[t]
                total = term if total is None else total + term
            if s == 0:
                total = total + jnp.where(
                    position == 0, preceding + has * float(GRAM[4, 4, 4]) * mu, F32(0.0)
                )
            band_values.append(total * weights)
        crossing = jnp.zeros_like(mu)
        for s in range(1, 5):
            crossing = jnp.where(position == count - s, band_values[s], crossing)
            inside = jnp.where(position >= count - s, F32(0.0), band_values[s])
            behind = pltpu.roll(inside, s, axis)
            if 2 * s == count:
                band[s] = inside + behind
                band[4 + s] = jnp.zeros_like(inside)
            else:
                band[s] = inside
                band[4 + s] = behind
        over[...] = last * crossing
        band[0] = band_values[0]

    y_next = y_recv[0, 0, 0:8]
    y_prev = y_recv[0, 1, 0:8]
    z_next = z_recv[0, 0]
    z_prev = z_recv[0, 1]

    def rows_of(value):
        return jnp.concatenate(
            [jnp.broadcast_to(value[x : x + 1], (8, LANES))[None] for x in range(4)], axis=0
        )

    def columns_of(value):
        return jnp.concatenate(
            [jnp.broadcast_to(value[:, x : x + 1], (8, LANES))[None] for x in range(4)], axis=0
        )

    stacked = lambda scale: jnp.concatenate([(scale(x))[None] for x in range(4)], axis=0)
    make_band(
        2,
        lane4,
        LANES,
        last_z * columns_of(z_next),
        columns_of(z_prev),
        stacked(lambda x: weight_x[x] * weight_y),
        has_z,
        last_z,
        band_z,
        over_z,
    )
    make_band(
        1,
        sub4,
        8,
        last_y * rows_of(y_next),
        rows_of(y_prev),
        stacked(lambda x: weight_x[x] * weight_z),
        has_y,
        last_y,
        band_y,
        over_y,
    )
    weight_yz = weight_y * weight_z
    planes = [mu[x] for x in range(4)] + [mu_next_x]
    for i in range(4):
        for j in range(i, 5):
            value = sum(float(GRAM[k, i, j]) * planes[k] for k in range(5))
            if i == 0 and j == 0:
                value = value + sum_prev_x + has_x * float(GRAM[4, 4, 4]) * mu[0]
            if j == 4:
                value = last_x * value
            band_x[5 * i + j] = value * weight_yz
    for x in range(4):
        band_z[0, x] = band_z[0, x] + band_y[0, x] + band_x[6 * x]

    def coupling_x(i, j):
        return band_x[5 * min(i, j) + max(i, j)]

    def face_values(number, ref):
        field = ref[...].reshape(3, 4, 8, LANES)
        for c in range(3):
            x_send[number, 0, c] = field[c, 0]
            x_send[number, 1, c] = sum(coupling_x(i, 4) * field[c, i] for i in range(4))
        y_send[number, 0, 0:12] = ref[pl.ds(0, 12, stride=8), :]
        part_ref[...] = (over_y[...][None] * field).reshape(96, LANES)
        y_send[number, 1, 0:12] = sum(
            part_ref[pl.ds(4 + k, 12, stride=8), :] for k in range(4)
        )
        z_send[number, 0] = columns_to_lanes(
            [field[c, x][:, 0:1] for c in range(3) for x in range(4)]
        )
        z_send[number, 1] = columns_to_lanes(
            [
                jnp.sum(over_z[x] * field[c, x], axis=1, keepdims=True)
                for c in range(3)
                for x in range(4)
            ]
        )
        return send_faces(number, 3, 16)

    def inner_stiffness(ref):
        field = ref[...].reshape(3, 4, 8, LANES)
        out = []
        for x in range(4):
            plane = field[:, x]
            total = band_z[0, x] * plane
            for s in range(1, 5):
                total = total + band_z[s, x] * pltpu.roll(plane, LANES - s, 2)
                total = total + band_z[4 + s, x] * pltpu.roll(plane, s, 2)
                total = total + band_y[s, x] * pltpu.roll(plane, 8 - s, 1)
                if s < 4:
                    total = total + band_y[4 + s, x] * pltpu.roll(plane, s, 1)
            for j in range(4):
                if j != x:
                    total = total + coupling_x(x, j) * field[:, j]
            out.append(total)
        return out

    def outer_stiffness(number, copies, inside):
        for copy in copies:
            copy.wait_recv()
        y_first = y_recv[number, 1, 0:12]
        y_after = y_recv[number, 0, 0:12]
        spread_ref[pl.ds(0, 12, stride=8), :] = y_first
        for k in range(4):
            spread_ref[pl.ds(4 + k, 12, stride=8), :] = y_after
        spread = spread_ref[...].reshape(3, 4, 8, LANES)
        z_first, z_after = z_recv[number, 1], z_recv[number, 0]
        x_after, x_first = x_recv[number, 0], x_recv[number, 1]
        out = []
        for x in range(4):
            rows = []
            for c in range(3):
                at = 4 * c + x
                row = inside[x][c] + coupling_x(x, 4) * x_after[c]
                row = row + jnp.where(sub == 0, F32(1.0), over_y[x]) * spread[c, x]
                row = row + jnp.where(
                    lane == 0,
                    jnp.broadcast_to(z_first[:, at : at + 1], (8, LANES)),
                    over_z[x] * jnp.broadcast_to(z_after[:, at : at + 1], (8, LANES)),
                )
                if x == 0:
                    row = row + x_first[c]
                rows.append(row)
            out.append(rows)
        return out

    spread_ref[...] = jnp.zeros((96, LANES), F32)
    loads["slab"].wait()
    now_copies = face_values(1, slab_ref)

    for copy in group_in:
        copy.wait_recv()
    total = group_send[gy]
    for step in range(1, n_gy):
        total = total + group_recv[step]
    rows16 = iota((n_gx, LANES), 0)
    lanes16 = iota((n_gx, LANES), 1)
    outgoing = jnp.zeros((n_gx, LANES), F32)
    for c in range(4):
        line = total[c : c + 1] if c < 3 else mark_ref[0:1]
        line = jnp.broadcast_to(line, (8, LANES))
        if (RANKS * (c + 1 - n_gx)) % LANES:
            line = pltpu.roll(line, (RANKS * (c + 1 - n_gx)) % LANES, 1)
        moved = pltpu.roll(
            jnp.broadcast_to(line[0:1], (n_gx, LANES)), 0, 1, stride=RANKS, stride_axis=0
        )
        outgoing = jnp.where(lanes16 >> 3 == c, moved, outgoing)
    owner_send[...] = outgoing.reshape(n_gx, 1, LANES)
    for step in range(1, n_gx):
        peer = away("gx", step)
        sent.append(
            push(
                owner_send.at[n_gx - 1 - peer["gx"]],
                owner_recv.at[step],
                owner_sems,
                (step,),
                peer,
            )
        )
    owner_in = sent[-(n_gx - 1) :]
    owner_recv[0] = owner_send[n_gx - 1 - gx]

    inside = inner_stiffness(slab_ref)
    loads["before"].wait()
    loads["mass"].wait()
    around = outer_stiffness(1, now_copies, inside)
    for x in range(4):
        scale = slab_factor * mass_ref[8 * x : 8 * x + 8, :]
        for c in range(3):
            at = 32 * c + 8 * x
            base_ref[at : at + 8, :] = (
                2.0 * slab_ref[at : at + 8, :]
                - before_ref[at : at + 8, :]
                - scale * around[x][c]
            )

    for copy in owner_in:
        copy.wait_recv()
    arrived = owner_recv[...].reshape(n_gx, LANES)
    lines = []
    moved = pltpu.roll(arrived, 0, 1, stride=RANKS, stride_axis=0)
    for c in range(4):
        own = ((lanes16 >> 3) - rows16 - c) & 15 == 0
        line = jnp.sum(jnp.where(own, moved, F32(0.0)), axis=0, keepdims=True)
        if c:
            line = pltpu.roll(jnp.broadcast_to(line, (8, LANES)), LANES - RANKS * c, 1)[0:1]
        lines.append(line)
    goal = lines[3].astype(jnp.int32)
    goal_row, goal_lane = goal >> 7, goal & 127
    rows32 = iota((32, LANES), 0)
    spots = jnp.concatenate(
        [jnp.where(rows32 == goal_row, lines[c], F32(0.0)) for c in range(3)], axis=0
    )
    high, low = halves(spots)
    on_lane = (iota((LANES, LANES), 0) == goal_lane).astype(F32).astype(BF16)
    force = dot_rows(
        jnp.concatenate([high, low], axis=1), jnp.concatenate([on_lane, on_lane], axis=1)
    )
    force_ref[...] = force
    outs.append(pltpu.make_async_copy(force_ref, force_out, out_sem.at[1]))
    outs[1].start()
    for x in range(4):
        scale = slab_factor * mass_ref[8 * x : 8 * x + 8, :]
        for c in range(3):
            at = 32 * c + 8 * x
            step_ref[at : at + 8, :] = base_ref[at : at + 8, :] + scale * force[at : at + 8]

    step_copies = face_values(2, step_ref)
    inside = inner_stiffness(step_ref)
    around = outer_stiffness(2, step_copies, inside)
    for x in range(4):
        scale = slab_factor * mass_ref[8 * x : 8 * x + 8, :]
        for c in range(3):
            at = 32 * c + 8 * x
            last_ref[at : at + 8, :] = (
                2.0 * step_ref[at : at + 8, :]
                - slab_ref[at : at + 8, :]
                + scale * (force_ref[at : at + 8, :] - around[x][c])
            )
    outs.append(pltpu.make_async_copy(last_ref, slab_out, out_sem.at[2]))
    outs[2].start()
    for copy in sent:
        copy.wait_send()
    for copy in outs:
        copy.wait()


def solution(mesh):
    n_gx, n_gy, n_gz = (mesh.shape[name] for name in ("gx", "gy", "gz"))

    def on_device(
        global_now,
        global_prev,
        cycle_modes,
        wave_speed,
        inv_radius,
        theta_second,
        theta_first,
        point_dest,
        point_target,
        point_source,
        point_azimuth,
        regional_now,
        regional_prev,
        moduli,
        inv_mass,
    ):
        points = point_target.shape[1]
        big = [((192, LANES), F32)] * 2 + [((8, LANES), F32)] * 2 + [((LANES, LANES), F32)] * 2
        big += [((1, points), jnp.int32)] * 3 + [((1, points), F32)]
        big += [((96, LANES), F32)] * 2 + [((32, LANES), F32)] * 2
        scratch = [pltpu.VMEM(shape, dtype) for shape, dtype in big]
        scratch += [
            pltpu.VMEM((192, LANES), F32),
            pltpu.VMEM((192, LANES), F32),
            pltpu.VMEM((192, LANES), F32),
            pltpu.VMEM((2 * LANES, 2 * LANES), BF16),
            pltpu.VMEM((2 * LANES, 2 * LANES), BF16),
            pltpu.VMEM((2 * LANES, points), BF16),
            pltpu.VMEM((8, 8, points), F32),
            pltpu.VMEM((LANES, points), BF16),
            pltpu.VMEM((8, LANES), F32),
            pltpu.VMEM((96, LANES), F32),
            pltpu.VMEM((96, LANES), F32),
            pltpu.VMEM((96, LANES), F32),
            pltpu.VMEM((96, LANES), F32),
            pltpu.VMEM((9, 4, 8, LANES), F32),
            pltpu.VMEM((9, 4, 8, LANES), F32),
            pltpu.VMEM((20, 8, LANES), F32),
            pltpu.VMEM((4, 8, LANES), F32),
            pltpu.VMEM((4, 8, LANES), F32),
            pltpu.VMEM((96, LANES), F32),
            pltpu.VMEM((96, LANES), F32),
            pltpu.VMEM((2, 56, LANES), F32),
            pltpu.VMEM((2, 56, LANES), F32),
            pltpu.VMEM((3, 2, 3, 8, LANES), F32),
            pltpu.VMEM((3, 2, 3, 8, LANES), F32),
            pltpu.VMEM((3, 2, 16, LANES), F32),
            pltpu.VMEM((3, 2, 16, LANES), F32),
            pltpu.VMEM((3, 2, 8, LANES), F32),
            pltpu.VMEM((3, 2, 8, LANES), F32),
            pltpu.VMEM((n_gy, 4, LANES), F32),
            pltpu.VMEM((n_gy, 4, LANES), F32),
            pltpu.VMEM((n_gx, 1, LANES), F32),
            pltpu.VMEM((n_gx, 1, LANES), F32),
            pltpu.SemaphoreType.DMA((14,)),
            pltpu.SemaphoreType.DMA((3,)),
            pltpu.SemaphoreType.DMA((2, 2)),
            pltpu.SemaphoreType.DMA((2, 3, 6)),
            pltpu.SemaphoreType.DMA((2, n_gy)),
            pltpu.SemaphoreType.DMA((2, n_gx)),
        ]
        hbm = pl.BlockSpec(memory_space=pl.ANY)
        two, slab, force = pl.pallas_call(
            functools.partial(kernel, (n_gx, n_gy, n_gz)),
            out_shape=[
                jax.ShapeDtypeStruct((192, LANES), F32),
                jax.ShapeDtypeStruct((96, LANES), F32),
                jax.ShapeDtypeStruct((96, LANES), F32),
            ],
            in_specs=[pl.BlockSpec(memory_space=pltpu.SMEM)] + [hbm] * 14,
            out_specs=[hbm] * 3,
            scratch_shapes=scratch,
            compiler_params=pltpu.CompilerParams(
                collective_id=0, has_side_effects=True, vmem_limit_bytes=48 * 2**20
            ),
        )(
            cycle_modes,
            global_now.reshape(192, LANES),
            global_prev.reshape(192, LANES),
            wave_speed,
            inv_radius,
            theta_second,
            theta_first,
            point_dest.reshape(1, points),
            point_target,
            point_source,
            point_azimuth,
            regional_now.reshape(96, LANES),
            regional_prev.reshape(96, LANES),
            moduli.reshape(32, LANES),
            inv_mass.reshape(32, LANES),
        )
        return (
            two.reshape(global_now.shape),
            slab.reshape(regional_now.shape),
            force.reshape(regional_now.shape),
        )

    return jax.shard_map(
        on_device,
        mesh=mesh,
        in_specs=(
            P("gy", None, "gx", None),
            P("gy", None, "gx", None),
            P("gx"),
            P("gx", None),
            P("gx", None),
            P(),
            P(),
            P("gz", "gx", None),
            P("gz", "gx"),
            P("gz", "gx"),
            P("gz", "gx"),
            P(None, "gx", "gy", "gz"),
            P(None, "gx", "gy", "gz"),
            P("gx", "gy", "gz"),
            P("gx", "gy", "gz"),
        ),
        out_specs=(P("gy", None, "gx", None), P(None, "gx", "gy", "gz"), P(None, "gx", "gy", "gz")),
        check_vma=False,
    )
```

```python
import functools
import math

import jax
import jax.numpy as jnp
import numpy as np
from jax import lax
from jax.experimental import pallas as pl
from jax.experimental.pallas import tpu as pltpu
from jax.sharding import PartitionSpec as P

F32 = jnp.float32
BF16 = jnp.bfloat16
MESH = pl.DeviceIdType.MESH

time_step = 0.3
time_sq = 0.09
impedance = 0.5
coupling = 0.05
slab_factor = 0.04

LANES = 128
RANKS = 8


def gll_products():
    nodes = np.array([-1.0, -math.sqrt(3.0 / 7.0), 0.0, math.sqrt(3.0 / 7.0), 1.0])
    weights = np.array([0.1, 49.0 / 90.0, 32.0 / 45.0, 49.0 / 90.0, 0.1])
    factor = np.array(
        [np.prod([nodes[i] - nodes[k] for k in range(5) if k != i]) for i in range(5)]
    )
    deriv = np.zeros((5, 5))
    for i in range(5):
        for j in range(5):
            if i != j:
                deriv[i, j] = factor[i] / factor[j] / (nodes[i] - nodes[j])
            else:
                deriv[i, j] = sum((1.0 / (nodes[i] - nodes[k]) for k in range(5) if k != i))
    return weights, np.einsum("ki,k,kj->kij", deriv, weights, deriv)


WEIGHTS, GRAM = gll_products()


def cosine_series():
    f = np.cos(np.linspace(0.0, np.pi / 2, 2001)) * 0.5
    fit = np.polynomial.chebyshev.Chebyshev.fit(f * f, np.cos(2 * np.pi * f), 8, domain=[0, 0.25])
    return [float(v) for v in fit.convert(kind=np.polynomial.Polynomial).coef]


COSINE = cosine_series()


def halves(x):
    high = x.astype(BF16)
    return high, (x - high.astype(F32)).astype(BF16)


def dot(a, b):
    return lax.dot_general(a, b, (((1,), (0,)), ((), ())), preferred_element_type=F32)


def dot_rows(a, b):
    return lax.dot_general(a, b, (((1,), (1,)), ((), ())), preferred_element_type=F32)


def operator_pair(t):
    high, low = halves(t)
    top = jnp.concatenate([high, low], axis=1)
    bottom = jnp.concatenate([high, jnp.zeros_like(low)], axis=1)
    return jnp.concatenate([top, bottom], axis=0)


def times_operator(x, pair_ref):
    high, low = halves(x)
    both = dot(jnp.concatenate([high, low], axis=1), pair_ref[...])
    return both[:, :LANES] + both[:, LANES:]


def iota(shape, axis):
    return lax.broadcasted_iota(jnp.int32, shape, axis)


def by_four(phase, values):
    out = jnp.full(phase.shape, values[3], F32)
    for i in (2, 1, 0):
        out = jnp.where(phase == i, F32(values[i]), out)
    return out


def kernel(
    sizes,
    modes_in,
    now_in,
    prev_in,
    speed_in,
    radius_in,
    second_in,
    first_in,
    dest_in,
    target_in,
    source_in,
    azimuth_in,
    slab_in,
    before_in,
    moduli_in,
    mass_in,
    g_out,
    slab_out,
    force_out,
    modes_ref,
    now_ref,
    prev_ref,
    speed_ref,
    radius_ref,
    second_ref,
    first_ref,
    dest_ref,
    target_ref,
    source_ref,
    azimuth_ref,
    slab_ref,
    before_ref,
    moduli_ref,
    mass_ref,
    one_ref,
    two_ref,
    edge_ref,
    pair_second,
    pair_first,
    pick_ref,
    trig_ref,
    slot_ref,
    mark_ref,
    base_ref,
    force_ref,
    step_ref,
    last_ref,
    band_z,
    band_y,
    band_x,
    over_z,
    over_y,
    spread_ref,
    part_ref,
    cycle_send,
    cycle_recv,
    x_send,
    x_recv,
    y_send,
    y_recv,
    z_send,
    z_recv,
    group_send,
    group_recv,
    owner_send,
    owner_recv,
    in_sem,
    out_sem,
    cycle_sems,
    face_sems,
    group_sems,
    owner_sems,
):
    n_gx, n_gy, n_gz = sizes
    gx, gy, gz = lax.axis_index("gx"), lax.axis_index("gy"), lax.axis_index("gz")
    points = dest_ref.shape[1]

    loads = {}
    for number, (name, src, dst) in enumerate(
        (
            ("modes", modes_in, modes_ref),
            ("now", now_in, now_ref),
            ("prev", prev_in, prev_ref),
            ("speed", speed_in, speed_ref),
            ("radius", radius_in, radius_ref),
            ("moduli", moduli_in, moduli_ref),
            ("second", second_in, second_ref),
            ("dest", dest_in, dest_ref),
            ("target", target_in, target_ref),
            ("source", source_in, source_ref),
            ("azimuth", azimuth_in, azimuth_ref),
            ("first", first_in, first_ref),
            ("slab", slab_in, slab_ref),
            ("before", before_in, before_ref),
            ("mass", mass_in, mass_ref),
        )
    ):
        loads[name] = pltpu.make_async_copy(src, dst, in_sem.at[number])
        loads[name].start()

    def away(axis, step):
        index, count = {"gx": (gx, n_gx), "gy": (gy, n_gy), "gz": (gz, n_gz)}[axis]
        return {axis: lax.rem(index + step + count, count)}

    barrier = pltpu.get_barrier_semaphore()
    for axis, steps in (
        ("gx", range(1, n_gx)),
        ("gy", range(1, n_gy)),
        ("gz", sorted({1, n_gz - 1})),
    ):
        for step in steps:
            pl.semaphore_signal(
                barrier, inc=1, device_id=away(axis, step), device_id_type=MESH
            )
    greeted = n_gx - 1 + n_gy - 1 + len({1, n_gz - 1})

    def push(src, dst, sems, index, device):
        copy = pltpu.make_async_remote_copy(
            src_ref=src,
            dst_ref=dst,
            send_sem=sems.at[(0, *index)],
            recv_sem=sems.at[(1, *index)],
            device_id=device,
            device_id_type=MESH,
        )
        copy.start()
        return copy

    sub = iota((8, LANES), 0)
    lane = iota((8, LANES), 1)

    mode_base = (4 * gy).astype(F32)
    row24 = iota((24, LANES), 0)
    order24 = mode_base + (
        (row24 >= 6).astype(F32) + (row24 >= 12).astype(F32) + (row24 >= 18).astype(F32)
    )
    square24 = order24 * order24
    for name in ("modes", "now", "prev", "speed", "radius"):
        loads[name].wait()
    for side, (edge, inner) in enumerate(((0, 1), (7, 6))):
        count = modes_ref[edge].astype(F32)
        mask = jnp.where(order24 < count, F32(1.0), F32(0.0))
        speed = speed_ref[edge : edge + 1, :]
        radius = radius_ref[edge : edge + 1, :]
        at_edge = now_ref[pl.ds(edge, 24, stride=8), :]
        cycle_send[side, 0:24, :] = at_edge
        cycle_send[side, 24:48, :] = mask * (
            (2.0 - 2.0 * time_sq * speed - time_sq * square24 * radius) * at_edge
            - prev_ref[pl.ds(edge, 24, stride=8), :]
            + time_sq * speed * now_ref[pl.ds(inner, 24, stride=8), :]
        )
        cycle_send[side, 48:56, :] = jnp.where(
            sub == 0, jnp.broadcast_to(speed, (8, LANES)), jnp.full((8, LANES), count, F32)
        )

    pl.semaphore_wait(barrier, greeted)

    sent = []
    cycle_in = []
    for side, step in ((0, -1), (1, 1)):
        copy = push(
            cycle_send.at[side], cycle_recv.at[side], cycle_sems, (side,), away("gx", step)
        )
        sent.append(copy)
        cycle_in.append(copy)

    last_x = jnp.where(gx < n_gx - 1, F32(1.0), F32(0.0))
    last_y = jnp.where(gy < n_gy - 1, F32(1.0), F32(0.0))
    last_z = jnp.where(gz < n_gz - 1, F32(1.0), F32(0.0))
    has_x = jnp.where(gx > 0, F32(1.0), F32(0.0))
    has_y = jnp.where(gy > 0, F32(1.0), F32(0.0))
    has_z = jnp.where(gz > 0, F32(1.0), F32(0.0))

    def send_faces(number, x_count, y_count):
        copies = []
        for side, step in ((0, -1), (1, 1)):
            for place, (axis, src, dst) in enumerate(
                (
                    ("gx", x_send.at[number, side, 0:x_count], x_recv.at[number, side, 0:x_count]),
                    ("gy", y_send.at[number, side, 0:y_count], y_recv.at[number, side, 0:y_count]),
                    ("gz", z_send.at[number, side], z_recv.at[number, side]),
                )
            ):
                copies.append(
                    push(src, dst, face_sems, (number, 2 * place + side), away(axis, step))
                )
        sent.extend(copies)
        return copies

    def columns_to_lanes(columns):
        out = jnp.zeros((8, LANES), F32)
        for number, column in enumerate(columns):
            out = jnp.where(lane == number, jnp.broadcast_to(column, (8, LANES)), out)
        return out

    loads["moduli"].wait()
    inner = [float(GRAM[k, 4, 4]) for k in range(5)]
    mu = moduli_ref[...].reshape(4, 8, LANES)
    x_send[0, 0, 0] = mu[0]
    x_send[0, 1, 0] = last_x * (
        inner[0] * mu[0] + inner[1] * mu[1] + inner[2] * mu[2] + inner[3] * mu[3]
    )
    y_send[0, 0, 0:8] = jnp.zeros((8, LANES), F32)
    y_send[0, 1, 0:8] = jnp.zeros((8, LANES), F32)
    y_send[0, 0, 0:4] = moduli_ref[pl.ds(0, 4, stride=8), :]
    y_send[0, 1, 0:4] = last_y * sum(
        inner[k] * moduli_ref[pl.ds(4 + k, 4, stride=8), :] for k in range(4)
    )
    tail = by_four(lane & 3, inner[:4]) * jnp.where(lane >= LANES - 4, last_z, F32(0.0))
    z_send[0, 0] = columns_to_lanes([mu[x][:, 0:1] for x in range(4)])
    z_send[0, 1] = columns_to_lanes(
        [jnp.sum(tail * mu[x], axis=1, keepdims=True) for x in range(4)]
    )
    moduli_copies = send_faces(0, 1, 8)

    loads["second"].wait()
    pair_second[...] = operator_pair(second_ref[...])
    counts = jnp.zeros((8, LANES), F32)
    for row in range(8):
        counts = jnp.where(sub == row, modes_ref[row].astype(F32), counts)
    order = mode_base + iota((4, 8, LANES), 0).astype(F32)
    mask = jnp.where(order < counts[None], F32(1.0), F32(0.0))
    speed, radius = speed_ref[...][None], radius_ref[...][None]
    hold = (mask * (2.0 - 2.0 * time_sq * speed - time_sq * (order * order) * radius))[:, None]
    side_weight = (mask * (time_sq * speed))[:, None]
    bend_weight = (mask * time_sq)[:, None]
    mask = mask[:, None]

    def section_sum(now, prev):
        cells = now.reshape(24, 8, LANES)
        rows = iota((24, 8, LANES), 1)
        near = jnp.where(rows == 0, F32(0.0), pltpu.roll(cells, 1, 1)) + jnp.where(
            rows == 7, F32(0.0), pltpu.roll(cells, 7, 1)
        )
        return (
            hold * now.reshape(4, 6, 8, LANES)
            - mask * prev.reshape(4, 6, 8, LANES)
            + side_weight * near.reshape(4, 6, 8, LANES)
            + bend_weight * times_operator(now, pair_second).reshape(4, 6, 8, LANES)
        )

    one_ref[...] = section_sum(now_ref[...], prev_ref[...]).reshape(192, LANES)
    edge_ref[...] = jnp.zeros((192, LANES), F32)

    for name in ("dest", "target", "source", "azimuth"):
        loads[name].wait()
    owner = dest_ref[...]
    blocks = points // LANES
    named = (iota((LANES, points), 0) == owner).astype(F32)
    named_rows = jnp.concatenate(
        [named[:, b * LANES : (b + 1) * LANES] for b in range(blocks)], axis=0
    ).astype(BF16)
    before = (iota((LANES, LANES), 0) < iota((LANES, LANES), 1)).astype(F32)
    counted = dot(
        named_rows, jnp.concatenate([before, jnp.ones_like(before)], axis=1).astype(BF16)
    )
    ranks, offset = [], None
    for b in range(blocks):
        piece = counted[b * LANES : (b + 1) * LANES]
        place = piece[:, :LANES] if offset is None else piece[:, :LANES] + offset
        ranks.append(
            jnp.sum(named[:, b * LANES : (b + 1) * LANES] * place, axis=0, keepdims=True)
        )
        offset = piece[:, LANES:] if offset is None else offset + piece[:, LANES:]
    rank = jnp.concatenate(ranks, axis=1).astype(jnp.int32)
    if n_gy == 8:
        owner_x, owner_y = owner >> 3, owner & 7
    else:
        owner_x, owner_y = owner >> 1, owner & 1
    slot = owner_x * RANKS + rank
    slot_ref[...] = (iota((LANES, points), 0) == slot).astype(F32).astype(BF16)
    target = target_ref[...]
    mine = jnp.where(owner_y == gy, F32(1.0), F32(0.0))
    sub_p = iota((8, points), 0)
    marks = jnp.where(
        sub_p == 0,
        (target >> 7).astype(F32) * mine,
        jnp.where(sub_p == 1, (target & 127).astype(F32) * mine, F32(0.0)),
    )
    marked = dot_rows(marks.astype(BF16), slot_ref[...])
    mark_ref[...] = jnp.broadcast_to(128.0 * marked[0:1] + marked[1:2], (8, LANES))
    source = source_ref[...]
    picked = (iota((LANES, points), 0) == (source & 127)).astype(F32).astype(BF16)
    pick_ref[0:LANES, :] = picked
    pick_ref[LANES:, :] = picked
    turns = (mode_base + (sub_p & 3).astype(F32)) * (azimuth_ref[...] * (0.5 / math.pi))
    turns = turns - jnp.where(sub_p >= 4, F32(0.25), F32(0.0))
    turns = turns - jnp.floor(turns + 0.5)
    square = turns * turns
    wave = jnp.full(square.shape, COSINE[-1], F32)
    for value in COSINE[-2::-1]:
        wave = wave * square + value
    in_cycle = sub_p == (source >> 7)
    for row in range(8):
        trig_ref[row] = jnp.where(
            in_cycle, jnp.broadcast_to(wave[row : row + 1], (8, points)), F32(0.0)
        )
    loads["first"].wait()
    pair_first[...] = operator_pair(first_ref[...])

    for copy in cycle_in:
        copy.wait_recv()
    flags = (last_x, has_x)
    near_edges = [cycle_recv[side, 0:24, :] for side in range(2)]
    bends = times_operator(jnp.concatenate(near_edges, axis=0), pair_second)
    beyond = []
    for side, edge in ((0, 7), (1, 0)):
        tail_rows = cycle_recv[side, 48:56, :]
        speed24 = tail_rows[0:1]
        mask24 = jnp.where(order24 < tail_rows[1:2], F32(1.0), F32(0.0))
        edge_ref[pl.ds(edge, 24, stride=8), :] = flags[side] * near_edges[side]
        value = cycle_recv[side, 24:48, :] + mask24 * time_sq * (
            speed24 * now_ref[pl.ds(edge, 24, stride=8), :] + bends[24 * side : 24 * side + 24]
        )
        beyond.append(flags[side] * value)
    one = one_ref[...].reshape(4, 6, 8, LANES) + side_weight * edge_ref[...].reshape(
        4, 6, 8, LANES
    )
    one = one.reshape(192, LANES)
    for side, edge in ((0, 7), (1, 0)):
        edge_ref[pl.ds(edge, 24, stride=8), :] = beyond[side]
    two = section_sum(one, now_ref[...]) + side_weight * edge_ref[...].reshape(4, 6, 8, LANES)
    two = two.reshape(192, LANES)
    two_ref[...] = two
    outs = [pltpu.make_async_copy(two_ref, g_out, out_sem.at[0])]
    outs[0].start()

    coef = coupling * times_operator(two, pair_first) + (coupling * impedance / time_step) * (
        two - one
    )
    high, low = halves(coef)
    at_points = dot(jnp.concatenate([high, low], axis=1), pick_ref[...]).reshape(
        4, 6, 8, points
    )
    values = jnp.zeros((8, points), F32)
    for c in range(3):
        total = jnp.zeros((8, points), F32)
        for m in range(4):
            total = total + at_points[m, 2 * c] * trig_ref[m]
            total = total + at_points[m, 2 * c + 1] * trig_ref[4 + m]
        values = jnp.where(
            (sub_p & 3) == c,
            jnp.broadcast_to(jnp.sum(total, axis=0, keepdims=True), (8, points)),
            values,
        )
    by_group = jnp.concatenate(
        [
            jnp.where(owner_y == 2 * t + (sub_p >> 2), values, F32(0.0))
            for t in range(n_gy // 2)
        ],
        axis=0,
    )
    high, low = halves(by_group)
    packed = dot_rows(jnp.concatenate([high, low], axis=0), slot_ref[...])
    packed = packed[: 4 * n_gy] + packed[4 * n_gy :]
    for group in range(n_gy):
        group_send[group] = packed[4 * group : 4 * group + 4]
    for step in range(1, n_gy):
        peer = away("gy", step)
        sent.append(
            push(
                group_send.at[peer["gy"]],
                group_recv.at[step],
                group_sems,
                (step,),
                peer,
            )
        )
    group_in = sent[-(n_gy - 1) :]

    for copy in moduli_copies:
        copy.wait_recv()
    mu_next_x = last_x * x_recv[0, 0, 0]
    sum_prev_x = x_recv[0, 1, 0]
    lane4 = iota((4, 8, LANES), 2)
    sub4 = iota((4, 8, LANES), 1)
    side_w = [0.2] + [float(v) for v in WEIGHTS[1:4]]
    first_weight = -float(WEIGHTS[4])
    weight_y = by_four(sub & 3, side_w) + jnp.where(
        sub == 0, (1.0 - has_y) * first_weight, F32(0.0)
    )
    weight_z = by_four(lane & 3, side_w) + jnp.where(
        lane == 0, (1.0 - has_z) * first_weight, F32(0.0)
    )
    weight_x = [side_w[0] + (1.0 - has_x) * first_weight] + side_w[1:]

    def make_band(axis, position, count, following, preceding, weights, has, last, band, over):
        shifted = {0: mu}
        for t in range(-4, 5):
            if t:
                rolled = pltpu.roll(mu, (-t) % count, axis)
                if t > 0:
                    rolled = jnp.where(position == count - t, following, rolled)
                shifted[t] = rolled
        pos2 = position[0]
        phase = pos2 & 3
        later = pos2 > 3
        band_values = []
        for s in range(5):
            total = None
            for t in range(s - 4, 5):
                row = [
                    GRAM[i + t, i, i + s] if 0 <= i + t <= 4 and i + s <= 4 else 0.0
                    for i in range(4)
                ]
                pattern = by_four(phase, row)
                if s == 0 and t <= 0:
                    pattern = pattern + jnp.where(
                        (phase == 0) & later, F32(GRAM[4 + t, 4, 4]), F32(0.0)
                    )
                term = pattern[None] * shifted[t]
                total = term if total is None else total + term
            if s == 0:
                total = total + jnp.where(
                    position == 0, preceding + has * float(GRAM[4, 4, 4]) * mu, F32(0.0)
                )
            band_values.append(total * weights)
        crossing = jnp.zeros_like(mu)
        for s in range(1, 5):
            crossing = jnp.where(position == count - s, band_values[s], crossing)
            inside = jnp.where(position >= count - s, F32(0.0), band_values[s])
            behind = pltpu.roll(inside, s, axis)
            if 2 * s == count:
                band[s] = inside + behind
                band[4 + s] = jnp.zeros_like(inside)
            else:
                band[s] = inside
                band[4 + s] = behind
        over[...] = last * crossing
        band[0] = band_values[0]

    y_next = y_recv[0, 0, 0:8]
    y_prev = y_recv[0, 1, 0:8]
    z_next = z_recv[0, 0]
    z_prev = z_recv[0, 1]

    def rows_of(value):
        return jnp.concatenate(
            [jnp.broadcast_to(value[x : x + 1], (8, LANES))[None] for x in range(4)], axis=0
        )

    def columns_of(value):
        return jnp.concatenate(
            [jnp.broadcast_to(value[:, x : x + 1], (8, LANES))[None] for x in range(4)], axis=0
        )

    stacked = lambda scale: jnp.concatenate([(scale(x))[None] for x in range(4)], axis=0)
    make_band(
        2,
        lane4,
        LANES,
        last_z * columns_of(z_next),
        columns_of(z_prev),
        stacked(lambda x: weight_x[x] * weight_y),
        has_z,
        last_z,
        band_z,
        over_z,
    )
    make_band(
        1,
        sub4,
        8,
        last_y * rows_of(y_next),
        rows_of(y_prev),
        stacked(lambda x: weight_x[x] * weight_z),
        has_y,
        last_y,
        band_y,
        over_y,
    )
    weight_yz = weight_y * weight_z
    planes = [mu[x] for x in range(4)] + [mu_next_x]
    for i in range(4):
        for j in range(i, 5):
            value = sum(float(GRAM[k, i, j]) * planes[k] for k in range(5))
            if i == 0 and j == 0:
                value = value + sum_prev_x + has_x * float(GRAM[4, 4, 4]) * mu[0]
            if j == 4:
                value = last_x * value
            band_x[5 * i + j] = value * weight_yz
    for x in range(4):
        band_z[0, x] = band_z[0, x] + band_y[0, x] + band_x[6 * x]

    def coupling_x(i, j):
        return band_x[5 * min(i, j) + max(i, j)]

    def face_values(number, ref):
        field = ref[...].reshape(3, 4, 8, LANES)
        for c in range(3):
            x_send[number, 0, c] = field[c, 0]
            x_send[number, 1, c] = sum(coupling_x(i, 4) * field[c, i] for i in range(4))
        y_send[number, 0, 0:12] = ref[pl.ds(0, 12, stride=8), :]
        part_ref[...] = (over_y[...][None] * field).reshape(96, LANES)
        y_send[number, 1, 0:12] = sum(
            part_ref[pl.ds(4 + k, 12, stride=8), :] for k in range(4)
        )
        z_send[number, 0] = columns_to_lanes(
            [field[c, x][:, 0:1] for c in range(3) for x in range(4)]
        )
        z_send[number, 1] = columns_to_lanes(
            [
                jnp.sum(over_z[x] * field[c, x], axis=1, keepdims=True)
                for c in range(3)
                for x in range(4)
            ]
        )
        return send_faces(number, 3, 16)

    def inner_stiffness(ref):
        field = ref[...].reshape(3, 4, 8, LANES)
        out = []
        for x in range(4):
            plane = field[:, x]
            total = band_z[0, x] * plane
            for s in range(1, 5):
                total = total + band_z[s, x] * pltpu.roll(plane, LANES - s, 2)
                total = total + band_z[4 + s, x] * pltpu.roll(plane, s, 2)
                total = total + band_y[s, x] * pltpu.roll(plane, 8 - s, 1)
                if s < 4:
                    total = total + band_y[4 + s, x] * pltpu.roll(plane, s, 1)
            for j in range(4):
                if j != x:
                    total = total + coupling_x(x, j) * field[:, j]
            out.append(total)
        return out

    def outer_stiffness(number, copies, inside):
        for copy in copies:
            copy.wait_recv()
        y_first = y_recv[number, 1, 0:12]
        y_after = y_recv[number, 0, 0:12]
        spread_ref[pl.ds(0, 12, stride=8), :] = y_first
        for k in range(4):
            spread_ref[pl.ds(4 + k, 12, stride=8), :] = y_after
        spread = spread_ref[...].reshape(3, 4, 8, LANES)
        z_first, z_after = z_recv[number, 1], z_recv[number, 0]
        x_after, x_first = x_recv[number, 0], x_recv[number, 1]
        out = []
        for x in range(4):
            rows = []
            for c in range(3):
                at = 4 * c + x
                row = inside[x][c] + coupling_x(x, 4) * x_after[c]
                row = row + jnp.where(sub == 0, F32(1.0), over_y[x]) * spread[c, x]
                row = row + jnp.where(
                    lane == 0,
                    jnp.broadcast_to(z_first[:, at : at + 1], (8, LANES)),
                    over_z[x] * jnp.broadcast_to(z_after[:, at : at + 1], (8, LANES)),
                )
                if x == 0:
                    row = row + x_first[c]
                rows.append(row)
            out.append(rows)
        return out

    spread_ref[...] = jnp.zeros((96, LANES), F32)
    loads["slab"].wait()
    now_copies = face_values(1, slab_ref)

    for copy in group_in:
        copy.wait_recv()
    total = group_send[gy]
    for step in range(1, n_gy):
        total = total + group_recv[step]
    rows16 = iota((n_gx, LANES), 0)
    lanes16 = iota((n_gx, LANES), 1)
    outgoing = jnp.zeros((n_gx, LANES), F32)
    for c in range(4):
        line = total[c : c + 1] if c < 3 else mark_ref[0:1]
        line = jnp.broadcast_to(line, (8, LANES))
        if (RANKS * (c + 1 - n_gx)) % LANES:
            line = pltpu.roll(line, (RANKS * (c + 1 - n_gx)) % LANES, 1)
        moved = pltpu.roll(
            jnp.broadcast_to(line[0:1], (n_gx, LANES)), 0, 1, stride=RANKS, stride_axis=0
        )
        outgoing = jnp.where(lanes16 >> 3 == c, moved, outgoing)
    owner_send[...] = outgoing.reshape(n_gx, 1, LANES)
    for step in range(1, n_gx):
        peer = away("gx", step)
        sent.append(
            push(
                owner_send.at[n_gx - 1 - peer["gx"]],
                owner_recv.at[step],
                owner_sems,
                (step,),
                peer,
            )
        )
    owner_in = sent[-(n_gx - 1) :]
    owner_recv[0] = owner_send[n_gx - 1 - gx]

    inside = inner_stiffness(slab_ref)
    loads["before"].wait()
    loads["mass"].wait()
    around = outer_stiffness(1, now_copies, inside)
    for x in range(4):
        scale = slab_factor * mass_ref[8 * x : 8 * x + 8, :]
        for c in range(3):
            at = 32 * c + 8 * x
            base_ref[at : at + 8, :] = (
                2.0 * slab_ref[at : at + 8, :]
                - before_ref[at : at + 8, :]
                - scale * around[x][c]
            )

    for copy in owner_in:
        copy.wait_recv()
    arrived = owner_recv[...].reshape(n_gx, LANES)
    lines = []
    moved = pltpu.roll(arrived, 0, 1, stride=RANKS, stride_axis=0)
    for c in range(4):
        own = ((lanes16 >> 3) - rows16 - c) & 15 == 0
        line = jnp.sum(jnp.where(own, moved, F32(0.0)), axis=0, keepdims=True)
        if c:
            line = pltpu.roll(jnp.broadcast_to(line, (8, LANES)), LANES - RANKS * c, 1)[0:1]
        lines.append(line)
    goal = lines[3].astype(jnp.int32)
    goal_row, goal_lane = goal >> 7, goal & 127
    rows32 = iota((32, LANES), 0)
    spots = jnp.concatenate(
        [jnp.where(rows32 == goal_row, lines[c], F32(0.0)) for c in range(3)], axis=0
    )
    high, low = halves(spots)
    on_lane = (iota((LANES, LANES), 0) == goal_lane).astype(F32).astype(BF16)
    force = dot_rows(
        jnp.concatenate([high, low], axis=1), jnp.concatenate([on_lane, on_lane], axis=1)
    )
    force_ref[...] = force
    outs.append(pltpu.make_async_copy(force_ref, force_out, out_sem.at[1]))
    outs[1].start()
    for x in range(4):
        scale = slab_factor * mass_ref[8 * x : 8 * x + 8, :]
        for c in range(3):
            at = 32 * c + 8 * x
            step_ref[at : at + 8, :] = base_ref[at : at + 8, :] + scale * force[at : at + 8]

    step_copies = face_values(2, step_ref)
    inside = inner_stiffness(step_ref)
    around = outer_stiffness(2, step_copies, inside)
    for x in range(4):
        scale = slab_factor * mass_ref[8 * x : 8 * x + 8, :]
        for c in range(3):
            at = 32 * c + 8 * x
            last_ref[at : at + 8, :] = (
                2.0 * step_ref[at : at + 8, :]
                - slab_ref[at : at + 8, :]
                + scale * (force_ref[at : at + 8, :] - around[x][c])
            )
    outs.append(pltpu.make_async_copy(last_ref, slab_out, out_sem.at[2]))
    outs[2].start()
    for copy in sent:
        copy.wait_send()
    for copy in outs:
        copy.wait()


def copy_out(*refs):
    sems = refs[6]
    copies = [pltpu.make_async_copy(refs[i], refs[3 + i], sems.at[i]) for i in range(3)]
    for copy in copies:
        copy.start()
    for copy in copies:
        copy.wait()


def solution(mesh):
    n_gx, n_gy, n_gz = (mesh.shape[name] for name in ("gx", "gy", "gz"))

    def on_device(
        global_now,
        global_prev,
        cycle_modes,
        wave_speed,
        inv_radius,
        theta_second,
        theta_first,
        point_dest,
        point_target,
        point_source,
        point_azimuth,
        regional_now,
        regional_prev,
        moduli,
        inv_mass,
    ):
        points = point_target.shape[1]
        big = [((192, LANES), F32)] * 2 + [((8, LANES), F32)] * 2 + [((LANES, LANES), F32)] * 2
        big += [((1, points), jnp.int32)] * 3 + [((1, points), F32)]
        big += [((96, LANES), F32)] * 2 + [((32, LANES), F32)] * 2
        scratch = [pltpu.SMEM(cycle_modes.shape, jnp.int32)]
        scratch += [pltpu.VMEM(shape, dtype) for shape, dtype in big]
        scratch += [
            pltpu.VMEM((192, LANES), F32),
            pltpu.VMEM((192, LANES), F32),
            pltpu.VMEM((192, LANES), F32),
            pltpu.VMEM((2 * LANES, 2 * LANES), BF16),
            pltpu.VMEM((2 * LANES, 2 * LANES), BF16),
            pltpu.VMEM((2 * LANES, points), BF16),
            pltpu.VMEM((8, 8, points), F32),
            pltpu.VMEM((LANES, points), BF16),
            pltpu.VMEM((8, LANES), F32),
            pltpu.VMEM((96, LANES), F32),
            pltpu.VMEM((96, LANES), F32),
            pltpu.VMEM((96, LANES), F32),
            pltpu.VMEM((96, LANES), F32),
            pltpu.VMEM((9, 4, 8, LANES), F32),
            pltpu.VMEM((9, 4, 8, LANES), F32),
            pltpu.VMEM((20, 8, LANES), F32),
            pltpu.VMEM((4, 8, LANES), F32),
            pltpu.VMEM((4, 8, LANES), F32),
            pltpu.VMEM((96, LANES), F32),
            pltpu.VMEM((96, LANES), F32),
            pltpu.VMEM((2, 56, LANES), F32),
            pltpu.VMEM((2, 56, LANES), F32),
            pltpu.VMEM((3, 2, 3, 8, LANES), F32),
            pltpu.VMEM((3, 2, 3, 8, LANES), F32),
            pltpu.VMEM((3, 2, 16, LANES), F32),
            pltpu.VMEM((3, 2, 16, LANES), F32),
            pltpu.VMEM((3, 2, 8, LANES), F32),
            pltpu.VMEM((3, 2, 8, LANES), F32),
            pltpu.VMEM((n_gy, 4, LANES), F32),
            pltpu.VMEM((n_gy, 4, LANES), F32),
            pltpu.VMEM((n_gx, 1, LANES), F32),
            pltpu.VMEM((n_gx, 1, LANES), F32),
            pltpu.SemaphoreType.DMA((15,)),
            pltpu.SemaphoreType.DMA((3,)),
            pltpu.SemaphoreType.DMA((2, 2)),
            pltpu.SemaphoreType.DMA((2, 3, 6)),
            pltpu.SemaphoreType.DMA((2, n_gy)),
            pltpu.SemaphoreType.DMA((2, n_gx)),
        ]
        hbm = pl.BlockSpec(memory_space=pl.ANY)
        two, slab, force = pl.pallas_call(
            functools.partial(kernel, (n_gx, n_gy, n_gz)),
            out_shape=[
                pltpu.VMEM((192, LANES), F32),
                pltpu.VMEM((96, LANES), F32),
                pltpu.VMEM((96, LANES), F32),
            ],
            in_specs=[hbm] * 15,
            out_specs=[hbm] * 3,
            scratch_shapes=scratch,
            compiler_params=pltpu.CompilerParams(
                collective_id=0, has_side_effects=True, vmem_limit_bytes=48 * 2**20
            ),
        )(
            *[
                pltpu.with_memory_space_constraint(x, pltpu.HBM)
                for x in (
            cycle_modes,
            global_now.reshape(192, LANES),
            global_prev.reshape(192, LANES),
            wave_speed,
            inv_radius,
            theta_second,
            theta_first,
            point_dest.reshape(1, points),
            point_target,
            point_source,
            point_azimuth,
            regional_now.reshape(96, LANES),
            regional_prev.reshape(96, LANES),
            moduli.reshape(32, LANES),
            inv_mass.reshape(32, LANES),
            )]
        )
        two, slab, force = pl.pallas_call(
            copy_out,
            out_shape=[
                jax.ShapeDtypeStruct((192, LANES), F32),
                jax.ShapeDtypeStruct((96, LANES), F32),
                jax.ShapeDtypeStruct((96, LANES), F32),
            ],
            in_specs=[hbm] * 3,
            out_specs=[hbm] * 3,
            scratch_shapes=[pltpu.SemaphoreType.DMA((3,))],
        )(two, slab, force)
        return (
            two.reshape(global_now.shape),
            slab.reshape(regional_now.shape),
            force.reshape(regional_now.shape),
        )

    return jax.shard_map(
        on_device,
        mesh=mesh,
        in_specs=(
            P("gy", None, "gx", None),
            P("gy", None, "gx", None),
            P("gx"),
            P("gx", None),
            P("gx", None),
            P(),
            P(),
            P("gz", "gx", None),
            P("gz", "gx"),
            P("gz", "gx"),
            P("gz", "gx"),
            P(None, "gx", "gy", "gz"),
            P(None, "gx", "gy", "gz"),
            P("gx", "gy", "gz"),
            P("gx", "gy", "gz"),
        ),
        out_specs=(P("gy", None, "gx", None), P(None, "gx", "gy", "gz"), P(None, "gx", "gy", "gz")),
        check_vma=False,
    )
```

```python
import functools
import math

import jax
import jax.numpy as jnp
import numpy as np
from jax import lax
from jax.experimental import pallas as pl
from jax.experimental.pallas import tpu as pltpu
from jax.sharding import PartitionSpec as P

F32 = jnp.float32
BF16 = jnp.bfloat16
MESH = pl.DeviceIdType.MESH

time_step = 0.3
time_sq = 0.09
impedance = 0.5
coupling = 0.05
slab_factor = 0.04

LANES = 128
RANKS = 8


def gll_products():
    nodes = np.array([-1.0, -math.sqrt(3.0 / 7.0), 0.0, math.sqrt(3.0 / 7.0), 1.0])
    weights = np.array([0.1, 49.0 / 90.0, 32.0 / 45.0, 49.0 / 90.0, 0.1])
    factor = np.array(
        [np.prod([nodes[i] - nodes[k] for k in range(5) if k != i]) for i in range(5)]
    )
    deriv = np.zeros((5, 5))
    for i in range(5):
        for j in range(5):
            if i != j:
                deriv[i, j] = factor[i] / factor[j] / (nodes[i] - nodes[j])
            else:
                deriv[i, j] = sum((1.0 / (nodes[i] - nodes[k]) for k in range(5) if k != i))
    return weights, np.einsum("ki,k,kj->kij", deriv, weights, deriv)


WEIGHTS, GRAM = gll_products()


def cosine_series():
    f = np.cos(np.linspace(0.0, np.pi / 2, 2001)) * 0.5
    fit = np.polynomial.chebyshev.Chebyshev.fit(f * f, np.cos(2 * np.pi * f), 8, domain=[0, 0.25])
    return [float(v) for v in fit.convert(kind=np.polynomial.Polynomial).coef]


COSINE = cosine_series()


def halves(x):
    high = x.astype(BF16)
    return high, (x - high.astype(F32)).astype(BF16)


def dot(a, b):
    return lax.dot_general(a, b, (((1,), (0,)), ((), ())), preferred_element_type=F32)


def dot_rows(a, b):
    return lax.dot_general(a, b, (((1,), (1,)), ((), ())), preferred_element_type=F32)


def operator_pair(t):
    high, low = halves(t)
    top = jnp.concatenate([high, low], axis=1)
    bottom = jnp.concatenate([high, jnp.zeros_like(low)], axis=1)
    return jnp.concatenate([top, bottom], axis=0)


def times_operator(x, pair_ref):
    high, low = halves(x)
    both = dot(jnp.concatenate([high, low], axis=1), pair_ref[...])
    return both[:, :LANES] + both[:, LANES:]


def iota(shape, axis):
    return lax.broadcasted_iota(jnp.int32, shape, axis)


def by_four(phase, values):
    out = jnp.full(phase.shape, values[3], F32)
    for i in (2, 1, 0):
        out = jnp.where(phase == i, F32(values[i]), out)
    return out


def kernel(
    sizes,
    modes_in,
    now_in,
    prev_in,
    speed_in,
    radius_in,
    second_in,
    first_in,
    dest_in,
    target_in,
    source_in,
    azimuth_in,
    slab_in,
    before_in,
    moduli_in,
    mass_in,
    g_out,
    slab_out,
    force_out,
    modes_ref,
    now_ref,
    prev_ref,
    speed_ref,
    radius_ref,
    second_ref,
    first_ref,
    dest_ref,
    target_ref,
    source_ref,
    azimuth_ref,
    slab_ref,
    before_ref,
    moduli_ref,
    mass_ref,
    one_ref,
    two_ref,
    edge_ref,
    pair_second,
    pair_first,
    pick_ref,
    trig_ref,
    slot_ref,
    mark_ref,
    base_ref,
    force_ref,
    step_ref,
    last_ref,
    band_z,
    band_y,
    band_x,
    over_z,
    over_y,
    spread_ref,
    part_ref,
    cycle_send,
    cycle_recv,
    x_send,
    x_recv,
    y_send,
    y_recv,
    z_send,
    z_recv,
    group_send,
    group_recv,
    owner_send,
    owner_recv,
    in_sem,
    out_sem,
    cycle_sems,
    face_sems,
    group_sems,
    owner_sems,
):
    n_gx, n_gy, n_gz = sizes
    gx, gy, gz = lax.axis_index("gx"), lax.axis_index("gy"), lax.axis_index("gz")
    points = dest_ref.shape[1]

    loads = {}
    for number, (name, src, dst) in enumerate(
        (
            ("modes", modes_in, modes_ref),
            ("now", now_in, now_ref),
            ("prev", prev_in, prev_ref),
            ("speed", speed_in, speed_ref),
            ("radius", radius_in, radius_ref),
            ("moduli", moduli_in, moduli_ref),
            ("second", second_in, second_ref),
            ("dest", dest_in, dest_ref),
            ("target", target_in, target_ref),
            ("source", source_in, source_ref),
            ("azimuth", azimuth_in, azimuth_ref),
            ("first", first_in, first_ref),
            ("slab", slab_in, slab_ref),
            ("before", before_in, before_ref),
            ("mass", mass_in, mass_ref),
        )
    ):
        loads[name] = pltpu.make_async_copy(src, dst, in_sem.at[number])
        loads[name].start()

    def away(axis, step):
        index, count = {"gx": (gx, n_gx), "gy": (gy, n_gy), "gz": (gz, n_gz)}[axis]
        return {axis: lax.rem(index + step + count, count)}

    barrier = pltpu.get_barrier_semaphore()
    for axis, steps in (
        ("gx", range(1, n_gx)),
        ("gy", range(1, n_gy)),
        ("gz", sorted({1, n_gz - 1})),
    ):
        for step in steps:
            pl.semaphore_signal(
                barrier, inc=1, device_id=away(axis, step), device_id_type=MESH
            )
    greeted = n_gx - 1 + n_gy - 1 + len({1, n_gz - 1})

    def push(src, dst, sems, index, device):
        copy = pltpu.make_async_remote_copy(
            src_ref=src,
            dst_ref=dst,
            send_sem=sems.at[(0, *index)],
            recv_sem=sems.at[(1, *index)],
            device_id=device,
            device_id_type=MESH,
        )
        copy.start()
        return copy

    sub = iota((8, LANES), 0)
    lane = iota((8, LANES), 1)

    mode_base = (4 * gy).astype(F32)
    row24 = iota((24, LANES), 0)
    order24 = mode_base + (
        (row24 >= 6).astype(F32) + (row24 >= 12).astype(F32) + (row24 >= 18).astype(F32)
    )
    square24 = order24 * order24
    for name in ("modes", "now", "prev", "speed", "radius"):
        loads[name].wait()
    for side, (edge, inner) in enumerate(((0, 1), (7, 6))):
        count = modes_ref[edge].astype(F32)
        mask = jnp.where(order24 < count, F32(1.0), F32(0.0))
        speed = speed_ref[edge : edge + 1, :]
        radius = radius_ref[edge : edge + 1, :]
        at_edge = now_ref[pl.ds(edge, 24, stride=8), :]
        cycle_send[side, 0:24, :] = at_edge
        cycle_send[side, 24:48, :] = mask * (
            (2.0 - 2.0 * time_sq * speed - time_sq * square24 * radius) * at_edge
            - prev_ref[pl.ds(edge, 24, stride=8), :]
            + time_sq * speed * now_ref[pl.ds(inner, 24, stride=8), :]
        )
        cycle_send[side, 48:56, :] = jnp.where(
            sub == 0, jnp.broadcast_to(speed, (8, LANES)), jnp.full((8, LANES), count, F32)
        )

    pl.semaphore_wait(barrier, greeted)

    sent = []
    cycle_in = []
    for side, step in ((0, -1), (1, 1)):
        copy = push(
            cycle_send.at[side], cycle_recv.at[side], cycle_sems, (side,), away("gx", step)
        )
        sent.append(copy)
        cycle_in.append(copy)

    last_x = jnp.where(gx < n_gx - 1, F32(1.0), F32(0.0))
    last_y = jnp.where(gy < n_gy - 1, F32(1.0), F32(0.0))
    last_z = jnp.where(gz < n_gz - 1, F32(1.0), F32(0.0))
    has_x = jnp.where(gx > 0, F32(1.0), F32(0.0))
    has_y = jnp.where(gy > 0, F32(1.0), F32(0.0))
    has_z = jnp.where(gz > 0, F32(1.0), F32(0.0))

    def send_faces(number, x_count, y_count):
        copies = []
        for side, step in ((0, -1), (1, 1)):
            for place, (axis, src, dst) in enumerate(
                (
                    ("gx", x_send.at[number, side, 0:x_count], x_recv.at[number, side, 0:x_count]),
                    ("gy", y_send.at[number, side, 0:y_count], y_recv.at[number, side, 0:y_count]),
                    ("gz", z_send.at[number, side], z_recv.at[number, side]),
                )
            ):
                copies.append(
                    push(src, dst, face_sems, (number, 2 * place + side), away(axis, step))
                )
        sent.extend(copies)
        return copies

    def columns_to_lanes(columns):
        out = jnp.zeros((8, LANES), F32)
        for number, column in enumerate(columns):
            out = jnp.where(lane == number, jnp.broadcast_to(column, (8, LANES)), out)
        return out

    loads["moduli"].wait()
    inner = [float(GRAM[k, 4, 4]) for k in range(5)]
    mu = moduli_ref[...].reshape(4, 8, LANES)
    x_send[0, 0, 0] = mu[0]
    x_send[0, 1, 0] = last_x * (
        inner[0] * mu[0] + inner[1] * mu[1] + inner[2] * mu[2] + inner[3] * mu[3]
    )
    y_send[0, 0, 0:8] = jnp.zeros((8, LANES), F32)
    y_send[0, 1, 0:8] = jnp.zeros((8, LANES), F32)
    y_send[0, 0, 0:4] = moduli_ref[pl.ds(0, 4, stride=8), :]
    y_send[0, 1, 0:4] = last_y * sum(
        inner[k] * moduli_ref[pl.ds(4 + k, 4, stride=8), :] for k in range(4)
    )
    tail = by_four(lane & 3, inner[:4]) * jnp.where(lane >= LANES - 4, last_z, F32(0.0))
    z_send[0, 0] = columns_to_lanes([mu[x][:, 0:1] for x in range(4)])
    z_send[0, 1] = columns_to_lanes(
        [jnp.sum(tail * mu[x], axis=1, keepdims=True) for x in range(4)]
    )
    moduli_copies = send_faces(0, 1, 8)

    loads["second"].wait()
    pair_second[...] = operator_pair(second_ref[...])
    counts = jnp.zeros((8, LANES), F32)
    for row in range(8):
        counts = jnp.where(sub == row, modes_ref[row].astype(F32), counts)
    order = mode_base + iota((4, 8, LANES), 0).astype(F32)
    mask = jnp.where(order < counts[None], F32(1.0), F32(0.0))
    speed, radius = speed_ref[...][None], radius_ref[...][None]
    hold = (mask * (2.0 - 2.0 * time_sq * speed - time_sq * (order * order) * radius))[:, None]
    side_weight = (mask * (time_sq * speed))[:, None]
    bend_weight = (mask * time_sq)[:, None]
    mask = mask[:, None]

    def section_sum(now, prev):
        cells = now.reshape(24, 8, LANES)
        rows = iota((24, 8, LANES), 1)
        near = jnp.where(rows == 0, F32(0.0), pltpu.roll(cells, 1, 1)) + jnp.where(
            rows == 7, F32(0.0), pltpu.roll(cells, 7, 1)
        )
        return (
            hold * now.reshape(4, 6, 8, LANES)
            - mask * prev.reshape(4, 6, 8, LANES)
            + side_weight * near.reshape(4, 6, 8, LANES)
            + bend_weight * times_operator(now, pair_second).reshape(4, 6, 8, LANES)
        )

    one_ref[...] = section_sum(now_ref[...], prev_ref[...]).reshape(192, LANES)
    edge_ref[...] = jnp.zeros((192, LANES), F32)

    for name in ("dest", "target", "source", "azimuth"):
        loads[name].wait()
    owner = dest_ref[...]
    blocks = points // LANES
    named = (iota((LANES, points), 0) == owner).astype(F32)
    named_rows = jnp.concatenate(
        [named[:, b * LANES : (b + 1) * LANES] for b in range(blocks)], axis=0
    ).astype(BF16)
    before = (iota((LANES, LANES), 0) < iota((LANES, LANES), 1)).astype(F32)
    counted = dot(
        named_rows, jnp.concatenate([before, jnp.ones_like(before)], axis=1).astype(BF16)
    )
    ranks, offset = [], None
    for b in range(blocks):
        piece = counted[b * LANES : (b + 1) * LANES]
        place = piece[:, :LANES] if offset is None else piece[:, :LANES] + offset
        ranks.append(
            jnp.sum(named[:, b * LANES : (b + 1) * LANES] * place, axis=0, keepdims=True)
        )
        offset = piece[:, LANES:] if offset is None else offset + piece[:, LANES:]
    rank = jnp.concatenate(ranks, axis=1).astype(jnp.int32)
    if n_gy == 8:
        owner_x, owner_y = owner >> 3, owner & 7
    else:
        owner_x, owner_y = owner >> 1, owner & 1
    slot = owner_x * RANKS + rank
    slot_ref[...] = (iota((LANES, points), 0) == slot).astype(F32).astype(BF16)
    target = target_ref[...]
    mine = jnp.where(owner_y == gy, F32(1.0), F32(0.0))
    sub_p = iota((8, points), 0)
    marks = jnp.where(
        sub_p == 0,
        (target >> 7).astype(F32) * mine,
        jnp.where(sub_p == 1, (target & 127).astype(F32) * mine, F32(0.0)),
    )
    marked = dot_rows(marks.astype(BF16), slot_ref[...])
    mark_ref[...] = jnp.broadcast_to(128.0 * marked[0:1] + marked[1:2], (8, LANES))
    source = source_ref[...]
    picked = (iota((LANES, points), 0) == (source & 127)).astype(F32).astype(BF16)
    pick_ref[0:LANES, :] = picked
    pick_ref[LANES:, :] = picked
    turns = (mode_base + (sub_p & 3).astype(F32)) * (azimuth_ref[...] * (0.5 / math.pi))
    turns = turns - jnp.where(sub_p >= 4, F32(0.25), F32(0.0))
    turns = turns - jnp.floor(turns + 0.5)
    square = turns * turns
    wave = jnp.full(square.shape, COSINE[-1], F32)
    for value in COSINE[-2::-1]:
        wave = wave * square + value
    in_cycle = sub_p == (source >> 7)
    for row in range(8):
        trig_ref[row] = jnp.where(
            in_cycle, jnp.broadcast_to(wave[row : row + 1], (8, points)), F32(0.0)
        )
    loads["first"].wait()
    pair_first[...] = operator_pair(first_ref[...])

    for copy in cycle_in:
        copy.wait_recv()
    flags = (last_x, has_x)
    near_edges = [cycle_recv[side, 0:24, :] for side in range(2)]
    bends = times_operator(jnp.concatenate(near_edges, axis=0), pair_second)
    beyond = []
    for side, edge in ((0, 7), (1, 0)):
        tail_rows = cycle_recv[side, 48:56, :]
        speed24 = tail_rows[0:1]
        mask24 = jnp.where(order24 < tail_rows[1:2], F32(1.0), F32(0.0))
        edge_ref[pl.ds(edge, 24, stride=8), :] = flags[side] * near_edges[side]
        value = cycle_recv[side, 24:48, :] + mask24 * time_sq * (
            speed24 * now_ref[pl.ds(edge, 24, stride=8), :] + bends[24 * side : 24 * side + 24]
        )
        beyond.append(flags[side] * value)
    one = one_ref[...].reshape(4, 6, 8, LANES) + side_weight * edge_ref[...].reshape(
        4, 6, 8, LANES
    )
    one = one.reshape(192, LANES)
    for side, edge in ((0, 7), (1, 0)):
        edge_ref[pl.ds(edge, 24, stride=8), :] = beyond[side]
    two = section_sum(one, now_ref[...]) + side_weight * edge_ref[...].reshape(4, 6, 8, LANES)
    two = two.reshape(192, LANES)
    two_ref[...] = two
    outs = [pltpu.make_async_copy(two_ref, g_out, out_sem.at[0])]
    outs[0].start()

    coef = coupling * times_operator(two, pair_first) + (coupling * impedance / time_step) * (
        two - one
    )
    high, low = halves(coef)
    at_points = dot(jnp.concatenate([high, low], axis=1), pick_ref[...]).reshape(
        4, 6, 8, points
    )
    values = jnp.zeros((8, points), F32)
    for c in range(3):
        total = jnp.zeros((8, points), F32)
        for m in range(4):
            total = total + at_points[m, 2 * c] * trig_ref[m]
            total = total + at_points[m, 2 * c + 1] * trig_ref[4 + m]
        values = jnp.where(
            (sub_p & 3) == c,
            jnp.broadcast_to(jnp.sum(total, axis=0, keepdims=True), (8, points)),
            values,
        )
    by_group = jnp.concatenate(
        [
            jnp.where(owner_y == 2 * t + (sub_p >> 2), values, F32(0.0))
            for t in range(n_gy // 2)
        ],
        axis=0,
    )
    high, low = halves(by_group)
    packed = dot_rows(jnp.concatenate([high, low], axis=0), slot_ref[...])
    packed = packed[: 4 * n_gy] + packed[4 * n_gy :]
    for group in range(n_gy):
        group_send[group] = packed[4 * group : 4 * group + 4]
    for step in range(1, n_gy):
        peer = away("gy", step)
        sent.append(
            push(
                group_send.at[peer["gy"]],
                group_recv.at[step],
                group_sems,
                (step,),
                peer,
            )
        )
    group_in = sent[-(n_gy - 1) :]

    for copy in moduli_copies:
        copy.wait_recv()
    mu_next_x = last_x * x_recv[0, 0, 0]
    sum_prev_x = x_recv[0, 1, 0]
    lane4 = iota((4, 8, LANES), 2)
    sub4 = iota((4, 8, LANES), 1)
    side_w = [0.2] + [float(v) for v in WEIGHTS[1:4]]
    first_weight = -float(WEIGHTS[4])
    weight_y = by_four(sub & 3, side_w) + jnp.where(
        sub == 0, (1.0 - has_y) * first_weight, F32(0.0)
    )
    weight_z = by_four(lane & 3, side_w) + jnp.where(
        lane == 0, (1.0 - has_z) * first_weight, F32(0.0)
    )
    weight_x = [side_w[0] + (1.0 - has_x) * first_weight] + side_w[1:]

    def make_band(axis, position, count, following, preceding, weights, has, last, band, over):
        shifted = {0: mu}
        for t in range(-4, 5):
            if t:
                rolled = pltpu.roll(mu, (-t) % count, axis)
                if t > 0:
                    rolled = jnp.where(position == count - t, following, rolled)
                shifted[t] = rolled
        pos2 = position[0]
        phase = pos2 & 3
        later = pos2 > 3
        band_values = []
        for s in range(5):
            total = None
            for t in range(s - 4, 5):
                row = [
                    GRAM[i + t, i, i + s] if 0 <= i + t <= 4 and i + s <= 4 else 0.0
                    for i in range(4)
                ]
                pattern = by_four(phase, row)
                if s == 0 and t <= 0:
                    pattern = pattern + jnp.where(
                        (phase == 0) & later, F32(GRAM[4 + t, 4, 4]), F32(0.0)
                    )
                term = pattern[None] * shifted[t]
                total = term if total is None else total + term
            if s == 0:
                total = total + jnp.where(
                    position == 0, preceding + has * float(GRAM[4, 4, 4]) * mu, F32(0.0)
                )
            band_values.append(total * weights)
        crossing = jnp.zeros_like(mu)
        for s in range(1, 5):
            crossing = jnp.where(position == count - s, band_values[s], crossing)
            inside = jnp.where(position >= count - s, F32(0.0), band_values[s])
            behind = pltpu.roll(inside, s, axis)
            if 2 * s == count:
                band[s] = inside + behind
                band[4 + s] = jnp.zeros_like(inside)
            else:
                band[s] = inside
                band[4 + s] = behind
        over[...] = last * crossing
        band[0] = band_values[0]

    y_next = y_recv[0, 0, 0:8]
    y_prev = y_recv[0, 1, 0:8]
    z_next = z_recv[0, 0]
    z_prev = z_recv[0, 1]

    def rows_of(value):
        return jnp.concatenate(
            [jnp.broadcast_to(value[x : x + 1], (8, LANES))[None] for x in range(4)], axis=0
        )

    def columns_of(value):
        return jnp.concatenate(
            [jnp.broadcast_to(value[:, x : x + 1], (8, LANES))[None] for x in range(4)], axis=0
        )

    stacked = lambda scale: jnp.concatenate([(scale(x))[None] for x in range(4)], axis=0)
    make_band(
        2,
        lane4,
        LANES,
        last_z * columns_of(z_next),
        columns_of(z_prev),
        stacked(lambda x: weight_x[x] * weight_y),
        has_z,
        last_z,
        band_z,
        over_z,
    )
    make_band(
        1,
        sub4,
        8,
        last_y * rows_of(y_next),
        rows_of(y_prev),
        stacked(lambda x: weight_x[x] * weight_z),
        has_y,
        last_y,
        band_y,
        over_y,
    )
    weight_yz = weight_y * weight_z
    planes = [mu[x] for x in range(4)] + [mu_next_x]
    for i in range(4):
        for j in range(i, 5):
            value = sum(float(GRAM[k, i, j]) * planes[k] for k in range(5))
            if i == 0 and j == 0:
                value = value + sum_prev_x + has_x * float(GRAM[4, 4, 4]) * mu[0]
            if j == 4:
                value = last_x * value
            band_x[5 * i + j] = value * weight_yz
    for x in range(4):
        band_z[0, x] = band_z[0, x] + band_y[0, x] + band_x[6 * x]

    def coupling_x(i, j):
        return band_x[5 * min(i, j) + max(i, j)]

    def face_values(number, ref):
        field = ref[...].reshape(3, 4, 8, LANES)
        for c in range(3):
            x_send[number, 0, c] = field[c, 0]
            x_send[number, 1, c] = sum(coupling_x(i, 4) * field[c, i] for i in range(4))
        y_send[number, 0, 0:12] = ref[pl.ds(0, 12, stride=8), :]
        part_ref[...] = (over_y[...][None] * field).reshape(96, LANES)
        y_send[number, 1, 0:12] = sum(
            part_ref[pl.ds(4 + k, 12, stride=8), :] for k in range(4)
        )
        z_send[number, 0] = columns_to_lanes(
            [field[c, x][:, 0:1] for c in range(3) for x in range(4)]
        )
        z_send[number, 1] = columns_to_lanes(
            [
                jnp.sum(over_z[x] * field[c, x], axis=1, keepdims=True)
                for c in range(3)
                for x in range(4)
            ]
        )
        return send_faces(number, 3, 16)

    def inner_stiffness(ref):
        field = ref[...].reshape(3, 4, 8, LANES)
        out = []
        for x in range(4):
            plane = field[:, x]
            total = band_z[0, x] * plane
            for s in range(1, 5):
                total = total + band_z[s, x] * pltpu.roll(plane, LANES - s, 2)
                total = total + band_z[4 + s, x] * pltpu.roll(plane, s, 2)
                total = total + band_y[s, x] * pltpu.roll(plane, 8 - s, 1)
                if s < 4:
                    total = total + band_y[4 + s, x] * pltpu.roll(plane, s, 1)
            for j in range(4):
                if j != x:
                    total = total + coupling_x(x, j) * field[:, j]
            out.append(total)
        return out

    def outer_stiffness(number, copies, inside):
        for copy in copies:
            copy.wait_recv()
        y_first = y_recv[number, 1, 0:12]
        y_after = y_recv[number, 0, 0:12]
        spread_ref[pl.ds(0, 12, stride=8), :] = y_first
        for k in range(4):
            spread_ref[pl.ds(4 + k, 12, stride=8), :] = y_after
        spread = spread_ref[...].reshape(3, 4, 8, LANES)
        z_first, z_after = z_recv[number, 1], z_recv[number, 0]
        x_after, x_first = x_recv[number, 0], x_recv[number, 1]
        out = []
        for x in range(4):
            rows = []
            for c in range(3):
                at = 4 * c + x
                row = inside[x][c] + coupling_x(x, 4) * x_after[c]
                row = row + jnp.where(sub == 0, F32(1.0), over_y[x]) * spread[c, x]
                row = row + jnp.where(
                    lane == 0,
                    jnp.broadcast_to(z_first[:, at : at + 1], (8, LANES)),
                    over_z[x] * jnp.broadcast_to(z_after[:, at : at + 1], (8, LANES)),
                )
                if x == 0:
                    row = row + x_first[c]
                rows.append(row)
            out.append(rows)
        return out

    spread_ref[...] = jnp.zeros((96, LANES), F32)
    loads["slab"].wait()
    now_copies = face_values(1, slab_ref)

    for copy in group_in:
        copy.wait_recv()
    total = group_send[gy]
    for step in range(1, n_gy):
        total = total + group_recv[step]
    rows16 = iota((n_gx, LANES), 0)
    lanes16 = iota((n_gx, LANES), 1)
    outgoing = jnp.zeros((n_gx, LANES), F32)
    for c in range(4):
        line = total[c : c + 1] if c < 3 else mark_ref[0:1]
        line = jnp.broadcast_to(line, (8, LANES))
        if (RANKS * (c + 1 - n_gx)) % LANES:
            line = pltpu.roll(line, (RANKS * (c + 1 - n_gx)) % LANES, 1)
        moved = pltpu.roll(
            jnp.broadcast_to(line[0:1], (n_gx, LANES)), 0, 1, stride=RANKS, stride_axis=0
        )
        outgoing = jnp.where(lanes16 >> 3 == c, moved, outgoing)
    owner_send[...] = outgoing.reshape(n_gx, 1, LANES)
    for step in range(1, n_gx):
        peer = away("gx", step)
        sent.append(
            push(
                owner_send.at[n_gx - 1 - peer["gx"]],
                owner_recv.at[step],
                owner_sems,
                (step,),
                peer,
            )
        )
    owner_in = sent[-(n_gx - 1) :]
    owner_recv[0] = owner_send[n_gx - 1 - gx]

    inside = inner_stiffness(slab_ref)
    loads["before"].wait()
    loads["mass"].wait()
    around = outer_stiffness(1, now_copies, inside)
    for x in range(4):
        scale = slab_factor * mass_ref[8 * x : 8 * x + 8, :]
        for c in range(3):
            at = 32 * c + 8 * x
            base_ref[at : at + 8, :] = (
                2.0 * slab_ref[at : at + 8, :]
                - before_ref[at : at + 8, :]
                - scale * around[x][c]
            )

    for copy in owner_in:
        copy.wait_recv()
    arrived = owner_recv[...].reshape(n_gx, LANES)
    lines = []
    moved = pltpu.roll(arrived, 0, 1, stride=RANKS, stride_axis=0)
    for c in range(4):
        own = ((lanes16 >> 3) - rows16 - c) & 15 == 0
        line = jnp.sum(jnp.where(own, moved, F32(0.0)), axis=0, keepdims=True)
        if c:
            line = pltpu.roll(jnp.broadcast_to(line, (8, LANES)), LANES - RANKS * c, 1)[0:1]
        lines.append(line)
    goal = lines[3].astype(jnp.int32)
    goal_row, goal_lane = goal >> 7, goal & 127
    rows32 = iota((32, LANES), 0)
    spots = jnp.concatenate(
        [jnp.where(rows32 == goal_row, lines[c], F32(0.0)) for c in range(3)], axis=0
    )
    high, low = halves(spots)
    on_lane = (iota((LANES, LANES), 0) == goal_lane).astype(F32).astype(BF16)
    force = dot_rows(
        jnp.concatenate([high, low], axis=1), jnp.concatenate([on_lane, on_lane], axis=1)
    )
    force_ref[...] = force
    outs.append(pltpu.make_async_copy(force_ref, force_out, out_sem.at[1]))
    outs[1].start()
    for x in range(4):
        scale = slab_factor * mass_ref[8 * x : 8 * x + 8, :]
        for c in range(3):
            at = 32 * c + 8 * x
            step_ref[at : at + 8, :] = base_ref[at : at + 8, :] + scale * force[at : at + 8]

    step_copies = face_values(2, step_ref)
    inside = inner_stiffness(step_ref)
    around = outer_stiffness(2, step_copies, inside)
    for x in range(4):
        scale = slab_factor * mass_ref[8 * x : 8 * x + 8, :]
        for c in range(3):
            at = 32 * c + 8 * x
            last_ref[at : at + 8, :] = (
                2.0 * step_ref[at : at + 8, :]
                - slab_ref[at : at + 8, :]
                + scale * (force_ref[at : at + 8, :] - around[x][c])
            )
    outs.append(pltpu.make_async_copy(last_ref, slab_out, out_sem.at[2]))
    outs[2].start()
    for copy in sent:
        copy.wait_send()
    for copy in outs:
        copy.wait()


def solution(mesh):
    n_gx, n_gy, n_gz = (mesh.shape[name] for name in ("gx", "gy", "gz"))

    def on_device(
        global_now,
        global_prev,
        cycle_modes,
        wave_speed,
        inv_radius,
        theta_second,
        theta_first,
        point_dest,
        point_target,
        point_source,
        point_azimuth,
        regional_now,
        regional_prev,
        moduli,
        inv_mass,
    ):
        points = point_target.shape[1]
        big = [((192, LANES), F32)] * 2 + [((8, LANES), F32)] * 2 + [((LANES, LANES), F32)] * 2
        big += [((1, points), jnp.int32)] * 3 + [((1, points), F32)]
        big += [((96, LANES), F32)] * 2 + [((32, LANES), F32)] * 2
        scratch = [pltpu.SMEM(cycle_modes.shape, jnp.int32)]
        scratch += [pltpu.VMEM(shape, dtype) for shape, dtype in big]
        scratch += [
            pltpu.VMEM((192, LANES), F32),
            pltpu.VMEM((192, LANES), F32),
            pltpu.VMEM((192, LANES), F32),
            pltpu.VMEM((2 * LANES, 2 * LANES), BF16),
            pltpu.VMEM((2 * LANES, 2 * LANES), BF16),
            pltpu.VMEM((2 * LANES, points), BF16),
            pltpu.VMEM((8, 8, points), F32),
            pltpu.VMEM((LANES, points), BF16),
            pltpu.VMEM((8, LANES), F32),
            pltpu.VMEM((96, LANES), F32),
            pltpu.VMEM((96, LANES), F32),
            pltpu.VMEM((96, LANES), F32),
            pltpu.VMEM((96, LANES), F32),
            pltpu.VMEM((9, 4, 8, LANES), F32),
            pltpu.VMEM((9, 4, 8, LANES), F32),
            pltpu.VMEM((20, 8, LANES), F32),
            pltpu.VMEM((4, 8, LANES), F32),
            pltpu.VMEM((4, 8, LANES), F32),
            pltpu.VMEM((96, LANES), F32),
            pltpu.VMEM((96, LANES), F32),
            pltpu.VMEM((2, 56, LANES), F32),
            pltpu.VMEM((2, 56, LANES), F32),
            pltpu.VMEM((3, 2, 3, 8, LANES), F32),
            pltpu.VMEM((3, 2, 3, 8, LANES), F32),
            pltpu.VMEM((3, 2, 16, LANES), F32),
            pltpu.VMEM((3, 2, 16, LANES), F32),
            pltpu.VMEM((3, 2, 8, LANES), F32),
            pltpu.VMEM((3, 2, 8, LANES), F32),
            pltpu.VMEM((n_gy, 4, LANES), F32),
            pltpu.VMEM((n_gy, 4, LANES), F32),
            pltpu.VMEM((n_gx, 1, LANES), F32),
            pltpu.VMEM((n_gx, 1, LANES), F32),
            pltpu.SemaphoreType.DMA((15,)),
            pltpu.SemaphoreType.DMA((3,)),
            pltpu.SemaphoreType.DMA((2, 2)),
            pltpu.SemaphoreType.DMA((2, 3, 6)),
            pltpu.SemaphoreType.DMA((2, n_gy)),
            pltpu.SemaphoreType.DMA((2, n_gx)),
        ]
        hbm = pl.BlockSpec(memory_space=pl.ANY)
        two, slab, force = pl.pallas_call(
            functools.partial(kernel, (n_gx, n_gy, n_gz)),
            out_shape=[
                pltpu.VMEM((192, LANES), F32),
                pltpu.VMEM((96, LANES), F32),
                pltpu.VMEM((96, LANES), F32),
            ],
            in_specs=[hbm] * 15,
            out_specs=[hbm] * 3,
            scratch_shapes=scratch,
            compiler_params=pltpu.CompilerParams(
                collective_id=0, has_side_effects=True, vmem_limit_bytes=48 * 2**20
            ),
        )(
            *[
                pltpu.with_memory_space_constraint(x, pltpu.HBM)
                for x in (
            cycle_modes,
            global_now.reshape(192, LANES),
            global_prev.reshape(192, LANES),
            wave_speed,
            inv_radius,
            theta_second,
            theta_first,
            point_dest.reshape(1, points),
            point_target,
            point_source,
            point_azimuth,
            regional_now.reshape(96, LANES),
            regional_prev.reshape(96, LANES),
            moduli.reshape(32, LANES),
            inv_mass.reshape(32, LANES),
            )]
        )
        return (
            two.reshape(global_now.shape),
            slab.reshape(regional_now.shape),
            force.reshape(regional_now.shape),
        )

    return jax.shard_map(
        on_device,
        mesh=mesh,
        in_specs=(
            P("gy", None, "gx", None),
            P("gy", None, "gx", None),
            P("gx"),
            P("gx", None),
            P("gx", None),
            P(),
            P(),
            P("gz", "gx", None),
            P("gz", "gx"),
            P("gz", "gx"),
            P("gz", "gx"),
            P(None, "gx", "gy", "gz"),
            P(None, "gx", "gy", "gz"),
            P("gx", "gy", "gz"),
            P("gx", "gy", "gz"),
        ),
        out_specs=(P("gy", None, "gx", None), P(None, "gx", "gy", "gz"), P(None, "gx", "gy", "gz")),
        check_vma=False,
    )
```

```python
import functools
import math

import jax
import jax.numpy as jnp
import numpy as np
from jax import lax
from jax.experimental import pallas as pl
from jax.experimental.pallas import tpu as pltpu
from jax.sharding import PartitionSpec as P

F32 = jnp.float32
BF16 = jnp.bfloat16
MESH = pl.DeviceIdType.MESH

time_step = 0.3
time_sq = 0.09
impedance = 0.5
coupling = 0.05
slab_factor = 0.04

LANES = 128
RANKS = 8


def gll_products():
    nodes = np.array([-1.0, -math.sqrt(3.0 / 7.0), 0.0, math.sqrt(3.0 / 7.0), 1.0])
    weights = np.array([0.1, 49.0 / 90.0, 32.0 / 45.0, 49.0 / 90.0, 0.1])
    factor = np.array(
        [np.prod([nodes[i] - nodes[k] for k in range(5) if k != i]) for i in range(5)]
    )
    deriv = np.zeros((5, 5))
    for i in range(5):
        for j in range(5):
            if i != j:
                deriv[i, j] = factor[i] / factor[j] / (nodes[i] - nodes[j])
            else:
                deriv[i, j] = sum((1.0 / (nodes[i] - nodes[k]) for k in range(5) if k != i))
    return weights, np.einsum("ki,k,kj->kij", deriv, weights, deriv)


WEIGHTS, GRAM = gll_products()


def cosine_series():
    f = np.cos(np.linspace(0.0, np.pi / 2, 2001)) * 0.5
    fit = np.polynomial.chebyshev.Chebyshev.fit(f * f, np.cos(2 * np.pi * f), 8, domain=[0, 0.25])
    return [float(v) for v in fit.convert(kind=np.polynomial.Polynomial).coef]


COSINE = cosine_series()


def halves(x):
    high = x.astype(BF16)
    return high, (x - high.astype(F32)).astype(BF16)


def dot(a, b):
    return lax.dot_general(a, b, (((1,), (0,)), ((), ())), preferred_element_type=F32)


def dot_rows(a, b):
    return lax.dot_general(a, b, (((1,), (1,)), ((), ())), preferred_element_type=F32)


def operator_pair(t):
    high, low = halves(t)
    top = jnp.concatenate([high, low], axis=1)
    bottom = jnp.concatenate([high, jnp.zeros_like(low)], axis=1)
    return jnp.concatenate([top, bottom], axis=0)


def times_operator(x, pair_ref):
    high, low = halves(x)
    both = dot(jnp.concatenate([high, low], axis=1), pair_ref[...])
    return both[:, :LANES] + both[:, LANES:]


def iota(shape, axis):
    return lax.broadcasted_iota(jnp.int32, shape, axis)


def by_four(phase, values):
    out = jnp.full(phase.shape, values[3], F32)
    for i in (2, 1, 0):
        out = jnp.where(phase == i, F32(values[i]), out)
    return out


def kernel(
    sizes,
    modes_in,
    now_in,
    prev_in,
    speed_in,
    radius_in,
    second_in,
    first_in,
    dest_in,
    target_in,
    source_in,
    azimuth_in,
    slab_in,
    before_in,
    moduli_in,
    mass_in,
    g_out,
    slab_out,
    force_out,
    modes_ref,
    now_ref,
    prev_ref,
    speed_ref,
    radius_ref,
    second_ref,
    first_ref,
    dest_ref,
    target_ref,
    source_ref,
    azimuth_ref,
    slab_ref,
    before_ref,
    moduli_ref,
    mass_ref,
    one_ref,
    two_ref,
    edge_ref,
    pair_second,
    pair_first,
    pick_ref,
    trig_ref,
    slot_ref,
    mark_ref,
    base_ref,
    force_ref,
    step_ref,
    last_ref,
    band_z,
    band_y,
    band_x,
    over_z,
    over_y,
    spread_ref,
    part_ref,
    cycle_send,
    cycle_recv,
    x_send,
    x_recv,
    y_send,
    y_recv,
    z_send,
    z_recv,
    group_send,
    group_recv,
    owner_send,
    owner_recv,
    in_sem,
    out_sem,
    cycle_sems,
    face_sems,
    group_sems,
    owner_sems,
    ring_sems,
):
    n_gx, n_gy, n_gz = sizes
    gx, gy, gz = lax.axis_index("gx"), lax.axis_index("gy"), lax.axis_index("gz")
    points = dest_ref.shape[1]

    loads = {}
    for number, (name, src, dst) in enumerate(
        (
            ("modes", modes_in, modes_ref),
            ("now", now_in, now_ref),
            ("prev", prev_in, prev_ref),
            ("speed", speed_in, speed_ref),
            ("radius", radius_in, radius_ref),
            ("moduli", moduli_in, moduli_ref),
            ("second", second_in, second_ref),
            ("dest", dest_in, dest_ref),
            ("target", target_in, target_ref),
            ("source", source_in, source_ref),
            ("azimuth", azimuth_in, azimuth_ref),
            ("first", first_in, first_ref),
            ("slab", slab_in, slab_ref),
            ("before", before_in, before_ref),
            ("mass", mass_in, mass_ref),
        )
    ):
        loads[name] = pltpu.make_async_copy(src, dst, in_sem.at[number])
        loads[name].start()

    def away(axis, step):
        index, count = {"gx": (gx, n_gx), "gy": (gy, n_gy), "gz": (gz, n_gz)}[axis]
        return {axis: lax.rem(index + step + count, count)}

    barrier = pltpu.get_barrier_semaphore()
    for axis, steps in (
        ("gx", sorted({1, n_gx - 1})),
        ("gy", range(1, n_gy)),
        ("gz", sorted({1, n_gz - 1})),
    ):
        for step in steps:
            pl.semaphore_signal(
                barrier, inc=1, device_id=away(axis, step), device_id_type=MESH
            )
    greeted = len({1, n_gx - 1}) + n_gy - 1 + len({1, n_gz - 1})

    def push(src, dst, sems, index, device):
        copy = pltpu.make_async_remote_copy(
            src_ref=src,
            dst_ref=dst,
            send_sem=sems.at[(0, *index)],
            recv_sem=sems.at[(1, *index)],
            device_id=device,
            device_id_type=MESH,
        )
        copy.start()
        return copy

    sub = iota((8, LANES), 0)
    lane = iota((8, LANES), 1)

    mode_base = (4 * gy).astype(F32)
    row24 = iota((24, LANES), 0)
    order24 = mode_base + (
        (row24 >= 6).astype(F32) + (row24 >= 12).astype(F32) + (row24 >= 18).astype(F32)
    )
    square24 = order24 * order24
    for name in ("modes", "now", "prev", "speed", "radius"):
        loads[name].wait()
    for side, (edge, inner) in enumerate(((0, 1), (7, 6))):
        count = modes_ref[edge].astype(F32)
        mask = jnp.where(order24 < count, F32(1.0), F32(0.0))
        speed = speed_ref[edge : edge + 1, :]
        radius = radius_ref[edge : edge + 1, :]
        at_edge = now_ref[pl.ds(edge, 24, stride=8), :]
        cycle_send[side, 0:24, :] = at_edge
        cycle_send[side, 24:48, :] = mask * (
            (2.0 - 2.0 * time_sq * speed - time_sq * square24 * radius) * at_edge
            - prev_ref[pl.ds(edge, 24, stride=8), :]
            + time_sq * speed * now_ref[pl.ds(inner, 24, stride=8), :]
        )
        cycle_send[side, 48:56, :] = jnp.where(
            sub == 0, jnp.broadcast_to(speed, (8, LANES)), jnp.full((8, LANES), count, F32)
        )

    pl.semaphore_wait(barrier, greeted)

    reaches = [reach for reach in (1, 2, 4) if 2 * reach < n_gx]

    def tell(level):
        for step in (reaches[level], -reaches[level]):
            pl.semaphore_signal(
                ring_sems.at[level], inc=1, device_id=away("gx", step), device_id_type=MESH
            )

    def hear(level):
        pl.semaphore_wait(ring_sems.at[level], 2)

    tell(0)
    sent = []
    cycle_in = []
    for side, step in ((0, -1), (1, 1)):
        copy = push(
            cycle_send.at[side], cycle_recv.at[side], cycle_sems, (side,), away("gx", step)
        )
        sent.append(copy)
        cycle_in.append(copy)

    last_x = jnp.where(gx < n_gx - 1, F32(1.0), F32(0.0))
    last_y = jnp.where(gy < n_gy - 1, F32(1.0), F32(0.0))
    last_z = jnp.where(gz < n_gz - 1, F32(1.0), F32(0.0))
    has_x = jnp.where(gx > 0, F32(1.0), F32(0.0))
    has_y = jnp.where(gy > 0, F32(1.0), F32(0.0))
    has_z = jnp.where(gz > 0, F32(1.0), F32(0.0))

    def send_faces(number, x_count, y_count):
        copies = []
        for side, step in ((0, -1), (1, 1)):
            for place, (axis, src, dst) in enumerate(
                (
                    ("gx", x_send.at[number, side, 0:x_count], x_recv.at[number, side, 0:x_count]),
                    ("gy", y_send.at[number, side, 0:y_count], y_recv.at[number, side, 0:y_count]),
                    ("gz", z_send.at[number, side], z_recv.at[number, side]),
                )
            ):
                copies.append(
                    push(src, dst, face_sems, (number, 2 * place + side), away(axis, step))
                )
        sent.extend(copies)
        return copies

    def columns_to_lanes(columns):
        out = jnp.zeros((8, LANES), F32)
        for number, column in enumerate(columns):
            out = jnp.where(lane == number, jnp.broadcast_to(column, (8, LANES)), out)
        return out

    loads["moduli"].wait()
    inner = [float(GRAM[k, 4, 4]) for k in range(5)]
    mu = moduli_ref[...].reshape(4, 8, LANES)
    x_send[0, 0, 0] = mu[0]
    x_send[0, 1, 0] = last_x * (
        inner[0] * mu[0] + inner[1] * mu[1] + inner[2] * mu[2] + inner[3] * mu[3]
    )
    y_send[0, 0, 0:8] = jnp.zeros((8, LANES), F32)
    y_send[0, 1, 0:8] = jnp.zeros((8, LANES), F32)
    y_send[0, 0, 0:4] = moduli_ref[pl.ds(0, 4, stride=8), :]
    y_send[0, 1, 0:4] = last_y * sum(
        inner[k] * moduli_ref[pl.ds(4 + k, 4, stride=8), :] for k in range(4)
    )
    tail = by_four(lane & 3, inner[:4]) * jnp.where(lane >= LANES - 4, last_z, F32(0.0))
    z_send[0, 0] = columns_to_lanes([mu[x][:, 0:1] for x in range(4)])
    z_send[0, 1] = columns_to_lanes(
        [jnp.sum(tail * mu[x], axis=1, keepdims=True) for x in range(4)]
    )
    moduli_copies = send_faces(0, 1, 8)

    hear(0)
    if len(reaches) > 1:
        tell(1)

    loads["second"].wait()
    pair_second[...] = operator_pair(second_ref[...])
    counts = jnp.zeros((8, LANES), F32)
    for row in range(8):
        counts = jnp.where(sub == row, modes_ref[row].astype(F32), counts)
    order = mode_base + iota((4, 8, LANES), 0).astype(F32)
    mask = jnp.where(order < counts[None], F32(1.0), F32(0.0))
    speed, radius = speed_ref[...][None], radius_ref[...][None]
    hold = (mask * (2.0 - 2.0 * time_sq * speed - time_sq * (order * order) * radius))[:, None]
    side_weight = (mask * (time_sq * speed))[:, None]
    bend_weight = (mask * time_sq)[:, None]
    mask = mask[:, None]

    def section_sum(now, prev):
        cells = now.reshape(24, 8, LANES)
        rows = iota((24, 8, LANES), 1)
        near = jnp.where(rows == 0, F32(0.0), pltpu.roll(cells, 1, 1)) + jnp.where(
            rows == 7, F32(0.0), pltpu.roll(cells, 7, 1)
        )
        return (
            hold * now.reshape(4, 6, 8, LANES)
            - mask * prev.reshape(4, 6, 8, LANES)
            + side_weight * near.reshape(4, 6, 8, LANES)
            + bend_weight * times_operator(now, pair_second).reshape(4, 6, 8, LANES)
        )

    one_ref[...] = section_sum(now_ref[...], prev_ref[...]).reshape(192, LANES)
    edge_ref[...] = jnp.zeros((192, LANES), F32)

    for name in ("dest", "target", "source", "azimuth"):
        loads[name].wait()
    owner = dest_ref[...]
    blocks = points // LANES
    named = (iota((LANES, points), 0) == owner).astype(F32)
    named_rows = jnp.concatenate(
        [named[:, b * LANES : (b + 1) * LANES] for b in range(blocks)], axis=0
    ).astype(BF16)
    before = (iota((LANES, LANES), 0) < iota((LANES, LANES), 1)).astype(F32)
    counted = dot(
        named_rows, jnp.concatenate([before, jnp.ones_like(before)], axis=1).astype(BF16)
    )
    ranks, offset = [], None
    for b in range(blocks):
        piece = counted[b * LANES : (b + 1) * LANES]
        place = piece[:, :LANES] if offset is None else piece[:, :LANES] + offset
        ranks.append(
            jnp.sum(named[:, b * LANES : (b + 1) * LANES] * place, axis=0, keepdims=True)
        )
        offset = piece[:, LANES:] if offset is None else offset + piece[:, LANES:]
    rank = jnp.concatenate(ranks, axis=1).astype(jnp.int32)
    if n_gy == 8:
        owner_x, owner_y = owner >> 3, owner & 7
    else:
        owner_x, owner_y = owner >> 1, owner & 1
    slot = owner_x * RANKS + rank
    slot_ref[...] = (iota((LANES, points), 0) == slot).astype(F32).astype(BF16)
    target = target_ref[...]
    mine = jnp.where(owner_y == gy, F32(1.0), F32(0.0))
    sub_p = iota((8, points), 0)
    marks = jnp.where(
        sub_p == 0,
        (target >> 7).astype(F32) * mine,
        jnp.where(sub_p == 1, (target & 127).astype(F32) * mine, F32(0.0)),
    )
    marked = dot_rows(marks.astype(BF16), slot_ref[...])
    mark_ref[...] = jnp.broadcast_to(128.0 * marked[0:1] + marked[1:2], (8, LANES))
    source = source_ref[...]
    picked = (iota((LANES, points), 0) == (source & 127)).astype(F32).astype(BF16)
    pick_ref[0:LANES, :] = picked
    pick_ref[LANES:, :] = picked
    turns = (mode_base + (sub_p & 3).astype(F32)) * (azimuth_ref[...] * (0.5 / math.pi))
    turns = turns - jnp.where(sub_p >= 4, F32(0.25), F32(0.0))
    turns = turns - jnp.floor(turns + 0.5)
    square = turns * turns
    wave = jnp.full(square.shape, COSINE[-1], F32)
    for value in COSINE[-2::-1]:
        wave = wave * square + value
    in_cycle = sub_p == (source >> 7)
    for row in range(8):
        trig_ref[row] = jnp.where(
            in_cycle, jnp.broadcast_to(wave[row : row + 1], (8, points)), F32(0.0)
        )
    loads["first"].wait()
    pair_first[...] = operator_pair(first_ref[...])

    for copy in cycle_in:
        copy.wait_recv()
    flags = (last_x, has_x)
    near_edges = [cycle_recv[side, 0:24, :] for side in range(2)]
    bends = times_operator(jnp.concatenate(near_edges, axis=0), pair_second)
    beyond = []
    for side, edge in ((0, 7), (1, 0)):
        tail_rows = cycle_recv[side, 48:56, :]
        speed24 = tail_rows[0:1]
        mask24 = jnp.where(order24 < tail_rows[1:2], F32(1.0), F32(0.0))
        edge_ref[pl.ds(edge, 24, stride=8), :] = flags[side] * near_edges[side]
        value = cycle_recv[side, 24:48, :] + mask24 * time_sq * (
            speed24 * now_ref[pl.ds(edge, 24, stride=8), :] + bends[24 * side : 24 * side + 24]
        )
        beyond.append(flags[side] * value)
    one = one_ref[...].reshape(4, 6, 8, LANES) + side_weight * edge_ref[...].reshape(
        4, 6, 8, LANES
    )
    one = one.reshape(192, LANES)
    for side, edge in ((0, 7), (1, 0)):
        edge_ref[pl.ds(edge, 24, stride=8), :] = beyond[side]
    two = section_sum(one, now_ref[...]) + side_weight * edge_ref[...].reshape(4, 6, 8, LANES)
    two = two.reshape(192, LANES)
    two_ref[...] = two
    outs = [pltpu.make_async_copy(two_ref, g_out, out_sem.at[0])]
    outs[0].start()

    coef = coupling * times_operator(two, pair_first) + (coupling * impedance / time_step) * (
        two - one
    )
    high, low = halves(coef)
    at_points = dot(jnp.concatenate([high, low], axis=1), pick_ref[...]).reshape(
        4, 6, 8, points
    )
    values = jnp.zeros((8, points), F32)
    for c in range(3):
        total = jnp.zeros((8, points), F32)
        for m in range(4):
            total = total + at_points[m, 2 * c] * trig_ref[m]
            total = total + at_points[m, 2 * c + 1] * trig_ref[4 + m]
        values = jnp.where(
            (sub_p & 3) == c,
            jnp.broadcast_to(jnp.sum(total, axis=0, keepdims=True), (8, points)),
            values,
        )
    by_group = jnp.concatenate(
        [
            jnp.where(owner_y == 2 * t + (sub_p >> 2), values, F32(0.0))
            for t in range(n_gy // 2)
        ],
        axis=0,
    )
    high, low = halves(by_group)
    packed = dot_rows(jnp.concatenate([high, low], axis=0), slot_ref[...])
    packed = packed[: 4 * n_gy] + packed[4 * n_gy :]
    for group in range(n_gy):
        group_send[group] = packed[4 * group : 4 * group + 4]
    for step in range(1, n_gy):
        peer = away("gy", step)
        sent.append(
            push(
                group_send.at[peer["gy"]],
                group_recv.at[step],
                group_sems,
                (step,),
                peer,
            )
        )
    group_in = sent[-(n_gy - 1) :]

    if len(reaches) > 1:
        hear(1)
    if len(reaches) > 2:
        tell(2)

    for copy in moduli_copies:
        copy.wait_recv()
    mu_next_x = last_x * x_recv[0, 0, 0]
    sum_prev_x = x_recv[0, 1, 0]
    lane4 = iota((4, 8, LANES), 2)
    sub4 = iota((4, 8, LANES), 1)
    side_w = [0.2] + [float(v) for v in WEIGHTS[1:4]]
    first_weight = -float(WEIGHTS[4])
    weight_y = by_four(sub & 3, side_w) + jnp.where(
        sub == 0, (1.0 - has_y) * first_weight, F32(0.0)
    )
    weight_z = by_four(lane & 3, side_w) + jnp.where(
        lane == 0, (1.0 - has_z) * first_weight, F32(0.0)
    )
    weight_x = [side_w[0] + (1.0 - has_x) * first_weight] + side_w[1:]

    def make_band(axis, position, count, following, preceding, weights, has, last, band, over):
        shifted = {0: mu}
        for t in range(-4, 5):
            if t:
                rolled = pltpu.roll(mu, (-t) % count, axis)
                if t > 0:
                    rolled = jnp.where(position == count - t, following, rolled)
                shifted[t] = rolled
        pos2 = position[0]
        phase = pos2 & 3
        later = pos2 > 3
        band_values = []
        for s in range(5):
            total = None
            for t in range(s - 4, 5):
                row = [
                    GRAM[i + t, i, i + s] if 0 <= i + t <= 4 and i + s <= 4 else 0.0
                    for i in range(4)
                ]
                pattern = by_four(phase, row)
                if s == 0 and t <= 0:
                    pattern = pattern + jnp.where(
                        (phase == 0) & later, F32(GRAM[4 + t, 4, 4]), F32(0.0)
                    )
                term = pattern[None] * shifted[t]
                total = term if total is None else total + term
            if s == 0:
                total = total + jnp.where(
                    position == 0, preceding + has * float(GRAM[4, 4, 4]) * mu, F32(0.0)
                )
            band_values.append(total * weights)
        crossing = jnp.zeros_like(mu)
        for s in range(1, 5):
            crossing = jnp.where(position == count - s, band_values[s], crossing)
            inside = jnp.where(position >= count - s, F32(0.0), band_values[s])
            behind = pltpu.roll(inside, s, axis)
            if 2 * s == count:
                band[s] = inside + behind
                band[4 + s] = jnp.zeros_like(inside)
            else:
                band[s] = inside
                band[4 + s] = behind
        over[...] = last * crossing
        band[0] = band_values[0]

    y_next = y_recv[0, 0, 0:8]
    y_prev = y_recv[0, 1, 0:8]
    z_next = z_recv[0, 0]
    z_prev = z_recv[0, 1]

    def rows_of(value):
        return jnp.concatenate(
            [jnp.broadcast_to(value[x : x + 1], (8, LANES))[None] for x in range(4)], axis=0
        )

    def columns_of(value):
        return jnp.concatenate(
            [jnp.broadcast_to(value[:, x : x + 1], (8, LANES))[None] for x in range(4)], axis=0
        )

    stacked = lambda scale: jnp.concatenate([(scale(x))[None] for x in range(4)], axis=0)
    make_band(
        2,
        lane4,
        LANES,
        last_z * columns_of(z_next),
        columns_of(z_prev),
        stacked(lambda x: weight_x[x] * weight_y),
        has_z,
        last_z,
        band_z,
        over_z,
    )
    make_band(
        1,
        sub4,
        8,
        last_y * rows_of(y_next),
        rows_of(y_prev),
        stacked(lambda x: weight_x[x] * weight_z),
        has_y,
        last_y,
        band_y,
        over_y,
    )
    weight_yz = weight_y * weight_z
    planes = [mu[x] for x in range(4)] + [mu_next_x]
    for i in range(4):
        for j in range(i, 5):
            value = sum(float(GRAM[k, i, j]) * planes[k] for k in range(5))
            if i == 0 and j == 0:
                value = value + sum_prev_x + has_x * float(GRAM[4, 4, 4]) * mu[0]
            if j == 4:
                value = last_x * value
            band_x[5 * i + j] = value * weight_yz
    for x in range(4):
        band_z[0, x] = band_z[0, x] + band_y[0, x] + band_x[6 * x]

    def coupling_x(i, j):
        return band_x[5 * min(i, j) + max(i, j)]

    def face_values(number, ref):
        field = ref[...].reshape(3, 4, 8, LANES)
        for c in range(3):
            x_send[number, 0, c] = field[c, 0]
            x_send[number, 1, c] = sum(coupling_x(i, 4) * field[c, i] for i in range(4))
        y_send[number, 0, 0:12] = ref[pl.ds(0, 12, stride=8), :]
        part_ref[...] = (over_y[...][None] * field).reshape(96, LANES)
        y_send[number, 1, 0:12] = sum(
            part_ref[pl.ds(4 + k, 12, stride=8), :] for k in range(4)
        )
        z_send[number, 0] = columns_to_lanes(
            [field[c, x][:, 0:1] for c in range(3) for x in range(4)]
        )
        z_send[number, 1] = columns_to_lanes(
            [
                jnp.sum(over_z[x] * field[c, x], axis=1, keepdims=True)
                for c in range(3)
                for x in range(4)
            ]
        )
        return send_faces(number, 3, 16)

    def inner_stiffness(ref):
        field = ref[...].reshape(3, 4, 8, LANES)
        out = []
        for x in range(4):
            plane = field[:, x]
            total = band_z[0, x] * plane
            for s in range(1, 5):
                total = total + band_z[s, x] * pltpu.roll(plane, LANES - s, 2)
                total = total + band_z[4 + s, x] * pltpu.roll(plane, s, 2)
                total = total + band_y[s, x] * pltpu.roll(plane, 8 - s, 1)
                if s < 4:
                    total = total + band_y[4 + s, x] * pltpu.roll(plane, s, 1)
            for j in range(4):
                if j != x:
                    total = total + coupling_x(x, j) * field[:, j]
            out.append(total)
        return out

    def outer_stiffness(number, copies, inside):
        for copy in copies:
            copy.wait_recv()
        y_first = y_recv[number, 1, 0:12]
        y_after = y_recv[number, 0, 0:12]
        spread_ref[pl.ds(0, 12, stride=8), :] = y_first
        for k in range(4):
            spread_ref[pl.ds(4 + k, 12, stride=8), :] = y_after
        spread = spread_ref[...].reshape(3, 4, 8, LANES)
        z_first, z_after = z_recv[number, 1], z_recv[number, 0]
        x_after, x_first = x_recv[number, 0], x_recv[number, 1]
        out = []
        for x in range(4):
            rows = []
            for c in range(3):
                at = 4 * c + x
                row = inside[x][c] + coupling_x(x, 4) * x_after[c]
                row = row + jnp.where(sub == 0, F32(1.0), over_y[x]) * spread[c, x]
                row = row + jnp.where(
                    lane == 0,
                    jnp.broadcast_to(z_first[:, at : at + 1], (8, LANES)),
                    over_z[x] * jnp.broadcast_to(z_after[:, at : at + 1], (8, LANES)),
                )
                if x == 0:
                    row = row + x_first[c]
                rows.append(row)
            out.append(rows)
        return out

    spread_ref[...] = jnp.zeros((96, LANES), F32)
    loads["slab"].wait()
    now_copies = face_values(1, slab_ref)

    for copy in group_in:
        copy.wait_recv()
    total = group_send[gy]
    for step in range(1, n_gy):
        total = total + group_recv[step]
    rows16 = iota((n_gx, LANES), 0)
    lanes16 = iota((n_gx, LANES), 1)
    outgoing = jnp.zeros((n_gx, LANES), F32)
    for c in range(4):
        line = total[c : c + 1] if c < 3 else mark_ref[0:1]
        line = jnp.broadcast_to(line, (8, LANES))
        if (RANKS * (c + 1 - n_gx)) % LANES:
            line = pltpu.roll(line, (RANKS * (c + 1 - n_gx)) % LANES, 1)
        moved = pltpu.roll(
            jnp.broadcast_to(line[0:1], (n_gx, LANES)), 0, 1, stride=RANKS, stride_axis=0
        )
        outgoing = jnp.where(lanes16 >> 3 == c, moved, outgoing)
    owner_send[...] = outgoing.reshape(n_gx, 1, LANES)
    if len(reaches) > 2:
        hear(2)
    for step in range(1, n_gx):
        peer = away("gx", step)
        sent.append(
            push(
                owner_send.at[n_gx - 1 - peer["gx"]],
                owner_recv.at[step],
                owner_sems,
                (step,),
                peer,
            )
        )
    owner_in = sent[-(n_gx - 1) :]
    owner_recv[0] = owner_send[n_gx - 1 - gx]

    inside = inner_stiffness(slab_ref)
    loads["before"].wait()
    loads["mass"].wait()
    around = outer_stiffness(1, now_copies, inside)
    for x in range(4):
        scale = slab_factor * mass_ref[8 * x : 8 * x + 8, :]
        for c in range(3):
            at = 32 * c + 8 * x
            base_ref[at : at + 8, :] = (
                2.0 * slab_ref[at : at + 8, :]
                - before_ref[at : at + 8, :]
                - scale * around[x][c]
            )

    for copy in owner_in:
        copy.wait_recv()
    arrived = owner_recv[...].reshape(n_gx, LANES)
    lines = []
    moved = pltpu.roll(arrived, 0, 1, stride=RANKS, stride_axis=0)
    for c in range(4):
        own = ((lanes16 >> 3) - rows16 - c) & 15 == 0
        line = jnp.sum(jnp.where(own, moved, F32(0.0)), axis=0, keepdims=True)
        if c:
            line = pltpu.roll(jnp.broadcast_to(line, (8, LANES)), LANES - RANKS * c, 1)[0:1]
        lines.append(line)
    goal = lines[3].astype(jnp.int32)
    goal_row, goal_lane = goal >> 7, goal & 127
    rows32 = iota((32, LANES), 0)
    spots = jnp.concatenate(
        [jnp.where(rows32 == goal_row, lines[c], F32(0.0)) for c in range(3)], axis=0
    )
    high, low = halves(spots)
    on_lane = (iota((LANES, LANES), 0) == goal_lane).astype(F32).astype(BF16)
    force = dot_rows(
        jnp.concatenate([high, low], axis=1), jnp.concatenate([on_lane, on_lane], axis=1)
    )
    force_ref[...] = force
    outs.append(pltpu.make_async_copy(force_ref, force_out, out_sem.at[1]))
    outs[1].start()
    for x in range(4):
        scale = slab_factor * mass_ref[8 * x : 8 * x + 8, :]
        for c in range(3):
            at = 32 * c + 8 * x
            step_ref[at : at + 8, :] = base_ref[at : at + 8, :] + scale * force[at : at + 8]

    step_copies = face_values(2, step_ref)
    inside = inner_stiffness(step_ref)
    around = outer_stiffness(2, step_copies, inside)
    for x in range(4):
        scale = slab_factor * mass_ref[8 * x : 8 * x + 8, :]
        for c in range(3):
            at = 32 * c + 8 * x
            last_ref[at : at + 8, :] = (
                2.0 * step_ref[at : at + 8, :]
                - slab_ref[at : at + 8, :]
                + scale * (force_ref[at : at + 8, :] - around[x][c])
            )
    outs.append(pltpu.make_async_copy(last_ref, slab_out, out_sem.at[2]))
    outs[2].start()
    for copy in sent:
        copy.wait_send()
    for copy in outs:
        copy.wait()


def solution(mesh):
    n_gx, n_gy, n_gz = (mesh.shape[name] for name in ("gx", "gy", "gz"))

    def on_device(
        global_now,
        global_prev,
        cycle_modes,
        wave_speed,
        inv_radius,
        theta_second,
        theta_first,
        point_dest,
        point_target,
        point_source,
        point_azimuth,
        regional_now,
        regional_prev,
        moduli,
        inv_mass,
    ):
        points = point_target.shape[1]
        big = [((192, LANES), F32)] * 2 + [((8, LANES), F32)] * 2 + [((LANES, LANES), F32)] * 2
        big += [((1, points), jnp.int32)] * 3 + [((1, points), F32)]
        big += [((96, LANES), F32)] * 2 + [((32, LANES), F32)] * 2
        scratch = [pltpu.SMEM(cycle_modes.shape, jnp.int32)]
        scratch += [pltpu.VMEM(shape, dtype) for shape, dtype in big]
        scratch += [
            pltpu.VMEM((192, LANES), F32),
            pltpu.VMEM((192, LANES), F32),
            pltpu.VMEM((192, LANES), F32),
            pltpu.VMEM((2 * LANES, 2 * LANES), BF16),
            pltpu.VMEM((2 * LANES, 2 * LANES), BF16),
            pltpu.VMEM((2 * LANES, points), BF16),
            pltpu.VMEM((8, 8, points), F32),
            pltpu.VMEM((LANES, points), BF16),
            pltpu.VMEM((8, LANES), F32),
            pltpu.VMEM((96, LANES), F32),
            pltpu.VMEM((96, LANES), F32),
            pltpu.VMEM((96, LANES), F32),
            pltpu.VMEM((96, LANES), F32),
            pltpu.VMEM((9, 4, 8, LANES), F32),
            pltpu.VMEM((9, 4, 8, LANES), F32),
            pltpu.VMEM((20, 8, LANES), F32),
            pltpu.VMEM((4, 8, LANES), F32),
            pltpu.VMEM((4, 8, LANES), F32),
            pltpu.VMEM((96, LANES), F32),
            pltpu.VMEM((96, LANES), F32),
            pltpu.VMEM((2, 56, LANES), F32),
            pltpu.VMEM((2, 56, LANES), F32),
            pltpu.VMEM((3, 2, 3, 8, LANES), F32),
            pltpu.VMEM((3, 2, 3, 8, LANES), F32),
            pltpu.VMEM((3, 2, 16, LANES), F32),
            pltpu.VMEM((3, 2, 16, LANES), F32),
            pltpu.VMEM((3, 2, 8, LANES), F32),
            pltpu.VMEM((3, 2, 8, LANES), F32),
            pltpu.VMEM((n_gy, 4, LANES), F32),
            pltpu.VMEM((n_gy, 4, LANES), F32),
            pltpu.VMEM((n_gx, 1, LANES), F32),
            pltpu.VMEM((n_gx, 1, LANES), F32),
            pltpu.SemaphoreType.DMA((15,)),
            pltpu.SemaphoreType.DMA((3,)),
            pltpu.SemaphoreType.DMA((2, 2)),
            pltpu.SemaphoreType.DMA((2, 3, 6)),
            pltpu.SemaphoreType.DMA((2, n_gy)),
            pltpu.SemaphoreType.DMA((2, n_gx)),
            pltpu.SemaphoreType.REGULAR((3,)),
        ]
        hbm = pl.BlockSpec(memory_space=pl.ANY)
        two, slab, force = pl.pallas_call(
            functools.partial(kernel, (n_gx, n_gy, n_gz)),
            out_shape=[
                pltpu.VMEM((192, LANES), F32),
                pltpu.VMEM((96, LANES), F32),
                pltpu.VMEM((96, LANES), F32),
            ],
            in_specs=[hbm] * 15,
            out_specs=[hbm] * 3,
            scratch_shapes=scratch,
            compiler_params=pltpu.CompilerParams(
                collective_id=0, has_side_effects=True, vmem_limit_bytes=48 * 2**20
            ),
        )(
            *[
                pltpu.with_memory_space_constraint(x, pltpu.HBM)
                for x in (
            cycle_modes,
            global_now.reshape(192, LANES),
            global_prev.reshape(192, LANES),
            wave_speed,
            inv_radius,
            theta_second,
            theta_first,
            point_dest.reshape(1, points),
            point_target,
            point_source,
            point_azimuth,
            regional_now.reshape(96, LANES),
            regional_prev.reshape(96, LANES),
            moduli.reshape(32, LANES),
            inv_mass.reshape(32, LANES),
            )]
        )
        return (
            two.reshape(global_now.shape),
            slab.reshape(regional_now.shape),
            force.reshape(regional_now.shape),
        )

    return jax.shard_map(
        on_device,
        mesh=mesh,
        in_specs=(
            P("gy", None, "gx", None),
            P("gy", None, "gx", None),
            P("gx"),
            P("gx", None),
            P("gx", None),
            P(),
            P(),
            P("gz", "gx", None),
            P("gz", "gx"),
            P("gz", "gx"),
            P("gz", "gx"),
            P(None, "gx", "gy", "gz"),
            P(None, "gx", "gy", "gz"),
            P("gx", "gy", "gz"),
            P("gx", "gy", "gz"),
        ),
        out_specs=(P("gy", None, "gx", None), P(None, "gx", "gy", "gz"), P(None, "gx", "gy", "gz")),
        check_vma=False,
    )
```

```python
import functools
import math

import jax
import jax.numpy as jnp
import numpy as np
from jax import lax
from jax.experimental import pallas as pl
from jax.experimental.pallas import tpu as pltpu
from jax.sharding import PartitionSpec as P

F32 = jnp.float32
BF16 = jnp.bfloat16
MESH = pl.DeviceIdType.MESH

time_step = 0.3
time_sq = 0.09
impedance = 0.5
coupling = 0.05
slab_factor = 0.04

LANES = 128
RANKS = 8


def gll_products():
    nodes = np.array([-1.0, -math.sqrt(3.0 / 7.0), 0.0, math.sqrt(3.0 / 7.0), 1.0])
    weights = np.array([0.1, 49.0 / 90.0, 32.0 / 45.0, 49.0 / 90.0, 0.1])
    factor = np.array(
        [np.prod([nodes[i] - nodes[k] for k in range(5) if k != i]) for i in range(5)]
    )
    deriv = np.zeros((5, 5))
    for i in range(5):
        for j in range(5):
            if i != j:
                deriv[i, j] = factor[i] / factor[j] / (nodes[i] - nodes[j])
            else:
                deriv[i, j] = sum((1.0 / (nodes[i] - nodes[k]) for k in range(5) if k != i))
    return weights, np.einsum("ki,k,kj->kij", deriv, weights, deriv)


WEIGHTS, GRAM = gll_products()


def cosine_series():
    f = np.cos(np.linspace(0.0, np.pi / 2, 2001)) * 0.5
    fit = np.polynomial.chebyshev.Chebyshev.fit(f * f, np.cos(2 * np.pi * f), 8, domain=[0, 0.25])
    return [float(v) for v in fit.convert(kind=np.polynomial.Polynomial).coef]


COSINE = cosine_series()


def halves(x):
    high = x.astype(BF16)
    return high, (x - high.astype(F32)).astype(BF16)


def dot(a, b):
    return lax.dot_general(a, b, (((1,), (0,)), ((), ())), preferred_element_type=F32)


def dot_rows(a, b):
    return lax.dot_general(a, b, (((1,), (1,)), ((), ())), preferred_element_type=F32)


def operator_pair(t):
    high, low = halves(t)
    top = jnp.concatenate([high, low], axis=1)
    bottom = jnp.concatenate([high, jnp.zeros_like(low)], axis=1)
    return jnp.concatenate([top, bottom], axis=0)


def times_operator(x, pair_ref):
    high, low = halves(x)
    both = dot(jnp.concatenate([high, low], axis=1), pair_ref[...])
    return both[:, :LANES] + both[:, LANES:]


def iota(shape, axis):
    return lax.broadcasted_iota(jnp.int32, shape, axis)


def by_four(phase, values):
    out = jnp.full(phase.shape, values[3], F32)
    for i in (2, 1, 0):
        out = jnp.where(phase == i, F32(values[i]), out)
    return out


def kernel(
    sizes,
    modes_in,
    now_in,
    prev_in,
    speed_in,
    radius_in,
    second_in,
    first_in,
    dest_in,
    target_in,
    source_in,
    azimuth_in,
    slab_in,
    before_in,
    moduli_in,
    mass_in,
    g_out,
    slab_out,
    force_out,
    modes_ref,
    now_ref,
    prev_ref,
    speed_ref,
    radius_ref,
    second_ref,
    first_ref,
    dest_ref,
    target_ref,
    source_ref,
    azimuth_ref,
    slab_ref,
    before_ref,
    moduli_ref,
    mass_ref,
    one_ref,
    edge_ref,
    pair_second,
    pair_first,
    pick_ref,
    trig_ref,
    slot_ref,
    mark_ref,
    base_ref,
    step_ref,
    band_z,
    band_y,
    band_x,
    over_z,
    over_y,
    spread_ref,
    part_ref,
    cycle_send,
    cycle_recv,
    x_send,
    x_recv,
    y_send,
    y_recv,
    z_send,
    z_recv,
    group_send,
    group_recv,
    owner_send,
    owner_recv,
    in_sem,
    cycle_sems,
    face_sems,
    group_sems,
    owner_sems,
    ring_sems,
):
    n_gx, n_gy, n_gz = sizes
    gx, gy, gz = lax.axis_index("gx"), lax.axis_index("gy"), lax.axis_index("gz")
    points = dest_ref.shape[1]

    loads = {}
    for number, (name, src, dst) in enumerate(
        (
            ("modes", modes_in, modes_ref),
            ("now", now_in, now_ref),
            ("prev", prev_in, prev_ref),
            ("speed", speed_in, speed_ref),
            ("radius", radius_in, radius_ref),
            ("moduli", moduli_in, moduli_ref),
            ("second", second_in, second_ref),
            ("dest", dest_in, dest_ref),
            ("target", target_in, target_ref),
            ("source", source_in, source_ref),
            ("azimuth", azimuth_in, azimuth_ref),
            ("first", first_in, first_ref),
            ("slab", slab_in, slab_ref),
            ("before", before_in, before_ref),
            ("mass", mass_in, mass_ref),
        )
    ):
        loads[name] = pltpu.make_async_copy(src, dst, in_sem.at[number])
        loads[name].start()

    def away(axis, step):
        index, count = {"gx": (gx, n_gx), "gy": (gy, n_gy), "gz": (gz, n_gz)}[axis]
        return {axis: lax.rem(index + step + count, count)}

    barrier = pltpu.get_barrier_semaphore()
    for step in range(1, n_gy):
        pl.semaphore_signal(barrier, inc=1, device_id=away("gy", step), device_id_type=MESH)
    there = {
        ("gx", -1): gx > 0,
        ("gx", 1): gx < n_gx - 1,
        ("gy", -1): gy > 0,
        ("gy", 1): gy < n_gy - 1,
        ("gz", -1): gz > 0,
        ("gz", 1): gz < n_gz - 1,
    }
    greeted = n_gy - 1 + len({1, n_gx - 1})
    for step in sorted({1, n_gx - 1}):
        pl.semaphore_signal(barrier, inc=1, device_id=away("gx", step), device_id_type=MESH)
    for step in (-1, 1):
        greeted = greeted + there["gz", step].astype(jnp.int32)

        @pl.when(there["gz", step])
        def _(step=step):
            pl.semaphore_signal(
                barrier, inc=1, device_id=away("gz", step), device_id_type=MESH
            )

    def push(src, dst, sems, index, device):
        copy = pltpu.make_async_remote_copy(
            src_ref=src,
            dst_ref=dst,
            send_sem=sems.at[(0, *index)],
            recv_sem=sems.at[(1, *index)],
            device_id=device,
            device_id_type=MESH,
        )
        copy.start()
        return copy

    class Neighbour:
        def __init__(self, src, dst, sems, index, axis, step):
            self.copy = pltpu.make_async_remote_copy(
                src_ref=src,
                dst_ref=dst,
                send_sem=sems.at[(0, *index)],
                recv_sem=sems.at[(1, *index)],
                device_id=away(axis, step),
                device_id_type=MESH,
            )
            self.sends, self.receives = there[axis, step], there[axis, -step]
            pl.when(self.sends)(lambda: self.copy.start())

        def wait_recv(self):
            pl.when(self.receives)(lambda: self.copy.wait_recv())

        def wait_send(self):
            pl.when(self.sends)(lambda: self.copy.wait_send())

    for (axis, step), here in there.items():

        @pl.when(jnp.logical_not(here))
        def _(axis=axis, side=(1 - step) // 2):
            if axis == "gx":
                cycle_recv[side] = jnp.zeros(cycle_recv.shape[1:], F32)
                x_recv[:, side] = jnp.zeros((3, 3, 8, LANES), F32)
            elif axis == "gy":
                y_recv[:, side] = jnp.zeros((3, 16, LANES), F32)
            else:
                z_recv[:, side] = jnp.zeros((3, 8, LANES), F32)

    sub = iota((8, LANES), 0)
    lane = iota((8, LANES), 1)

    mode_base = (4 * gy).astype(F32)
    row24 = iota((24, LANES), 0)
    order24 = mode_base + (
        (row24 >= 6).astype(F32) + (row24 >= 12).astype(F32) + (row24 >= 18).astype(F32)
    )
    square24 = order24 * order24
    for name in ("modes", "now", "prev", "speed", "radius"):
        loads[name].wait()
    for side, (edge, inner) in enumerate(((0, 1), (7, 6))):
        count = modes_ref[edge].astype(F32)
        mask = jnp.where(order24 < count, F32(1.0), F32(0.0))
        speed = speed_ref[edge : edge + 1, :]
        radius = radius_ref[edge : edge + 1, :]
        at_edge = now_ref[pl.ds(edge, 24, stride=8), :]
        cycle_send[side, 0:24, :] = at_edge
        cycle_send[side, 24:48, :] = mask * (
            (2.0 - 2.0 * time_sq * speed - time_sq * square24 * radius) * at_edge
            - prev_ref[pl.ds(edge, 24, stride=8), :]
            + time_sq * speed * now_ref[pl.ds(inner, 24, stride=8), :]
        )
        cycle_send[side, 48:56, :] = jnp.where(
            sub == 0, jnp.broadcast_to(speed, (8, LANES)), jnp.full((8, LANES), count, F32)
        )

    pl.semaphore_wait(barrier, greeted)

    reaches = [reach for reach in (1, 2, 4) if 2 * reach < n_gx]

    def tell(level):
        for step in (reaches[level], -reaches[level]):
            pl.semaphore_signal(
                ring_sems.at[level], inc=1, device_id=away("gx", step), device_id_type=MESH
            )

    def hear(level):
        pl.semaphore_wait(ring_sems.at[level], 2)

    tell(0)
    sent = []
    cycle_in = []
    for side, step in ((0, -1), (1, 1)):
        copy = Neighbour(
            cycle_send.at[side], cycle_recv.at[side], cycle_sems, (side,), "gx", step
        )
        sent.append(copy)
        cycle_in.append(copy)

    last_x = jnp.where(gx < n_gx - 1, F32(1.0), F32(0.0))
    last_y = jnp.where(gy < n_gy - 1, F32(1.0), F32(0.0))
    last_z = jnp.where(gz < n_gz - 1, F32(1.0), F32(0.0))
    has_x = jnp.where(gx > 0, F32(1.0), F32(0.0))
    has_y = jnp.where(gy > 0, F32(1.0), F32(0.0))
    has_z = jnp.where(gz > 0, F32(1.0), F32(0.0))

    def send_faces(number, x_count, y_count):
        copies = []
        for side, step in ((0, -1), (1, 1)):
            for place, (axis, src, dst) in enumerate(
                (
                    ("gx", x_send.at[number, side, 0:x_count], x_recv.at[number, side, 0:x_count]),
                    ("gy", y_send.at[number, side, 0:y_count], y_recv.at[number, side, 0:y_count]),
                    ("gz", z_send.at[number, side], z_recv.at[number, side]),
                )
            ):
                copies.append(
                    Neighbour(src, dst, face_sems, (number, 2 * place + side), axis, step)
                )
        sent.extend(copies)
        return copies

    def columns_to_lanes(columns):
        out = jnp.zeros((8, LANES), F32)
        for number, column in enumerate(columns):
            out = jnp.where(lane == number, jnp.broadcast_to(column, (8, LANES)), out)
        return out

    loads["moduli"].wait()
    inner = [float(GRAM[k, 4, 4]) for k in range(5)]
    mu = moduli_ref[...].reshape(4, 8, LANES)
    x_send[0, 0, 0] = mu[0]
    x_send[0, 1, 0] = last_x * (
        inner[0] * mu[0] + inner[1] * mu[1] + inner[2] * mu[2] + inner[3] * mu[3]
    )
    y_send[0, 0, 0:8] = jnp.zeros((8, LANES), F32)
    y_send[0, 1, 0:8] = jnp.zeros((8, LANES), F32)
    y_send[0, 0, 0:4] = moduli_ref[pl.ds(0, 4, stride=8), :]
    y_send[0, 1, 0:4] = last_y * sum(
        inner[k] * moduli_ref[pl.ds(4 + k, 4, stride=8), :] for k in range(4)
    )
    tail = by_four(lane & 3, inner[:4]) * jnp.where(lane >= LANES - 4, last_z, F32(0.0))
    z_send[0, 0] = columns_to_lanes([mu[x][:, 0:1] for x in range(4)])
    z_send[0, 1] = columns_to_lanes(
        [jnp.sum(tail * mu[x], axis=1, keepdims=True) for x in range(4)]
    )
    moduli_copies = send_faces(0, 1, 8)

    hear(0)
    if len(reaches) > 1:
        tell(1)

    loads["second"].wait()
    pair_second[...] = operator_pair(second_ref[...])
    counts = jnp.zeros((8, LANES), F32)
    for row in range(8):
        counts = jnp.where(sub == row, modes_ref[row].astype(F32), counts)
    order = mode_base + iota((4, 8, LANES), 0).astype(F32)
    mask = jnp.where(order < counts[None], F32(1.0), F32(0.0))
    speed, radius = speed_ref[...][None], radius_ref[...][None]
    hold = (mask * (2.0 - 2.0 * time_sq * speed - time_sq * (order * order) * radius))[:, None]
    side_weight = (mask * (time_sq * speed))[:, None]
    bend_weight = (mask * time_sq)[:, None]
    mask = mask[:, None]

    def section_sum(now, prev):
        cells = now.reshape(24, 8, LANES)
        rows = iota((24, 8, LANES), 1)
        near = jnp.where(rows == 0, F32(0.0), pltpu.roll(cells, 1, 1)) + jnp.where(
            rows == 7, F32(0.0), pltpu.roll(cells, 7, 1)
        )
        return (
            hold * now.reshape(4, 6, 8, LANES)
            - mask * prev.reshape(4, 6, 8, LANES)
            + side_weight * near.reshape(4, 6, 8, LANES)
            + bend_weight * times_operator(now, pair_second).reshape(4, 6, 8, LANES)
        )

    one_ref[...] = section_sum(now_ref[...], prev_ref[...]).reshape(192, LANES)
    edge_ref[...] = jnp.zeros((192, LANES), F32)

    for name in ("dest", "target", "source", "azimuth"):
        loads[name].wait()
    owner = dest_ref[...]
    blocks = points // LANES
    named = (iota((LANES, points), 0) == owner).astype(F32)
    named_rows = jnp.concatenate(
        [named[:, b * LANES : (b + 1) * LANES] for b in range(blocks)], axis=0
    ).astype(BF16)
    before = (iota((LANES, LANES), 0) < iota((LANES, LANES), 1)).astype(F32)
    counted = dot(
        named_rows, jnp.concatenate([before, jnp.ones_like(before)], axis=1).astype(BF16)
    )
    ranks, offset = [], None
    for b in range(blocks):
        piece = counted[b * LANES : (b + 1) * LANES]
        place = piece[:, :LANES] if offset is None else piece[:, :LANES] + offset
        ranks.append(
            jnp.sum(named[:, b * LANES : (b + 1) * LANES] * place, axis=0, keepdims=True)
        )
        offset = piece[:, LANES:] if offset is None else offset + piece[:, LANES:]
    rank = jnp.concatenate(ranks, axis=1).astype(jnp.int32)
    if n_gy == 8:
        owner_x, owner_y = owner >> 3, owner & 7
    else:
        owner_x, owner_y = owner >> 1, owner & 1
    slot = owner_x * RANKS + rank
    slot_ref[...] = (iota((LANES, points), 0) == slot).astype(F32).astype(BF16)
    target = target_ref[...]
    mine = jnp.where(owner_y == gy, F32(1.0), F32(0.0))
    sub_p = iota((8, points), 0)
    marks = jnp.where(
        sub_p == 0,
        (target >> 7).astype(F32) * mine,
        jnp.where(sub_p == 1, (target & 127).astype(F32) * mine, F32(0.0)),
    )
    marked = dot_rows(marks.astype(BF16), slot_ref[...])
    mark_ref[...] = jnp.broadcast_to(128.0 * marked[0:1] + marked[1:2], (8, LANES))
    source = source_ref[...]
    picked = (iota((LANES, points), 0) == (source & 127)).astype(F32).astype(BF16)
    pick_ref[0:LANES, :] = picked
    pick_ref[LANES:, :] = picked
    turns = (mode_base + (sub_p & 3).astype(F32)) * (azimuth_ref[...] * (0.5 / math.pi))
    turns = turns - jnp.where(sub_p >= 4, F32(0.25), F32(0.0))
    turns = turns - jnp.floor(turns + 0.5)
    square = turns * turns
    wave = jnp.full(square.shape, COSINE[-1], F32)
    for value in COSINE[-2::-1]:
        wave = wave * square + value
    in_cycle = sub_p == (source >> 7)
    for row in range(8):
        trig_ref[row] = jnp.where(
            in_cycle, jnp.broadcast_to(wave[row : row + 1], (8, points)), F32(0.0)
        )
    loads["first"].wait()
    pair_first[...] = operator_pair(first_ref[...])

    for copy in cycle_in:
        copy.wait_recv()
    flags = (last_x, has_x)
    near_edges = [cycle_recv[side, 0:24, :] for side in range(2)]
    bends = times_operator(jnp.concatenate(near_edges, axis=0), pair_second)
    beyond = []
    for side, edge in ((0, 7), (1, 0)):
        tail_rows = cycle_recv[side, 48:56, :]
        speed24 = tail_rows[0:1]
        mask24 = jnp.where(order24 < tail_rows[1:2], F32(1.0), F32(0.0))
        edge_ref[pl.ds(edge, 24, stride=8), :] = flags[side] * near_edges[side]
        value = cycle_recv[side, 24:48, :] + mask24 * time_sq * (
            speed24 * now_ref[pl.ds(edge, 24, stride=8), :] + bends[24 * side : 24 * side + 24]
        )
        beyond.append(flags[side] * value)
    one = one_ref[...].reshape(4, 6, 8, LANES) + side_weight * edge_ref[...].reshape(
        4, 6, 8, LANES
    )
    one = one.reshape(192, LANES)
    for side, edge in ((0, 7), (1, 0)):
        edge_ref[pl.ds(edge, 24, stride=8), :] = beyond[side]
    two = section_sum(one, now_ref[...]) + side_weight * edge_ref[...].reshape(4, 6, 8, LANES)
    two = two.reshape(192, LANES)
    g_out[...] = two

    coef = coupling * times_operator(two, pair_first) + (coupling * impedance / time_step) * (
        two - one
    )
    high, low = halves(coef)
    at_points = dot(jnp.concatenate([high, low], axis=1), pick_ref[...]).reshape(
        4, 6, 8, points
    )
    values = jnp.zeros((8, points), F32)
    for c in range(3):
        total = jnp.zeros((8, points), F32)
        for m in range(4):
            total = total + at_points[m, 2 * c] * trig_ref[m]
            total = total + at_points[m, 2 * c + 1] * trig_ref[4 + m]
        values = jnp.where(
            (sub_p & 3) == c,
            jnp.broadcast_to(jnp.sum(total, axis=0, keepdims=True), (8, points)),
            values,
        )
    by_group = jnp.concatenate(
        [
            jnp.where(owner_y == 2 * t + (sub_p >> 2), values, F32(0.0))
            for t in range(n_gy // 2)
        ],
        axis=0,
    )
    high, low = halves(by_group)
    packed = dot_rows(jnp.concatenate([high, low], axis=0), slot_ref[...])
    packed = packed[: 4 * n_gy] + packed[4 * n_gy :]
    for group in range(n_gy):
        group_send[group] = packed[4 * group : 4 * group + 4]
    for step in range(1, n_gy):
        peer = away("gy", step)
        sent.append(
            push(
                group_send.at[peer["gy"]],
                group_recv.at[step],
                group_sems,
                (step,),
                peer,
            )
        )
    group_in = sent[-(n_gy - 1) :]

    if len(reaches) > 1:
        hear(1)
    if len(reaches) > 2:
        tell(2)

    for copy in moduli_copies:
        copy.wait_recv()
    mu_next_x = last_x * x_recv[0, 0, 0]
    sum_prev_x = x_recv[0, 1, 0]
    lane4 = iota((4, 8, LANES), 2)
    sub4 = iota((4, 8, LANES), 1)
    side_w = [0.2] + [float(v) for v in WEIGHTS[1:4]]
    first_weight = -float(WEIGHTS[4])
    weight_y = by_four(sub & 3, side_w) + jnp.where(
        sub == 0, (1.0 - has_y) * first_weight, F32(0.0)
    )
    weight_z = by_four(lane & 3, side_w) + jnp.where(
        lane == 0, (1.0 - has_z) * first_weight, F32(0.0)
    )
    weight_x = [side_w[0] + (1.0 - has_x) * first_weight] + side_w[1:]

    def make_band(axis, position, count, following, preceding, weights, has, last, band, over):
        shifted = {0: mu}
        for t in range(-4, 5):
            if t:
                rolled = pltpu.roll(mu, (-t) % count, axis)
                if t > 0:
                    rolled = jnp.where(position == count - t, following, rolled)
                shifted[t] = rolled
        pos2 = position[0]
        phase = pos2 & 3
        later = pos2 > 3
        band_values = []
        for s in range(5):
            total = None
            for t in range(s - 4, 5):
                row = [
                    GRAM[i + t, i, i + s] if 0 <= i + t <= 4 and i + s <= 4 else 0.0
                    for i in range(4)
                ]
                pattern = by_four(phase, row)
                if s == 0 and t <= 0:
                    pattern = pattern + jnp.where(
                        (phase == 0) & later, F32(GRAM[4 + t, 4, 4]), F32(0.0)
                    )
                term = pattern[None] * shifted[t]
                total = term if total is None else total + term
            if s == 0:
                total = total + jnp.where(
                    position == 0, preceding + has * float(GRAM[4, 4, 4]) * mu, F32(0.0)
                )
            band_values.append(total * weights)
        crossing = jnp.zeros_like(mu)
        for s in range(1, 5):
            crossing = jnp.where(position == count - s, band_values[s], crossing)
            inside = jnp.where(position >= count - s, F32(0.0), band_values[s])
            behind = pltpu.roll(inside, s, axis)
            if 2 * s == count:
                band[s] = inside + behind
                band[4 + s] = jnp.zeros_like(inside)
            else:
                band[s] = inside
                band[4 + s] = behind
        over[...] = last * crossing
        band[0] = band_values[0]

    y_next = y_recv[0, 0, 0:8]
    y_prev = y_recv[0, 1, 0:8]
    z_next = z_recv[0, 0]
    z_prev = z_recv[0, 1]

    def rows_of(value):
        return jnp.concatenate(
            [jnp.broadcast_to(value[x : x + 1], (8, LANES))[None] for x in range(4)], axis=0
        )

    def columns_of(value):
        return jnp.concatenate(
            [jnp.broadcast_to(value[:, x : x + 1], (8, LANES))[None] for x in range(4)], axis=0
        )

    stacked = lambda scale: jnp.concatenate([(scale(x))[None] for x in range(4)], axis=0)
    make_band(
        2,
        lane4,
        LANES,
        last_z * columns_of(z_next),
        columns_of(z_prev),
        stacked(lambda x: weight_x[x] * weight_y),
        has_z,
        last_z,
        band_z,
        over_z,
    )
    make_band(
        1,
        sub4,
        8,
        last_y * rows_of(y_next),
        rows_of(y_prev),
        stacked(lambda x: weight_x[x] * weight_z),
        has_y,
        last_y,
        band_y,
        over_y,
    )
    weight_yz = weight_y * weight_z
    planes = [mu[x] for x in range(4)] + [mu_next_x]
    for i in range(4):
        for j in range(i, 5):
            value = sum(float(GRAM[k, i, j]) * planes[k] for k in range(5))
            if i == 0 and j == 0:
                value = value + sum_prev_x + has_x * float(GRAM[4, 4, 4]) * mu[0]
            if j == 4:
                value = last_x * value
            band_x[5 * i + j] = value * weight_yz
    for x in range(4):
        band_z[0, x] = band_z[0, x] + band_y[0, x] + band_x[6 * x]

    def coupling_x(i, j):
        return band_x[5 * min(i, j) + max(i, j)]

    def face_values(number, ref):
        field = ref[...].reshape(3, 4, 8, LANES)
        for c in range(3):
            x_send[number, 0, c] = field[c, 0]
            x_send[number, 1, c] = sum(coupling_x(i, 4) * field[c, i] for i in range(4))
        y_send[number, 0, 0:12] = ref[pl.ds(0, 12, stride=8), :]
        part_ref[...] = (over_y[...][None] * field).reshape(96, LANES)
        y_send[number, 1, 0:12] = sum(
            part_ref[pl.ds(4 + k, 12, stride=8), :] for k in range(4)
        )
        z_send[number, 0] = columns_to_lanes(
            [field[c, x][:, 0:1] for c in range(3) for x in range(4)]
        )
        z_send[number, 1] = columns_to_lanes(
            [
                jnp.sum(over_z[x] * field[c, x], axis=1, keepdims=True)
                for c in range(3)
                for x in range(4)
            ]
        )
        return send_faces(number, 3, 16)

    def inner_stiffness(ref):
        field = ref[...].reshape(3, 4, 8, LANES)
        out = []
        for x in range(4):
            plane = field[:, x]
            total = band_z[0, x] * plane
            for s in range(1, 5):
                total = total + band_z[s, x] * pltpu.roll(plane, LANES - s, 2)
                total = total + band_z[4 + s, x] * pltpu.roll(plane, s, 2)
                total = total + band_y[s, x] * pltpu.roll(plane, 8 - s, 1)
                if s < 4:
                    total = total + band_y[4 + s, x] * pltpu.roll(plane, s, 1)
            for j in range(4):
                if j != x:
                    total = total + coupling_x(x, j) * field[:, j]
            out.append(total)
        return out

    def outer_stiffness(number, copies, inside):
        for copy in copies:
            copy.wait_recv()
        y_first = y_recv[number, 1, 0:12]
        y_after = y_recv[number, 0, 0:12]
        spread_ref[pl.ds(0, 12, stride=8), :] = y_first
        for k in range(4):
            spread_ref[pl.ds(4 + k, 12, stride=8), :] = y_after
        spread = spread_ref[...].reshape(3, 4, 8, LANES)
        z_first, z_after = z_recv[number, 1], z_recv[number, 0]
        x_after, x_first = x_recv[number, 0], x_recv[number, 1]
        out = []
        for x in range(4):
            rows = []
            for c in range(3):
                at = 4 * c + x
                row = inside[x][c] + coupling_x(x, 4) * x_after[c]
                row = row + jnp.where(sub == 0, F32(1.0), over_y[x]) * spread[c, x]
                row = row + jnp.where(
                    lane == 0,
                    jnp.broadcast_to(z_first[:, at : at + 1], (8, LANES)),
                    over_z[x] * jnp.broadcast_to(z_after[:, at : at + 1], (8, LANES)),
                )
                if x == 0:
                    row = row + x_first[c]
                rows.append(row)
            out.append(rows)
        return out

    spread_ref[...] = jnp.zeros((96, LANES), F32)
    loads["slab"].wait()
    now_copies = face_values(1, slab_ref)

    for copy in group_in:
        copy.wait_recv()
    total = group_send[gy]
    for step in range(1, n_gy):
        total = total + group_recv[step]
    rows16 = iota((n_gx, LANES), 0)
    lanes16 = iota((n_gx, LANES), 1)
    outgoing = jnp.zeros((n_gx, LANES), F32)
    for c in range(4):
        line = total[c : c + 1] if c < 3 else mark_ref[0:1]
        line = jnp.broadcast_to(line, (8, LANES))
        if (RANKS * (c + 1 - n_gx)) % LANES:
            line = pltpu.roll(line, (RANKS * (c + 1 - n_gx)) % LANES, 1)
        moved = pltpu.roll(
            jnp.broadcast_to(line[0:1], (n_gx, LANES)), 0, 1, stride=RANKS, stride_axis=0
        )
        outgoing = jnp.where(lanes16 >> 3 == c, moved, outgoing)
    owner_send[...] = outgoing.reshape(n_gx, 1, LANES)
    if len(reaches) > 2:
        hear(2)
    for step in range(1, n_gx):
        peer = away("gx", step)
        sent.append(
            push(
                owner_send.at[n_gx - 1 - peer["gx"]],
                owner_recv.at[step],
                owner_sems,
                (step,),
                peer,
            )
        )
    owner_in = sent[-(n_gx - 1) :]
    owner_recv[0] = owner_send[n_gx - 1 - gx]

    inside = inner_stiffness(slab_ref)
    loads["before"].wait()
    loads["mass"].wait()
    around = outer_stiffness(1, now_copies, inside)
    for x in range(4):
        scale = slab_factor * mass_ref[8 * x : 8 * x + 8, :]
        for c in range(3):
            at = 32 * c + 8 * x
            base_ref[at : at + 8, :] = (
                2.0 * slab_ref[at : at + 8, :]
                - before_ref[at : at + 8, :]
                - scale * around[x][c]
            )

    for copy in owner_in:
        copy.wait_recv()
    arrived = owner_recv[...].reshape(n_gx, LANES)
    lines = []
    moved = pltpu.roll(arrived, 0, 1, stride=RANKS, stride_axis=0)
    for c in range(4):
        own = ((lanes16 >> 3) - rows16 - c) & 15 == 0
        line = jnp.sum(jnp.where(own, moved, F32(0.0)), axis=0, keepdims=True)
        if c:
            line = pltpu.roll(jnp.broadcast_to(line, (8, LANES)), LANES - RANKS * c, 1)[0:1]
        lines.append(line)
    goal = lines[3].astype(jnp.int32)
    goal_row, goal_lane = goal >> 7, goal & 127
    rows32 = iota((32, LANES), 0)
    spots = jnp.concatenate(
        [jnp.where(rows32 == goal_row, lines[c], F32(0.0)) for c in range(3)], axis=0
    )
    high, low = halves(spots)
    on_lane = (iota((LANES, LANES), 0) == goal_lane).astype(F32).astype(BF16)
    force = dot_rows(
        jnp.concatenate([high, low], axis=1), jnp.concatenate([on_lane, on_lane], axis=1)
    )
    force_out[...] = force
    for x in range(4):
        scale = slab_factor * mass_ref[8 * x : 8 * x + 8, :]
        for c in range(3):
            at = 32 * c + 8 * x
            step_ref[at : at + 8, :] = base_ref[at : at + 8, :] + scale * force[at : at + 8]

    step_copies = face_values(2, step_ref)
    inside = inner_stiffness(step_ref)
    around = outer_stiffness(2, step_copies, inside)
    for x in range(4):
        scale = slab_factor * mass_ref[8 * x : 8 * x + 8, :]
        for c in range(3):
            at = 32 * c + 8 * x
            slab_out[at : at + 8, :] = (
                2.0 * step_ref[at : at + 8, :]
                - slab_ref[at : at + 8, :]
                + scale * (force_out[at : at + 8, :] - around[x][c])
            )
    for copy in sent:
        copy.wait_send()


def copy_out(*refs):
    sems = refs[6]
    copies = [pltpu.make_async_copy(refs[i], refs[3 + i], sems.at[i]) for i in range(3)]
    for copy in copies:
        copy.start()
    for copy in copies:
        copy.wait()


def solution(mesh):
    n_gx, n_gy, n_gz = (mesh.shape[name] for name in ("gx", "gy", "gz"))

    def on_device(
        global_now,
        global_prev,
        cycle_modes,
        wave_speed,
        inv_radius,
        theta_second,
        theta_first,
        point_dest,
        point_target,
        point_source,
        point_azimuth,
        regional_now,
        regional_prev,
        moduli,
        inv_mass,
    ):
        points = point_target.shape[1]
        big = [((192, LANES), F32)] * 2 + [((8, LANES), F32)] * 2 + [((LANES, LANES), F32)] * 2
        big += [((1, points), jnp.int32)] * 3 + [((1, points), F32)]
        big += [((96, LANES), F32)] * 2 + [((32, LANES), F32)] * 2
        scratch = [pltpu.SMEM(cycle_modes.shape, jnp.int32)]
        scratch += [pltpu.VMEM(shape, dtype) for shape, dtype in big]
        scratch += [
            pltpu.VMEM((192, LANES), F32),
            pltpu.VMEM((192, LANES), F32),
            pltpu.VMEM((2 * LANES, 2 * LANES), BF16),
            pltpu.VMEM((2 * LANES, 2 * LANES), BF16),
            pltpu.VMEM((2 * LANES, points), BF16),
            pltpu.VMEM((8, 8, points), F32),
            pltpu.VMEM((LANES, points), BF16),
            pltpu.VMEM((8, LANES), F32),
            pltpu.VMEM((96, LANES), F32),
            pltpu.VMEM((96, LANES), F32),
            pltpu.VMEM((9, 4, 8, LANES), F32),
            pltpu.VMEM((9, 4, 8, LANES), F32),
            pltpu.VMEM((20, 8, LANES), F32),
            pltpu.VMEM((4, 8, LANES), F32),
            pltpu.VMEM((4, 8, LANES), F32),
            pltpu.VMEM((96, LANES), F32),
            pltpu.VMEM((96, LANES), F32),
            pltpu.VMEM((2, 56, LANES), F32),
            pltpu.VMEM((2, 56, LANES), F32),
            pltpu.VMEM((3, 2, 3, 8, LANES), F32),
            pltpu.VMEM((3, 2, 3, 8, LANES), F32),
            pltpu.VMEM((3, 2, 16, LANES), F32),
            pltpu.VMEM((3, 2, 16, LANES), F32),
            pltpu.VMEM((3, 2, 8, LANES), F32),
            pltpu.VMEM((3, 2, 8, LANES), F32),
            pltpu.VMEM((n_gy, 4, LANES), F32),
            pltpu.VMEM((n_gy, 4, LANES), F32),
            pltpu.VMEM((n_gx, 1, LANES), F32),
            pltpu.VMEM((n_gx, 1, LANES), F32),
            pltpu.SemaphoreType.DMA((15,)),
            pltpu.SemaphoreType.DMA((2, 2)),
            pltpu.SemaphoreType.DMA((2, 3, 6)),
            pltpu.SemaphoreType.DMA((2, n_gy)),
            pltpu.SemaphoreType.DMA((2, n_gx)),
            pltpu.SemaphoreType.REGULAR((3,)),
        ]
        hbm = pl.BlockSpec(memory_space=pl.ANY)
        two, slab, force = pl.pallas_call(
            functools.partial(kernel, (n_gx, n_gy, n_gz)),
            out_shape=[
                pltpu.VMEM((192, LANES), F32),
                pltpu.VMEM((96, LANES), F32),
                pltpu.VMEM((96, LANES), F32),
            ],
            in_specs=[hbm] * 15,
            out_specs=[pl.BlockSpec(memory_space=pltpu.VMEM)] * 3,
            scratch_shapes=scratch,
            compiler_params=pltpu.CompilerParams(
                collective_id=0, has_side_effects=True, vmem_limit_bytes=48 * 2**20
            ),
        )(
            *[
                pltpu.with_memory_space_constraint(x, pltpu.HBM)
                for x in (
            cycle_modes,
            global_now.reshape(192, LANES),
            global_prev.reshape(192, LANES),
            wave_speed,
            inv_radius,
            theta_second,
            theta_first,
            point_dest.reshape(1, points),
            point_target,
            point_source,
            point_azimuth,
            regional_now.reshape(96, LANES),
            regional_prev.reshape(96, LANES),
            moduli.reshape(32, LANES),
            inv_mass.reshape(32, LANES),
            )]
        )
        two, slab, force = pl.pallas_call(
            copy_out,
            out_shape=[
                pltpu.HBM((192, LANES), F32),
                pltpu.HBM((96, LANES), F32),
                pltpu.HBM((96, LANES), F32),
            ],
            in_specs=[hbm] * 3,
            out_specs=[hbm] * 3,
            scratch_shapes=[pltpu.SemaphoreType.DMA((3,))],
        )(*[pltpu.with_memory_space_constraint(x, pltpu.VMEM) for x in (two, slab, force)])
        return (
            two.reshape(global_now.shape),
            slab.reshape(regional_now.shape),
            force.reshape(regional_now.shape),
        )

    return jax.shard_map(
        on_device,
        mesh=mesh,
        in_specs=(
            P("gy", None, "gx", None),
            P("gy", None, "gx", None),
            P("gx"),
            P("gx", None),
            P("gx", None),
            P(),
            P(),
            P("gz", "gx", None),
            P("gz", "gx"),
            P("gz", "gx"),
            P("gz", "gx"),
            P(None, "gx", "gy", "gz"),
            P(None, "gx", "gy", "gz"),
            P("gx", "gy", "gz"),
            P("gx", "gy", "gz"),
        ),
        out_specs=(P("gy", None, "gx", None), P(None, "gx", "gy", "gz"), P(None, "gx", "gy", "gz")),
        check_vma=False,
    )
```

```python
import functools
import math

import jax
import jax.numpy as jnp
import numpy as np
from jax import lax
from jax.experimental import pallas as pl
from jax.experimental.pallas import tpu as pltpu
from jax.sharding import PartitionSpec as P

F32 = jnp.float32
BF16 = jnp.bfloat16
MESH = pl.DeviceIdType.MESH

time_step = 0.3
time_sq = 0.09
impedance = 0.5
coupling = 0.05
slab_factor = 0.04

LANES = 128
RANKS = 8


def gll_products():
    nodes = np.array([-1.0, -math.sqrt(3.0 / 7.0), 0.0, math.sqrt(3.0 / 7.0), 1.0])
    weights = np.array([0.1, 49.0 / 90.0, 32.0 / 45.0, 49.0 / 90.0, 0.1])
    factor = np.array(
        [np.prod([nodes[i] - nodes[k] for k in range(5) if k != i]) for i in range(5)]
    )
    deriv = np.zeros((5, 5))
    for i in range(5):
        for j in range(5):
            if i != j:
                deriv[i, j] = factor[i] / factor[j] / (nodes[i] - nodes[j])
            else:
                deriv[i, j] = sum((1.0 / (nodes[i] - nodes[k]) for k in range(5) if k != i))
    return weights, np.einsum("ki,k,kj->kij", deriv, weights, deriv)


WEIGHTS, GRAM = gll_products()


def cosine_series():
    f = np.cos(np.linspace(0.0, np.pi / 2, 2001)) * 0.5
    fit = np.polynomial.chebyshev.Chebyshev.fit(f * f, np.cos(2 * np.pi * f), 8, domain=[0, 0.25])
    return [float(v) for v in fit.convert(kind=np.polynomial.Polynomial).coef]


COSINE = cosine_series()


def halves(x):
    high = x.astype(BF16)
    return high, (x - high.astype(F32)).astype(BF16)


def dot(a, b):
    return lax.dot_general(a, b, (((1,), (0,)), ((), ())), preferred_element_type=F32)


def dot_rows(a, b):
    return lax.dot_general(a, b, (((1,), (1,)), ((), ())), preferred_element_type=F32)


def operator_pair(t):
    high, low = halves(t)
    top = jnp.concatenate([high, low], axis=1)
    bottom = jnp.concatenate([high, jnp.zeros_like(low)], axis=1)
    return jnp.concatenate([top, bottom], axis=0)


def times_operator(x, pair_ref):
    high, low = halves(x)
    both = dot(jnp.concatenate([high, low], axis=1), pair_ref[...])
    return both[:, :LANES] + both[:, LANES:]


def iota(shape, axis):
    return lax.broadcasted_iota(jnp.int32, shape, axis)


def by_four(phase, values):
    out = jnp.full(phase.shape, values[3], F32)
    for i in (2, 1, 0):
        out = jnp.where(phase == i, F32(values[i]), out)
    return out


def kernel(
    sizes,
    modes_in,
    now_in,
    prev_in,
    speed_in,
    radius_in,
    second_in,
    first_in,
    dest_in,
    target_in,
    source_in,
    azimuth_in,
    slab_in,
    before_in,
    moduli_in,
    mass_in,
    g_out,
    slab_out,
    force_out,
    modes_ref,
    now_ref,
    prev_ref,
    speed_ref,
    radius_ref,
    second_ref,
    first_ref,
    dest_ref,
    target_ref,
    source_ref,
    azimuth_ref,
    slab_ref,
    before_ref,
    moduli_ref,
    mass_ref,
    one_ref,
    edge_ref,
    pair_second,
    pair_first,
    pick_ref,
    trig_ref,
    slot_ref,
    mark_ref,
    base_ref,
    step_ref,
    band_z,
    band_y,
    band_x,
    over_z,
    over_y,
    spread_ref,
    part_ref,
    cycle_send,
    cycle_recv,
    x_send,
    x_recv,
    y_send,
    y_recv,
    z_send,
    z_recv,
    group_send,
    group_recv,
    owner_send,
    owner_recv,
    in_sem,
    cycle_sems,
    face_sems,
    group_sems,
    owner_sems,
    ring_sems,
):
    n_gx, n_gy, n_gz = sizes
    gx, gy, gz = lax.axis_index("gx"), lax.axis_index("gy"), lax.axis_index("gz")
    points = dest_ref.shape[1]
    core, chip = lax.rem(gy, 2), lax.div(gy, 2)
    chips = n_gy // 2

    loads = {}
    for number, (name, src, dst) in enumerate(
        (
            ("modes", modes_in, modes_ref),
            ("now", now_in, now_ref),
            ("prev", prev_in, prev_ref),
            ("speed", speed_in, speed_ref),
            ("radius", radius_in, radius_ref),
            ("moduli", moduli_in, moduli_ref),
            ("second", second_in, second_ref),
            ("dest", dest_in, dest_ref),
            ("target", target_in, target_ref),
            ("source", source_in, source_ref),
            ("azimuth", azimuth_in, azimuth_ref),
            ("first", first_in, first_ref),
            ("slab", slab_in, slab_ref),
            ("before", before_in, before_ref),
            ("mass", mass_in, mass_ref),
        )
    ):
        loads[name] = pltpu.make_async_copy(src, dst, in_sem.at[number])
        loads[name].start()

    def away(axis, step):
        index, count = {"gx": (gx, n_gx), "gy": (gy, n_gy), "gz": (gz, n_gz)}[axis]
        return {axis: lax.rem(index + step + count, count)}

    barrier = pltpu.get_barrier_semaphore()
    for step in range(1, n_gy):
        pl.semaphore_signal(barrier, inc=1, device_id=away("gy", step), device_id_type=MESH)
    there = {
        ("gx", -1): gx > 0,
        ("gx", 1): gx < n_gx - 1,
        ("gy", -1): gy > 0,
        ("gy", 1): gy < n_gy - 1,
        ("gz", -1): gz > 0,
        ("gz", 1): gz < n_gz - 1,
    }
    greeted = n_gy - 1 + len({1, n_gx - 1})
    for step in sorted({1, n_gx - 1}):
        pl.semaphore_signal(barrier, inc=1, device_id=away("gx", step), device_id_type=MESH)
    for step in (-1, 1):
        greeted = greeted + there["gz", step].astype(jnp.int32)

        @pl.when(there["gz", step])
        def _(step=step):
            pl.semaphore_signal(
                barrier, inc=1, device_id=away("gz", step), device_id_type=MESH
            )

    def push(src, dst, sems, index, device):
        copy = pltpu.make_async_remote_copy(
            src_ref=src,
            dst_ref=dst,
            send_sem=sems.at[(0, *index)],
            recv_sem=sems.at[(1, *index)],
            device_id=device,
            device_id_type=MESH,
        )
        copy.start()
        return copy

    class Neighbour:
        def __init__(self, src, dst, sems, index, axis, step):
            self.copy = pltpu.make_async_remote_copy(
                src_ref=src,
                dst_ref=dst,
                send_sem=sems.at[(0, *index)],
                recv_sem=sems.at[(1, *index)],
                device_id=away(axis, step),
                device_id_type=MESH,
            )
            self.sends, self.receives = there[axis, step], there[axis, -step]
            pl.when(self.sends)(lambda: self.copy.start())

        def wait_recv(self):
            pl.when(self.receives)(lambda: self.copy.wait_recv())

        def wait_send(self):
            pl.when(self.sends)(lambda: self.copy.wait_send())

    for (axis, step), here in there.items():

        @pl.when(jnp.logical_not(here))
        def _(axis=axis, side=(1 - step) // 2):
            if axis == "gx":
                cycle_recv[side] = jnp.zeros(cycle_recv.shape[1:], F32)
                x_recv[:, side] = jnp.zeros((3, 3, 8, LANES), F32)
            elif axis == "gy":
                y_recv[:, side] = jnp.zeros((3, 16, LANES), F32)
            else:
                z_recv[:, side] = jnp.zeros((3, 8, LANES), F32)

    sub = iota((8, LANES), 0)
    lane = iota((8, LANES), 1)

    mode_base = (4 * gy).astype(F32)
    row24 = iota((24, LANES), 0)
    order24 = mode_base + (
        (row24 >= 6).astype(F32) + (row24 >= 12).astype(F32) + (row24 >= 18).astype(F32)
    )
    square24 = order24 * order24
    for name in ("modes", "now", "prev", "speed", "radius"):
        loads[name].wait()
    for side, (edge, inner) in enumerate(((0, 1), (7, 6))):
        count = modes_ref[edge].astype(F32)
        mask = jnp.where(order24 < count, F32(1.0), F32(0.0))
        speed = speed_ref[edge : edge + 1, :]
        radius = radius_ref[edge : edge + 1, :]
        at_edge = now_ref[pl.ds(edge, 24, stride=8), :]
        cycle_send[side, 0:24, :] = at_edge
        cycle_send[side, 24:48, :] = mask * (
            (2.0 - 2.0 * time_sq * speed - time_sq * square24 * radius) * at_edge
            - prev_ref[pl.ds(edge, 24, stride=8), :]
            + time_sq * speed * now_ref[pl.ds(inner, 24, stride=8), :]
        )
        cycle_send[side, 48:56, :] = jnp.where(
            sub == 0, jnp.broadcast_to(speed, (8, LANES)), jnp.full((8, LANES), count, F32)
        )

    pl.semaphore_wait(barrier, greeted)

    reaches, known = [], 0
    while known < n_gx // 2:
        reaches.append(min(known + 1, n_gx // 2 - known))
        known += reaches[-1]

    def tell(level):
        for step in (reaches[level], -reaches[level]):
            pl.semaphore_signal(
                ring_sems.at[level], inc=1, device_id=away("gx", step), device_id_type=MESH
            )

    def hear(level):
        pl.semaphore_wait(ring_sems.at[level], 2)

    def advance(level):
        if level < len(reaches):
            hear(level)
        if level + 1 < len(reaches):
            tell(level + 1)

    tell(0)
    sent = []
    cycle_in = []
    for side, step in ((0, -1), (1, 1)):
        copy = Neighbour(
            cycle_send.at[side], cycle_recv.at[side], cycle_sems, (side,), "gx", step
        )
        sent.append(copy)
        cycle_in.append(copy)

    last_x = jnp.where(gx < n_gx - 1, F32(1.0), F32(0.0))
    last_y = jnp.where(gy < n_gy - 1, F32(1.0), F32(0.0))
    last_z = jnp.where(gz < n_gz - 1, F32(1.0), F32(0.0))
    has_x = jnp.where(gx > 0, F32(1.0), F32(0.0))
    has_y = jnp.where(gy > 0, F32(1.0), F32(0.0))
    has_z = jnp.where(gz > 0, F32(1.0), F32(0.0))

    def send_faces(number, x_count, y_count):
        copies = []
        for side, step in ((0, -1), (1, 1)):
            for place, (axis, src, dst) in enumerate(
                (
                    ("gx", x_send.at[number, side, 0:x_count], x_recv.at[number, side, 0:x_count]),
                    ("gy", y_send.at[number, side, 0:y_count], y_recv.at[number, side, 0:y_count]),
                    ("gz", z_send.at[number, side], z_recv.at[number, side]),
                )
            ):
                copies.append(
                    Neighbour(src, dst, face_sems, (number, 2 * place + side), axis, step)
                )
        sent.extend(copies)
        return copies

    def columns_to_lanes(columns):
        out = jnp.zeros((8, LANES), F32)
        for number, column in enumerate(columns):
            out = jnp.where(lane == number, jnp.broadcast_to(column, (8, LANES)), out)
        return out

    loads["moduli"].wait()
    inner = [float(GRAM[k, 4, 4]) for k in range(5)]
    mu = moduli_ref[...].reshape(4, 8, LANES)
    x_send[0, 0, 0] = mu[0]
    x_send[0, 1, 0] = last_x * (
        inner[0] * mu[0] + inner[1] * mu[1] + inner[2] * mu[2] + inner[3] * mu[3]
    )
    y_send[0, 0, 0:8] = jnp.zeros((8, LANES), F32)
    y_send[0, 1, 0:8] = jnp.zeros((8, LANES), F32)
    y_send[0, 0, 0:4] = moduli_ref[pl.ds(0, 4, stride=8), :]
    y_send[0, 1, 0:4] = last_y * sum(
        inner[k] * moduli_ref[pl.ds(4 + k, 4, stride=8), :] for k in range(4)
    )
    tail = by_four(lane & 3, inner[:4]) * jnp.where(lane >= LANES - 4, last_z, F32(0.0))
    z_send[0, 0] = columns_to_lanes([mu[x][:, 0:1] for x in range(4)])
    z_send[0, 1] = columns_to_lanes(
        [jnp.sum(tail * mu[x], axis=1, keepdims=True) for x in range(4)]
    )
    moduli_copies = send_faces(0, 1, 8)

    chain = min(n_gx - 1, 10)

    @pl.when((gx > 0) & (gx <= chain))
    def _():
        pl.semaphore_wait(ring_sems.at[len(reaches)], 1)

    @pl.when(gx < chain)
    def _():
        pl.semaphore_signal(
            ring_sems.at[len(reaches)], inc=1, device_id=away("gx", 1), device_id_type=MESH
        )

    advance(0)

    loads["second"].wait()
    pair_second[...] = operator_pair(second_ref[...])
    counts = jnp.zeros((8, LANES), F32)
    for row in range(8):
        counts = jnp.where(sub == row, modes_ref[row].astype(F32), counts)
    order = mode_base + iota((4, 8, LANES), 0).astype(F32)
    mask = jnp.where(order < counts[None], F32(1.0), F32(0.0))
    speed, radius = speed_ref[...][None], radius_ref[...][None]
    hold = (mask * (2.0 - 2.0 * time_sq * speed - time_sq * (order * order) * radius))[:, None]
    side_weight = (mask * (time_sq * speed))[:, None]
    bend_weight = (mask * time_sq)[:, None]
    mask = mask[:, None]

    def section_sum(now, prev):
        cells = now.reshape(24, 8, LANES)
        rows = iota((24, 8, LANES), 1)
        near = jnp.where(rows == 0, F32(0.0), pltpu.roll(cells, 1, 1)) + jnp.where(
            rows == 7, F32(0.0), pltpu.roll(cells, 7, 1)
        )
        return (
            hold * now.reshape(4, 6, 8, LANES)
            - mask * prev.reshape(4, 6, 8, LANES)
            + side_weight * near.reshape(4, 6, 8, LANES)
            + bend_weight * times_operator(now, pair_second).reshape(4, 6, 8, LANES)
        )

    one_ref[...] = section_sum(now_ref[...], prev_ref[...]).reshape(192, LANES)
    edge_ref[...] = jnp.zeros((192, LANES), F32)

    for name in ("dest", "target", "source", "azimuth"):
        loads[name].wait()
    owner = dest_ref[...]
    blocks = points // LANES
    named = (iota((LANES, points), 0) == owner).astype(F32)
    named_rows = jnp.concatenate(
        [named[:, b * LANES : (b + 1) * LANES] for b in range(blocks)], axis=0
    ).astype(BF16)
    before = (iota((LANES, LANES), 0) < iota((LANES, LANES), 1)).astype(F32)
    counted = dot(
        named_rows, jnp.concatenate([before, jnp.ones_like(before)], axis=1).astype(BF16)
    )
    ranks, offset = [], None
    for b in range(blocks):
        piece = counted[b * LANES : (b + 1) * LANES]
        place = piece[:, :LANES] if offset is None else piece[:, :LANES] + offset
        ranks.append(
            jnp.sum(named[:, b * LANES : (b + 1) * LANES] * place, axis=0, keepdims=True)
        )
        offset = piece[:, LANES:] if offset is None else offset + piece[:, LANES:]
    rank = jnp.concatenate(ranks, axis=1).astype(jnp.int32)
    if n_gy == 8:
        owner_x, owner_y = owner >> 3, owner & 7
    else:
        owner_x, owner_y = owner >> 1, owner & 1
    slot = owner_x * RANKS + rank
    slot_ref[...] = (iota((LANES, points), 0) == slot).astype(F32).astype(BF16)
    target = target_ref[...]
    sub_p = iota((8, points), 0)
    mine = owner_y == 2 * (sub_p & 3) + core
    marks = jnp.where(sub_p < 4, target >> 7, target & 127).astype(F32)
    marked = dot_rows(jnp.where(mine, marks, F32(0.0)).astype(BF16), slot_ref[...])
    mark_ref[0:4, :] = (128.0 / chips) * marked[0:4] + (1.0 / chips) * marked[4:8]
    source = source_ref[...]
    picked = (iota((LANES, points), 0) == (source & 127)).astype(F32).astype(BF16)
    pick_ref[0:LANES, :] = picked
    pick_ref[LANES:, :] = picked
    turns = (mode_base + (sub_p & 3).astype(F32)) * (azimuth_ref[...] * (0.5 / math.pi))
    turns = turns - jnp.where(sub_p >= 4, F32(0.25), F32(0.0))
    turns = turns - jnp.floor(turns + 0.5)
    square = turns * turns
    wave = jnp.full(square.shape, COSINE[-1], F32)
    for value in COSINE[-2::-1]:
        wave = wave * square + value
    in_cycle = sub_p == (source >> 7)
    for row in range(8):
        trig_ref[row] = jnp.where(
            in_cycle, jnp.broadcast_to(wave[row : row + 1], (8, points)), F32(0.0)
        )
    loads["first"].wait()
    pair_first[...] = operator_pair(first_ref[...])

    advance(1)

    for copy in cycle_in:
        copy.wait_recv()
    flags = (last_x, has_x)
    near_edges = [cycle_recv[side, 0:24, :] for side in range(2)]
    bends = times_operator(jnp.concatenate(near_edges, axis=0), pair_second)
    beyond = []
    for side, edge in ((0, 7), (1, 0)):
        tail_rows = cycle_recv[side, 48:56, :]
        speed24 = tail_rows[0:1]
        mask24 = jnp.where(order24 < tail_rows[1:2], F32(1.0), F32(0.0))
        edge_ref[pl.ds(edge, 24, stride=8), :] = flags[side] * near_edges[side]
        value = cycle_recv[side, 24:48, :] + mask24 * time_sq * (
            speed24 * now_ref[pl.ds(edge, 24, stride=8), :] + bends[24 * side : 24 * side + 24]
        )
        beyond.append(flags[side] * value)
    one = one_ref[...].reshape(4, 6, 8, LANES) + side_weight * edge_ref[...].reshape(
        4, 6, 8, LANES
    )
    one = one.reshape(192, LANES)
    for side, edge in ((0, 7), (1, 0)):
        edge_ref[pl.ds(edge, 24, stride=8), :] = beyond[side]
    two = section_sum(one, now_ref[...]) + side_weight * edge_ref[...].reshape(4, 6, 8, LANES)
    two = two.reshape(192, LANES)
    g_out[...] = two

    coef = coupling * times_operator(two, pair_first) + (coupling * impedance / time_step) * (
        two - one
    )
    high, low = halves(coef)
    at_points = dot(jnp.concatenate([high, low], axis=1), pick_ref[...]).reshape(
        4, 6, 8, points
    )
    values = jnp.zeros((8, points), F32)
    for c in range(3):
        total = jnp.zeros((8, points), F32)
        for m in range(4):
            total = total + at_points[m, 2 * c] * trig_ref[m]
            total = total + at_points[m, 2 * c + 1] * trig_ref[4 + m]
        values = jnp.where(
            (sub_p & 3) == c,
            jnp.broadcast_to(jnp.sum(total, axis=0, keepdims=True), (8, points)),
            values,
        )
    half = 8 * max(1, chips // 2)
    by_group = jnp.concatenate(
        [
            jnp.where(owner_y == 2 * (2 * tile + (sub_p >> 2)) + side, values, F32(0.0))
            for side in range(2)
            for tile in range(half // 8)
        ],
        axis=0,
    )
    high, low = halves(by_group)
    packed = dot_rows(jnp.concatenate([high, low], axis=0), slot_ref[...])
    packed = packed[: 2 * half] + packed[2 * half :]
    for side in range(2):
        group_send[side] = packed[half * side : half * side + half]
    pair = push(
        group_send.at[1 - core], group_recv, group_sems, (), {"gy": gy + 1 - 2 * core}
    )
    sent.append(pair)

    pair.wait_recv()
    total = group_send[core] + group_recv[...]
    rows16 = iota((n_gx, LANES), 0)
    lanes16 = iota((n_gx, LANES), 1)
    for place in range(chips):
        outgoing = jnp.zeros((n_gx, LANES), F32)
        for c in range(4):
            at = 4 * place + c
            line = total[at : at + 1] if c < 3 else mark_ref[place : place + 1]
            line = jnp.broadcast_to(line, (8, LANES))
            if (RANKS * (c + 1 - n_gx)) % LANES:
                line = pltpu.roll(line, (RANKS * (c + 1 - n_gx)) % LANES, 1)
            moved = pltpu.roll(
                jnp.broadcast_to(line[0:1], (n_gx, LANES)), 0, 1, stride=RANKS, stride_axis=0
            )
            outgoing = jnp.where(lanes16 >> 3 == c, moved, outgoing)
        owner_send[place] = outgoing.reshape(n_gx, 1, LANES)

    def to_row(a):
        for b in range(chips):
            if a or b:
                peer_x, peer_chip = away("gx", a)["gx"], lax.rem(chip + b, chips)
                pltpu.make_async_remote_copy(
                    src_ref=owner_send.at[peer_chip, n_gx - 1 - peer_x],
                    dst_ref=owner_recv.at[b * n_gx + a],
                    send_sem=owner_sems.at[0],
                    recv_sem=owner_sems.at[1],
                    device_id={"gx": peer_x, "gy": 2 * peer_chip + core},
                    device_id_type=MESH,
                ).start()

    far_first = sorted(range(n_gx), key=lambda a: -min(a, n_gx - a))
    early = {a: (gx <= chain) & (gx + a >= n_gx) for a in far_first}
    for a in far_first:
        pl.when(early[a])(functools.partial(to_row, a))
    first = min(2, len(reaches) - 1)
    for level in range(first, len(reaches)):
        if level >= 2:
            advance(level)
        reach = sum(reaches[: level + 1])
        for a in far_first:
            distance = min(a, n_gx - a)
            if distance <= reach and (level == first or distance > reach - reaches[level]):
                pl.when(jnp.logical_not(early[a]))(functools.partial(to_row, a))
    owner_recv[0] = owner_send[chip, n_gx - 1 - gx]
    rows_all = chips * n_gx
    owner_in = pltpu.make_async_remote_copy(
        src_ref=owner_recv.at[1:rows_all],
        dst_ref=owner_recv.at[1:rows_all],
        send_sem=owner_sems.at[0],
        recv_sem=owner_sems.at[1],
        device_id=away("gx", 1),
        device_id_type=MESH,
    )

    for copy in moduli_copies:
        copy.wait_recv()
    mu_next_x = last_x * x_recv[0, 0, 0]
    sum_prev_x = x_recv[0, 1, 0]
    lane4 = iota((4, 8, LANES), 2)
    sub4 = iota((4, 8, LANES), 1)
    side_w = [0.2] + [float(v) for v in WEIGHTS[1:4]]
    first_weight = -float(WEIGHTS[4])
    weight_y = by_four(sub & 3, side_w) + jnp.where(
        sub == 0, (1.0 - has_y) * first_weight, F32(0.0)
    )
    weight_z = by_four(lane & 3, side_w) + jnp.where(
        lane == 0, (1.0 - has_z) * first_weight, F32(0.0)
    )
    weight_x = [side_w[0] + (1.0 - has_x) * first_weight] + side_w[1:]

    def make_band(axis, position, count, following, preceding, weights, has, last, band, over):
        shifted = {0: mu}
        for t in range(-4, 5):
            if t:
                rolled = pltpu.roll(mu, (-t) % count, axis)
                if t > 0:
                    rolled = jnp.where(position == count - t, following, rolled)
                shifted[t] = rolled
        pos2 = position[0]
        phase = pos2 & 3
        later = pos2 > 3
        band_values = []
        for s in range(5):
            total = None
            for t in range(s - 4, 5):
                row = [
                    GRAM[i + t, i, i + s] if 0 <= i + t <= 4 and i + s <= 4 else 0.0
                    for i in range(4)
                ]
                pattern = by_four(phase, row)
                if s == 0 and t <= 0:
                    pattern = pattern + jnp.where(
                        (phase == 0) & later, F32(GRAM[4 + t, 4, 4]), F32(0.0)
                    )
                term = pattern[None] * shifted[t]
                total = term if total is None else total + term
            if s == 0:
                total = total + jnp.where(
                    position == 0, preceding + has * float(GRAM[4, 4, 4]) * mu, F32(0.0)
                )
            band_values.append(total * weights)
        crossing = jnp.zeros_like(mu)
        for s in range(1, 5):
            crossing = jnp.where(position == count - s, band_values[s], crossing)
            inside = jnp.where(position >= count - s, F32(0.0), band_values[s])
            behind = pltpu.roll(inside, s, axis)
            if 2 * s == count:
                band[s] = inside + behind
                band[4 + s] = jnp.zeros_like(inside)
            else:
                band[s] = inside
                band[4 + s] = behind
        over[...] = last * crossing
        band[0] = band_values[0]

    y_next = y_recv[0, 0, 0:8]
    y_prev = y_recv[0, 1, 0:8]
    z_next = z_recv[0, 0]
    z_prev = z_recv[0, 1]

    def rows_of(value):
        return jnp.concatenate(
            [jnp.broadcast_to(value[x : x + 1], (8, LANES))[None] for x in range(4)], axis=0
        )

    def columns_of(value):
        return jnp.concatenate(
            [jnp.broadcast_to(value[:, x : x + 1], (8, LANES))[None] for x in range(4)], axis=0
        )

    stacked = lambda scale: jnp.concatenate([(scale(x))[None] for x in range(4)], axis=0)
    make_band(
        2,
        lane4,
        LANES,
        last_z * columns_of(z_next),
        columns_of(z_prev),
        stacked(lambda x: weight_x[x] * weight_y),
        has_z,
        last_z,
        band_z,
        over_z,
    )
    make_band(
        1,
        sub4,
        8,
        last_y * rows_of(y_next),
        rows_of(y_prev),
        stacked(lambda x: weight_x[x] * weight_z),
        has_y,
        last_y,
        band_y,
        over_y,
    )
    weight_yz = weight_y * weight_z
    planes = [mu[x] for x in range(4)] + [mu_next_x]
    for i in range(4):
        for j in range(i, 5):
            value = sum(float(GRAM[k, i, j]) * planes[k] for k in range(5))
            if i == 0 and j == 0:
                value = value + sum_prev_x + has_x * float(GRAM[4, 4, 4]) * mu[0]
            if j == 4:
                value = last_x * value
            band_x[5 * i + j] = value * weight_yz
    for x in range(4):
        band_z[0, x] = band_z[0, x] + band_y[0, x] + band_x[6 * x]

    def coupling_x(i, j):
        return band_x[5 * min(i, j) + max(i, j)]

    def face_values(number, ref):
        field = ref[...].reshape(3, 4, 8, LANES)
        for c in range(3):
            x_send[number, 0, c] = field[c, 0]
            x_send[number, 1, c] = sum(coupling_x(i, 4) * field[c, i] for i in range(4))
        y_send[number, 0, 0:12] = ref[pl.ds(0, 12, stride=8), :]
        part_ref[...] = (over_y[...][None] * field).reshape(96, LANES)
        y_send[number, 1, 0:12] = sum(
            part_ref[pl.ds(4 + k, 12, stride=8), :] for k in range(4)
        )
        z_send[number, 0] = columns_to_lanes(
            [field[c, x][:, 0:1] for c in range(3) for x in range(4)]
        )
        z_send[number, 1] = columns_to_lanes(
            [
                jnp.sum(over_z[x] * field[c, x], axis=1, keepdims=True)
                for c in range(3)
                for x in range(4)
            ]
        )
        return send_faces(number, 3, 16)

    def inner_stiffness(ref):
        field = ref[...].reshape(3, 4, 8, LANES)
        out = []
        for x in range(4):
            plane = field[:, x]
            total = band_z[0, x] * plane
            for s in range(1, 5):
                total = total + band_z[s, x] * pltpu.roll(plane, LANES - s, 2)
                total = total + band_z[4 + s, x] * pltpu.roll(plane, s, 2)
                total = total + band_y[s, x] * pltpu.roll(plane, 8 - s, 1)
                if s < 4:
                    total = total + band_y[4 + s, x] * pltpu.roll(plane, s, 1)
            for j in range(4):
                if j != x:
                    total = total + coupling_x(x, j) * field[:, j]
            out.append(total)
        return out

    def outer_stiffness(number, copies, inside):
        for copy in copies:
            copy.wait_recv()
        y_first = y_recv[number, 1, 0:12]
        y_after = y_recv[number, 0, 0:12]
        spread_ref[pl.ds(0, 12, stride=8), :] = y_first
        for k in range(4):
            spread_ref[pl.ds(4 + k, 12, stride=8), :] = y_after
        spread = spread_ref[...].reshape(3, 4, 8, LANES)
        z_first, z_after = z_recv[number, 1], z_recv[number, 0]
        x_after, x_first = x_recv[number, 0], x_recv[number, 1]
        out = []
        for x in range(4):
            rows = []
            for c in range(3):
                at = 4 * c + x
                row = inside[x][c] + coupling_x(x, 4) * x_after[c]
                row = row + jnp.where(sub == 0, F32(1.0), over_y[x]) * spread[c, x]
                row = row + jnp.where(
                    lane == 0,
                    jnp.broadcast_to(z_first[:, at : at + 1], (8, LANES)),
                    over_z[x] * jnp.broadcast_to(z_after[:, at : at + 1], (8, LANES)),
                )
                if x == 0:
                    row = row + x_first[c]
                rows.append(row)
            out.append(rows)
        return out

    spread_ref[...] = jnp.zeros((96, LANES), F32)
    loads["slab"].wait()
    now_copies = face_values(1, slab_ref)

    inside = inner_stiffness(slab_ref)
    loads["before"].wait()
    loads["mass"].wait()
    around = outer_stiffness(1, now_copies, inside)
    for x in range(4):
        scale = slab_factor * mass_ref[8 * x : 8 * x + 8, :]
        for c in range(3):
            at = 32 * c + 8 * x
            base_ref[at : at + 8, :] = (
                2.0 * slab_ref[at : at + 8, :]
                - before_ref[at : at + 8, :]
                - scale * around[x][c]
            )

    owner_in.wait_recv()
    arrived = sum(
        owner_recv[b * n_gx : (b + 1) * n_gx].reshape(n_gx, LANES) for b in range(chips)
    )
    lines = []
    moved = pltpu.roll(arrived, 0, 1, stride=RANKS, stride_axis=0)
    for c in range(4):
        own = ((lanes16 >> 3) - rows16 - c) & 15 == 0
        line = jnp.sum(jnp.where(own, moved, F32(0.0)), axis=0, keepdims=True)
        if c:
            line = pltpu.roll(jnp.broadcast_to(line, (8, LANES)), LANES - RANKS * c, 1)[0:1]
        lines.append(line)
    goal = lines[3].astype(jnp.int32)
    goal_row, goal_lane = goal >> 7, goal & 127
    rows32 = iota((32, LANES), 0)
    spots = jnp.concatenate(
        [jnp.where(rows32 == goal_row, lines[c], F32(0.0)) for c in range(3)], axis=0
    )
    high, low = halves(spots)
    on_lane = (iota((LANES, LANES), 0) == goal_lane).astype(F32).astype(BF16)
    force = dot_rows(
        jnp.concatenate([high, low], axis=1), jnp.concatenate([on_lane, on_lane], axis=1)
    )
    force_out[...] = force
    for x in range(4):
        scale = slab_factor * mass_ref[8 * x : 8 * x + 8, :]
        for c in range(3):
            at = 32 * c + 8 * x
            step_ref[at : at + 8, :] = base_ref[at : at + 8, :] + scale * force[at : at + 8]

    step_copies = face_values(2, step_ref)
    inside = inner_stiffness(step_ref)
    around = outer_stiffness(2, step_copies, inside)
    for x in range(4):
        scale = slab_factor * mass_ref[8 * x : 8 * x + 8, :]
        for c in range(3):
            at = 32 * c + 8 * x
            slab_out[at : at + 8, :] = (
                2.0 * step_ref[at : at + 8, :]
                - slab_ref[at : at + 8, :]
                + scale * (force_out[at : at + 8, :] - around[x][c])
            )
    for copy in sent:
        copy.wait_send()
    owner_in.wait_send()


def copy_out(*refs):
    sems = refs[6]
    copies = [pltpu.make_async_copy(refs[i], refs[3 + i], sems.at[i]) for i in range(3)]
    for copy in copies:
        copy.start()
    for copy in copies:
        copy.wait()


def solution(mesh):
    n_gx, n_gy, n_gz = (mesh.shape[name] for name in ("gx", "gy", "gz"))

    def on_device(
        global_now,
        global_prev,
        cycle_modes,
        wave_speed,
        inv_radius,
        theta_second,
        theta_first,
        point_dest,
        point_target,
        point_source,
        point_azimuth,
        regional_now,
        regional_prev,
        moduli,
        inv_mass,
    ):
        points = point_target.shape[1]
        big = [((192, LANES), F32)] * 2 + [((8, LANES), F32)] * 2 + [((LANES, LANES), F32)] * 2
        big += [((1, points), jnp.int32)] * 3 + [((1, points), F32)]
        big += [((96, LANES), F32)] * 2 + [((32, LANES), F32)] * 2
        scratch = [pltpu.SMEM(cycle_modes.shape, jnp.int32)]
        scratch += [pltpu.VMEM(shape, dtype) for shape, dtype in big]
        scratch += [
            pltpu.VMEM((192, LANES), F32),
            pltpu.VMEM((192, LANES), F32),
            pltpu.VMEM((2 * LANES, 2 * LANES), BF16),
            pltpu.VMEM((2 * LANES, 2 * LANES), BF16),
            pltpu.VMEM((2 * LANES, points), BF16),
            pltpu.VMEM((8, 8, points), F32),
            pltpu.VMEM((LANES, points), BF16),
            pltpu.VMEM((8, LANES), F32),
            pltpu.VMEM((96, LANES), F32),
            pltpu.VMEM((96, LANES), F32),
            pltpu.VMEM((9, 4, 8, LANES), F32),
            pltpu.VMEM((9, 4, 8, LANES), F32),
            pltpu.VMEM((20, 8, LANES), F32),
            pltpu.VMEM((4, 8, LANES), F32),
            pltpu.VMEM((4, 8, LANES), F32),
            pltpu.VMEM((96, LANES), F32),
            pltpu.VMEM((96, LANES), F32),
            pltpu.VMEM((2, 56, LANES), F32),
            pltpu.VMEM((2, 56, LANES), F32),
            pltpu.VMEM((3, 2, 3, 8, LANES), F32),
            pltpu.VMEM((3, 2, 3, 8, LANES), F32),
            pltpu.VMEM((3, 2, 16, LANES), F32),
            pltpu.VMEM((3, 2, 16, LANES), F32),
            pltpu.VMEM((3, 2, 8, LANES), F32),
            pltpu.VMEM((3, 2, 8, LANES), F32),
            pltpu.VMEM((2, 8 * max(1, n_gy // 4), LANES), F32),
            pltpu.VMEM((8 * max(1, n_gy // 4), LANES), F32),
            pltpu.VMEM((n_gy // 2, n_gx, 1, LANES), F32),
            pltpu.VMEM((n_gy // 2 * n_gx, 1, LANES), F32),
            pltpu.SemaphoreType.DMA((15,)),
            pltpu.SemaphoreType.DMA((2, 2)),
            pltpu.SemaphoreType.DMA((2, 3, 6)),
            pltpu.SemaphoreType.DMA((2,)),
            pltpu.SemaphoreType.DMA((2,)),
            pltpu.SemaphoreType.REGULAR((5,)),
        ]
        hbm = pl.BlockSpec(memory_space=pl.ANY)
        two, slab, force = pl.pallas_call(
            functools.partial(kernel, (n_gx, n_gy, n_gz)),
            out_shape=[
                pltpu.VMEM((192, LANES), F32),
                pltpu.VMEM((96, LANES), F32),
                pltpu.VMEM((96, LANES), F32),
            ],
            in_specs=[hbm] * 15,
            out_specs=[pl.BlockSpec(memory_space=pltpu.VMEM)] * 3,
            scratch_shapes=scratch,
            compiler_params=pltpu.CompilerParams(
                collective_id=0, has_side_effects=True, vmem_limit_bytes=48 * 2**20
            ),
        )(
            *[
                pltpu.with_memory_space_constraint(x, pltpu.HBM)
                for x in (
            cycle_modes,
            global_now.reshape(192, LANES),
            global_prev.reshape(192, LANES),
            wave_speed,
            inv_radius,
            theta_second,
            theta_first,
            point_dest.reshape(1, points),
            point_target,
            point_source,
            point_azimuth,
            regional_now.reshape(96, LANES),
            regional_prev.reshape(96, LANES),
            moduli.reshape(32, LANES),
            inv_mass.reshape(32, LANES),
            )]
        )
        two, slab, force = pl.pallas_call(
            copy_out,
            out_shape=[
                pltpu.HBM((192, LANES), F32),
                pltpu.HBM((96, LANES), F32),
                pltpu.HBM((96, LANES), F32),
            ],
            in_specs=[hbm] * 3,
            out_specs=[hbm] * 3,
            scratch_shapes=[pltpu.SemaphoreType.DMA((3,))],
        )(*[pltpu.with_memory_space_constraint(x, pltpu.VMEM) for x in (two, slab, force)])
        return (
            two.reshape(global_now.shape),
            slab.reshape(regional_now.shape),
            force.reshape(regional_now.shape),
        )

    return jax.shard_map(
        on_device,
        mesh=mesh,
        in_specs=(
            P("gy", None, "gx", None),
            P("gy", None, "gx", None),
            P("gx"),
            P("gx", None),
            P("gx", None),
            P(),
            P(),
            P("gz", "gx", None),
            P("gz", "gx"),
            P("gz", "gx"),
            P("gz", "gx"),
            P(None, "gx", "gy", "gz"),
            P(None, "gx", "gy", "gz"),
            P("gx", "gy", "gz"),
            P("gx", "gy", "gz"),
        ),
        out_specs=(P("gy", None, "gx", None), P(None, "gx", "gy", "gz"), P(None, "gx", "gy", "gz")),
        check_vma=False,
    )
```

```python
import functools
import math

import jax
import jax.numpy as jnp
import numpy as np
from jax import lax
from jax.experimental import pallas as pl
from jax.experimental.pallas import tpu as pltpu
from jax.sharding import PartitionSpec as P

F32 = jnp.float32
BF16 = jnp.bfloat16
MESH = pl.DeviceIdType.MESH

time_step = 0.3
time_sq = 0.09
impedance = 0.5
coupling = 0.05
slab_factor = 0.04

LANES = 128
RANKS = 8


def gll_products():
    nodes = np.array([-1.0, -math.sqrt(3.0 / 7.0), 0.0, math.sqrt(3.0 / 7.0), 1.0])
    weights = np.array([0.1, 49.0 / 90.0, 32.0 / 45.0, 49.0 / 90.0, 0.1])
    factor = np.array(
        [np.prod([nodes[i] - nodes[k] for k in range(5) if k != i]) for i in range(5)]
    )
    deriv = np.zeros((5, 5))
    for i in range(5):
        for j in range(5):
            if i != j:
                deriv[i, j] = factor[i] / factor[j] / (nodes[i] - nodes[j])
            else:
                deriv[i, j] = sum((1.0 / (nodes[i] - nodes[k]) for k in range(5) if k != i))
    return weights, np.einsum("ki,k,kj->kij", deriv, weights, deriv)


WEIGHTS, GRAM = gll_products()


def cosine_series():
    f = np.cos(np.linspace(0.0, np.pi / 2, 2001)) * 0.5
    fit = np.polynomial.chebyshev.Chebyshev.fit(f * f, np.cos(2 * np.pi * f), 8, domain=[0, 0.25])
    return [float(v) for v in fit.convert(kind=np.polynomial.Polynomial).coef]


COSINE = cosine_series()


def halves(x):
    high = x.astype(BF16)
    return high, (x - high.astype(F32)).astype(BF16)


def dot(a, b):
    return lax.dot_general(a, b, (((1,), (0,)), ((), ())), preferred_element_type=F32)


def dot_rows(a, b):
    return lax.dot_general(a, b, (((1,), (1,)), ((), ())), preferred_element_type=F32)


def operator_pair(t):
    high, low = halves(t)
    top = jnp.concatenate([high, low], axis=1)
    bottom = jnp.concatenate([high, jnp.zeros_like(low)], axis=1)
    return jnp.concatenate([top, bottom], axis=0)


def times_operator(x, pair_ref):
    high, low = halves(x)
    both = dot(jnp.concatenate([high, low], axis=1), pair_ref[...])
    return both[:, :LANES] + both[:, LANES:]


def iota(shape, axis):
    return lax.broadcasted_iota(jnp.int32, shape, axis)


def by_four(phase, values):
    out = jnp.full(phase.shape, values[3], F32)
    for i in (2, 1, 0):
        out = jnp.where(phase == i, F32(values[i]), out)
    return out


def kernel(
    sizes,
    modes_in,
    now_in,
    prev_in,
    speed_in,
    radius_in,
    second_in,
    first_in,
    dest_in,
    target_in,
    source_in,
    azimuth_in,
    slab_in,
    before_in,
    moduli_in,
    mass_in,
    g_out,
    slab_out,
    force_out,
    modes_ref,
    now_ref,
    prev_ref,
    speed_ref,
    radius_ref,
    second_ref,
    first_ref,
    dest_ref,
    target_ref,
    source_ref,
    azimuth_ref,
    slab_ref,
    before_ref,
    moduli_ref,
    mass_ref,
    one_ref,
    edge_ref,
    pair_second,
    pair_first,
    pick_ref,
    trig_ref,
    slot_ref,
    mark_ref,
    base_ref,
    step_ref,
    band_z,
    band_y,
    band_x,
    over_z,
    over_y,
    spread_ref,
    part_ref,
    cycle_send,
    cycle_recv,
    x_send,
    x_recv,
    y_send,
    y_recv,
    z_send,
    z_recv,
    group_send,
    group_recv,
    owner_send,
    owner_recv,
    in_sem,
    cycle_sems,
    face_sems,
    group_sems,
    owner_sems,
    ring_sems,
):
    n_gx, n_gy, n_gz = sizes
    gx, gy, gz = lax.axis_index("gx"), lax.axis_index("gy"), lax.axis_index("gz")
    points = dest_ref.shape[1]
    core, chip = lax.rem(gy, 2), lax.div(gy, 2)
    chips = n_gy // 2

    def away(axis, step):
        index, count = {"gx": (gx, n_gx), "gy": (gy, n_gy), "gz": (gz, n_gz)}[axis]
        return {axis: lax.rem(index + step + count, count)}

    barrier = pltpu.get_barrier_semaphore()
    for step in range(1, n_gy):
        pl.semaphore_signal(barrier, inc=1, device_id=away("gy", step), device_id_type=MESH)
    there = {
        ("gx", -1): gx > 0,
        ("gx", 1): gx < n_gx - 1,
        ("gy", -1): gy > 0,
        ("gy", 1): gy < n_gy - 1,
        ("gz", -1): gz > 0,
        ("gz", 1): gz < n_gz - 1,
    }
    greeted = n_gy - 1 + chips * len({1, n_gx - 1})
    for step in sorted({1, n_gx - 1}):
        for b in range(chips):
            pl.semaphore_signal(
                barrier,
                inc=1,
                device_id={
                    "gx": away("gx", step)["gx"],
                    "gy": 2 * lax.rem(chip + b, chips) + core,
                },
                device_id_type=MESH,
            )
    for step in (-1, 1):
        greeted = greeted + there["gz", step].astype(jnp.int32)

        @pl.when(there["gz", step])
        def _(step=step):
            pl.semaphore_signal(
                barrier, inc=1, device_id=away("gz", step), device_id_type=MESH
            )

    loads = {}
    for number, (name, src, dst) in enumerate(
        (
            ("modes", modes_in, modes_ref),
            ("now", now_in, now_ref),
            ("prev", prev_in, prev_ref),
            ("speed", speed_in, speed_ref),
            ("radius", radius_in, radius_ref),
            ("moduli", moduli_in, moduli_ref),
            ("second", second_in, second_ref),
            ("dest", dest_in, dest_ref),
            ("target", target_in, target_ref),
            ("source", source_in, source_ref),
            ("azimuth", azimuth_in, azimuth_ref),
            ("first", first_in, first_ref),
            ("slab", slab_in, slab_ref),
            ("before", before_in, before_ref),
            ("mass", mass_in, mass_ref),
        )
    ):
        loads[name] = pltpu.make_async_copy(src, dst, in_sem.at[number])
        loads[name].start()

    def push(src, dst, sems, index, device):
        copy = pltpu.make_async_remote_copy(
            src_ref=src,
            dst_ref=dst,
            send_sem=sems.at[(0, *index)],
            recv_sem=sems.at[(1, *index)],
            device_id=device,
            device_id_type=MESH,
        )
        copy.start()
        return copy

    class Neighbour:
        def __init__(self, src, dst, sems, index, axis, step):
            self.copy = pltpu.make_async_remote_copy(
                src_ref=src,
                dst_ref=dst,
                send_sem=sems.at[(0, *index)],
                recv_sem=sems.at[(1, *index)],
                device_id=away(axis, step),
                device_id_type=MESH,
            )
            self.sends, self.receives = there[axis, step], there[axis, -step]
            pl.when(self.sends)(lambda: self.copy.start())

        def wait_recv(self):
            pl.when(self.receives)(lambda: self.copy.wait_recv())

        def wait_send(self):
            pl.when(self.sends)(lambda: self.copy.wait_send())

    for (axis, step), here in there.items():

        @pl.when(jnp.logical_not(here))
        def _(axis=axis, side=(1 - step) // 2):
            if axis == "gx":
                cycle_recv[side] = jnp.zeros(cycle_recv.shape[1:], F32)
                x_recv[:, side] = jnp.zeros((3, 3, 8, LANES), F32)
            elif axis == "gy":
                y_recv[:, side] = jnp.zeros((3, 16, LANES), F32)
            else:
                z_recv[:, side] = jnp.zeros((3, 8, LANES), F32)

    sub = iota((8, LANES), 0)
    lane = iota((8, LANES), 1)

    mode_base = (4 * gy).astype(F32)
    row24 = iota((24, LANES), 0)
    order24 = mode_base + (
        (row24 >= 6).astype(F32) + (row24 >= 12).astype(F32) + (row24 >= 18).astype(F32)
    )
    square24 = order24 * order24
    for name in ("modes", "now", "prev", "speed", "radius"):
        loads[name].wait()
    for side, (edge, inner) in enumerate(((0, 1), (7, 6))):
        count = modes_ref[edge].astype(F32)
        mask = jnp.where(order24 < count, F32(1.0), F32(0.0))
        speed = speed_ref[edge : edge + 1, :]
        radius = radius_ref[edge : edge + 1, :]
        at_edge = now_ref[pl.ds(edge, 24, stride=8), :]
        cycle_send[side, 0:24, :] = at_edge
        cycle_send[side, 24:48, :] = mask * (
            (2.0 - 2.0 * time_sq * speed - time_sq * square24 * radius) * at_edge
            - prev_ref[pl.ds(edge, 24, stride=8), :]
            + time_sq * speed * now_ref[pl.ds(inner, 24, stride=8), :]
        )
        cycle_send[side, 48:56, :] = jnp.where(
            sub == 0, jnp.broadcast_to(speed, (8, LANES)), jnp.full((8, LANES), count, F32)
        )

    pl.semaphore_wait(barrier, greeted)

    reaches, known = [], 1
    while known < n_gx // 2:
        reaches.append(min(known, n_gx // 2 - known))
        known += reaches[-1]

    def tell(level):
        for step in (reaches[level], -reaches[level]):
            pl.semaphore_signal(
                ring_sems.at[level], inc=1, device_id=away("gx", step), device_id_type=MESH
            )

    def hear(level):
        pl.semaphore_wait(ring_sems.at[level], 2)

    def advance(level):
        if level < len(reaches):
            hear(level)
        if level + 1 < len(reaches):
            tell(level + 1)

    tell(0)
    sent = []
    cycle_in = []
    for side, step in ((0, -1), (1, 1)):
        copy = Neighbour(
            cycle_send.at[side], cycle_recv.at[side], cycle_sems, (side,), "gx", step
        )
        sent.append(copy)
        cycle_in.append(copy)

    last_x = jnp.where(gx < n_gx - 1, F32(1.0), F32(0.0))
    last_y = jnp.where(gy < n_gy - 1, F32(1.0), F32(0.0))
    last_z = jnp.where(gz < n_gz - 1, F32(1.0), F32(0.0))
    has_x = jnp.where(gx > 0, F32(1.0), F32(0.0))
    has_y = jnp.where(gy > 0, F32(1.0), F32(0.0))
    has_z = jnp.where(gz > 0, F32(1.0), F32(0.0))

    def send_face(number, axis, count):
        place = ("gx", "gy", "gz").index(axis)
        out, into = ((x_send, x_recv), (y_send, y_recv), (z_send, z_recv))[place]
        copies = [
            Neighbour(
                out.at[number, side, 0:count],
                into.at[number, side, 0:count],
                face_sems,
                (number, 2 * place + side),
                axis,
                step,
            )
            for side, step in ((0, -1), (1, 1))
        ]
        sent.extend(copies)
        return copies

    def columns_to_lanes(columns):
        out = jnp.zeros((8, LANES), F32)
        for number, column in enumerate(columns):
            out = jnp.where(lane == number, jnp.broadcast_to(column, (8, LANES)), out)
        return out

    loads["moduli"].wait()
    inner = [float(GRAM[k, 4, 4]) for k in range(5)]
    mu = moduli_ref[...].reshape(4, 8, LANES)
    x_send[0, 0, 0] = mu[0]
    x_send[0, 1, 0] = last_x * (
        inner[0] * mu[0] + inner[1] * mu[1] + inner[2] * mu[2] + inner[3] * mu[3]
    )
    y_send[0, 0, 0:8] = jnp.zeros((8, LANES), F32)
    y_send[0, 1, 0:8] = jnp.zeros((8, LANES), F32)
    y_send[0, 0, 0:4] = moduli_ref[pl.ds(0, 4, stride=8), :]
    y_send[0, 1, 0:4] = last_y * sum(
        inner[k] * moduli_ref[pl.ds(4 + k, 4, stride=8), :] for k in range(4)
    )
    tail = by_four(lane & 3, inner[:4]) * jnp.where(lane >= LANES - 4, last_z, F32(0.0))
    z_send[0, 0] = columns_to_lanes([mu[x][:, 0:1] for x in range(4)])
    z_send[0, 1] = columns_to_lanes(
        [jnp.sum(tail * mu[x], axis=1, keepdims=True) for x in range(4)]
    )
    moduli_copies = [
        copy
        for axis, count in (("gy", 8), ("gz", 8), ("gx", 1))
        for copy in send_face(0, axis, count)
    ]

    advance(0)

    loads["second"].wait()
    pair_second[...] = operator_pair(second_ref[...])
    counts = jnp.zeros((8, LANES), F32)
    for row in range(8):
        counts = jnp.where(sub == row, modes_ref[row].astype(F32), counts)
    order = mode_base + iota((4, 8, LANES), 0).astype(F32)
    mask = jnp.where(order < counts[None], F32(1.0), F32(0.0))
    speed, radius = speed_ref[...][None], radius_ref[...][None]
    hold = (mask * (2.0 - 2.0 * time_sq * speed - time_sq * (order * order) * radius))[:, None]
    side_weight = (mask * (time_sq * speed))[:, None]
    bend_weight = (mask * time_sq)[:, None]
    mask = mask[:, None]

    def section_sum(now, prev):
        cells = now.reshape(24, 8, LANES)
        rows = iota((24, 8, LANES), 1)
        near = jnp.where(rows == 0, F32(0.0), pltpu.roll(cells, 1, 1)) + jnp.where(
            rows == 7, F32(0.0), pltpu.roll(cells, 7, 1)
        )
        return (
            hold * now.reshape(4, 6, 8, LANES)
            - mask * prev.reshape(4, 6, 8, LANES)
            + side_weight * near.reshape(4, 6, 8, LANES)
            + bend_weight * times_operator(now, pair_second).reshape(4, 6, 8, LANES)
        )

    one_ref[...] = section_sum(now_ref[...], prev_ref[...]).reshape(192, LANES)
    edge_ref[...] = jnp.zeros((192, LANES), F32)

    for name in ("dest", "target", "source", "azimuth"):
        loads[name].wait()
    owner = dest_ref[...]
    blocks = points // LANES
    named = (iota((LANES, points), 0) == owner).astype(F32)
    named_rows = jnp.concatenate(
        [named[:, b * LANES : (b + 1) * LANES] for b in range(blocks)], axis=0
    ).astype(BF16)
    before = (iota((LANES, LANES), 0) < iota((LANES, LANES), 1)).astype(F32)
    counted = dot(
        named_rows, jnp.concatenate([before, jnp.ones_like(before)], axis=1).astype(BF16)
    )
    ranks, offset = [], None
    for b in range(blocks):
        piece = counted[b * LANES : (b + 1) * LANES]
        place = piece[:, :LANES] if offset is None else piece[:, :LANES] + offset
        ranks.append(
            jnp.sum(named[:, b * LANES : (b + 1) * LANES] * place, axis=0, keepdims=True)
        )
        offset = piece[:, LANES:] if offset is None else offset + piece[:, LANES:]
    rank = jnp.concatenate(ranks, axis=1).astype(jnp.int32)
    if n_gy == 8:
        owner_x, owner_y = owner >> 3, owner & 7
    else:
        owner_x, owner_y = owner >> 1, owner & 1
    slot = owner_x * RANKS + rank
    slot_ref[...] = (iota((LANES, points), 0) == slot).astype(F32).astype(BF16)
    target = target_ref[...]
    sub_p = iota((8, points), 0)
    mine = owner_y == 2 * (sub_p & 3) + core
    marks = jnp.where(sub_p < 4, target >> 7, target & 127).astype(F32)
    marked = dot_rows(jnp.where(mine, marks, F32(0.0)).astype(BF16), slot_ref[...])
    mark_ref[0:4, :] = (128.0 / chips) * marked[0:4] + (1.0 / chips) * marked[4:8]
    source = source_ref[...]
    picked = (iota((LANES, points), 0) == (source & 127)).astype(F32).astype(BF16)
    pick_ref[0:LANES, :] = picked
    pick_ref[LANES:, :] = picked
    turns = (mode_base + (sub_p & 3).astype(F32)) * (azimuth_ref[...] * (0.5 / math.pi))
    turns = turns - jnp.where(sub_p >= 4, F32(0.25), F32(0.0))
    turns = turns - jnp.floor(turns + 0.5)
    square = turns * turns
    wave = jnp.full(square.shape, COSINE[-1], F32)
    for value in COSINE[-2::-1]:
        wave = wave * square + value
    in_cycle = sub_p == (source >> 7)
    for row in range(8):
        trig_ref[row] = jnp.where(
            in_cycle, jnp.broadcast_to(wave[row : row + 1], (8, points)), F32(0.0)
        )
    loads["first"].wait()
    pair_first[...] = operator_pair(first_ref[...])

    advance(1)

    for copy in cycle_in:
        copy.wait_recv()
    flags = (last_x, has_x)
    near_edges = [cycle_recv[side, 0:24, :] for side in range(2)]
    bends = times_operator(jnp.concatenate(near_edges, axis=0), pair_second)
    beyond = []
    for side, edge in ((0, 7), (1, 0)):
        tail_rows = cycle_recv[side, 48:56, :]
        speed24 = tail_rows[0:1]
        mask24 = jnp.where(order24 < tail_rows[1:2], F32(1.0), F32(0.0))
        edge_ref[pl.ds(edge, 24, stride=8), :] = flags[side] * near_edges[side]
        value = cycle_recv[side, 24:48, :] + mask24 * time_sq * (
            speed24 * now_ref[pl.ds(edge, 24, stride=8), :] + bends[24 * side : 24 * side + 24]
        )
        beyond.append(flags[side] * value)
    one = one_ref[...].reshape(4, 6, 8, LANES) + side_weight * edge_ref[...].reshape(
        4, 6, 8, LANES
    )
    one = one.reshape(192, LANES)
    for side, edge in ((0, 7), (1, 0)):
        edge_ref[pl.ds(edge, 24, stride=8), :] = beyond[side]
    two = section_sum(one, now_ref[...]) + side_weight * edge_ref[...].reshape(4, 6, 8, LANES)
    two = two.reshape(192, LANES)
    g_out[...] = two

    coef = coupling * times_operator(two, pair_first) + (coupling * impedance / time_step) * (
        two - one
    )
    high, low = halves(coef)
    at_points = dot(jnp.concatenate([high, low], axis=1), pick_ref[...]).reshape(
        4, 6, 8, points
    )
    values = jnp.zeros((8, points), F32)
    for c in range(3):
        total = jnp.zeros((8, points), F32)
        for m in range(4):
            total = total + at_points[m, 2 * c] * trig_ref[m]
            total = total + at_points[m, 2 * c + 1] * trig_ref[4 + m]
        values = jnp.where(
            (sub_p & 3) == c,
            jnp.broadcast_to(jnp.sum(total, axis=0, keepdims=True), (8, points)),
            values,
        )
    half = 8 * max(1, chips // 2)
    by_group = jnp.concatenate(
        [
            jnp.where(owner_y == 2 * (2 * tile + (sub_p >> 2)) + side, values, F32(0.0))
            for side in range(2)
            for tile in range(half // 8)
        ],
        axis=0,
    )
    high, low = halves(by_group)
    packed = dot_rows(jnp.concatenate([high, low], axis=0), slot_ref[...])
    packed = packed[: 2 * half] + packed[2 * half :]
    for side in range(2):
        group_send[side] = packed[half * side : half * side + half]
    pair = push(
        group_send.at[1 - core], group_recv, group_sems, (), {"gy": gy + 1 - 2 * core}
    )
    sent.append(pair)

    pair.wait_recv()
    total = group_send[core] + group_recv[...]
    rows16 = iota((n_gx, LANES), 0)
    lanes16 = iota((n_gx, LANES), 1)
    for place in range(chips):
        outgoing = jnp.zeros((n_gx, LANES), F32)
        for c in range(4):
            at = 4 * place + c
            line = total[at : at + 1] if c < 3 else mark_ref[place : place + 1]
            line = jnp.broadcast_to(line, (8, LANES))
            if (RANKS * (c + 1 - n_gx)) % LANES:
                line = pltpu.roll(line, (RANKS * (c + 1 - n_gx)) % LANES, 1)
            moved = pltpu.roll(
                jnp.broadcast_to(line[0:1], (n_gx, LANES)), 0, 1, stride=RANKS, stride_axis=0
            )
            outgoing = jnp.where(lanes16 >> 3 == c, moved, outgoing)
        owner_send[place] = outgoing.reshape(n_gx, 1, LANES)

    def to_row(a, first=0):
        peer_x = lax.rem(gx + a, n_gx)
        for b in range(first, chips):
            peer_chip = lax.rem(chip + b, chips)
            pltpu.make_async_remote_copy(
                src_ref=owner_send.at[peer_chip, n_gx - 1 - peer_x],
                dst_ref=owner_recv.at[b * n_gx + a],
                send_sem=owner_sems.at[0],
                recv_sem=owner_sems.at[1],
                device_id={"gx": peer_x, "gy": 2 * peer_chip + core},
                device_id_type=MESH,
            ).start()

    def far_first(first, last, when=None):
        def body(number, carry):
            away_by = (number + 1) // 2
            a = n_gx // 2 + jnp.where(number % 2 == 1, -away_by, away_by)
            if when is None:
                to_row(a)
            else:
                pl.when(when(a))(lambda: to_row(a))
            return carry

        lax.fori_loop(first, last, body, 0)

    near = n_gx // 2 - 1 if n_gx > 8 else 0
    far_first(near, n_gx - 1)
    to_row(0, 1)
    for level in range(2, len(reaches)):
        advance(level)
    far_first(0, near)
    owner_recv[0] = owner_send[chip, n_gx - 1 - gx]
    rows_all = chips * n_gx
    owner_in = pltpu.make_async_remote_copy(
        src_ref=owner_recv.at[1:rows_all],
        dst_ref=owner_recv.at[1:rows_all],
        send_sem=owner_sems.at[0],
        recv_sem=owner_sems.at[1],
        device_id=away("gx", 1),
        device_id_type=MESH,
    )

    for copy in moduli_copies:
        copy.wait_recv()
    mu_next_x = last_x * x_recv[0, 0, 0]
    sum_prev_x = x_recv[0, 1, 0]
    lane4 = iota((4, 8, LANES), 2)
    sub4 = iota((4, 8, LANES), 1)
    side_w = [0.2] + [float(v) for v in WEIGHTS[1:4]]
    first_weight = -float(WEIGHTS[4])
    weight_y = by_four(sub & 3, side_w) + jnp.where(
        sub == 0, (1.0 - has_y) * first_weight, F32(0.0)
    )
    weight_z = by_four(lane & 3, side_w) + jnp.where(
        lane == 0, (1.0 - has_z) * first_weight, F32(0.0)
    )
    weight_x = [side_w[0] + (1.0 - has_x) * first_weight] + side_w[1:]

    def make_band(axis, position, count, following, preceding, weights, has, last, band, over):
        shifted = {0: mu}
        for t in range(-4, 5):
            if t:
                rolled = pltpu.roll(mu, (-t) % count, axis)
                if t > 0:
                    rolled = jnp.where(position == count - t, following, rolled)
                shifted[t] = rolled
        pos2 = position[0]
        phase = pos2 & 3
        later = pos2 > 3
        band_values = []
        for s in range(5):
            total = None
            for t in range(s - 4, 5):
                row = [
                    GRAM[i + t, i, i + s] if 0 <= i + t <= 4 and i + s <= 4 else 0.0
                    for i in range(4)
                ]
                pattern = by_four(phase, row)
                if s == 0 and t <= 0:
                    pattern = pattern + jnp.where(
                        (phase == 0) & later, F32(GRAM[4 + t, 4, 4]), F32(0.0)
                    )
                term = pattern[None] * shifted[t]
                total = term if total is None else total + term
            if s == 0:
                total = total + jnp.where(
                    position == 0, preceding + has * float(GRAM[4, 4, 4]) * mu, F32(0.0)
                )
            band_values.append(total * weights)
        crossing = jnp.zeros_like(mu)
        for s in range(1, 5):
            crossing = jnp.where(position == count - s, band_values[s], crossing)
            inside = jnp.where(position >= count - s, F32(0.0), band_values[s])
            behind = pltpu.roll(inside, s, axis)
            if 2 * s == count:
                band[s] = inside + behind
                band[4 + s] = jnp.zeros_like(inside)
            else:
                band[s] = inside
                band[4 + s] = behind
        over[...] = last * crossing
        band[0] = band_values[0]

    y_next = y_recv[0, 0, 0:8]
    y_prev = y_recv[0, 1, 0:8]
    z_next = z_recv[0, 0]
    z_prev = z_recv[0, 1]

    def rows_of(value):
        return jnp.concatenate(
            [jnp.broadcast_to(value[x : x + 1], (8, LANES))[None] for x in range(4)], axis=0
        )

    def columns_of(value):
        return jnp.concatenate(
            [jnp.broadcast_to(value[:, x : x + 1], (8, LANES))[None] for x in range(4)], axis=0
        )

    stacked = lambda scale: jnp.concatenate([(scale(x))[None] for x in range(4)], axis=0)
    make_band(
        2,
        lane4,
        LANES,
        last_z * columns_of(z_next),
        columns_of(z_prev),
        stacked(lambda x: weight_x[x] * weight_y),
        has_z,
        last_z,
        band_z,
        over_z,
    )
    make_band(
        1,
        sub4,
        8,
        last_y * rows_of(y_next),
        rows_of(y_prev),
        stacked(lambda x: weight_x[x] * weight_z),
        has_y,
        last_y,
        band_y,
        over_y,
    )
    weight_yz = weight_y * weight_z
    planes = [mu[x] for x in range(4)] + [mu_next_x]
    for i in range(4):
        for j in range(i, 5):
            value = sum(float(GRAM[k, i, j]) * planes[k] for k in range(5))
            if i == 0 and j == 0:
                value = value + sum_prev_x + has_x * float(GRAM[4, 4, 4]) * mu[0]
            if j == 4:
                value = last_x * value
            band_x[5 * i + j] = value * weight_yz
    for x in range(4):
        band_z[0, x] = band_z[0, x] + band_y[0, x] + band_x[6 * x]

    def coupling_x(i, j):
        return band_x[5 * min(i, j) + max(i, j)]

    def face_values(number, ref):
        field = ref[...].reshape(3, 4, 8, LANES)
        y_send[number, 0, 0:12] = ref[pl.ds(0, 12, stride=8), :]
        part_ref[...] = (over_y[...][None] * field).reshape(96, LANES)
        y_send[number, 1, 0:12] = sum(
            part_ref[pl.ds(4 + k, 12, stride=8), :] for k in range(4)
        )
        copies = send_face(number, "gy", 16)
        for c in range(3):
            x_send[number, 0, c] = field[c, 0]
            x_send[number, 1, c] = sum(coupling_x(i, 4) * field[c, i] for i in range(4))
        copies += send_face(number, "gx", 3)
        z_send[number, 0] = columns_to_lanes(
            [field[c, x][:, 0:1] for c in range(3) for x in range(4)]
        )
        z_send[number, 1] = columns_to_lanes(
            [
                jnp.sum(over_z[x] * field[c, x], axis=1, keepdims=True)
                for c in range(3)
                for x in range(4)
            ]
        )
        return copies + send_face(number, "gz", 8)

    def inner_stiffness(ref):
        field = ref[...].reshape(3, 4, 8, LANES)
        out = []
        for x in range(4):
            plane = field[:, x]
            total = band_z[0, x] * plane
            for s in range(1, 5):
                total = total + band_z[s, x] * pltpu.roll(plane, LANES - s, 2)
                total = total + band_z[4 + s, x] * pltpu.roll(plane, s, 2)
                total = total + band_y[s, x] * pltpu.roll(plane, 8 - s, 1)
                if s < 4:
                    total = total + band_y[4 + s, x] * pltpu.roll(plane, s, 1)
            for j in range(4):
                if j != x:
                    total = total + coupling_x(x, j) * field[:, j]
            out.append(total)
        return out

    def outer_stiffness(number, copies, inside):
        for copy in copies:
            copy.wait_recv()
        y_first = y_recv[number, 1, 0:12]
        y_after = y_recv[number, 0, 0:12]
        spread_ref[pl.ds(0, 12, stride=8), :] = y_first
        for k in range(4):
            spread_ref[pl.ds(4 + k, 12, stride=8), :] = y_after
        spread = spread_ref[...].reshape(3, 4, 8, LANES)
        z_first, z_after = z_recv[number, 1], z_recv[number, 0]
        x_after, x_first = x_recv[number, 0], x_recv[number, 1]
        out = []
        for x in range(4):
            rows = []
            for c in range(3):
                at = 4 * c + x
                row = inside[x][c] + coupling_x(x, 4) * x_after[c]
                row = row + jnp.where(sub == 0, F32(1.0), over_y[x]) * spread[c, x]
                row = row + jnp.where(
                    lane == 0,
                    jnp.broadcast_to(z_first[:, at : at + 1], (8, LANES)),
                    over_z[x] * jnp.broadcast_to(z_after[:, at : at + 1], (8, LANES)),
                )
                if x == 0:
                    row = row + x_first[c]
                rows.append(row)
            out.append(rows)
        return out

    spread_ref[...] = jnp.zeros((96, LANES), F32)
    loads["slab"].wait()
    now_copies = face_values(1, slab_ref)

    inside = inner_stiffness(slab_ref)
    loads["before"].wait()
    loads["mass"].wait()
    around = outer_stiffness(1, now_copies, inside)
    for x in range(4):
        scale = slab_factor * mass_ref[8 * x : 8 * x + 8, :]
        for c in range(3):
            at = 32 * c + 8 * x
            base_ref[at : at + 8, :] = (
                2.0 * slab_ref[at : at + 8, :]
                - before_ref[at : at + 8, :]
                - scale * around[x][c]
            )

    owner_in.wait_recv()
    arrived = sum(
        owner_recv[b * n_gx : (b + 1) * n_gx].reshape(n_gx, LANES) for b in range(chips)
    )
    lines = []
    moved = pltpu.roll(arrived, 0, 1, stride=RANKS, stride_axis=0)
    for c in range(4):
        own = ((lanes16 >> 3) - rows16 - c) & 15 == 0
        line = jnp.sum(jnp.where(own, moved, F32(0.0)), axis=0, keepdims=True)
        if c:
            line = pltpu.roll(jnp.broadcast_to(line, (8, LANES)), LANES - RANKS * c, 1)[0:1]
        lines.append(line)
    goal = lines[3].astype(jnp.int32)
    goal_row, goal_lane = goal >> 7, goal & 127
    rows32 = iota((32, LANES), 0)
    spots = jnp.concatenate(
        [jnp.where(rows32 == goal_row, lines[c], F32(0.0)) for c in range(3)], axis=0
    )
    high, low = halves(spots)
    on_lane = (iota((LANES, LANES), 0) == goal_lane).astype(F32).astype(BF16)
    force = dot_rows(
        jnp.concatenate([high, low], axis=1), jnp.concatenate([on_lane, on_lane], axis=1)
    )
    force_out[...] = force
    for x in range(4):
        scale = slab_factor * mass_ref[8 * x : 8 * x + 8, :]
        for c in range(3):
            at = 32 * c + 8 * x
            step_ref[at : at + 8, :] = base_ref[at : at + 8, :] + scale * force[at : at + 8]

    step_copies = face_values(2, step_ref)
    inside = inner_stiffness(step_ref)
    around = outer_stiffness(2, step_copies, inside)
    for x in range(4):
        scale = slab_factor * mass_ref[8 * x : 8 * x + 8, :]
        for c in range(3):
            at = 32 * c + 8 * x
            slab_out[at : at + 8, :] = (
                2.0 * step_ref[at : at + 8, :]
                - slab_ref[at : at + 8, :]
                + scale * (force_out[at : at + 8, :] - around[x][c])
            )
    for copy in sent:
        copy.wait_send()
    owner_in.wait_send()


def copy_out(*refs):
    sems = refs[6]
    copies = [pltpu.make_async_copy(refs[i], refs[3 + i], sems.at[i]) for i in range(3)]
    for copy in copies:
        copy.start()
    for copy in copies:
        copy.wait()


def solution(mesh):
    n_gx, n_gy, n_gz = (mesh.shape[name] for name in ("gx", "gy", "gz"))

    def on_device(
        global_now,
        global_prev,
        cycle_modes,
        wave_speed,
        inv_radius,
        theta_second,
        theta_first,
        point_dest,
        point_target,
        point_source,
        point_azimuth,
        regional_now,
        regional_prev,
        moduli,
        inv_mass,
    ):
        points = point_target.shape[1]
        big = [((192, LANES), F32)] * 2 + [((8, LANES), F32)] * 2 + [((LANES, LANES), F32)] * 2
        big += [((1, points), jnp.int32)] * 3 + [((1, points), F32)]
        big += [((96, LANES), F32)] * 2 + [((32, LANES), F32)] * 2
        scratch = [pltpu.SMEM(cycle_modes.shape, jnp.int32)]
        scratch += [pltpu.VMEM(shape, dtype) for shape, dtype in big]
        scratch += [
            pltpu.VMEM((192, LANES), F32),
            pltpu.VMEM((192, LANES), F32),
            pltpu.VMEM((2 * LANES, 2 * LANES), BF16),
            pltpu.VMEM((2 * LANES, 2 * LANES), BF16),
            pltpu.VMEM((2 * LANES, points), BF16),
            pltpu.VMEM((8, 8, points), F32),
            pltpu.VMEM((LANES, points), BF16),
            pltpu.VMEM((8, LANES), F32),
            pltpu.VMEM((96, LANES), F32),
            pltpu.VMEM((96, LANES), F32),
            pltpu.VMEM((9, 4, 8, LANES), F32),
            pltpu.VMEM((9, 4, 8, LANES), F32),
            pltpu.VMEM((20, 8, LANES), F32),
            pltpu.VMEM((4, 8, LANES), F32),
            pltpu.VMEM((4, 8, LANES), F32),
            pltpu.VMEM((96, LANES), F32),
            pltpu.VMEM((96, LANES), F32),
            pltpu.VMEM((2, 56, LANES), F32),
            pltpu.VMEM((2, 56, LANES), F32),
            pltpu.VMEM((3, 2, 3, 8, LANES), F32),
            pltpu.VMEM((3, 2, 3, 8, LANES), F32),
            pltpu.VMEM((3, 2, 16, LANES), F32),
            pltpu.VMEM((3, 2, 16, LANES), F32),
            pltpu.VMEM((3, 2, 8, LANES), F32),
            pltpu.VMEM((3, 2, 8, LANES), F32),
            pltpu.VMEM((2, 8 * max(1, n_gy // 4), LANES), F32),
            pltpu.VMEM((8 * max(1, n_gy // 4), LANES), F32),
            pltpu.VMEM((n_gy // 2, n_gx, 1, LANES), F32),
            pltpu.VMEM((n_gy // 2 * n_gx, 1, LANES), F32),
            pltpu.SemaphoreType.DMA((15,)),
            pltpu.SemaphoreType.DMA((2, 2)),
            pltpu.SemaphoreType.DMA((2, 3, 6)),
            pltpu.SemaphoreType.DMA((2,)),
            pltpu.SemaphoreType.DMA((2,)),
            pltpu.SemaphoreType.REGULAR((5,)),
        ]
        hbm = pl.BlockSpec(memory_space=pl.ANY)
        two, slab, force = pl.pallas_call(
            functools.partial(kernel, (n_gx, n_gy, n_gz)),
            out_shape=[
                pltpu.VMEM((192, LANES), F32),
                pltpu.VMEM((96, LANES), F32),
                pltpu.VMEM((96, LANES), F32),
            ],
            in_specs=[hbm] * 15,
            out_specs=[pl.BlockSpec(memory_space=pltpu.VMEM)] * 3,
            scratch_shapes=scratch,
            compiler_params=pltpu.CompilerParams(
                collective_id=0, has_side_effects=True, vmem_limit_bytes=48 * 2**20
            ),
        )(
            *[
                pltpu.with_memory_space_constraint(x, pltpu.HBM)
                for x in (
            cycle_modes,
            global_now.reshape(192, LANES),
            global_prev.reshape(192, LANES),
            wave_speed,
            inv_radius,
            theta_second,
            theta_first,
            point_dest.reshape(1, points),
            point_target,
            point_source,
            point_azimuth,
            regional_now.reshape(96, LANES),
            regional_prev.reshape(96, LANES),
            moduli.reshape(32, LANES),
            inv_mass.reshape(32, LANES),
            )]
        )
        two, slab, force = pl.pallas_call(
            copy_out,
            out_shape=[
                pltpu.HBM((192, LANES), F32),
                pltpu.HBM((96, LANES), F32),
                pltpu.HBM((96, LANES), F32),
            ],
            in_specs=[hbm] * 3,
            out_specs=[hbm] * 3,
            scratch_shapes=[pltpu.SemaphoreType.DMA((3,))],
        )(*[pltpu.with_memory_space_constraint(x, pltpu.VMEM) for x in (two, slab, force)])
        return (
            two.reshape(global_now.shape),
            slab.reshape(regional_now.shape),
            force.reshape(regional_now.shape),
        )

    return jax.shard_map(
        on_device,
        mesh=mesh,
        in_specs=(
            P("gy", None, "gx", None),
            P("gy", None, "gx", None),
            P("gx"),
            P("gx", None),
            P("gx", None),
            P(),
            P(),
            P("gz", "gx", None),
            P("gz", "gx"),
            P("gz", "gx"),
            P("gz", "gx"),
            P(None, "gx", "gy", "gz"),
            P(None, "gx", "gy", "gz"),
            P("gx", "gy", "gz"),
            P("gx", "gy", "gz"),
        ),
        out_specs=(P("gy", None, "gx", None), P(None, "gx", "gy", "gz"), P(None, "gx", "gy", "gz")),
        check_vma=False,
    )
```

```python
import functools
import math

import jax
import jax.numpy as jnp
import numpy as np
from jax import lax
from jax.experimental import pallas as pl
from jax.experimental.pallas import tpu as pltpu
from jax.sharding import PartitionSpec as P

F32 = jnp.float32
BF16 = jnp.bfloat16
MESH = pl.DeviceIdType.MESH

time_step = 0.3
time_sq = 0.09
impedance = 0.5
coupling = 0.05
slab_factor = 0.04

LANES = 128
RANKS = 8


def gll_products():
    nodes = np.array([-1.0, -math.sqrt(3.0 / 7.0), 0.0, math.sqrt(3.0 / 7.0), 1.0])
    weights = np.array([0.1, 49.0 / 90.0, 32.0 / 45.0, 49.0 / 90.0, 0.1])
    factor = np.array(
        [np.prod([nodes[i] - nodes[k] for k in range(5) if k != i]) for i in range(5)]
    )
    deriv = np.zeros((5, 5))
    for i in range(5):
        for j in range(5):
            if i != j:
                deriv[i, j] = factor[i] / factor[j] / (nodes[i] - nodes[j])
            else:
                deriv[i, j] = sum((1.0 / (nodes[i] - nodes[k]) for k in range(5) if k != i))
    return weights, np.einsum("ki,k,kj->kij", deriv, weights, deriv)


WEIGHTS, GRAM = gll_products()


def cosine_series():
    f = np.cos(np.linspace(0.0, np.pi / 2, 2001)) * 0.5
    fit = np.polynomial.chebyshev.Chebyshev.fit(f * f, np.cos(2 * np.pi * f), 8, domain=[0, 0.25])
    return [float(v) for v in fit.convert(kind=np.polynomial.Polynomial).coef]


COSINE = cosine_series()


def halves(x):
    high = x.astype(BF16)
    return high, (x - high.astype(F32)).astype(BF16)


def dot(a, b):
    return lax.dot_general(a, b, (((1,), (0,)), ((), ())), preferred_element_type=F32)


def dot_rows(a, b):
    return lax.dot_general(a, b, (((1,), (1,)), ((), ())), preferred_element_type=F32)


def operator_pair(t):
    high, low = halves(t)
    top = jnp.concatenate([high, low], axis=1)
    bottom = jnp.concatenate([high, jnp.zeros_like(low)], axis=1)
    return jnp.concatenate([top, bottom], axis=0)


def times_operator(x, pair_ref):
    high, low = halves(x)
    both = dot(jnp.concatenate([high, low], axis=1), pair_ref[...])
    return both[:, :LANES] + both[:, LANES:]


def iota(shape, axis):
    return lax.broadcasted_iota(jnp.int32, shape, axis)


def by_four(phase, values):
    out = jnp.full(phase.shape, values[3], F32)
    for i in (2, 1, 0):
        out = jnp.where(phase == i, F32(values[i]), out)
    return out


def kernel(
    sizes,
    modes_in,
    now_in,
    prev_in,
    speed_in,
    radius_in,
    second_in,
    first_in,
    dest_in,
    target_in,
    source_in,
    azimuth_in,
    slab_in,
    before_in,
    moduli_in,
    mass_in,
    g_out,
    slab_out,
    force_out,
    modes_ref,
    now_ref,
    prev_ref,
    speed_ref,
    radius_ref,
    second_ref,
    first_ref,
    dest_ref,
    target_ref,
    source_ref,
    azimuth_ref,
    slab_ref,
    before_ref,
    moduli_ref,
    mass_ref,
    one_ref,
    edge_ref,
    pair_second,
    pair_first,
    pick_ref,
    trig_ref,
    slot_ref,
    mark_ref,
    base_ref,
    step_ref,
    band_z,
    band_y,
    band_x,
    over_z,
    over_y,
    spread_ref,
    part_ref,
    cycle_send,
    cycle_recv,
    x_send,
    x_recv,
    y_send,
    y_recv,
    z_send,
    z_recv,
    group_send,
    group_recv,
    owner_send,
    owner_recv,
    in_sem,
    cycle_sems,
    face_sems,
    group_sems,
    owner_sems,
    ring_sems,
):
    n_gx, n_gy, n_gz = sizes
    gx, gy, gz = lax.axis_index("gx"), lax.axis_index("gy"), lax.axis_index("gz")
    points = dest_ref.shape[1]
    core, chip = lax.rem(gy, 2), lax.div(gy, 2)
    chips = n_gy // 2

    def away(axis, step):
        index, count = {"gx": (gx, n_gx), "gy": (gy, n_gy), "gz": (gz, n_gz)}[axis]
        return {axis: lax.rem(index + step + count, count)}

    barrier = pltpu.get_barrier_semaphore()
    for step in range(1, n_gy):
        pl.semaphore_signal(barrier, inc=1, device_id=away("gy", step), device_id_type=MESH)
    there = {
        ("gx", -1): gx > 0,
        ("gx", 1): gx < n_gx - 1,
        ("gy", -1): gy > 0,
        ("gy", 1): gy < n_gy - 1,
        ("gz", -1): gz > 0,
        ("gz", 1): gz < n_gz - 1,
    }
    greeted = n_gy - 1 + len({1, n_gx - 1}) + jnp.where(gx == 1, chips - 1, 0)
    for step in sorted({1, n_gx - 1}):
        pl.semaphore_signal(barrier, inc=1, device_id=away("gx", step), device_id_type=MESH)

    @pl.when(gx == 0)
    def _():
        for b in range(1, chips):
            pl.semaphore_signal(
                barrier,
                inc=1,
                device_id={"gx": 1, "gy": 2 * lax.rem(chip + b, chips) + core},
                device_id_type=MESH,
            )

    for step in (-1, 1):
        greeted = greeted + there["gz", step].astype(jnp.int32)

        @pl.when(there["gz", step])
        def _(step=step):
            pl.semaphore_signal(
                barrier, inc=1, device_id=away("gz", step), device_id_type=MESH
            )

    loads = {}
    for number, (name, src, dst) in enumerate(
        (
            ("modes", modes_in, modes_ref),
            ("now", now_in, now_ref),
            ("prev", prev_in, prev_ref),
            ("speed", speed_in, speed_ref),
            ("radius", radius_in, radius_ref),
            ("moduli", moduli_in, moduli_ref),
            ("second", second_in, second_ref),
            ("dest", dest_in, dest_ref),
            ("target", target_in, target_ref),
            ("source", source_in, source_ref),
            ("azimuth", azimuth_in, azimuth_ref),
            ("first", first_in, first_ref),
            ("slab", slab_in, slab_ref),
            ("before", before_in, before_ref),
            ("mass", mass_in, mass_ref),
        )
    ):
        loads[name] = pltpu.make_async_copy(src, dst, in_sem.at[number])
        loads[name].start()

    def push(src, dst, sems, index, device):
        copy = pltpu.make_async_remote_copy(
            src_ref=src,
            dst_ref=dst,
            send_sem=sems.at[(0, *index)],
            recv_sem=sems.at[(1, *index)],
            device_id=device,
            device_id_type=MESH,
        )
        copy.start()
        return copy

    class Neighbour:
        def __init__(self, src, dst, sems, index, axis, step):
            self.copy = pltpu.make_async_remote_copy(
                src_ref=src,
                dst_ref=dst,
                send_sem=sems.at[(0, *index)],
                recv_sem=sems.at[(1, *index)],
                device_id=away(axis, step),
                device_id_type=MESH,
            )
            self.sends, self.receives = there[axis, step], there[axis, -step]
            pl.when(self.sends)(lambda: self.copy.start())

        def wait_recv(self):
            pl.when(self.receives)(lambda: self.copy.wait_recv())

        def wait_send(self):
            pl.when(self.sends)(lambda: self.copy.wait_send())

    for (axis, step), here in there.items():

        @pl.when(jnp.logical_not(here))
        def _(axis=axis, side=(1 - step) // 2):
            if axis == "gx":
                cycle_recv[side] = jnp.zeros(cycle_recv.shape[1:], F32)
                x_recv[:, side] = jnp.zeros((3, 3, 8, LANES), F32)
            elif axis == "gy":
                y_recv[:, side] = jnp.zeros((3, 16, LANES), F32)
            else:
                z_recv[:, side] = jnp.zeros((3, 8, LANES), F32)

    sub = iota((8, LANES), 0)
    lane = iota((8, LANES), 1)

    mode_base = (4 * gy).astype(F32)
    row24 = iota((24, LANES), 0)
    order24 = mode_base + (
        (row24 >= 6).astype(F32) + (row24 >= 12).astype(F32) + (row24 >= 18).astype(F32)
    )
    square24 = order24 * order24
    for name in ("modes", "now", "prev", "speed", "radius"):
        loads[name].wait()
    for side, (edge, inner) in enumerate(((0, 1), (7, 6))):
        count = modes_ref[edge].astype(F32)
        mask = jnp.where(order24 < count, F32(1.0), F32(0.0))
        speed = speed_ref[edge : edge + 1, :]
        radius = radius_ref[edge : edge + 1, :]
        at_edge = now_ref[pl.ds(edge, 24, stride=8), :]
        cycle_send[side, 0:24, :] = at_edge
        cycle_send[side, 24:48, :] = mask * (
            (2.0 - 2.0 * time_sq * speed - time_sq * square24 * radius) * at_edge
            - prev_ref[pl.ds(edge, 24, stride=8), :]
            + time_sq * speed * now_ref[pl.ds(inner, 24, stride=8), :]
        )
        cycle_send[side, 48:56, :] = jnp.where(
            sub == 0, jnp.broadcast_to(speed, (8, LANES)), jnp.full((8, LANES), count, F32)
        )

    pl.semaphore_wait(barrier, greeted)

    reaches, known = [], 0
    while known < n_gx // 2:
        reaches.append(min(known + 1, n_gx // 2 - known))
        known += reaches[-1]

    def tell(level):
        for step in (reaches[level], -reaches[level]):
            pl.semaphore_signal(
                ring_sems.at[level], inc=1, device_id=away("gx", step), device_id_type=MESH
            )

    def hear(level):
        pl.semaphore_wait(ring_sems.at[level], 2)

    def advance(level):
        if level < len(reaches):
            hear(level)
        if level + 1 < len(reaches):
            tell(level + 1)

    told_last = min(9, n_gx - 1)

    def hear_below():
        pl.semaphore_wait(ring_sems.at[4], 1)

    def pass_on(first, last):
        @pl.when((gx >= first) & (gx <= min(last, told_last - 1)))
        def _():
            pl.when(gx >= 2)(hear_below)
            pl.semaphore_signal(
                ring_sems.at[4], inc=1, device_id=away("gx", 1), device_id_type=MESH
            )

    tell(0)
    pass_on(1, 4)
    sent = []
    cycle_in = []
    for side, step in ((0, -1), (1, 1)):
        copy = Neighbour(
            cycle_send.at[side], cycle_recv.at[side], cycle_sems, (side,), "gx", step
        )
        sent.append(copy)
        cycle_in.append(copy)

    last_x = jnp.where(gx < n_gx - 1, F32(1.0), F32(0.0))
    last_y = jnp.where(gy < n_gy - 1, F32(1.0), F32(0.0))
    last_z = jnp.where(gz < n_gz - 1, F32(1.0), F32(0.0))
    has_x = jnp.where(gx > 0, F32(1.0), F32(0.0))
    has_y = jnp.where(gy > 0, F32(1.0), F32(0.0))
    has_z = jnp.where(gz > 0, F32(1.0), F32(0.0))

    def send_face(number, axis, count):
        place = ("gx", "gy", "gz").index(axis)
        out, into = ((x_send, x_recv), (y_send, y_recv), (z_send, z_recv))[place]
        copies = [
            Neighbour(
                out.at[number, side, 0:count],
                into.at[number, side, 0:count],
                face_sems,
                (number, 2 * place + side),
                axis,
                step,
            )
            for side, step in ((0, -1), (1, 1))
        ]
        sent.extend(copies)
        return copies

    def columns_to_lanes(columns):
        out = jnp.zeros((8, LANES), F32)
        for number, column in enumerate(columns):
            out = jnp.where(lane == number, jnp.broadcast_to(column, (8, LANES)), out)
        return out

    loads["moduli"].wait()
    inner = [float(GRAM[k, 4, 4]) for k in range(5)]
    mu = moduli_ref[...].reshape(4, 8, LANES)
    x_send[0, 0, 0] = mu[0]
    x_send[0, 1, 0] = last_x * (
        inner[0] * mu[0] + inner[1] * mu[1] + inner[2] * mu[2] + inner[3] * mu[3]
    )
    y_send[0, 0, 0:8] = jnp.zeros((8, LANES), F32)
    y_send[0, 1, 0:8] = jnp.zeros((8, LANES), F32)
    y_send[0, 0, 0:4] = moduli_ref[pl.ds(0, 4, stride=8), :]
    y_send[0, 1, 0:4] = last_y * sum(
        inner[k] * moduli_ref[pl.ds(4 + k, 4, stride=8), :] for k in range(4)
    )
    tail = by_four(lane & 3, inner[:4]) * jnp.where(lane >= LANES - 4, last_z, F32(0.0))
    z_send[0, 0] = columns_to_lanes([mu[x][:, 0:1] for x in range(4)])
    z_send[0, 1] = columns_to_lanes(
        [jnp.sum(tail * mu[x], axis=1, keepdims=True) for x in range(4)]
    )
    moduli_copies = [
        copy
        for axis, count in (("gy", 8), ("gz", 8), ("gx", 1))
        for copy in send_face(0, axis, count)
    ]

    pass_on(5, 7)
    advance(0)

    loads["second"].wait()
    pair_second[...] = operator_pair(second_ref[...])
    counts = jnp.zeros((8, LANES), F32)
    for row in range(8):
        counts = jnp.where(sub == row, modes_ref[row].astype(F32), counts)
    order = mode_base + iota((4, 8, LANES), 0).astype(F32)
    mask = jnp.where(order < counts[None], F32(1.0), F32(0.0))
    speed, radius = speed_ref[...][None], radius_ref[...][None]
    hold = (mask * (2.0 - 2.0 * time_sq * speed - time_sq * (order * order) * radius))[:, None]
    side_weight = (mask * (time_sq * speed))[:, None]
    bend_weight = (mask * time_sq)[:, None]
    mask = mask[:, None]

    def section_sum(now, prev):
        cells = now.reshape(24, 8, LANES)
        rows = iota((24, 8, LANES), 1)
        near = jnp.where(rows == 0, F32(0.0), pltpu.roll(cells, 1, 1)) + jnp.where(
            rows == 7, F32(0.0), pltpu.roll(cells, 7, 1)
        )
        return (
            hold * now.reshape(4, 6, 8, LANES)
            - mask * prev.reshape(4, 6, 8, LANES)
            + side_weight * near.reshape(4, 6, 8, LANES)
            + bend_weight * times_operator(now, pair_second).reshape(4, 6, 8, LANES)
        )

    one_ref[...] = section_sum(now_ref[...], prev_ref[...]).reshape(192, LANES)
    edge_ref[...] = jnp.zeros((192, LANES), F32)

    for name in ("dest", "target", "source", "azimuth"):
        loads[name].wait()
    owner = dest_ref[...]
    blocks = points // LANES
    named = (iota((LANES, points), 0) == owner).astype(F32)
    named_rows = jnp.concatenate(
        [named[:, b * LANES : (b + 1) * LANES] for b in range(blocks)], axis=0
    ).astype(BF16)
    before = (iota((LANES, LANES), 0) < iota((LANES, LANES), 1)).astype(F32)
    counted = dot(
        named_rows, jnp.concatenate([before, jnp.ones_like(before)], axis=1).astype(BF16)
    )
    ranks, offset = [], None
    for b in range(blocks):
        piece = counted[b * LANES : (b + 1) * LANES]
        place = piece[:, :LANES] if offset is None else piece[:, :LANES] + offset
        ranks.append(
            jnp.sum(named[:, b * LANES : (b + 1) * LANES] * place, axis=0, keepdims=True)
        )
        offset = piece[:, LANES:] if offset is None else offset + piece[:, LANES:]
    rank = jnp.concatenate(ranks, axis=1).astype(jnp.int32)
    if n_gy == 8:
        owner_x, owner_y = owner >> 3, owner & 7
    else:
        owner_x, owner_y = owner >> 1, owner & 1
    slot = owner_x * RANKS + rank
    slot_ref[...] = (iota((LANES, points), 0) == slot).astype(F32).astype(BF16)
    target = target_ref[...]
    sub_p = iota((8, points), 0)
    mine = owner_y == 2 * (sub_p & 3) + core
    marks = jnp.where(sub_p < 4, target >> 7, target & 127).astype(F32)
    marked = dot_rows(jnp.where(mine, marks, F32(0.0)).astype(BF16), slot_ref[...])
    mark_ref[0:4, :] = (128.0 / chips) * marked[0:4] + (1.0 / chips) * marked[4:8]
    source = source_ref[...]
    picked = (iota((LANES, points), 0) == (source & 127)).astype(F32).astype(BF16)
    pick_ref[0:LANES, :] = picked
    pick_ref[LANES:, :] = picked
    turns = (mode_base + (sub_p & 3).astype(F32)) * (azimuth_ref[...] * (0.5 / math.pi))
    turns = turns - jnp.where(sub_p >= 4, F32(0.25), F32(0.0))
    turns = turns - jnp.floor(turns + 0.5)
    square = turns * turns
    wave = jnp.full(square.shape, COSINE[-1], F32)
    for value in COSINE[-2::-1]:
        wave = wave * square + value
    in_cycle = sub_p == (source >> 7)
    for row in range(8):
        trig_ref[row] = jnp.where(
            in_cycle, jnp.broadcast_to(wave[row : row + 1], (8, points)), F32(0.0)
        )
    loads["first"].wait()
    pair_first[...] = operator_pair(first_ref[...])

    advance(1)
    pass_on(8, 8)

    for copy in cycle_in:
        copy.wait_recv()
    flags = (last_x, has_x)
    near_edges = [cycle_recv[side, 0:24, :] for side in range(2)]
    bends = times_operator(jnp.concatenate(near_edges, axis=0), pair_second)
    beyond = []
    for side, edge in ((0, 7), (1, 0)):
        tail_rows = cycle_recv[side, 48:56, :]
        speed24 = tail_rows[0:1]
        mask24 = jnp.where(order24 < tail_rows[1:2], F32(1.0), F32(0.0))
        edge_ref[pl.ds(edge, 24, stride=8), :] = flags[side] * near_edges[side]
        value = cycle_recv[side, 24:48, :] + mask24 * time_sq * (
            speed24 * now_ref[pl.ds(edge, 24, stride=8), :] + bends[24 * side : 24 * side + 24]
        )
        beyond.append(flags[side] * value)
    one = one_ref[...].reshape(4, 6, 8, LANES) + side_weight * edge_ref[...].reshape(
        4, 6, 8, LANES
    )
    one = one.reshape(192, LANES)
    for side, edge in ((0, 7), (1, 0)):
        edge_ref[pl.ds(edge, 24, stride=8), :] = beyond[side]
    two = section_sum(one, now_ref[...]) + side_weight * edge_ref[...].reshape(4, 6, 8, LANES)
    two = two.reshape(192, LANES)
    g_out[...] = two

    coef = coupling * times_operator(two, pair_first) + (coupling * impedance / time_step) * (
        two - one
    )
    high, low = halves(coef)
    at_points = dot(jnp.concatenate([high, low], axis=1), pick_ref[...]).reshape(
        4, 6, 8, points
    )
    values = jnp.zeros((8, points), F32)
    for c in range(3):
        total = jnp.zeros((8, points), F32)
        for m in range(4):
            total = total + at_points[m, 2 * c] * trig_ref[m]
            total = total + at_points[m, 2 * c + 1] * trig_ref[4 + m]
        values = jnp.where(
            (sub_p & 3) == c,
            jnp.broadcast_to(jnp.sum(total, axis=0, keepdims=True), (8, points)),
            values,
        )
    half = 8 * max(1, chips // 2)
    by_group = jnp.concatenate(
        [
            jnp.where(owner_y == 2 * (2 * tile + (sub_p >> 2)) + side, values, F32(0.0))
            for side in range(2)
            for tile in range(half // 8)
        ],
        axis=0,
    )
    high, low = halves(by_group)
    packed = dot_rows(jnp.concatenate([high, low], axis=0), slot_ref[...])
    packed = packed[: 2 * half] + packed[2 * half :]
    for side in range(2):
        group_send[side] = packed[half * side : half * side + half]
    pair = push(
        group_send.at[1 - core], group_recv, group_sems, (), {"gy": gy + 1 - 2 * core}
    )
    sent.append(pair)

    pair.wait_recv()
    total = group_send[core] + group_recv[...]
    rows16 = iota((n_gx, LANES), 0)
    lanes16 = iota((n_gx, LANES), 1)
    for place in range(chips):
        outgoing = jnp.zeros((n_gx, LANES), F32)
        for c in range(4):
            at = 4 * place + c
            line = total[at : at + 1] if c < 3 else mark_ref[place : place + 1]
            line = jnp.broadcast_to(line, (8, LANES))
            if (RANKS * (c + 1 - n_gx)) % LANES:
                line = pltpu.roll(line, (RANKS * (c + 1 - n_gx)) % LANES, 1)
            moved = pltpu.roll(
                jnp.broadcast_to(line[0:1], (n_gx, LANES)), 0, 1, stride=RANKS, stride_axis=0
            )
            outgoing = jnp.where(lanes16 >> 3 == c, moved, outgoing)
        owner_send[place] = outgoing.reshape(n_gx, 1, LANES)

    def to_row(a, first=0):
        peer_x = lax.rem(gx + a, n_gx)
        for b in range(first, chips):
            peer_chip = lax.rem(chip + b, chips)
            pltpu.make_async_remote_copy(
                src_ref=owner_send.at[peer_chip, n_gx - 1 - peer_x],
                dst_ref=owner_recv.at[b * n_gx + a],
                send_sem=owner_sems.at[0],
                recv_sem=owner_sems.at[1],
                device_id={"gx": peer_x, "gy": 2 * peer_chip + core},
                device_id_type=MESH,
            ).start()

    def far_first(first, last, when=None):
        def body(number, carry):
            away_by = (number + 1) // 2
            a = n_gx // 2 + jnp.where(number % 2 == 1, -away_by, away_by)
            if when is None:
                to_row(a)
            else:
                pl.when(when(a))(lambda: to_row(a))
            return carry

        lax.fori_loop(first, last, body, 0)

    pl.when(gx == told_last)(hear_below)
    chained = (gx >= min(8, told_last)) & (gx <= told_last)

    def below(a):
        return chained & (gx + a >= n_gx)

    def others(a):
        return jnp.logical_not(below(a))

    pl.when(chained)(lambda: far_first(0, n_gx - 1, below))
    first = min(1, len(reaches) - 1)
    done = n_gx - 1
    for level in range(first, len(reaches)):
        if level >= 2:
            advance(level)
        start = max(0, 2 * (n_gx // 2 - sum(reaches[: level + 1])) - 1)
        far_first(start, done, others)
        done = start
        if level == first:
            to_row(0, 1)
    owner_recv[0] = owner_send[chip, n_gx - 1 - gx]
    rows_all = chips * n_gx
    owner_in = pltpu.make_async_remote_copy(
        src_ref=owner_recv.at[1:rows_all],
        dst_ref=owner_recv.at[1:rows_all],
        send_sem=owner_sems.at[0],
        recv_sem=owner_sems.at[1],
        device_id=away("gx", 1),
        device_id_type=MESH,
    )

    for copy in moduli_copies:
        copy.wait_recv()
    mu_next_x = last_x * x_recv[0, 0, 0]
    sum_prev_x = x_recv[0, 1, 0]
    lane4 = iota((4, 8, LANES), 2)
    sub4 = iota((4, 8, LANES), 1)
    side_w = [0.2] + [float(v) for v in WEIGHTS[1:4]]
    first_weight = -float(WEIGHTS[4])
    weight_y = by_four(sub & 3, side_w) + jnp.where(
        sub == 0, (1.0 - has_y) * first_weight, F32(0.0)
    )
    weight_z = by_four(lane & 3, side_w) + jnp.where(
        lane == 0, (1.0 - has_z) * first_weight, F32(0.0)
    )
    weight_x = [side_w[0] + (1.0 - has_x) * first_weight] + side_w[1:]

    def make_band(axis, position, count, following, preceding, weights, has, last, band, over):
        shifted = {0: mu}
        for t in range(-4, 5):
            if t:
                rolled = pltpu.roll(mu, (-t) % count, axis)
                if t > 0:
                    rolled = jnp.where(position == count - t, following, rolled)
                shifted[t] = rolled
        pos2 = position[0]
        phase = pos2 & 3
        later = pos2 > 3
        band_values = []
        for s in range(5):
            total = None
            for t in range(s - 4, 5):
                row = [
                    GRAM[i + t, i, i + s] if 0 <= i + t <= 4 and i + s <= 4 else 0.0
                    for i in range(4)
                ]
                pattern = by_four(phase, row)
                if s == 0 and t <= 0:
                    pattern = pattern + jnp.where(
                        (phase == 0) & later, F32(GRAM[4 + t, 4, 4]), F32(0.0)
                    )
                term = pattern[None] * shifted[t]
                total = term if total is None else total + term
            if s == 0:
                total = total + jnp.where(
                    position == 0, preceding + has * float(GRAM[4, 4, 4]) * mu, F32(0.0)
                )
            band_values.append(total * weights)
        crossing = jnp.zeros_like(mu)
        for s in range(1, 5):
            crossing = jnp.where(position == count - s, band_values[s], crossing)
            inside = jnp.where(position >= count - s, F32(0.0), band_values[s])
            behind = pltpu.roll(inside, s, axis)
            if 2 * s == count:
                band[s] = inside + behind
                band[4 + s] = jnp.zeros_like(inside)
            else:
                band[s] = inside
                band[4 + s] = behind
        over[...] = last * crossing
        band[0] = band_values[0]

    y_next = y_recv[0, 0, 0:8]
    y_prev = y_recv[0, 1, 0:8]
    z_next = z_recv[0, 0]
    z_prev = z_recv[0, 1]

    def rows_of(value):
        return jnp.concatenate(
            [jnp.broadcast_to(value[x : x + 1], (8, LANES))[None] for x in range(4)], axis=0
        )

    def columns_of(value):
        return jnp.concatenate(
            [jnp.broadcast_to(value[:, x : x + 1], (8, LANES))[None] for x in range(4)], axis=0
        )

    stacked = lambda scale: jnp.concatenate([(scale(x))[None] for x in range(4)], axis=0)
    make_band(
        2,
        lane4,
        LANES,
        last_z * columns_of(z_next),
        columns_of(z_prev),
        stacked(lambda x: weight_x[x] * weight_y),
        has_z,
        last_z,
        band_z,
        over_z,
    )
    make_band(
        1,
        sub4,
        8,
        last_y * rows_of(y_next),
        rows_of(y_prev),
        stacked(lambda x: weight_x[x] * weight_z),
        has_y,
        last_y,
        band_y,
        over_y,
    )
    weight_yz = weight_y * weight_z
    planes = [mu[x] for x in range(4)] + [mu_next_x]
    for i in range(4):
        for j in range(i, 5):
            value = sum(float(GRAM[k, i, j]) * planes[k] for k in range(5))
            if i == 0 and j == 0:
                value = value + sum_prev_x + has_x * float(GRAM[4, 4, 4]) * mu[0]
            if j == 4:
                value = last_x * value
            band_x[5 * i + j] = value * weight_yz
    for x in range(4):
        band_z[0, x] = band_z[0, x] + band_y[0, x] + band_x[6 * x]

    def coupling_x(i, j):
        return band_x[5 * min(i, j) + max(i, j)]

    def face_values(number, ref):
        field = ref[...].reshape(3, 4, 8, LANES)
        y_send[number, 0, 0:12] = ref[pl.ds(0, 12, stride=8), :]
        part_ref[...] = (over_y[...][None] * field).reshape(96, LANES)
        y_send[number, 1, 0:12] = sum(
            part_ref[pl.ds(4 + k, 12, stride=8), :] for k in range(4)
        )
        copies = send_face(number, "gy", 16)
        for c in range(3):
            x_send[number, 0, c] = field[c, 0]
            x_send[number, 1, c] = sum(coupling_x(i, 4) * field[c, i] for i in range(4))
        copies += send_face(number, "gx", 3)
        z_send[number, 0] = columns_to_lanes(
            [field[c, x][:, 0:1] for c in range(3) for x in range(4)]
        )
        z_send[number, 1] = columns_to_lanes(
            [
                jnp.sum(over_z[x] * field[c, x], axis=1, keepdims=True)
                for c in range(3)
                for x in range(4)
            ]
        )
        return copies + send_face(number, "gz", 8)

    def inner_stiffness(ref):
        field = ref[...].reshape(3, 4, 8, LANES)
        out = []
        for x in range(4):
            plane = field[:, x]
            total = band_z[0, x] * plane
            for s in range(1, 5):
                total = total + band_z[s, x] * pltpu.roll(plane, LANES - s, 2)
                total = total + band_z[4 + s, x] * pltpu.roll(plane, s, 2)
                total = total + band_y[s, x] * pltpu.roll(plane, 8 - s, 1)
                if s < 4:
                    total = total + band_y[4 + s, x] * pltpu.roll(plane, s, 1)
            for j in range(4):
                if j != x:
                    total = total + coupling_x(x, j) * field[:, j]
            out.append(total)
        return out

    def outer_stiffness(number, copies, inside):
        for copy in copies:
            copy.wait_recv()
        y_first = y_recv[number, 1, 0:12]
        y_after = y_recv[number, 0, 0:12]
        spread_ref[pl.ds(0, 12, stride=8), :] = y_first
        for k in range(4):
            spread_ref[pl.ds(4 + k, 12, stride=8), :] = y_after
        spread = spread_ref[...].reshape(3, 4, 8, LANES)
        z_first, z_after = z_recv[number, 1], z_recv[number, 0]
        x_after, x_first = x_recv[number, 0], x_recv[number, 1]
        out = []
        for x in range(4):
            rows = []
            for c in range(3):
                at = 4 * c + x
                row = inside[x][c] + coupling_x(x, 4) * x_after[c]
                row = row + jnp.where(sub == 0, F32(1.0), over_y[x]) * spread[c, x]
                row = row + jnp.where(
                    lane == 0,
                    jnp.broadcast_to(z_first[:, at : at + 1], (8, LANES)),
                    over_z[x] * jnp.broadcast_to(z_after[:, at : at + 1], (8, LANES)),
                )
                if x == 0:
                    row = row + x_first[c]
                rows.append(row)
            out.append(rows)
        return out

    spread_ref[...] = jnp.zeros((96, LANES), F32)
    loads["slab"].wait()
    now_copies = face_values(1, slab_ref)

    inside = inner_stiffness(slab_ref)
    loads["before"].wait()
    loads["mass"].wait()
    around = outer_stiffness(1, now_copies, inside)
    for x in range(4):
        scale = slab_factor * mass_ref[8 * x : 8 * x + 8, :]
        for c in range(3):
            at = 32 * c + 8 * x
            base_ref[at : at + 8, :] = (
                2.0 * slab_ref[at : at + 8, :]
                - before_ref[at : at + 8, :]
                - scale * around[x][c]
            )

    owner_in.wait_recv()
    arrived = sum(
        owner_recv[b * n_gx : (b + 1) * n_gx].reshape(n_gx, LANES) for b in range(chips)
    )
    lines = []
    moved = pltpu.roll(arrived, 0, 1, stride=RANKS, stride_axis=0)
    for c in range(4):
        own = ((lanes16 >> 3) - rows16 - c) & 15 == 0
        line = jnp.sum(jnp.where(own, moved, F32(0.0)), axis=0, keepdims=True)
        if c:
            line = pltpu.roll(jnp.broadcast_to(line, (8, LANES)), LANES - RANKS * c, 1)[0:1]
        lines.append(line)
    goal = lines[3].astype(jnp.int32)
    goal_row, goal_lane = goal >> 7, goal & 127
    rows32 = iota((32, LANES), 0)
    spots = jnp.concatenate(
        [jnp.where(rows32 == goal_row, lines[c], F32(0.0)) for c in range(3)], axis=0
    )
    high, low = halves(spots)
    on_lane = (iota((LANES, LANES), 0) == goal_lane).astype(F32).astype(BF16)
    force = dot_rows(
        jnp.concatenate([high, low], axis=1), jnp.concatenate([on_lane, on_lane], axis=1)
    )
    force_out[...] = force
    for x in range(4):
        scale = slab_factor * mass_ref[8 * x : 8 * x + 8, :]
        for c in range(3):
            at = 32 * c + 8 * x
            step_ref[at : at + 8, :] = base_ref[at : at + 8, :] + scale * force[at : at + 8]

    step_copies = face_values(2, step_ref)
    inside = inner_stiffness(step_ref)
    around = outer_stiffness(2, step_copies, inside)
    for x in range(4):
        scale = slab_factor * mass_ref[8 * x : 8 * x + 8, :]
        for c in range(3):
            at = 32 * c + 8 * x
            slab_out[at : at + 8, :] = (
                2.0 * step_ref[at : at + 8, :]
                - slab_ref[at : at + 8, :]
                + scale * (force_out[at : at + 8, :] - around[x][c])
            )
    for copy in sent:
        copy.wait_send()
    owner_in.wait_send()


def copy_out(*refs):
    sems = refs[6]
    copies = [pltpu.make_async_copy(refs[i], refs[3 + i], sems.at[i]) for i in range(3)]
    for copy in copies:
        copy.start()
    for copy in copies:
        copy.wait()


def solution(mesh):
    n_gx, n_gy, n_gz = (mesh.shape[name] for name in ("gx", "gy", "gz"))

    def on_device(
        global_now,
        global_prev,
        cycle_modes,
        wave_speed,
        inv_radius,
        theta_second,
        theta_first,
        point_dest,
        point_target,
        point_source,
        point_azimuth,
        regional_now,
        regional_prev,
        moduli,
        inv_mass,
    ):
        points = point_target.shape[1]
        big = [((192, LANES), F32)] * 2 + [((8, LANES), F32)] * 2 + [((LANES, LANES), F32)] * 2
        big += [((1, points), jnp.int32)] * 3 + [((1, points), F32)]
        big += [((96, LANES), F32)] * 2 + [((32, LANES), F32)] * 2
        scratch = [pltpu.SMEM(cycle_modes.shape, jnp.int32)]
        scratch += [pltpu.VMEM(shape, dtype) for shape, dtype in big]
        scratch += [
            pltpu.VMEM((192, LANES), F32),
            pltpu.VMEM((192, LANES), F32),
            pltpu.VMEM((2 * LANES, 2 * LANES), BF16),
            pltpu.VMEM((2 * LANES, 2 * LANES), BF16),
            pltpu.VMEM((2 * LANES, points), BF16),
            pltpu.VMEM((8, 8, points), F32),
            pltpu.VMEM((LANES, points), BF16),
            pltpu.VMEM((8, LANES), F32),
            pltpu.VMEM((96, LANES), F32),
            pltpu.VMEM((96, LANES), F32),
            pltpu.VMEM((9, 4, 8, LANES), F32),
            pltpu.VMEM((9, 4, 8, LANES), F32),
            pltpu.VMEM((20, 8, LANES), F32),
            pltpu.VMEM((4, 8, LANES), F32),
            pltpu.VMEM((4, 8, LANES), F32),
            pltpu.VMEM((96, LANES), F32),
            pltpu.VMEM((96, LANES), F32),
            pltpu.VMEM((2, 56, LANES), F32),
            pltpu.VMEM((2, 56, LANES), F32),
            pltpu.VMEM((3, 2, 3, 8, LANES), F32),
            pltpu.VMEM((3, 2, 3, 8, LANES), F32),
            pltpu.VMEM((3, 2, 16, LANES), F32),
            pltpu.VMEM((3, 2, 16, LANES), F32),
            pltpu.VMEM((3, 2, 8, LANES), F32),
            pltpu.VMEM((3, 2, 8, LANES), F32),
            pltpu.VMEM((2, 8 * max(1, n_gy // 4), LANES), F32),
            pltpu.VMEM((8 * max(1, n_gy // 4), LANES), F32),
            pltpu.VMEM((n_gy // 2, n_gx, 1, LANES), F32),
            pltpu.VMEM((n_gy // 2 * n_gx, 1, LANES), F32),
            pltpu.SemaphoreType.DMA((15,)),
            pltpu.SemaphoreType.DMA((2, 2)),
            pltpu.SemaphoreType.DMA((2, 3, 6)),
            pltpu.SemaphoreType.DMA((2,)),
            pltpu.SemaphoreType.DMA((2,)),
            pltpu.SemaphoreType.REGULAR((5,)),
        ]
        hbm = pl.BlockSpec(memory_space=pl.ANY)
        two, slab, force = pl.pallas_call(
            functools.partial(kernel, (n_gx, n_gy, n_gz)),
            out_shape=[
                pltpu.VMEM((192, LANES), F32),
                pltpu.VMEM((96, LANES), F32),
                pltpu.VMEM((96, LANES), F32),
            ],
            in_specs=[hbm] * 15,
            out_specs=[pl.BlockSpec(memory_space=pltpu.VMEM)] * 3,
            scratch_shapes=scratch,
            compiler_params=pltpu.CompilerParams(
                collective_id=0, has_side_effects=True, vmem_limit_bytes=48 * 2**20
            ),
        )(
            *[
                pltpu.with_memory_space_constraint(x, pltpu.HBM)
                for x in (
            cycle_modes,
            global_now.reshape(192, LANES),
            global_prev.reshape(192, LANES),
            wave_speed,
            inv_radius,
            theta_second,
            theta_first,
            point_dest.reshape(1, points),
            point_target,
            point_source,
            point_azimuth,
            regional_now.reshape(96, LANES),
            regional_prev.reshape(96, LANES),
            moduli.reshape(32, LANES),
            inv_mass.reshape(32, LANES),
            )]
        )
        two, slab, force = pl.pallas_call(
            copy_out,
            out_shape=[
                pltpu.HBM((192, LANES), F32),
                pltpu.HBM((96, LANES), F32),
                pltpu.HBM((96, LANES), F32),
            ],
            in_specs=[hbm] * 3,
            out_specs=[hbm] * 3,
            scratch_shapes=[pltpu.SemaphoreType.DMA((3,))],
        )(*[pltpu.with_memory_space_constraint(x, pltpu.VMEM) for x in (two, slab, force)])
        return (
            two.reshape(global_now.shape),
            slab.reshape(regional_now.shape),
            force.reshape(regional_now.shape),
        )

    return jax.shard_map(
        on_device,
        mesh=mesh,
        in_specs=(
            P("gy", None, "gx", None),
            P("gy", None, "gx", None),
            P("gx"),
            P("gx", None),
            P("gx", None),
            P(),
            P(),
            P("gz", "gx", None),
            P("gz", "gx"),
            P("gz", "gx"),
            P("gz", "gx"),
            P(None, "gx", "gy", "gz"),
            P(None, "gx", "gy", "gz"),
            P("gx", "gy", "gz"),
            P("gx", "gy", "gz"),
        ),
        out_specs=(P("gy", None, "gx", None), P(None, "gx", "gy", "gz"), P(None, "gx", "gy", "gz")),
        check_vma=False,
    )
```

```python
import functools
import math

import jax
import jax.numpy as jnp
import numpy as np
from jax import lax
from jax.experimental import pallas as pl
from jax.experimental.pallas import tpu as pltpu
from jax.sharding import PartitionSpec as P

F32 = jnp.float32
BF16 = jnp.bfloat16
MESH = pl.DeviceIdType.MESH

time_step = 0.3
time_sq = 0.09
impedance = 0.5
coupling = 0.05
slab_factor = 0.04

LANES = 128
RANKS = 8


def gll_products():
    nodes = np.array([-1.0, -math.sqrt(3.0 / 7.0), 0.0, math.sqrt(3.0 / 7.0), 1.0])
    weights = np.array([0.1, 49.0 / 90.0, 32.0 / 45.0, 49.0 / 90.0, 0.1])
    factor = np.array(
        [np.prod([nodes[i] - nodes[k] for k in range(5) if k != i]) for i in range(5)]
    )
    deriv = np.zeros((5, 5))
    for i in range(5):
        for j in range(5):
            if i != j:
                deriv[i, j] = factor[i] / factor[j] / (nodes[i] - nodes[j])
            else:
                deriv[i, j] = sum((1.0 / (nodes[i] - nodes[k]) for k in range(5) if k != i))
    return weights, np.einsum("ki,k,kj->kij", deriv, weights, deriv)


WEIGHTS, GRAM = gll_products()


def cosine_series():
    f = np.cos(np.linspace(0.0, np.pi / 2, 2001)) * 0.5
    fit = np.polynomial.chebyshev.Chebyshev.fit(f * f, np.cos(2 * np.pi * f), 8, domain=[0, 0.25])
    return [float(v) for v in fit.convert(kind=np.polynomial.Polynomial).coef]


COSINE = cosine_series()


def halves(x):
    high = x.astype(BF16)
    return high, (x - high.astype(F32)).astype(BF16)


def dot(a, b):
    return lax.dot_general(a, b, (((1,), (0,)), ((), ())), preferred_element_type=F32)


def dot_rows(a, b):
    return lax.dot_general(a, b, (((1,), (1,)), ((), ())), preferred_element_type=F32)


def operator_pair(t):
    high, low = halves(t)
    top = jnp.concatenate([high, low], axis=1)
    bottom = jnp.concatenate([high, jnp.zeros_like(low)], axis=1)
    return jnp.concatenate([top, bottom], axis=0)


def times_operator(x, pair_ref):
    high, low = halves(x)
    both = dot(jnp.concatenate([high, low], axis=1), pair_ref[...])
    return both[:, :LANES] + both[:, LANES:]


def iota(shape, axis):
    return lax.broadcasted_iota(jnp.int32, shape, axis)


def by_four(phase, values):
    out = jnp.full(phase.shape, values[3], F32)
    for i in (2, 1, 0):
        out = jnp.where(phase == i, F32(values[i]), out)
    return out


def kernel(
    sizes,
    modes_in,
    now_in,
    prev_in,
    speed_in,
    radius_in,
    second_in,
    first_in,
    dest_in,
    target_in,
    source_in,
    azimuth_in,
    slab_in,
    before_in,
    moduli_in,
    mass_in,
    g_out,
    slab_out,
    force_out,
    modes_ref,
    now_ref,
    prev_ref,
    speed_ref,
    radius_ref,
    second_ref,
    first_ref,
    dest_ref,
    target_ref,
    source_ref,
    azimuth_ref,
    slab_ref,
    before_ref,
    moduli_ref,
    mass_ref,
    one_ref,
    edge_ref,
    pair_second,
    pair_first,
    pick_ref,
    trig_ref,
    slot_ref,
    mark_ref,
    base_ref,
    step_ref,
    band_z,
    band_y,
    band_x,
    over_z,
    over_y,
    spread_ref,
    part_ref,
    cycle_send,
    cycle_recv,
    x_send,
    x_recv,
    y_send,
    y_recv,
    z_send,
    z_recv,
    group_send,
    group_recv,
    owner_send,
    owner_recv,
    in_sem,
    cycle_sems,
    face_sems,
    group_sems,
    owner_sems,
    ring_sems,
):
    n_gx, n_gy, n_gz = sizes
    gx, gy, gz = lax.axis_index("gx"), lax.axis_index("gy"), lax.axis_index("gz")
    points = dest_ref.shape[1]
    core, chip = lax.rem(gy, 2), lax.div(gy, 2)
    chips = n_gy // 2

    def away(axis, step):
        index, count = {"gx": (gx, n_gx), "gy": (gy, n_gy), "gz": (gz, n_gz)}[axis]
        return {axis: lax.rem(index + step + count, count)}

    barrier = pltpu.get_barrier_semaphore()
    for step in range(1, n_gy):
        pl.semaphore_signal(barrier, inc=1, device_id=away("gy", step), device_id_type=MESH)
    there = {
        ("gx", -1): gx > 0,
        ("gx", 1): gx < n_gx - 1,
        ("gy", -1): gy > 0,
        ("gy", 1): gy < n_gy - 1,
        ("gz", -1): gz > 0,
        ("gz", 1): gz < n_gz - 1,
    }
    greeted = n_gy - 1 + chips * len({1, n_gx - 1})
    for step in sorted({1, n_gx - 1}):
        for b in range(chips):
            pl.semaphore_signal(
                barrier,
                inc=1,
                device_id={
                    "gx": away("gx", step)["gx"],
                    "gy": 2 * lax.rem(chip + b, chips) + core,
                },
                device_id_type=MESH,
            )
    for step in (-1, 1):
        greeted = greeted + there["gz", step].astype(jnp.int32)

        @pl.when(there["gz", step])
        def _(step=step):
            pl.semaphore_signal(
                barrier, inc=1, device_id=away("gz", step), device_id_type=MESH
            )

    loads = {}
    for number, (name, src, dst) in enumerate(
        (
            ("modes", modes_in, modes_ref),
            ("now", now_in, now_ref),
            ("prev", prev_in, prev_ref),
            ("speed", speed_in, speed_ref),
            ("radius", radius_in, radius_ref),
            ("moduli", moduli_in, moduli_ref),
            ("second", second_in, second_ref),
            ("dest", dest_in, dest_ref),
            ("target", target_in, target_ref),
            ("source", source_in, source_ref),
            ("azimuth", azimuth_in, azimuth_ref),
            ("first", first_in, first_ref),
            ("slab", slab_in, slab_ref),
            ("before", before_in, before_ref),
            ("mass", mass_in, mass_ref),
        )
    ):
        loads[name] = pltpu.make_async_copy(src, dst, in_sem.at[number])
        loads[name].start()

    def push(src, dst, sems, index, device):
        copy = pltpu.make_async_remote_copy(
            src_ref=src,
            dst_ref=dst,
            send_sem=sems.at[(0, *index)],
            recv_sem=sems.at[(1, *index)],
            device_id=device,
            device_id_type=MESH,
        )
        copy.start()
        return copy

    class Neighbour:
        def __init__(self, src, dst, sems, index, axis, step):
            self.copy = pltpu.make_async_remote_copy(
                src_ref=src,
                dst_ref=dst,
                send_sem=sems.at[(0, *index)],
                recv_sem=sems.at[(1, *index)],
                device_id=away(axis, step),
                device_id_type=MESH,
            )
            self.sends, self.receives = there[axis, step], there[axis, -step]
            pl.when(self.sends)(lambda: self.copy.start())

        def wait_recv(self):
            pl.when(self.receives)(lambda: self.copy.wait_recv())

        def wait_send(self):
            pl.when(self.sends)(lambda: self.copy.wait_send())

    for (axis, step), here in there.items():

        @pl.when(jnp.logical_not(here))
        def _(axis=axis, side=(1 - step) // 2):
            if axis == "gx":
                cycle_recv[side] = jnp.zeros(cycle_recv.shape[1:], F32)
                x_recv[:, side] = jnp.zeros((3, 3, 8, LANES), F32)
            elif axis == "gy":
                y_recv[:, side] = jnp.zeros((3, 16, LANES), F32)
            else:
                z_recv[:, side] = jnp.zeros((3, 8, LANES), F32)

    sub = iota((8, LANES), 0)
    lane = iota((8, LANES), 1)

    mode_base = (4 * gy).astype(F32)
    row24 = iota((24, LANES), 0)
    order24 = mode_base + (
        (row24 >= 6).astype(F32) + (row24 >= 12).astype(F32) + (row24 >= 18).astype(F32)
    )
    square24 = order24 * order24
    for name in ("modes", "now", "prev", "speed", "radius"):
        loads[name].wait()
    for side, (edge, inner) in enumerate(((0, 1), (7, 6))):
        count = modes_ref[edge].astype(F32)
        mask = jnp.where(order24 < count, F32(1.0), F32(0.0))
        speed = speed_ref[edge : edge + 1, :]
        radius = radius_ref[edge : edge + 1, :]
        at_edge = now_ref[pl.ds(edge, 24, stride=8), :]
        cycle_send[side, 0:24, :] = at_edge
        cycle_send[side, 24:48, :] = mask * (
            (2.0 - 2.0 * time_sq * speed - time_sq * square24 * radius) * at_edge
            - prev_ref[pl.ds(edge, 24, stride=8), :]
            + time_sq * speed * now_ref[pl.ds(inner, 24, stride=8), :]
        )
        cycle_send[side, 48:56, :] = jnp.where(
            sub == 0, jnp.broadcast_to(speed, (8, LANES)), jnp.full((8, LANES), count, F32)
        )

    pl.semaphore_wait(barrier, greeted)

    reaches, known = [], 1
    while known < n_gx // 2:
        reaches.append(min(known, n_gx // 2 - known))
        known += reaches[-1]

    def tell(level):
        for step in (reaches[level], -reaches[level]):
            pl.semaphore_signal(
                ring_sems.at[level], inc=1, device_id=away("gx", step), device_id_type=MESH
            )

    def hear(level):
        pl.semaphore_wait(ring_sems.at[level], 2)

    def advance(level):
        if level < len(reaches):
            hear(level)
        if level + 1 < len(reaches):
            tell(level + 1)

    told_last = min(9, n_gx - 1)

    def hear_below():
        pl.semaphore_wait(ring_sems.at[4], 1)

    def pass_on(first, last):
        @pl.when((gx >= first) & (gx <= min(last, told_last - 1)))
        def _():
            pl.when(gx >= 2)(hear_below)
            pl.semaphore_signal(
                ring_sems.at[4], inc=1, device_id=away("gx", 1), device_id_type=MESH
            )

    tell(0)
    pass_on(1, 4)
    sent = []
    cycle_in = []
    for side, step in ((0, -1), (1, 1)):
        copy = Neighbour(
            cycle_send.at[side], cycle_recv.at[side], cycle_sems, (side,), "gx", step
        )
        sent.append(copy)
        cycle_in.append(copy)

    last_x = jnp.where(gx < n_gx - 1, F32(1.0), F32(0.0))
    last_y = jnp.where(gy < n_gy - 1, F32(1.0), F32(0.0))
    last_z = jnp.where(gz < n_gz - 1, F32(1.0), F32(0.0))
    has_x = jnp.where(gx > 0, F32(1.0), F32(0.0))
    has_y = jnp.where(gy > 0, F32(1.0), F32(0.0))
    has_z = jnp.where(gz > 0, F32(1.0), F32(0.0))

    def send_face(number, axis, count):
        place = ("gx", "gy", "gz").index(axis)
        out, into = ((x_send, x_recv), (y_send, y_recv), (z_send, z_recv))[place]
        copies = [
            Neighbour(
                out.at[number, side, 0:count],
                into.at[number, side, 0:count],
                face_sems,
                (number, 2 * place + side),
                axis,
                step,
            )
            for side, step in ((0, -1), (1, 1))
        ]
        sent.extend(copies)
        return copies

    def columns_to_lanes(columns):
        out = jnp.zeros((8, LANES), F32)
        for number, column in enumerate(columns):
            out = jnp.where(lane == number, jnp.broadcast_to(column, (8, LANES)), out)
        return out

    loads["moduli"].wait()
    inner = [float(GRAM[k, 4, 4]) for k in range(5)]
    mu = moduli_ref[...].reshape(4, 8, LANES)
    x_send[0, 0, 0] = mu[0]
    x_send[0, 1, 0] = last_x * (
        inner[0] * mu[0] + inner[1] * mu[1] + inner[2] * mu[2] + inner[3] * mu[3]
    )
    y_send[0, 0, 0:8] = jnp.zeros((8, LANES), F32)
    y_send[0, 1, 0:8] = jnp.zeros((8, LANES), F32)
    y_send[0, 0, 0:4] = moduli_ref[pl.ds(0, 4, stride=8), :]
    y_send[0, 1, 0:4] = last_y * sum(
        inner[k] * moduli_ref[pl.ds(4 + k, 4, stride=8), :] for k in range(4)
    )
    tail = by_four(lane & 3, inner[:4]) * jnp.where(lane >= LANES - 4, last_z, F32(0.0))
    z_send[0, 0] = columns_to_lanes([mu[x][:, 0:1] for x in range(4)])
    z_send[0, 1] = columns_to_lanes(
        [jnp.sum(tail * mu[x], axis=1, keepdims=True) for x in range(4)]
    )
    moduli_copies = [
        copy
        for axis, count in (("gy", 8), ("gz", 8), ("gx", 1))
        for copy in send_face(0, axis, count)
    ]

    pass_on(5, 7)
    advance(0)

    loads["second"].wait()
    pair_second[...] = operator_pair(second_ref[...])
    counts = jnp.zeros((8, LANES), F32)
    for row in range(8):
        counts = jnp.where(sub == row, modes_ref[row].astype(F32), counts)
    order = mode_base + iota((4, 8, LANES), 0).astype(F32)
    mask = jnp.where(order < counts[None], F32(1.0), F32(0.0))
    speed, radius = speed_ref[...][None], radius_ref[...][None]
    hold = (mask * (2.0 - 2.0 * time_sq * speed - time_sq * (order * order) * radius))[:, None]
    side_weight = (mask * (time_sq * speed))[:, None]
    bend_weight = (mask * time_sq)[:, None]
    mask = mask[:, None]

    def section_sum(now, prev):
        cells = now.reshape(24, 8, LANES)
        rows = iota((24, 8, LANES), 1)
        near = jnp.where(rows == 0, F32(0.0), pltpu.roll(cells, 1, 1)) + jnp.where(
            rows == 7, F32(0.0), pltpu.roll(cells, 7, 1)
        )
        return (
            hold * now.reshape(4, 6, 8, LANES)
            - mask * prev.reshape(4, 6, 8, LANES)
            + side_weight * near.reshape(4, 6, 8, LANES)
            + bend_weight * times_operator(now, pair_second).reshape(4, 6, 8, LANES)
        )

    one_ref[...] = section_sum(now_ref[...], prev_ref[...]).reshape(192, LANES)
    edge_ref[...] = jnp.zeros((192, LANES), F32)

    for name in ("dest", "target", "source", "azimuth"):
        loads[name].wait()
    owner = dest_ref[...]
    blocks = points // LANES
    named = (iota((LANES, points), 0) == owner).astype(F32)
    named_rows = jnp.concatenate(
        [named[:, b * LANES : (b + 1) * LANES] for b in range(blocks)], axis=0
    ).astype(BF16)
    before = (iota((LANES, LANES), 0) < iota((LANES, LANES), 1)).astype(F32)
    counted = dot(
        named_rows, jnp.concatenate([before, jnp.ones_like(before)], axis=1).astype(BF16)
    )
    ranks, offset = [], None
    for b in range(blocks):
        piece = counted[b * LANES : (b + 1) * LANES]
        place = piece[:, :LANES] if offset is None else piece[:, :LANES] + offset
        ranks.append(
            jnp.sum(named[:, b * LANES : (b + 1) * LANES] * place, axis=0, keepdims=True)
        )
        offset = piece[:, LANES:] if offset is None else offset + piece[:, LANES:]
    rank = jnp.concatenate(ranks, axis=1).astype(jnp.int32)
    if n_gy == 8:
        owner_x, owner_y = owner >> 3, owner & 7
    else:
        owner_x, owner_y = owner >> 1, owner & 1
    slot = owner_x * RANKS + rank
    slot_ref[...] = (iota((LANES, points), 0) == slot).astype(F32).astype(BF16)
    target = target_ref[...]
    sub_p = iota((8, points), 0)
    mine = owner_y == 2 * (sub_p & 3) + core
    marks = jnp.where(sub_p < 4, target >> 7, target & 127).astype(F32)
    marked = dot_rows(jnp.where(mine, marks, F32(0.0)).astype(BF16), slot_ref[...])
    mark_ref[0:4, :] = (128.0 / chips) * marked[0:4] + (1.0 / chips) * marked[4:8]
    source = source_ref[...]
    picked = (iota((LANES, points), 0) == (source & 127)).astype(F32).astype(BF16)
    pick_ref[0:LANES, :] = picked
    pick_ref[LANES:, :] = picked
    turns = (mode_base + (sub_p & 3).astype(F32)) * (azimuth_ref[...] * (0.5 / math.pi))
    turns = turns - jnp.where(sub_p >= 4, F32(0.25), F32(0.0))
    turns = turns - jnp.floor(turns + 0.5)
    square = turns * turns
    wave = jnp.full(square.shape, COSINE[-1], F32)
    for value in COSINE[-2::-1]:
        wave = wave * square + value
    in_cycle = sub_p == (source >> 7)
    for row in range(8):
        trig_ref[row] = jnp.where(
            in_cycle, jnp.broadcast_to(wave[row : row + 1], (8, points)), F32(0.0)
        )
    loads["first"].wait()
    pair_first[...] = operator_pair(first_ref[...])

    advance(1)
    pass_on(8, 8)

    for copy in cycle_in:
        copy.wait_recv()
    flags = (last_x, has_x)
    near_edges = [cycle_recv[side, 0:24, :] for side in range(2)]
    bends = times_operator(jnp.concatenate(near_edges, axis=0), pair_second)
    beyond = []
    for side, edge in ((0, 7), (1, 0)):
        tail_rows = cycle_recv[side, 48:56, :]
        speed24 = tail_rows[0:1]
        mask24 = jnp.where(order24 < tail_rows[1:2], F32(1.0), F32(0.0))
        edge_ref[pl.ds(edge, 24, stride=8), :] = flags[side] * near_edges[side]
        value = cycle_recv[side, 24:48, :] + mask24 * time_sq * (
            speed24 * now_ref[pl.ds(edge, 24, stride=8), :] + bends[24 * side : 24 * side + 24]
        )
        beyond.append(flags[side] * value)
    one = one_ref[...].reshape(4, 6, 8, LANES) + side_weight * edge_ref[...].reshape(
        4, 6, 8, LANES
    )
    one = one.reshape(192, LANES)
    for side, edge in ((0, 7), (1, 0)):
        edge_ref[pl.ds(edge, 24, stride=8), :] = beyond[side]
    two = section_sum(one, now_ref[...]) + side_weight * edge_ref[...].reshape(4, 6, 8, LANES)
    two = two.reshape(192, LANES)
    g_out[...] = two

    coef = coupling * times_operator(two, pair_first) + (coupling * impedance / time_step) * (
        two - one
    )
    high, low = halves(coef)
    at_points = dot(jnp.concatenate([high, low], axis=1), pick_ref[...]).reshape(
        4, 6, 8, points
    )
    values = jnp.zeros((8, points), F32)
    for c in range(3):
        total = jnp.zeros((8, points), F32)
        for m in range(4):
            total = total + at_points[m, 2 * c] * trig_ref[m]
            total = total + at_points[m, 2 * c + 1] * trig_ref[4 + m]
        values = jnp.where(
            (sub_p & 3) == c,
            jnp.broadcast_to(jnp.sum(total, axis=0, keepdims=True), (8, points)),
            values,
        )
    half = 8 * max(1, chips // 2)
    by_group = jnp.concatenate(
        [
            jnp.where(owner_y == 2 * (2 * tile + (sub_p >> 2)) + side, values, F32(0.0))
            for side in range(2)
            for tile in range(half // 8)
        ],
        axis=0,
    )
    high, low = halves(by_group)
    packed = dot_rows(jnp.concatenate([high, low], axis=0), slot_ref[...])
    packed = packed[: 2 * half] + packed[2 * half :]
    for side in range(2):
        group_send[side] = packed[half * side : half * side + half]
    pair = push(
        group_send.at[1 - core], group_recv, group_sems, (), {"gy": gy + 1 - 2 * core}
    )
    sent.append(pair)

    pair.wait_recv()
    total = group_send[core] + group_recv[...]
    rows16 = iota((n_gx, LANES), 0)
    lanes16 = iota((n_gx, LANES), 1)
    for place in range(chips):
        outgoing = jnp.zeros((n_gx, LANES), F32)
        for c in range(4):
            at = 4 * place + c
            line = total[at : at + 1] if c < 3 else mark_ref[place : place + 1]
            line = jnp.broadcast_to(line, (8, LANES))
            if (RANKS * (c + 1 - n_gx)) % LANES:
                line = pltpu.roll(line, (RANKS * (c + 1 - n_gx)) % LANES, 1)
            moved = pltpu.roll(
                jnp.broadcast_to(line[0:1], (n_gx, LANES)), 0, 1, stride=RANKS, stride_axis=0
            )
            outgoing = jnp.where(lanes16 >> 3 == c, moved, outgoing)
        owner_send[place] = outgoing.reshape(n_gx, 1, LANES)

    def to_row(a, first=0):
        peer_x = lax.rem(gx + a, n_gx)
        for b in range(first, chips):
            peer_chip = lax.rem(chip + b, chips)
            pltpu.make_async_remote_copy(
                src_ref=owner_send.at[peer_chip, n_gx - 1 - peer_x],
                dst_ref=owner_recv.at[b * n_gx + a],
                send_sem=owner_sems.at[0],
                recv_sem=owner_sems.at[1],
                device_id={"gx": peer_x, "gy": 2 * peer_chip + core},
                device_id_type=MESH,
            ).start()

    def far_first(first, last, when=None):
        def body(number, carry):
            away_by = (number + 1) // 2
            a = n_gx // 2 + jnp.where(number % 2 == 1, -away_by, away_by)
            if when is None:
                to_row(a)
            else:
                pl.when(when(a))(lambda: to_row(a))
            return carry

        lax.fori_loop(first, last, body, 0)

    pl.when(gx == told_last)(hear_below)
    chained = (gx >= min(8, told_last)) & (gx <= told_last)

    def below(a):
        return chained & (gx + a >= n_gx)

    def others(a):
        return jnp.logical_not(below(a))

    near = n_gx // 2 - 1 if n_gx > 8 else 0
    pl.when(chained)(lambda: far_first(0, near, below))
    far_first(near, n_gx - 1)
    to_row(0, 1)
    for copy in moduli_copies:
        copy.wait_recv()
    mu_next_x = last_x * x_recv[0, 0, 0]
    sum_prev_x = x_recv[0, 1, 0]
    lane4 = iota((4, 8, LANES), 2)
    sub4 = iota((4, 8, LANES), 1)
    side_w = [0.2] + [float(v) for v in WEIGHTS[1:4]]
    first_weight = -float(WEIGHTS[4])
    weight_y = by_four(sub & 3, side_w) + jnp.where(
        sub == 0, (1.0 - has_y) * first_weight, F32(0.0)
    )
    weight_z = by_four(lane & 3, side_w) + jnp.where(
        lane == 0, (1.0 - has_z) * first_weight, F32(0.0)
    )
    weight_x = [side_w[0] + (1.0 - has_x) * first_weight] + side_w[1:]

    def make_band(axis, position, count, following, preceding, weights, has, last, band, over):
        shifted = {0: mu}
        for t in range(-4, 5):
            if t:
                rolled = pltpu.roll(mu, (-t) % count, axis)
                if t > 0:
                    rolled = jnp.where(position == count - t, following, rolled)
                shifted[t] = rolled
        pos2 = position[0]
        phase = pos2 & 3
        later = pos2 > 3
        band_values = []
        for s in range(5):
            total = None
            for t in range(s - 4, 5):
                row = [
                    GRAM[i + t, i, i + s] if 0 <= i + t <= 4 and i + s <= 4 else 0.0
                    for i in range(4)
                ]
                pattern = by_four(phase, row)
                if s == 0 and t <= 0:
                    pattern = pattern + jnp.where(
                        (phase == 0) & later, F32(GRAM[4 + t, 4, 4]), F32(0.0)
                    )
                term = pattern[None] * shifted[t]
                total = term if total is None else total + term
            if s == 0:
                total = total + jnp.where(
                    position == 0, preceding + has * float(GRAM[4, 4, 4]) * mu, F32(0.0)
                )
            band_values.append(total * weights)
        crossing = jnp.zeros_like(mu)
        for s in range(1, 5):
            crossing = jnp.where(position == count - s, band_values[s], crossing)
            inside = jnp.where(position >= count - s, F32(0.0), band_values[s])
            behind = pltpu.roll(inside, s, axis)
            if 2 * s == count:
                band[s] = inside + behind
                band[4 + s] = jnp.zeros_like(inside)
            else:
                band[s] = inside
                band[4 + s] = behind
        over[...] = last * crossing
        band[0] = band_values[0]

    y_next = y_recv[0, 0, 0:8]
    y_prev = y_recv[0, 1, 0:8]
    z_next = z_recv[0, 0]
    z_prev = z_recv[0, 1]

    def rows_of(value):
        return jnp.concatenate(
            [jnp.broadcast_to(value[x : x + 1], (8, LANES))[None] for x in range(4)], axis=0
        )

    def columns_of(value):
        return jnp.concatenate(
            [jnp.broadcast_to(value[:, x : x + 1], (8, LANES))[None] for x in range(4)], axis=0
        )

    stacked = lambda scale: jnp.concatenate([(scale(x))[None] for x in range(4)], axis=0)
    make_band(
        2,
        lane4,
        LANES,
        last_z * columns_of(z_next),
        columns_of(z_prev),
        stacked(lambda x: weight_x[x] * weight_y),
        has_z,
        last_z,
        band_z,
        over_z,
    )
    make_band(
        1,
        sub4,
        8,
        last_y * rows_of(y_next),
        rows_of(y_prev),
        stacked(lambda x: weight_x[x] * weight_z),
        has_y,
        last_y,
        band_y,
        over_y,
    )
    weight_yz = weight_y * weight_z
    planes = [mu[x] for x in range(4)] + [mu_next_x]
    for i in range(4):
        for j in range(i, 5):
            value = sum(float(GRAM[k, i, j]) * planes[k] for k in range(5))
            if i == 0 and j == 0:
                value = value + sum_prev_x + has_x * float(GRAM[4, 4, 4]) * mu[0]
            if j == 4:
                value = last_x * value
            band_x[5 * i + j] = value * weight_yz
    for x in range(4):
        band_z[0, x] = band_z[0, x] + band_y[0, x] + band_x[6 * x]

    def coupling_x(i, j):
        return band_x[5 * min(i, j) + max(i, j)]

    def face_values(number, ref):
        field = ref[...].reshape(3, 4, 8, LANES)
        y_send[number, 0, 0:12] = ref[pl.ds(0, 12, stride=8), :]
        part_ref[...] = (over_y[...][None] * field).reshape(96, LANES)
        y_send[number, 1, 0:12] = sum(
            part_ref[pl.ds(4 + k, 12, stride=8), :] for k in range(4)
        )
        copies = send_face(number, "gy", 16)
        for c in range(3):
            x_send[number, 0, c] = field[c, 0]
            x_send[number, 1, c] = sum(coupling_x(i, 4) * field[c, i] for i in range(4))
        copies += send_face(number, "gx", 3)
        z_send[number, 0] = columns_to_lanes(
            [field[c, x][:, 0:1] for c in range(3) for x in range(4)]
        )
        z_send[number, 1] = columns_to_lanes(
            [
                jnp.sum(over_z[x] * field[c, x], axis=1, keepdims=True)
                for c in range(3)
                for x in range(4)
            ]
        )
        return copies + send_face(number, "gz", 8)

    def inner_stiffness(ref):
        field = ref[...].reshape(3, 4, 8, LANES)
        out = []
        for x in range(4):
            plane = field[:, x]
            total = band_z[0, x] * plane
            for s in range(1, 5):
                total = total + band_z[s, x] * pltpu.roll(plane, LANES - s, 2)
                total = total + band_z[4 + s, x] * pltpu.roll(plane, s, 2)
                total = total + band_y[s, x] * pltpu.roll(plane, 8 - s, 1)
                if s < 4:
                    total = total + band_y[4 + s, x] * pltpu.roll(plane, s, 1)
            for j in range(4):
                if j != x:
                    total = total + coupling_x(x, j) * field[:, j]
            out.append(total)
        return out

    def outer_stiffness(number, copies, inside):
        for copy in copies:
            copy.wait_recv()
        y_first = y_recv[number, 1, 0:12]
        y_after = y_recv[number, 0, 0:12]
        spread_ref[pl.ds(0, 12, stride=8), :] = y_first
        for k in range(4):
            spread_ref[pl.ds(4 + k, 12, stride=8), :] = y_after
        spread = spread_ref[...].reshape(3, 4, 8, LANES)
        z_first, z_after = z_recv[number, 1], z_recv[number, 0]
        x_after, x_first = x_recv[number, 0], x_recv[number, 1]
        out = []
        for x in range(4):
            rows = []
            for c in range(3):
                at = 4 * c + x
                row = inside[x][c] + coupling_x(x, 4) * x_after[c]
                row = row + jnp.where(sub == 0, F32(1.0), over_y[x]) * spread[c, x]
                row = row + jnp.where(
                    lane == 0,
                    jnp.broadcast_to(z_first[:, at : at + 1], (8, LANES)),
                    over_z[x] * jnp.broadcast_to(z_after[:, at : at + 1], (8, LANES)),
                )
                if x == 0:
                    row = row + x_first[c]
                rows.append(row)
            out.append(rows)
        return out

    spread_ref[...] = jnp.zeros((96, LANES), F32)
    loads["slab"].wait()
    now_copies = face_values(1, slab_ref)

    for level in range(2, len(reaches)):
        advance(level)
    far_first(0, near, others)
    owner_recv[0] = owner_send[chip, n_gx - 1 - gx]
    rows_all = chips * n_gx
    owner_in = pltpu.make_async_remote_copy(
        src_ref=owner_recv.at[1:rows_all],
        dst_ref=owner_recv.at[1:rows_all],
        send_sem=owner_sems.at[0],
        recv_sem=owner_sems.at[1],
        device_id=away("gx", 1),
        device_id_type=MESH,
    )

    inside = inner_stiffness(slab_ref)
    loads["before"].wait()
    loads["mass"].wait()
    around = outer_stiffness(1, now_copies, inside)
    for x in range(4):
        scale = slab_factor * mass_ref[8 * x : 8 * x + 8, :]
        for c in range(3):
            at = 32 * c + 8 * x
            base_ref[at : at + 8, :] = (
                2.0 * slab_ref[at : at + 8, :]
                - before_ref[at : at + 8, :]
                - scale * around[x][c]
            )

    owner_in.wait_recv()
    arrived = sum(
        owner_recv[b * n_gx : (b + 1) * n_gx].reshape(n_gx, LANES) for b in range(chips)
    )
    lines = []
    moved = pltpu.roll(arrived, 0, 1, stride=RANKS, stride_axis=0)
    for c in range(4):
        own = ((lanes16 >> 3) - rows16 - c) & 15 == 0
        line = jnp.sum(jnp.where(own, moved, F32(0.0)), axis=0, keepdims=True)
        if c:
            line = pltpu.roll(jnp.broadcast_to(line, (8, LANES)), LANES - RANKS * c, 1)[0:1]
        lines.append(line)
    goal = lines[3].astype(jnp.int32)
    goal_row, goal_lane = goal >> 7, goal & 127
    rows32 = iota((32, LANES), 0)
    spots = jnp.concatenate(
        [jnp.where(rows32 == goal_row, lines[c], F32(0.0)) for c in range(3)], axis=0
    )
    high, low = halves(spots)
    on_lane = (iota((LANES, LANES), 0) == goal_lane).astype(F32).astype(BF16)
    force = dot_rows(
        jnp.concatenate([high, low], axis=1), jnp.concatenate([on_lane, on_lane], axis=1)
    )
    force_out[...] = force
    for x in range(4):
        scale = slab_factor * mass_ref[8 * x : 8 * x + 8, :]
        for c in range(3):
            at = 32 * c + 8 * x
            step_ref[at : at + 8, :] = base_ref[at : at + 8, :] + scale * force[at : at + 8]

    step_copies = face_values(2, step_ref)
    inside = inner_stiffness(step_ref)
    around = outer_stiffness(2, step_copies, inside)
    for x in range(4):
        scale = slab_factor * mass_ref[8 * x : 8 * x + 8, :]
        for c in range(3):
            at = 32 * c + 8 * x
            slab_out[at : at + 8, :] = (
                2.0 * step_ref[at : at + 8, :]
                - slab_ref[at : at + 8, :]
                + scale * (force_out[at : at + 8, :] - around[x][c])
            )
    for copy in sent:
        copy.wait_send()
    owner_in.wait_send()


def copy_out(*refs):
    sems = refs[6]
    copies = [pltpu.make_async_copy(refs[i], refs[3 + i], sems.at[i]) for i in range(3)]
    for copy in copies:
        copy.start()
    for copy in copies:
        copy.wait()


def solution(mesh):
    n_gx, n_gy, n_gz = (mesh.shape[name] for name in ("gx", "gy", "gz"))

    def on_device(
        global_now,
        global_prev,
        cycle_modes,
        wave_speed,
        inv_radius,
        theta_second,
        theta_first,
        point_dest,
        point_target,
        point_source,
        point_azimuth,
        regional_now,
        regional_prev,
        moduli,
        inv_mass,
    ):
        points = point_target.shape[1]
        big = [((192, LANES), F32)] * 2 + [((8, LANES), F32)] * 2 + [((LANES, LANES), F32)] * 2
        big += [((1, points), jnp.int32)] * 3 + [((1, points), F32)]
        big += [((96, LANES), F32)] * 2 + [((32, LANES), F32)] * 2
        scratch = [pltpu.SMEM(cycle_modes.shape, jnp.int32)]
        scratch += [pltpu.VMEM(shape, dtype) for shape, dtype in big]
        scratch += [
            pltpu.VMEM((192, LANES), F32),
            pltpu.VMEM((192, LANES), F32),
            pltpu.VMEM((2 * LANES, 2 * LANES), BF16),
            pltpu.VMEM((2 * LANES, 2 * LANES), BF16),
            pltpu.VMEM((2 * LANES, points), BF16),
            pltpu.VMEM((8, 8, points), F32),
            pltpu.VMEM((LANES, points), BF16),
            pltpu.VMEM((8, LANES), F32),
            pltpu.VMEM((96, LANES), F32),
            pltpu.VMEM((96, LANES), F32),
            pltpu.VMEM((9, 4, 8, LANES), F32),
            pltpu.VMEM((9, 4, 8, LANES), F32),
            pltpu.VMEM((20, 8, LANES), F32),
            pltpu.VMEM((4, 8, LANES), F32),
            pltpu.VMEM((4, 8, LANES), F32),
            pltpu.VMEM((96, LANES), F32),
            pltpu.VMEM((96, LANES), F32),
            pltpu.VMEM((2, 56, LANES), F32),
            pltpu.VMEM((2, 56, LANES), F32),
            pltpu.VMEM((3, 2, 3, 8, LANES), F32),
            pltpu.VMEM((3, 2, 3, 8, LANES), F32),
            pltpu.VMEM((3, 2, 16, LANES), F32),
            pltpu.VMEM((3, 2, 16, LANES), F32),
            pltpu.VMEM((3, 2, 8, LANES), F32),
            pltpu.VMEM((3, 2, 8, LANES), F32),
            pltpu.VMEM((2, 8 * max(1, n_gy // 4), LANES), F32),
            pltpu.VMEM((8 * max(1, n_gy // 4), LANES), F32),
            pltpu.VMEM((n_gy // 2, n_gx, 1, LANES), F32),
            pltpu.VMEM((n_gy // 2 * n_gx, 1, LANES), F32),
            pltpu.SemaphoreType.DMA((15,)),
            pltpu.SemaphoreType.DMA((2, 2)),
            pltpu.SemaphoreType.DMA((2, 3, 6)),
            pltpu.SemaphoreType.DMA((2,)),
            pltpu.SemaphoreType.DMA((2,)),
            pltpu.SemaphoreType.REGULAR((5,)),
        ]
        hbm = pl.BlockSpec(memory_space=pl.ANY)
        two, slab, force = pl.pallas_call(
            functools.partial(kernel, (n_gx, n_gy, n_gz)),
            out_shape=[
                pltpu.VMEM((192, LANES), F32),
                pltpu.VMEM((96, LANES), F32),
                pltpu.VMEM((96, LANES), F32),
            ],
            in_specs=[hbm] * 15,
            out_specs=[pl.BlockSpec(memory_space=pltpu.VMEM)] * 3,
            scratch_shapes=scratch,
            compiler_params=pltpu.CompilerParams(
                collective_id=0, has_side_effects=True, vmem_limit_bytes=48 * 2**20
            ),
        )(
            *[
                pltpu.with_memory_space_constraint(x, pltpu.HBM)
                for x in (
            cycle_modes,
            global_now.reshape(192, LANES),
            global_prev.reshape(192, LANES),
            wave_speed,
            inv_radius,
            theta_second,
            theta_first,
            point_dest.reshape(1, points),
            point_target,
            point_source,
            point_azimuth,
            regional_now.reshape(96, LANES),
            regional_prev.reshape(96, LANES),
            moduli.reshape(32, LANES),
            inv_mass.reshape(32, LANES),
            )]
        )
        two, slab, force = pl.pallas_call(
            copy_out,
            out_shape=[
                pltpu.HBM((192, LANES), F32),
                pltpu.HBM((96, LANES), F32),
                pltpu.HBM((96, LANES), F32),
            ],
            in_specs=[hbm] * 3,
            out_specs=[hbm] * 3,
            scratch_shapes=[pltpu.SemaphoreType.DMA((3,))],
        )(*[pltpu.with_memory_space_constraint(x, pltpu.VMEM) for x in (two, slab, force)])
        return (
            two.reshape(global_now.shape),
            slab.reshape(regional_now.shape),
            force.reshape(regional_now.shape),
        )

    return jax.shard_map(
        on_device,
        mesh=mesh,
        in_specs=(
            P("gy", None, "gx", None),
            P("gy", None, "gx", None),
            P("gx"),
            P("gx", None),
            P("gx", None),
            P(),
            P(),
            P("gz", "gx", None),
            P("gz", "gx"),
            P("gz", "gx"),
            P("gz", "gx"),
            P(None, "gx", "gy", "gz"),
            P(None, "gx", "gy", "gz"),
            P("gx", "gy", "gz"),
            P("gx", "gy", "gz"),
        ),
        out_specs=(P("gy", None, "gx", None), P(None, "gx", "gy", "gz"), P(None, "gx", "gy", "gz")),
        check_vma=False,
    )
```

```python
import functools
import math

import jax
import jax.numpy as jnp
import numpy as np
from jax import lax
from jax.experimental import pallas as pl
from jax.experimental.pallas import tpu as pltpu
from jax.sharding import PartitionSpec as P

F32 = jnp.float32
BF16 = jnp.bfloat16
MESH = pl.DeviceIdType.MESH

time_step = 0.3
time_sq = 0.09
impedance = 0.5
coupling = 0.05
slab_factor = 0.04

LANES = 128
RANKS = 8


def gll_products():
    nodes = np.array([-1.0, -math.sqrt(3.0 / 7.0), 0.0, math.sqrt(3.0 / 7.0), 1.0])
    weights = np.array([0.1, 49.0 / 90.0, 32.0 / 45.0, 49.0 / 90.0, 0.1])
    factor = np.array(
        [np.prod([nodes[i] - nodes[k] for k in range(5) if k != i]) for i in range(5)]
    )
    deriv = np.zeros((5, 5))
    for i in range(5):
        for j in range(5):
            if i != j:
                deriv[i, j] = factor[i] / factor[j] / (nodes[i] - nodes[j])
            else:
                deriv[i, j] = sum((1.0 / (nodes[i] - nodes[k]) for k in range(5) if k != i))
    return weights, np.einsum("ki,k,kj->kij", deriv, weights, deriv)


WEIGHTS, GRAM = gll_products()


def cosine_series():
    f = np.cos(np.linspace(0.0, np.pi / 2, 2001)) * 0.5
    fit = np.polynomial.chebyshev.Chebyshev.fit(f * f, np.cos(2 * np.pi * f), 8, domain=[0, 0.25])
    return [float(v) for v in fit.convert(kind=np.polynomial.Polynomial).coef]


COSINE = cosine_series()


def halves(x):
    high = x.astype(BF16)
    return high, (x - high.astype(F32)).astype(BF16)


def dot(a, b):
    return lax.dot_general(a, b, (((1,), (0,)), ((), ())), preferred_element_type=F32)


def dot_rows(a, b):
    return lax.dot_general(a, b, (((1,), (1,)), ((), ())), preferred_element_type=F32)


def operator_pair(t):
    high, low = halves(t)
    top = jnp.concatenate([high, low], axis=1)
    bottom = jnp.concatenate([high, jnp.zeros_like(low)], axis=1)
    return jnp.concatenate([top, bottom], axis=0)


def times_operator(x, pair_ref):
    high, low = halves(x)
    both = dot(jnp.concatenate([high, low], axis=1), pair_ref[...])
    return both[:, :LANES] + both[:, LANES:]


def iota(shape, axis):
    return lax.broadcasted_iota(jnp.int32, shape, axis)


def by_four(phase, values):
    out = jnp.full(phase.shape, values[3], F32)
    for i in (2, 1, 0):
        out = jnp.where(phase == i, F32(values[i]), out)
    return out


def kernel(
    sizes,
    modes_in,
    now_in,
    prev_in,
    speed_in,
    radius_in,
    second_in,
    first_in,
    dest_in,
    target_in,
    source_in,
    azimuth_in,
    slab_in,
    before_in,
    moduli_in,
    mass_in,
    g_out,
    slab_out,
    force_out,
    modes_ref,
    now_ref,
    prev_ref,
    speed_ref,
    radius_ref,
    second_ref,
    first_ref,
    dest_ref,
    target_ref,
    source_ref,
    azimuth_ref,
    slab_ref,
    before_ref,
    moduli_ref,
    mass_ref,
    one_ref,
    edge_ref,
    pair_second,
    pair_first,
    pick_ref,
    trig_ref,
    slot_ref,
    mark_ref,
    base_ref,
    step_ref,
    band_z,
    band_y,
    band_x,
    over_z,
    over_y,
    spread_ref,
    part_ref,
    cycle_send,
    cycle_recv,
    x_send,
    x_recv,
    y_send,
    y_recv,
    z_send,
    z_recv,
    group_send,
    group_recv,
    owner_send,
    owner_recv,
    in_sem,
    cycle_sems,
    face_sems,
    group_sems,
    owner_sems,
    ring_sems,
):
    n_gx, n_gy, n_gz = sizes
    gx, gy, gz = lax.axis_index("gx"), lax.axis_index("gy"), lax.axis_index("gz")
    points = dest_ref.shape[1]
    core, chip = lax.rem(gy, 2), lax.div(gy, 2)
    chips = n_gy // 2

    def away(axis, step):
        index, count = {"gx": (gx, n_gx), "gy": (gy, n_gy), "gz": (gz, n_gz)}[axis]
        return {axis: lax.rem(index + step + count, count)}

    barrier = pltpu.get_barrier_semaphore()
    for step in range(1, n_gy):
        pl.semaphore_signal(barrier, inc=1, device_id=away("gy", step), device_id_type=MESH)
    there = {
        ("gx", -1): gx > 0,
        ("gx", 1): gx < n_gx - 1,
        ("gy", -1): gy > 0,
        ("gy", 1): gy < n_gy - 1,
        ("gz", -1): gz > 0,
        ("gz", 1): gz < n_gz - 1,
    }
    greeted = n_gy - 1 + chips * len({1, n_gx - 1})
    for step in sorted({1, n_gx - 1}):
        for b in range(chips):
            pl.semaphore_signal(
                barrier,
                inc=1,
                device_id={
                    "gx": away("gx", step)["gx"],
                    "gy": 2 * lax.rem(chip + b, chips) + core,
                },
                device_id_type=MESH,
            )
    for step in (-1, 1):
        greeted = greeted + there["gz", step].astype(jnp.int32)

        @pl.when(there["gz", step])
        def _(step=step):
            pl.semaphore_signal(
                barrier, inc=1, device_id=away("gz", step), device_id_type=MESH
            )

    loads = {}
    for number, (name, src, dst) in enumerate(
        (
            ("modes", modes_in, modes_ref),
            ("now", now_in, now_ref),
            ("prev", prev_in, prev_ref),
            ("speed", speed_in, speed_ref),
            ("radius", radius_in, radius_ref),
            ("moduli", moduli_in, moduli_ref),
            ("second", second_in, second_ref),
            ("dest", dest_in, dest_ref),
            ("target", target_in, target_ref),
            ("source", source_in, source_ref),
            ("azimuth", azimuth_in, azimuth_ref),
            ("first", first_in, first_ref),
            ("slab", slab_in, slab_ref),
            ("before", before_in, before_ref),
            ("mass", mass_in, mass_ref),
        )
    ):
        loads[name] = pltpu.make_async_copy(src, dst, in_sem.at[number])
        loads[name].start()

    def push(src, dst, sems, index, device):
        copy = pltpu.make_async_remote_copy(
            src_ref=src,
            dst_ref=dst,
            send_sem=sems.at[(0, *index)],
            recv_sem=sems.at[(1, *index)],
            device_id=device,
            device_id_type=MESH,
        )
        copy.start()
        return copy

    class Neighbour:
        def __init__(self, src, dst, sems, index, axis, step):
            self.copy = pltpu.make_async_remote_copy(
                src_ref=src,
                dst_ref=dst,
                send_sem=sems.at[(0, *index)],
                recv_sem=sems.at[(1, *index)],
                device_id=away(axis, step),
                device_id_type=MESH,
            )
            self.sends, self.receives = there[axis, step], there[axis, -step]
            pl.when(self.sends)(lambda: self.copy.start())

        def wait_recv(self):
            pl.when(self.receives)(lambda: self.copy.wait_recv())

        def wait_send(self):
            pl.when(self.sends)(lambda: self.copy.wait_send())

    for (axis, step), here in there.items():

        @pl.when(jnp.logical_not(here))
        def _(axis=axis, side=(1 - step) // 2):
            if axis == "gx":
                cycle_recv[side] = jnp.zeros(cycle_recv.shape[1:], F32)
                x_recv[:, side] = jnp.zeros((3, 3, 8, LANES), F32)
            elif axis == "gy":
                y_recv[:, side] = jnp.zeros((3, 16, LANES), F32)
            else:
                z_recv[:, side] = jnp.zeros((3, 8, LANES), F32)

    sub = iota((8, LANES), 0)
    lane = iota((8, LANES), 1)

    mode_base = (4 * gy).astype(F32)
    row24 = iota((24, LANES), 0)
    order24 = mode_base + (
        (row24 >= 6).astype(F32) + (row24 >= 12).astype(F32) + (row24 >= 18).astype(F32)
    )
    square24 = order24 * order24
    for name in ("modes", "now", "prev", "speed", "radius"):
        loads[name].wait()
    for side, (edge, inner) in enumerate(((0, 1), (7, 6))):
        count = modes_ref[edge].astype(F32)
        mask = jnp.where(order24 < count, F32(1.0), F32(0.0))
        speed = speed_ref[edge : edge + 1, :]
        radius = radius_ref[edge : edge + 1, :]
        at_edge = now_ref[pl.ds(edge, 24, stride=8), :]
        cycle_send[side, 0:24, :] = at_edge
        cycle_send[side, 24:48, :] = mask * (
            (2.0 - 2.0 * time_sq * speed - time_sq * square24 * radius) * at_edge
            - prev_ref[pl.ds(edge, 24, stride=8), :]
            + time_sq * speed * now_ref[pl.ds(inner, 24, stride=8), :]
        )
        cycle_send[side, 48:56, :] = jnp.where(
            sub == 0, jnp.broadcast_to(speed, (8, LANES)), jnp.full((8, LANES), count, F32)
        )

    pl.semaphore_wait(barrier, greeted)

    reaches, known = [], 1
    while known < n_gx // 2:
        reaches.append(min(known, n_gx // 2 - known))
        known += reaches[-1]

    def tell(level):
        for step in (reaches[level], -reaches[level]):
            pl.semaphore_signal(
                ring_sems.at[level], inc=1, device_id=away("gx", step), device_id_type=MESH
            )

    def hear(level):
        pl.semaphore_wait(ring_sems.at[level], 2)

    def advance(level):
        if level < len(reaches):
            hear(level)
        if level + 1 < len(reaches):
            tell(level + 1)

    told_last = min(10, n_gx - 1)

    def hear_below():
        pl.semaphore_wait(ring_sems.at[4], 1)

    def pass_on(first, last):
        @pl.when((gx >= first) & (gx <= min(last, told_last - 1)))
        def _():
            pl.when(gx >= 2)(hear_below)
            pl.semaphore_signal(
                ring_sems.at[4], inc=1, device_id=away("gx", 1), device_id_type=MESH
            )

    tell(0)
    pass_on(1, 4)
    sent = []
    cycle_in = []
    for side, step in ((0, -1), (1, 1)):
        copy = Neighbour(
            cycle_send.at[side], cycle_recv.at[side], cycle_sems, (side,), "gx", step
        )
        sent.append(copy)
        cycle_in.append(copy)

    last_x = jnp.where(gx < n_gx - 1, F32(1.0), F32(0.0))
    last_y = jnp.where(gy < n_gy - 1, F32(1.0), F32(0.0))
    last_z = jnp.where(gz < n_gz - 1, F32(1.0), F32(0.0))
    has_x = jnp.where(gx > 0, F32(1.0), F32(0.0))
    has_y = jnp.where(gy > 0, F32(1.0), F32(0.0))
    has_z = jnp.where(gz > 0, F32(1.0), F32(0.0))

    def send_face(number, axis, count):
        place = ("gx", "gy", "gz").index(axis)
        out, into = ((x_send, x_recv), (y_send, y_recv), (z_send, z_recv))[place]
        copies = [
            Neighbour(
                out.at[number, side, 0:count],
                into.at[number, side, 0:count],
                face_sems,
                (number, 2 * place + side),
                axis,
                step,
            )
            for side, step in ((0, -1), (1, 1))
        ]
        sent.extend(copies)
        return copies

    def columns_to_lanes(columns):
        out = jnp.zeros((8, LANES), F32)
        for number, column in enumerate(columns):
            out = jnp.where(lane == number, jnp.broadcast_to(column, (8, LANES)), out)
        return out

    loads["moduli"].wait()
    inner = [float(GRAM[k, 4, 4]) for k in range(5)]
    mu = moduli_ref[...].reshape(4, 8, LANES)
    x_send[0, 0, 0] = mu[0]
    x_send[0, 1, 0] = last_x * (
        inner[0] * mu[0] + inner[1] * mu[1] + inner[2] * mu[2] + inner[3] * mu[3]
    )
    y_send[0, 0, 0:8] = jnp.zeros((8, LANES), F32)
    y_send[0, 1, 0:8] = jnp.zeros((8, LANES), F32)
    y_send[0, 0, 0:4] = moduli_ref[pl.ds(0, 4, stride=8), :]
    y_send[0, 1, 0:4] = last_y * sum(
        inner[k] * moduli_ref[pl.ds(4 + k, 4, stride=8), :] for k in range(4)
    )
    tail = by_four(lane & 3, inner[:4]) * jnp.where(lane >= LANES - 4, last_z, F32(0.0))
    z_send[0, 0] = columns_to_lanes([mu[x][:, 0:1] for x in range(4)])
    z_send[0, 1] = columns_to_lanes(
        [jnp.sum(tail * mu[x], axis=1, keepdims=True) for x in range(4)]
    )
    moduli_copies = [
        copy
        for axis, count in (("gy", 8), ("gz", 8), ("gx", 1))
        for copy in send_face(0, axis, count)
    ]

    pass_on(5, 7)
    advance(0)

    loads["second"].wait()
    pair_second[...] = operator_pair(second_ref[...])
    counts = jnp.zeros((8, LANES), F32)
    for row in range(8):
        counts = jnp.where(sub == row, modes_ref[row].astype(F32), counts)
    order = mode_base + iota((4, 8, LANES), 0).astype(F32)
    mask = jnp.where(order < counts[None], F32(1.0), F32(0.0))
    speed, radius = speed_ref[...][None], radius_ref[...][None]
    hold = (mask * (2.0 - 2.0 * time_sq * speed - time_sq * (order * order) * radius))[:, None]
    side_weight = (mask * (time_sq * speed))[:, None]
    bend_weight = (mask * time_sq)[:, None]
    mask = mask[:, None]

    def section_sum(now, prev):
        cells = now.reshape(24, 8, LANES)
        rows = iota((24, 8, LANES), 1)
        near = jnp.where(rows == 0, F32(0.0), pltpu.roll(cells, 1, 1)) + jnp.where(
            rows == 7, F32(0.0), pltpu.roll(cells, 7, 1)
        )
        return (
            hold * now.reshape(4, 6, 8, LANES)
            - mask * prev.reshape(4, 6, 8, LANES)
            + side_weight * near.reshape(4, 6, 8, LANES)
            + bend_weight * times_operator(now, pair_second).reshape(4, 6, 8, LANES)
        )

    one_ref[...] = section_sum(now_ref[...], prev_ref[...]).reshape(192, LANES)
    edge_ref[...] = jnp.zeros((192, LANES), F32)

    for name in ("dest", "target", "source", "azimuth"):
        loads[name].wait()
    owner = dest_ref[...]
    blocks = points // LANES
    named = (iota((LANES, points), 0) == owner).astype(F32)
    named_rows = jnp.concatenate(
        [named[:, b * LANES : (b + 1) * LANES] for b in range(blocks)], axis=0
    ).astype(BF16)
    before = (iota((LANES, LANES), 0) < iota((LANES, LANES), 1)).astype(F32)
    counted = dot(
        named_rows, jnp.concatenate([before, jnp.ones_like(before)], axis=1).astype(BF16)
    )
    ranks, offset = [], None
    for b in range(blocks):
        piece = counted[b * LANES : (b + 1) * LANES]
        place = piece[:, :LANES] if offset is None else piece[:, :LANES] + offset
        ranks.append(
            jnp.sum(named[:, b * LANES : (b + 1) * LANES] * place, axis=0, keepdims=True)
        )
        offset = piece[:, LANES:] if offset is None else offset + piece[:, LANES:]
    rank = jnp.concatenate(ranks, axis=1).astype(jnp.int32)
    if n_gy == 8:
        owner_x, owner_y = owner >> 3, owner & 7
    else:
        owner_x, owner_y = owner >> 1, owner & 1
    slot = owner_x * RANKS + rank
    slot_ref[...] = (iota((LANES, points), 0) == slot).astype(F32).astype(BF16)
    target = target_ref[...]
    sub_p = iota((8, points), 0)
    mine = owner_y == 2 * (sub_p & 3) + core
    marks = jnp.where(sub_p < 4, target >> 7, target & 127).astype(F32)
    marked = dot_rows(jnp.where(mine, marks, F32(0.0)).astype(BF16), slot_ref[...])
    mark_ref[0:4, :] = (128.0 / chips) * marked[0:4] + (1.0 / chips) * marked[4:8]
    source = source_ref[...]
    picked = (iota((LANES, points), 0) == (source & 127)).astype(F32).astype(BF16)
    pick_ref[0:LANES, :] = picked
    pick_ref[LANES:, :] = picked
    turns = (mode_base + (sub_p & 3).astype(F32)) * (azimuth_ref[...] * (0.5 / math.pi))
    turns = turns - jnp.where(sub_p >= 4, F32(0.25), F32(0.0))
    turns = turns - jnp.floor(turns + 0.5)
    square = turns * turns
    wave = jnp.full(square.shape, COSINE[-1], F32)
    for value in COSINE[-2::-1]:
        wave = wave * square + value
    in_cycle = sub_p == (source >> 7)
    for row in range(8):
        trig_ref[row] = jnp.where(
            in_cycle, jnp.broadcast_to(wave[row : row + 1], (8, points)), F32(0.0)
        )
    loads["first"].wait()
    pair_first[...] = operator_pair(first_ref[...])

    advance(1)
    pass_on(8, 8)

    for copy in cycle_in:
        copy.wait_recv()
    flags = (last_x, has_x)
    near_edges = [cycle_recv[side, 0:24, :] for side in range(2)]
    bends = times_operator(jnp.concatenate(near_edges, axis=0), pair_second)
    beyond = []
    for side, edge in ((0, 7), (1, 0)):
        tail_rows = cycle_recv[side, 48:56, :]
        speed24 = tail_rows[0:1]
        mask24 = jnp.where(order24 < tail_rows[1:2], F32(1.0), F32(0.0))
        edge_ref[pl.ds(edge, 24, stride=8), :] = flags[side] * near_edges[side]
        value = cycle_recv[side, 24:48, :] + mask24 * time_sq * (
            speed24 * now_ref[pl.ds(edge, 24, stride=8), :] + bends[24 * side : 24 * side + 24]
        )
        beyond.append(flags[side] * value)
    one = one_ref[...].reshape(4, 6, 8, LANES) + side_weight * edge_ref[...].reshape(
        4, 6, 8, LANES
    )
    one = one.reshape(192, LANES)
    for side, edge in ((0, 7), (1, 0)):
        edge_ref[pl.ds(edge, 24, stride=8), :] = beyond[side]
    two = section_sum(one, now_ref[...]) + side_weight * edge_ref[...].reshape(4, 6, 8, LANES)
    two = two.reshape(192, LANES)
    g_out[...] = two

    coef = coupling * times_operator(two, pair_first) + (coupling * impedance / time_step) * (
        two - one
    )
    high, low = halves(coef)
    at_points = dot(jnp.concatenate([high, low], axis=1), pick_ref[...]).reshape(
        4, 6, 8, points
    )
    values = jnp.zeros((8, points), F32)
    for c in range(3):
        total = jnp.zeros((8, points), F32)
        for m in range(4):
            total = total + at_points[m, 2 * c] * trig_ref[m]
            total = total + at_points[m, 2 * c + 1] * trig_ref[4 + m]
        values = jnp.where(
            (sub_p & 3) == c,
            jnp.broadcast_to(jnp.sum(total, axis=0, keepdims=True), (8, points)),
            values,
        )
    half = 8 * max(1, chips // 2)
    by_group = jnp.concatenate(
        [
            jnp.where(owner_y == 2 * (2 * tile + (sub_p >> 2)) + side, values, F32(0.0))
            for side in range(2)
            for tile in range(half // 8)
        ],
        axis=0,
    )
    high, low = halves(by_group)
    packed = dot_rows(jnp.concatenate([high, low], axis=0), slot_ref[...])
    packed = packed[: 2 * half] + packed[2 * half :]
    for side in range(2):
        group_send[side] = packed[half * side : half * side + half]
    pair = push(
        group_send.at[1 - core], group_recv, group_sems, (), {"gy": gy + 1 - 2 * core}
    )
    sent.append(pair)

    pair.wait_recv()
    total = group_send[core] + group_recv[...]
    rows16 = iota((n_gx, LANES), 0)
    lanes16 = iota((n_gx, LANES), 1)
    for place in range(chips):
        outgoing = jnp.zeros((n_gx, LANES), F32)
        for c in range(4):
            at = 4 * place + c
            line = total[at : at + 1] if c < 3 else mark_ref[place : place + 1]
            line = jnp.broadcast_to(line, (8, LANES))
            if (RANKS * (c + 1 - n_gx)) % LANES:
                line = pltpu.roll(line, (RANKS * (c + 1 - n_gx)) % LANES, 1)
            moved = pltpu.roll(
                jnp.broadcast_to(line[0:1], (n_gx, LANES)), 0, 1, stride=RANKS, stride_axis=0
            )
            outgoing = jnp.where(lanes16 >> 3 == c, moved, outgoing)
        owner_send[place] = outgoing.reshape(n_gx, 1, LANES)

    def to_row(a, first=0):
        peer_x = lax.rem(gx + a, n_gx)
        for b in range(first, chips):
            peer_chip = lax.rem(chip + b, chips)
            pltpu.make_async_remote_copy(
                src_ref=owner_send.at[peer_chip, n_gx - 1 - peer_x],
                dst_ref=owner_recv.at[b * n_gx + a],
                send_sem=owner_sems.at[0],
                recv_sem=owner_sems.at[1],
                device_id={"gx": peer_x, "gy": 2 * peer_chip + core},
                device_id_type=MESH,
            ).start()

    def far_first(first, last, when=None):
        def body(number, carry):
            away_by = (number + 1) // 2
            a = n_gx // 2 + jnp.where(number % 2 == 1, -away_by, away_by)
            if when is None:
                to_row(a)
            else:
                pl.when(when(a))(lambda: to_row(a))
            return carry

        lax.fori_loop(first, last, body, 0)

    pass_on(9, 9)
    pl.when(gx == told_last)(hear_below)
    chained = (gx >= min(8, told_last)) & (gx <= told_last)

    def below(a):
        return chained & (gx + a >= n_gx)

    def others(a):
        return jnp.logical_not(below(a))

    near = n_gx // 2 - 1 if n_gx > 8 else 0
    pl.when(chained)(lambda: far_first(0, near, below))
    far_first(near, n_gx - 1)
    to_row(0, 1)
    for copy in moduli_copies:
        copy.wait_recv()
    mu_next_x = last_x * x_recv[0, 0, 0]
    sum_prev_x = x_recv[0, 1, 0]
    lane4 = iota((4, 8, LANES), 2)
    sub4 = iota((4, 8, LANES), 1)
    side_w = [0.2] + [float(v) for v in WEIGHTS[1:4]]
    first_weight = -float(WEIGHTS[4])
    weight_y = by_four(sub & 3, side_w) + jnp.where(
        sub == 0, (1.0 - has_y) * first_weight, F32(0.0)
    )
    weight_z = by_four(lane & 3, side_w) + jnp.where(
        lane == 0, (1.0 - has_z) * first_weight, F32(0.0)
    )
    weight_x = [side_w[0] + (1.0 - has_x) * first_weight] + side_w[1:]

    def make_band(axis, position, count, following, preceding, weights, has, last, band, over):
        shifted = {0: mu}
        for t in range(-4, 5):
            if t:
                rolled = pltpu.roll(mu, (-t) % count, axis)
                if t > 0:
                    rolled = jnp.where(position == count - t, following, rolled)
                shifted[t] = rolled
        pos2 = position[0]
        phase = pos2 & 3
        later = pos2 > 3
        band_values = []
        for s in range(5):
            total = None
            for t in range(s - 4, 5):
                row = [
                    GRAM[i + t, i, i + s] if 0 <= i + t <= 4 and i + s <= 4 else 0.0
                    for i in range(4)
                ]
                pattern = by_four(phase, row)
                if s == 0 and t <= 0:
                    pattern = pattern + jnp.where(
                        (phase == 0) & later, F32(GRAM[4 + t, 4, 4]), F32(0.0)
                    )
                term = pattern[None] * shifted[t]
                total = term if total is None else total + term
            if s == 0:
                total = total + jnp.where(
                    position == 0, preceding + has * float(GRAM[4, 4, 4]) * mu, F32(0.0)
                )
            band_values.append(total * weights)
        crossing = jnp.zeros_like(mu)
        for s in range(1, 5):
            crossing = jnp.where(position == count - s, band_values[s], crossing)
            inside = jnp.where(position >= count - s, F32(0.0), band_values[s])
            behind = pltpu.roll(inside, s, axis)
            if 2 * s == count:
                band[s] = inside + behind
                band[4 + s] = jnp.zeros_like(inside)
            else:
                band[s] = inside
                band[4 + s] = behind
        over[...] = last * crossing
        band[0] = band_values[0]

    y_next = y_recv[0, 0, 0:8]
    y_prev = y_recv[0, 1, 0:8]
    z_next = z_recv[0, 0]
    z_prev = z_recv[0, 1]

    def rows_of(value):
        return jnp.concatenate(
            [jnp.broadcast_to(value[x : x + 1], (8, LANES))[None] for x in range(4)], axis=0
        )

    def columns_of(value):
        return jnp.concatenate(
            [jnp.broadcast_to(value[:, x : x + 1], (8, LANES))[None] for x in range(4)], axis=0
        )

    stacked = lambda scale: jnp.concatenate([(scale(x))[None] for x in range(4)], axis=0)
    make_band(
        2,
        lane4,
        LANES,
        last_z * columns_of(z_next),
        columns_of(z_prev),
        stacked(lambda x: weight_x[x] * weight_y),
        has_z,
        last_z,
        band_z,
        over_z,
    )
    make_band(
        1,
        sub4,
        8,
        last_y * rows_of(y_next),
        rows_of(y_prev),
        stacked(lambda x: weight_x[x] * weight_z),
        has_y,
        last_y,
        band_y,
        over_y,
    )
    weight_yz = weight_y * weight_z
    planes = [mu[x] for x in range(4)] + [mu_next_x]
    for i in range(4):
        for j in range(i, 5):
            value = sum(float(GRAM[k, i, j]) * planes[k] for k in range(5))
            if i == 0 and j == 0:
                value = value + sum_prev_x + has_x * float(GRAM[4, 4, 4]) * mu[0]
            if j == 4:
                value = last_x * value
            band_x[5 * i + j] = value * weight_yz
    for x in range(4):
        band_z[0, x] = band_z[0, x] + band_y[0, x] + band_x[6 * x]

    def coupling_x(i, j):
        return band_x[5 * min(i, j) + max(i, j)]

    def face_values(number, ref):
        field = ref[...].reshape(3, 4, 8, LANES)
        y_send[number, 0, 0:12] = ref[pl.ds(0, 12, stride=8), :]
        part_ref[...] = (over_y[...][None] * field).reshape(96, LANES)
        y_send[number, 1, 0:12] = sum(
            part_ref[pl.ds(4 + k, 12, stride=8), :] for k in range(4)
        )
        copies = send_face(number, "gy", 16)
        for c in range(3):
            x_send[number, 0, c] = field[c, 0]
            x_send[number, 1, c] = sum(coupling_x(i, 4) * field[c, i] for i in range(4))
        copies += send_face(number, "gx", 3)
        z_send[number, 0] = columns_to_lanes(
            [field[c, x][:, 0:1] for c in range(3) for x in range(4)]
        )
        z_send[number, 1] = columns_to_lanes(
            [
                jnp.sum(over_z[x] * field[c, x], axis=1, keepdims=True)
                for c in range(3)
                for x in range(4)
            ]
        )
        return copies + send_face(number, "gz", 8)

    def inner_stiffness(ref):
        field = ref[...].reshape(3, 4, 8, LANES)
        out = []
        for x in range(4):
            plane = field[:, x]
            total = band_z[0, x] * plane
            for s in range(1, 5):
                total = total + band_z[s, x] * pltpu.roll(plane, LANES - s, 2)
                total = total + band_z[4 + s, x] * pltpu.roll(plane, s, 2)
                total = total + band_y[s, x] * pltpu.roll(plane, 8 - s, 1)
                if s < 4:
                    total = total + band_y[4 + s, x] * pltpu.roll(plane, s, 1)
            for j in range(4):
                if j != x:
                    total = total + coupling_x(x, j) * field[:, j]
            out.append(total)
        return out

    def outer_stiffness(number, copies, inside):
        for copy in copies:
            copy.wait_recv()
        y_first = y_recv[number, 1, 0:12]
        y_after = y_recv[number, 0, 0:12]
        spread_ref[pl.ds(0, 12, stride=8), :] = y_first
        for k in range(4):
            spread_ref[pl.ds(4 + k, 12, stride=8), :] = y_after
        spread = spread_ref[...].reshape(3, 4, 8, LANES)
        z_first, z_after = z_recv[number, 1], z_recv[number, 0]
        x_after, x_first = x_recv[number, 0], x_recv[number, 1]
        out = []
        for x in range(4):
            rows = []
            for c in range(3):
                at = 4 * c + x
                row = inside[x][c] + coupling_x(x, 4) * x_after[c]
                row = row + jnp.where(sub == 0, F32(1.0), over_y[x]) * spread[c, x]
                row = row + jnp.where(
                    lane == 0,
                    jnp.broadcast_to(z_first[:, at : at + 1], (8, LANES)),
                    over_z[x] * jnp.broadcast_to(z_after[:, at : at + 1], (8, LANES)),
                )
                if x == 0:
                    row = row + x_first[c]
                rows.append(row)
            out.append(rows)
        return out

    spread_ref[...] = jnp.zeros((96, LANES), F32)
    loads["slab"].wait()
    now_copies = face_values(1, slab_ref)

    for level in range(2, len(reaches)):
        advance(level)
    far_first(0, near, others)
    owner_recv[0] = owner_send[chip, n_gx - 1 - gx]
    rows_all = chips * n_gx
    owner_in = pltpu.make_async_remote_copy(
        src_ref=owner_recv.at[1:rows_all],
        dst_ref=owner_recv.at[1:rows_all],
        send_sem=owner_sems.at[0],
        recv_sem=owner_sems.at[1],
        device_id=away("gx", 1),
        device_id_type=MESH,
    )

    inside = inner_stiffness(slab_ref)
    loads["before"].wait()
    loads["mass"].wait()
    around = outer_stiffness(1, now_copies, inside)
    for x in range(4):
        scale = slab_factor * mass_ref[8 * x : 8 * x + 8, :]
        for c in range(3):
            at = 32 * c + 8 * x
            base_ref[at : at + 8, :] = (
                2.0 * slab_ref[at : at + 8, :]
                - before_ref[at : at + 8, :]
                - scale * around[x][c]
            )

    owner_in.wait_recv()
    arrived = sum(
        owner_recv[b * n_gx : (b + 1) * n_gx].reshape(n_gx, LANES) for b in range(chips)
    )
    lines = []
    moved = pltpu.roll(arrived, 0, 1, stride=RANKS, stride_axis=0)
    for c in range(4):
        own = ((lanes16 >> 3) - rows16 - c) & 15 == 0
        line = jnp.sum(jnp.where(own, moved, F32(0.0)), axis=0, keepdims=True)
        if c:
            line = pltpu.roll(jnp.broadcast_to(line, (8, LANES)), LANES - RANKS * c, 1)[0:1]
        lines.append(line)
    goal = lines[3].astype(jnp.int32)
    goal_row, goal_lane = goal >> 7, goal & 127
    rows32 = iota((32, LANES), 0)
    spots = jnp.concatenate(
        [jnp.where(rows32 == goal_row, lines[c], F32(0.0)) for c in range(3)], axis=0
    )
    high, low = halves(spots)
    on_lane = (iota((LANES, LANES), 0) == goal_lane).astype(F32).astype(BF16)
    force = dot_rows(
        jnp.concatenate([high, low], axis=1), jnp.concatenate([on_lane, on_lane], axis=1)
    )
    force_out[...] = force
    for x in range(4):
        scale = slab_factor * mass_ref[8 * x : 8 * x + 8, :]
        for c in range(3):
            at = 32 * c + 8 * x
            step_ref[at : at + 8, :] = base_ref[at : at + 8, :] + scale * force[at : at + 8]

    step_copies = face_values(2, step_ref)
    inside = inner_stiffness(step_ref)
    around = outer_stiffness(2, step_copies, inside)
    for x in range(4):
        scale = slab_factor * mass_ref[8 * x : 8 * x + 8, :]
        for c in range(3):
            at = 32 * c + 8 * x
            slab_out[at : at + 8, :] = (
                2.0 * step_ref[at : at + 8, :]
                - slab_ref[at : at + 8, :]
                + scale * (force_out[at : at + 8, :] - around[x][c])
            )
    for copy in sent:
        copy.wait_send()
    owner_in.wait_send()


def copy_out(*refs):
    sems = refs[6]
    copies = [pltpu.make_async_copy(refs[i], refs[3 + i], sems.at[i]) for i in range(3)]
    for copy in copies:
        copy.start()
    for copy in copies:
        copy.wait()


def solution(mesh):
    n_gx, n_gy, n_gz = (mesh.shape[name] for name in ("gx", "gy", "gz"))

    def on_device(
        global_now,
        global_prev,
        cycle_modes,
        wave_speed,
        inv_radius,
        theta_second,
        theta_first,
        point_dest,
        point_target,
        point_source,
        point_azimuth,
        regional_now,
        regional_prev,
        moduli,
        inv_mass,
    ):
        points = point_target.shape[1]
        big = [((192, LANES), F32)] * 2 + [((8, LANES), F32)] * 2 + [((LANES, LANES), F32)] * 2
        big += [((1, points), jnp.int32)] * 3 + [((1, points), F32)]
        big += [((96, LANES), F32)] * 2 + [((32, LANES), F32)] * 2
        scratch = [pltpu.SMEM(cycle_modes.shape, jnp.int32)]
        scratch += [pltpu.VMEM(shape, dtype) for shape, dtype in big]
        scratch += [
            pltpu.VMEM((192, LANES), F32),
            pltpu.VMEM((192, LANES), F32),
            pltpu.VMEM((2 * LANES, 2 * LANES), BF16),
            pltpu.VMEM((2 * LANES, 2 * LANES), BF16),
            pltpu.VMEM((2 * LANES, points), BF16),
            pltpu.VMEM((8, 8, points), F32),
            pltpu.VMEM((LANES, points), BF16),
            pltpu.VMEM((8, LANES), F32),
            pltpu.VMEM((96, LANES), F32),
            pltpu.VMEM((96, LANES), F32),
            pltpu.VMEM((9, 4, 8, LANES), F32),
            pltpu.VMEM((9, 4, 8, LANES), F32),
            pltpu.VMEM((20, 8, LANES), F32),
            pltpu.VMEM((4, 8, LANES), F32),
            pltpu.VMEM((4, 8, LANES), F32),
            pltpu.VMEM((96, LANES), F32),
            pltpu.VMEM((96, LANES), F32),
            pltpu.VMEM((2, 56, LANES), F32),
            pltpu.VMEM((2, 56, LANES), F32),
            pltpu.VMEM((3, 2, 3, 8, LANES), F32),
            pltpu.VMEM((3, 2, 3, 8, LANES), F32),
            pltpu.VMEM((3, 2, 16, LANES), F32),
            pltpu.VMEM((3, 2, 16, LANES), F32),
            pltpu.VMEM((3, 2, 8, LANES), F32),
            pltpu.VMEM((3, 2, 8, LANES), F32),
            pltpu.VMEM((2, 8 * max(1, n_gy // 4), LANES), F32),
            pltpu.VMEM((8 * max(1, n_gy // 4), LANES), F32),
            pltpu.VMEM((n_gy // 2, n_gx, 1, LANES), F32),
            pltpu.VMEM((n_gy // 2 * n_gx, 1, LANES), F32),
            pltpu.SemaphoreType.DMA((15,)),
            pltpu.SemaphoreType.DMA((2, 2)),
            pltpu.SemaphoreType.DMA((2, 3, 6)),
            pltpu.SemaphoreType.DMA((2,)),
            pltpu.SemaphoreType.DMA((2,)),
            pltpu.SemaphoreType.REGULAR((5,)),
        ]
        hbm = pl.BlockSpec(memory_space=pl.ANY)
        two, slab, force = pl.pallas_call(
            functools.partial(kernel, (n_gx, n_gy, n_gz)),
            out_shape=[
                pltpu.VMEM((192, LANES), F32),
                pltpu.VMEM((96, LANES), F32),
                pltpu.VMEM((96, LANES), F32),
            ],
            in_specs=[hbm] * 15,
            out_specs=[pl.BlockSpec(memory_space=pltpu.VMEM)] * 3,
            scratch_shapes=scratch,
            compiler_params=pltpu.CompilerParams(
                collective_id=0, has_side_effects=True, vmem_limit_bytes=48 * 2**20
            ),
        )(
            *[
                pltpu.with_memory_space_constraint(x, pltpu.HBM)
                for x in (
            cycle_modes,
            global_now.reshape(192, LANES),
            global_prev.reshape(192, LANES),
            wave_speed,
            inv_radius,
            theta_second,
            theta_first,
            point_dest.reshape(1, points),
            point_target,
            point_source,
            point_azimuth,
            regional_now.reshape(96, LANES),
            regional_prev.reshape(96, LANES),
            moduli.reshape(32, LANES),
            inv_mass.reshape(32, LANES),
            )]
        )
        two, slab, force = pl.pallas_call(
            copy_out,
            out_shape=[
                pltpu.HBM((192, LANES), F32),
                pltpu.HBM((96, LANES), F32),
                pltpu.HBM((96, LANES), F32),
            ],
            in_specs=[hbm] * 3,
            out_specs=[hbm] * 3,
            scratch_shapes=[pltpu.SemaphoreType.DMA((3,))],
        )(*[pltpu.with_memory_space_constraint(x, pltpu.VMEM) for x in (two, slab, force)])
        return (
            two.reshape(global_now.shape),
            slab.reshape(regional_now.shape),
            force.reshape(regional_now.shape),
        )

    return jax.shard_map(
        on_device,
        mesh=mesh,
        in_specs=(
            P("gy", None, "gx", None),
            P("gy", None, "gx", None),
            P("gx"),
            P("gx", None),
            P("gx", None),
            P(),
            P(),
            P("gz", "gx", None),
            P("gz", "gx"),
            P("gz", "gx"),
            P("gz", "gx"),
            P(None, "gx", "gy", "gz"),
            P(None, "gx", "gy", "gz"),
            P("gx", "gy", "gz"),
            P("gx", "gy", "gz"),
        ),
        out_specs=(P("gy", None, "gx", None), P(None, "gx", "gy", "gz"), P(None, "gx", "gy", "gz")),
        check_vma=False,
    )
```

```python
import functools
import math

import jax
import jax.numpy as jnp
import numpy as np
from jax import lax
from jax.experimental import pallas as pl
from jax.experimental.pallas import tpu as pltpu
from jax.sharding import PartitionSpec as P

F32 = jnp.float32
BF16 = jnp.bfloat16
MESH = pl.DeviceIdType.MESH

time_step = 0.3
time_sq = 0.09
impedance = 0.5
coupling = 0.05
slab_factor = 0.04

LANES = 128
RANKS = 8


def gll_products():
    nodes = np.array([-1.0, -math.sqrt(3.0 / 7.0), 0.0, math.sqrt(3.0 / 7.0), 1.0])
    weights = np.array([0.1, 49.0 / 90.0, 32.0 / 45.0, 49.0 / 90.0, 0.1])
    factor = np.array(
        [np.prod([nodes[i] - nodes[k] for k in range(5) if k != i]) for i in range(5)]
    )
    deriv = np.zeros((5, 5))
    for i in range(5):
        for j in range(5):
            if i != j:
                deriv[i, j] = factor[i] / factor[j] / (nodes[i] - nodes[j])
            else:
                deriv[i, j] = sum((1.0 / (nodes[i] - nodes[k]) for k in range(5) if k != i))
    return weights, np.einsum("ki,k,kj->kij", deriv, weights, deriv)


WEIGHTS, GRAM = gll_products()


def cosine_series():
    f = np.cos(np.linspace(0.0, np.pi / 2, 2001)) * 0.5
    fit = np.polynomial.chebyshev.Chebyshev.fit(f * f, np.cos(2 * np.pi * f), 8, domain=[0, 0.25])
    return [float(v) for v in fit.convert(kind=np.polynomial.Polynomial).coef]


COSINE = cosine_series()


def halves(x):
    high = x.astype(BF16)
    return high, (x - high.astype(F32)).astype(BF16)


def dot(a, b):
    return lax.dot_general(a, b, (((1,), (0,)), ((), ())), preferred_element_type=F32)


def dot_rows(a, b):
    return lax.dot_general(a, b, (((1,), (1,)), ((), ())), preferred_element_type=F32)


def operator_pair(t):
    high, low = halves(t)
    top = jnp.concatenate([high, low], axis=1)
    bottom = jnp.concatenate([high, jnp.zeros_like(low)], axis=1)
    return jnp.concatenate([top, bottom], axis=0)


def times_operator(x, pair_ref):
    high, low = halves(x)
    both = dot(jnp.concatenate([high, low], axis=1), pair_ref[...])
    return both[:, :LANES] + both[:, LANES:]


def iota(shape, axis):
    return lax.broadcasted_iota(jnp.int32, shape, axis)


def by_four(phase, values):
    out = jnp.full(phase.shape, values[3], F32)
    for i in (2, 1, 0):
        out = jnp.where(phase == i, F32(values[i]), out)
    return out


def kernel(
    sizes,
    modes_in,
    now_in,
    prev_in,
    speed_in,
    radius_in,
    second_in,
    first_in,
    dest_in,
    target_in,
    source_in,
    azimuth_in,
    slab_in,
    before_in,
    moduli_in,
    mass_in,
    g_out,
    slab_out,
    force_out,
    modes_ref,
    now_ref,
    prev_ref,
    speed_ref,
    radius_ref,
    second_ref,
    first_ref,
    dest_ref,
    target_ref,
    source_ref,
    azimuth_ref,
    slab_ref,
    before_ref,
    moduli_ref,
    mass_ref,
    one_ref,
    edge_ref,
    pair_second,
    pair_first,
    pick_ref,
    trig_ref,
    slot_ref,
    mark_ref,
    base_ref,
    step_ref,
    band_z,
    band_y,
    band_x,
    over_z,
    over_y,
    spread_ref,
    part_ref,
    cycle_send,
    cycle_recv,
    x_send,
    x_recv,
    y_send,
    y_recv,
    z_send,
    z_recv,
    group_send,
    group_recv,
    owner_send,
    owner_recv,
    in_sem,
    cycle_sems,
    face_sems,
    group_sems,
    owner_sems,
    ring_sems,
):
    n_gx, n_gy, n_gz = sizes
    gx, gy, gz = lax.axis_index("gx"), lax.axis_index("gy"), lax.axis_index("gz")
    points = dest_ref.shape[1]
    core, chip = lax.rem(gy, 2), lax.div(gy, 2)
    chips = n_gy // 2

    def away(axis, step):
        index, count = {"gx": (gx, n_gx), "gy": (gy, n_gy), "gz": (gz, n_gz)}[axis]
        return {axis: lax.rem(index + step + count, count)}

    barrier = pltpu.get_barrier_semaphore()
    for step in range(1, n_gy):
        pl.semaphore_signal(barrier, inc=1, device_id=away("gy", step), device_id_type=MESH)
    there = {
        ("gx", -1): gx > 0,
        ("gx", 1): gx < n_gx - 1,
        ("gy", -1): gy > 0,
        ("gy", 1): gy < n_gy - 1,
        ("gz", -1): gz > 0,
        ("gz", 1): gz < n_gz - 1,
    }
    greeted = n_gy - 1 + chips * len({1, n_gx - 1})
    for step in sorted({1, n_gx - 1}):
        for b in range(chips):
            pl.semaphore_signal(
                barrier,
                inc=1,
                device_id={
                    "gx": away("gx", step)["gx"],
                    "gy": 2 * lax.rem(chip + b, chips) + core,
                },
                device_id_type=MESH,
            )
    for step in (-1, 1):
        greeted = greeted + there["gz", step].astype(jnp.int32)

        @pl.when(there["gz", step])
        def _(step=step):
            pl.semaphore_signal(
                barrier, inc=1, device_id=away("gz", step), device_id_type=MESH
            )

    loads = {}
    for number, (name, src, dst) in enumerate(
        (
            ("modes", modes_in, modes_ref),
            ("now", now_in, now_ref),
            ("prev", prev_in, prev_ref),
            ("speed", speed_in, speed_ref),
            ("radius", radius_in, radius_ref),
            ("moduli", moduli_in, moduli_ref),
            ("second", second_in, second_ref),
            ("dest", dest_in, dest_ref),
            ("target", target_in, target_ref),
            ("source", source_in, source_ref),
            ("azimuth", azimuth_in, azimuth_ref),
            ("first", first_in, first_ref),
            ("slab", slab_in, slab_ref),
            ("before", before_in, before_ref),
            ("mass", mass_in, mass_ref),
        )
    ):
        loads[name] = pltpu.make_async_copy(src, dst, in_sem.at[number])
        loads[name].start()

    def push(src, dst, sems, index, device):
        copy = pltpu.make_async_remote_copy(
            src_ref=src,
            dst_ref=dst,
            send_sem=sems.at[(0, *index)],
            recv_sem=sems.at[(1, *index)],
            device_id=device,
            device_id_type=MESH,
        )
        copy.start()
        return copy

    class Neighbour:
        def __init__(self, src, dst, sems, index, axis, step):
            self.copy = pltpu.make_async_remote_copy(
                src_ref=src,
                dst_ref=dst,
                send_sem=sems.at[(0, *index)],
                recv_sem=sems.at[(1, *index)],
                device_id=away(axis, step),
                device_id_type=MESH,
            )
            self.sends, self.receives = there[axis, step], there[axis, -step]
            pl.when(self.sends)(lambda: self.copy.start())

        def wait_recv(self):
            pl.when(self.receives)(lambda: self.copy.wait_recv())

        def wait_send(self):
            pl.when(self.sends)(lambda: self.copy.wait_send())

    for (axis, step), here in there.items():

        @pl.when(jnp.logical_not(here))
        def _(axis=axis, side=(1 - step) // 2):
            if axis == "gx":
                cycle_recv[side] = jnp.zeros(cycle_recv.shape[1:], F32)
                x_recv[:, side] = jnp.zeros((3, 3, 8, LANES), F32)
            elif axis == "gy":
                y_recv[:, side] = jnp.zeros((3, 16, LANES), F32)
            else:
                z_recv[:, side] = jnp.zeros((3, 8, LANES), F32)

    sub = iota((8, LANES), 0)
    lane = iota((8, LANES), 1)

    mode_base = (4 * gy).astype(F32)
    row24 = iota((24, LANES), 0)
    order24 = mode_base + (
        (row24 >= 6).astype(F32) + (row24 >= 12).astype(F32) + (row24 >= 18).astype(F32)
    )
    square24 = order24 * order24
    for name in ("modes", "now", "prev", "speed", "radius"):
        loads[name].wait()
    for side, (edge, inner) in enumerate(((0, 1), (7, 6))):
        count = modes_ref[edge].astype(F32)
        mask = jnp.where(order24 < count, F32(1.0), F32(0.0))
        speed = speed_ref[edge : edge + 1, :]
        radius = radius_ref[edge : edge + 1, :]
        at_edge = now_ref[pl.ds(edge, 24, stride=8), :]
        cycle_send[side, 0:24, :] = at_edge
        cycle_send[side, 24:48, :] = mask * (
            (2.0 - 2.0 * time_sq * speed - time_sq * square24 * radius) * at_edge
            - prev_ref[pl.ds(edge, 24, stride=8), :]
            + time_sq * speed * now_ref[pl.ds(inner, 24, stride=8), :]
        )
        cycle_send[side, 48:56, :] = jnp.where(
            sub == 0, jnp.broadcast_to(speed, (8, LANES)), jnp.full((8, LANES), count, F32)
        )

    pl.semaphore_wait(barrier, greeted)

    reaches, known = [], 1
    while known < n_gx // 2:
        reaches.append(min(known, n_gx // 2 - known))
        known += reaches[-1]

    def tell(level):
        for step in (reaches[level], -reaches[level]):
            pl.semaphore_signal(
                ring_sems.at[level], inc=1, device_id=away("gx", step), device_id_type=MESH
            )

    def hear(level):
        pl.semaphore_wait(ring_sems.at[level], 2)

    def advance(level):
        if level < len(reaches):
            hear(level)
        if level + 1 < len(reaches):
            tell(level + 1)

    told_last = min(10, n_gx - 1)

    def hear_below():
        pl.semaphore_wait(ring_sems.at[4], 1)

    def pass_on(first, last):
        @pl.when((gx >= first) & (gx <= min(last, told_last - 1)))
        def _():
            pl.when(gx >= 2)(hear_below)
            pl.semaphore_signal(
                ring_sems.at[4], inc=1, device_id=away("gx", 1), device_id_type=MESH
            )

    tell(0)
    pass_on(1, 4)
    sent = []
    cycle_in = []
    for side, step in ((0, -1), (1, 1)):
        copy = Neighbour(
            cycle_send.at[side], cycle_recv.at[side], cycle_sems, (side,), "gx", step
        )
        sent.append(copy)
        cycle_in.append(copy)

    last_x = jnp.where(gx < n_gx - 1, F32(1.0), F32(0.0))
    last_y = jnp.where(gy < n_gy - 1, F32(1.0), F32(0.0))
    last_z = jnp.where(gz < n_gz - 1, F32(1.0), F32(0.0))
    has_x = jnp.where(gx > 0, F32(1.0), F32(0.0))
    has_y = jnp.where(gy > 0, F32(1.0), F32(0.0))
    has_z = jnp.where(gz > 0, F32(1.0), F32(0.0))

    def send_face(number, axis, count):
        place = ("gx", "gy", "gz").index(axis)
        out, into = ((x_send, x_recv), (y_send, y_recv), (z_send, z_recv))[place]
        copies = [
            Neighbour(
                out.at[number, side, 0:count],
                into.at[number, side, 0:count],
                face_sems,
                (number, 2 * place + side),
                axis,
                step,
            )
            for side, step in ((0, -1), (1, 1))
        ]
        sent.extend(copies)
        return copies

    def columns_to_lanes(columns):
        out = jnp.zeros((8, LANES), F32)
        for number, column in enumerate(columns):
            out = jnp.where(lane == number, jnp.broadcast_to(column, (8, LANES)), out)
        return out

    loads["moduli"].wait()
    inner = [float(GRAM[k, 4, 4]) for k in range(5)]
    mu = moduli_ref[...].reshape(4, 8, LANES)
    x_send[0, 0, 0] = mu[0]
    x_send[0, 1, 0] = last_x * (
        inner[0] * mu[0] + inner[1] * mu[1] + inner[2] * mu[2] + inner[3] * mu[3]
    )
    y_send[0, 0, 0:8] = jnp.zeros((8, LANES), F32)
    y_send[0, 1, 0:8] = jnp.zeros((8, LANES), F32)
    y_send[0, 0, 0:4] = moduli_ref[pl.ds(0, 4, stride=8), :]
    y_send[0, 1, 0:4] = last_y * sum(
        inner[k] * moduli_ref[pl.ds(4 + k, 4, stride=8), :] for k in range(4)
    )
    tail = by_four(lane & 3, inner[:4]) * jnp.where(lane >= LANES - 4, last_z, F32(0.0))
    z_send[0, 0] = columns_to_lanes([mu[x][:, 0:1] for x in range(4)])
    z_send[0, 1] = columns_to_lanes(
        [jnp.sum(tail * mu[x], axis=1, keepdims=True) for x in range(4)]
    )
    moduli_copies = [
        copy
        for axis, count in (("gy", 8), ("gz", 8), ("gx", 1))
        for copy in send_face(0, axis, count)
    ]

    pass_on(5, 7)
    advance(0)

    loads["second"].wait()
    pair_second[...] = operator_pair(second_ref[...])
    counts = jnp.zeros((8, LANES), F32)
    for row in range(8):
        counts = jnp.where(sub == row, modes_ref[row].astype(F32), counts)
    order = mode_base + iota((4, 8, LANES), 0).astype(F32)
    mask = jnp.where(order < counts[None], F32(1.0), F32(0.0))
    speed, radius = speed_ref[...][None], radius_ref[...][None]
    hold = (mask * (2.0 - 2.0 * time_sq * speed - time_sq * (order * order) * radius))[:, None]
    side_weight = (mask * (time_sq * speed))[:, None]
    bend_weight = (mask * time_sq)[:, None]
    mask = mask[:, None]

    def section_sum(now, prev):
        cells = now.reshape(24, 8, LANES)
        rows = iota((24, 8, LANES), 1)
        near = jnp.where(rows == 0, F32(0.0), pltpu.roll(cells, 1, 1)) + jnp.where(
            rows == 7, F32(0.0), pltpu.roll(cells, 7, 1)
        )
        return (
            hold * now.reshape(4, 6, 8, LANES)
            - mask * prev.reshape(4, 6, 8, LANES)
            + side_weight * near.reshape(4, 6, 8, LANES)
            + bend_weight * times_operator(now, pair_second).reshape(4, 6, 8, LANES)
        )

    one_ref[...] = section_sum(now_ref[...], prev_ref[...]).reshape(192, LANES)
    edge_ref[...] = jnp.zeros((192, LANES), F32)

    for name in ("dest", "target", "source", "azimuth"):
        loads[name].wait()
    owner = dest_ref[...]
    blocks = points // LANES
    named = (iota((LANES, points), 0) == owner).astype(F32)
    named_rows = jnp.concatenate(
        [named[:, b * LANES : (b + 1) * LANES] for b in range(blocks)], axis=0
    ).astype(BF16)
    before = (iota((LANES, LANES), 0) < iota((LANES, LANES), 1)).astype(F32)
    counted = dot(
        named_rows, jnp.concatenate([before, jnp.ones_like(before)], axis=1).astype(BF16)
    )
    ranks, offset = [], None
    for b in range(blocks):
        piece = counted[b * LANES : (b + 1) * LANES]
        place = piece[:, :LANES] if offset is None else piece[:, :LANES] + offset
        ranks.append(
            jnp.sum(named[:, b * LANES : (b + 1) * LANES] * place, axis=0, keepdims=True)
        )
        offset = piece[:, LANES:] if offset is None else offset + piece[:, LANES:]
    rank = jnp.concatenate(ranks, axis=1).astype(jnp.int32)
    if n_gy == 8:
        owner_x, owner_y = owner >> 3, owner & 7
    else:
        owner_x, owner_y = owner >> 1, owner & 1
    slot = owner_x * RANKS + rank
    slot_ref[...] = (iota((LANES, points), 0) == slot).astype(F32).astype(BF16)
    target = target_ref[...]
    sub_p = iota((8, points), 0)
    mine = owner_y == 2 * (sub_p & 3) + core
    marks = jnp.where(sub_p < 4, target >> 7, target & 127).astype(F32)
    marked = dot_rows(jnp.where(mine, marks, F32(0.0)).astype(BF16), slot_ref[...])
    mark_ref[0:4, :] = (128.0 / chips) * marked[0:4] + (1.0 / chips) * marked[4:8]
    source = source_ref[...]
    picked = (iota((LANES, points), 0) == (source & 127)).astype(F32).astype(BF16)
    pick_ref[0:LANES, :] = picked
    pick_ref[LANES:, :] = picked
    turns = (mode_base + (sub_p & 3).astype(F32)) * (azimuth_ref[...] * (0.5 / math.pi))
    turns = turns - jnp.where(sub_p >= 4, F32(0.25), F32(0.0))
    turns = turns - jnp.floor(turns + 0.5)
    square = turns * turns
    wave = jnp.full(square.shape, COSINE[-1], F32)
    for value in COSINE[-2::-1]:
        wave = wave * square + value
    in_cycle = sub_p == (source >> 7)
    for row in range(8):
        trig_ref[row] = jnp.where(
            in_cycle, jnp.broadcast_to(wave[row : row + 1], (8, points)), F32(0.0)
        )
    loads["first"].wait()
    pair_first[...] = operator_pair(first_ref[...])

    advance(1)
    pass_on(8, 8)

    for copy in cycle_in:
        copy.wait_recv()
    flags = (last_x, has_x)
    near_edges = [cycle_recv[side, 0:24, :] for side in range(2)]
    bends = times_operator(jnp.concatenate(near_edges, axis=0), pair_second)
    beyond = []
    for side, edge in ((0, 7), (1, 0)):
        tail_rows = cycle_recv[side, 48:56, :]
        speed24 = tail_rows[0:1]
        mask24 = jnp.where(order24 < tail_rows[1:2], F32(1.0), F32(0.0))
        edge_ref[pl.ds(edge, 24, stride=8), :] = flags[side] * near_edges[side]
        value = cycle_recv[side, 24:48, :] + mask24 * time_sq * (
            speed24 * now_ref[pl.ds(edge, 24, stride=8), :] + bends[24 * side : 24 * side + 24]
        )
        beyond.append(flags[side] * value)
    one = one_ref[...].reshape(4, 6, 8, LANES) + side_weight * edge_ref[...].reshape(
        4, 6, 8, LANES
    )
    one = one.reshape(192, LANES)
    for side, edge in ((0, 7), (1, 0)):
        edge_ref[pl.ds(edge, 24, stride=8), :] = beyond[side]
    two = section_sum(one, now_ref[...]) + side_weight * edge_ref[...].reshape(4, 6, 8, LANES)
    two = two.reshape(192, LANES)
    g_out[...] = two

    coef = coupling * times_operator(two, pair_first) + (coupling * impedance / time_step) * (
        two - one
    )
    high, low = halves(coef)
    at_points = dot(jnp.concatenate([high, low], axis=1), pick_ref[...]).reshape(
        4, 6, 8, points
    )
    values = jnp.zeros((8, points), F32)
    for c in range(3):
        total = jnp.zeros((8, points), F32)
        for m in range(4):
            total = total + at_points[m, 2 * c] * trig_ref[m]
            total = total + at_points[m, 2 * c + 1] * trig_ref[4 + m]
        values = jnp.where(
            (sub_p & 3) == c,
            jnp.broadcast_to(jnp.sum(total, axis=0, keepdims=True), (8, points)),
            values,
        )
    half = 8 * max(1, chips // 2)
    by_group = jnp.concatenate(
        [
            jnp.where(owner_y == 2 * (2 * tile + (sub_p >> 2)) + side, values, F32(0.0))
            for side in range(2)
            for tile in range(half // 8)
        ],
        axis=0,
    )
    high, low = halves(by_group)
    packed = dot_rows(jnp.concatenate([high, low], axis=0), slot_ref[...])
    packed = packed[: 2 * half] + packed[2 * half :]
    for side in range(2):
        group_send[side] = packed[half * side : half * side + half]
    pair = push(
        group_send.at[1 - core], group_recv, group_sems, (), {"gy": gy + 1 - 2 * core}
    )
    sent.append(pair)

    pair.wait_recv()
    total = group_send[core] + group_recv[...]
    rows16 = iota((n_gx, LANES), 0)
    lanes16 = iota((n_gx, LANES), 1)
    for place in range(chips):
        outgoing = jnp.zeros((n_gx, LANES), F32)
        for c in range(4):
            at = 4 * place + c
            line = total[at : at + 1] if c < 3 else mark_ref[place : place + 1]
            line = jnp.broadcast_to(line, (8, LANES))
            if (RANKS * (c + 1 - n_gx)) % LANES:
                line = pltpu.roll(line, (RANKS * (c + 1 - n_gx)) % LANES, 1)
            moved = pltpu.roll(
                jnp.broadcast_to(line[0:1], (n_gx, LANES)), 0, 1, stride=RANKS, stride_axis=0
            )
            outgoing = jnp.where(lanes16 >> 3 == c, moved, outgoing)
        owner_send[place] = outgoing.reshape(n_gx, 1, LANES)

    def to_row(a, first=0):
        peer_x = lax.rem(gx + a, n_gx)
        for b in range(first, chips):
            peer_chip = lax.rem(chip + b, chips)
            pltpu.make_async_remote_copy(
                src_ref=owner_send.at[peer_chip, n_gx - 1 - peer_x],
                dst_ref=owner_recv.at[b * n_gx + a],
                send_sem=owner_sems.at[0],
                recv_sem=owner_sems.at[1],
                device_id={"gx": peer_x, "gy": 2 * peer_chip + core},
                device_id_type=MESH,
            ).start()

    def far_first(first, last, when=None):
        def body(number, carry):
            away_by = (number + 1) // 2
            a = n_gx // 2 + jnp.where(number % 2 == 1, -away_by, away_by)
            if when is None:
                to_row(a)
            else:
                pl.when(when(a))(lambda: to_row(a))
            return carry

        lax.fori_loop(first, last, body, 0)

    pass_on(9, 9)
    pl.when(gx == told_last)(hear_below)
    chained = (gx >= min(8, told_last)) & (gx <= told_last)

    def below(a):
        return chained & (gx + a >= n_gx)

    def others(a):
        return jnp.logical_not(below(a))

    near = n_gx // 2 + 3 if n_gx > 8 else 0
    pl.when(chained)(lambda: far_first(0, near, below))
    far_first(near, n_gx - 1)
    to_row(0, 1)
    for copy in moduli_copies:
        copy.wait_recv()
    mu_next_x = last_x * x_recv[0, 0, 0]
    sum_prev_x = x_recv[0, 1, 0]
    lane4 = iota((4, 8, LANES), 2)
    sub4 = iota((4, 8, LANES), 1)
    side_w = [0.2] + [float(v) for v in WEIGHTS[1:4]]
    first_weight = -float(WEIGHTS[4])
    weight_y = by_four(sub & 3, side_w) + jnp.where(
        sub == 0, (1.0 - has_y) * first_weight, F32(0.0)
    )
    weight_z = by_four(lane & 3, side_w) + jnp.where(
        lane == 0, (1.0 - has_z) * first_weight, F32(0.0)
    )
    weight_x = [side_w[0] + (1.0 - has_x) * first_weight] + side_w[1:]

    def make_band(axis, position, count, following, preceding, weights, has, last, band, over):
        shifted = {0: mu}
        for t in range(-4, 5):
            if t:
                rolled = pltpu.roll(mu, (-t) % count, axis)
                if t > 0:
                    rolled = jnp.where(position == count - t, following, rolled)
                shifted[t] = rolled
        pos2 = position[0]
        phase = pos2 & 3
        later = pos2 > 3
        band_values = []
        for s in range(5):
            total = None
            for t in range(s - 4, 5):
                row = [
                    GRAM[i + t, i, i + s] if 0 <= i + t <= 4 and i + s <= 4 else 0.0
                    for i in range(4)
                ]
                pattern = by_four(phase, row)
                if s == 0 and t <= 0:
                    pattern = pattern + jnp.where(
                        (phase == 0) & later, F32(GRAM[4 + t, 4, 4]), F32(0.0)
                    )
                term = pattern[None] * shifted[t]
                total = term if total is None else total + term
            if s == 0:
                total = total + jnp.where(
                    position == 0, preceding + has * float(GRAM[4, 4, 4]) * mu, F32(0.0)
                )
            band_values.append(total * weights)
        crossing = jnp.zeros_like(mu)
        for s in range(1, 5):
            crossing = jnp.where(position == count - s, band_values[s], crossing)
            inside = jnp.where(position >= count - s, F32(0.0), band_values[s])
            behind = pltpu.roll(inside, s, axis)
            if 2 * s == count:
                band[s] = inside + behind
                band[4 + s] = jnp.zeros_like(inside)
            else:
                band[s] = inside
                band[4 + s] = behind
        over[...] = last * crossing
        band[0] = band_values[0]

    y_next = y_recv[0, 0, 0:8]
    y_prev = y_recv[0, 1, 0:8]
    z_next = z_recv[0, 0]
    z_prev = z_recv[0, 1]

    def rows_of(value):
        return jnp.concatenate(
            [jnp.broadcast_to(value[x : x + 1], (8, LANES))[None] for x in range(4)], axis=0
        )

    def columns_of(value):
        return jnp.concatenate(
            [jnp.broadcast_to(value[:, x : x + 1], (8, LANES))[None] for x in range(4)], axis=0
        )

    stacked = lambda scale: jnp.concatenate([(scale(x))[None] for x in range(4)], axis=0)
    make_band(
        2,
        lane4,
        LANES,
        last_z * columns_of(z_next),
        columns_of(z_prev),
        stacked(lambda x: weight_x[x] * weight_y),
        has_z,
        last_z,
        band_z,
        over_z,
    )
    make_band(
        1,
        sub4,
        8,
        last_y * rows_of(y_next),
        rows_of(y_prev),
        stacked(lambda x: weight_x[x] * weight_z),
        has_y,
        last_y,
        band_y,
        over_y,
    )
    weight_yz = weight_y * weight_z
    planes = [mu[x] for x in range(4)] + [mu_next_x]
    for i in range(4):
        for j in range(i, 5):
            value = sum(float(GRAM[k, i, j]) * planes[k] for k in range(5))
            if i == 0 and j == 0:
                value = value + sum_prev_x + has_x * float(GRAM[4, 4, 4]) * mu[0]
            if j == 4:
                value = last_x * value
            band_x[5 * i + j] = value * weight_yz
    for x in range(4):
        band_z[0, x] = band_z[0, x] + band_y[0, x] + band_x[6 * x]

    def coupling_x(i, j):
        return band_x[5 * min(i, j) + max(i, j)]

    def face_values(number, ref):
        field = ref[...].reshape(3, 4, 8, LANES)
        y_send[number, 0, 0:12] = ref[pl.ds(0, 12, stride=8), :]
        part_ref[...] = (over_y[...][None] * field).reshape(96, LANES)
        y_send[number, 1, 0:12] = sum(
            part_ref[pl.ds(4 + k, 12, stride=8), :] for k in range(4)
        )
        copies = send_face(number, "gy", 16)
        for c in range(3):
            x_send[number, 0, c] = field[c, 0]
            x_send[number, 1, c] = sum(coupling_x(i, 4) * field[c, i] for i in range(4))
        copies += send_face(number, "gx", 3)
        z_send[number, 0] = columns_to_lanes(
            [field[c, x][:, 0:1] for c in range(3) for x in range(4)]
        )
        z_send[number, 1] = columns_to_lanes(
            [
                jnp.sum(over_z[x] * field[c, x], axis=1, keepdims=True)
                for c in range(3)
                for x in range(4)
            ]
        )
        return copies + send_face(number, "gz", 8)

    def inner_stiffness(ref):
        field = ref[...].reshape(3, 4, 8, LANES)
        out = []
        for x in range(4):
            plane = field[:, x]
            total = band_z[0, x] * plane
            for s in range(1, 5):
                total = total + band_z[s, x] * pltpu.roll(plane, LANES - s, 2)
                total = total + band_z[4 + s, x] * pltpu.roll(plane, s, 2)
                total = total + band_y[s, x] * pltpu.roll(plane, 8 - s, 1)
                if s < 4:
                    total = total + band_y[4 + s, x] * pltpu.roll(plane, s, 1)
            for j in range(4):
                if j != x:
                    total = total + coupling_x(x, j) * field[:, j]
            out.append(total)
        return out

    def outer_stiffness(number, copies, inside):
        for copy in copies:
            copy.wait_recv()
        y_first = y_recv[number, 1, 0:12]
        y_after = y_recv[number, 0, 0:12]
        spread_ref[pl.ds(0, 12, stride=8), :] = y_first
        for k in range(4):
            spread_ref[pl.ds(4 + k, 12, stride=8), :] = y_after
        spread = spread_ref[...].reshape(3, 4, 8, LANES)
        z_first, z_after = z_recv[number, 1], z_recv[number, 0]
        x_after, x_first = x_recv[number, 0], x_recv[number, 1]
        out = []
        for x in range(4):
            rows = []
            for c in range(3):
                at = 4 * c + x
                row = inside[x][c] + coupling_x(x, 4) * x_after[c]
                row = row + jnp.where(sub == 0, F32(1.0), over_y[x]) * spread[c, x]
                row = row + jnp.where(
                    lane == 0,
                    jnp.broadcast_to(z_first[:, at : at + 1], (8, LANES)),
                    over_z[x] * jnp.broadcast_to(z_after[:, at : at + 1], (8, LANES)),
                )
                if x == 0:
                    row = row + x_first[c]
                rows.append(row)
            out.append(rows)
        return out

    spread_ref[...] = jnp.zeros((96, LANES), F32)
    loads["slab"].wait()
    now_copies = face_values(1, slab_ref)

    for level in range(2, len(reaches)):
        advance(level)
    far_first(0, near, others)
    owner_recv[0] = owner_send[chip, n_gx - 1 - gx]
    rows_all = chips * n_gx
    owner_in = pltpu.make_async_remote_copy(
        src_ref=owner_recv.at[1:rows_all],
        dst_ref=owner_recv.at[1:rows_all],
        send_sem=owner_sems.at[0],
        recv_sem=owner_sems.at[1],
        device_id=away("gx", 1),
        device_id_type=MESH,
    )

    inside = inner_stiffness(slab_ref)
    loads["before"].wait()
    loads["mass"].wait()
    around = outer_stiffness(1, now_copies, inside)
    for x in range(4):
        scale = slab_factor * mass_ref[8 * x : 8 * x + 8, :]
        for c in range(3):
            at = 32 * c + 8 * x
            base_ref[at : at + 8, :] = (
                2.0 * slab_ref[at : at + 8, :]
                - before_ref[at : at + 8, :]
                - scale * around[x][c]
            )

    owner_in.wait_recv()
    arrived = sum(
        owner_recv[b * n_gx : (b + 1) * n_gx].reshape(n_gx, LANES) for b in range(chips)
    )
    lines = []
    moved = pltpu.roll(arrived, 0, 1, stride=RANKS, stride_axis=0)
    for c in range(4):
        own = ((lanes16 >> 3) - rows16 - c) & 15 == 0
        line = jnp.sum(jnp.where(own, moved, F32(0.0)), axis=0, keepdims=True)
        if c:
            line = pltpu.roll(jnp.broadcast_to(line, (8, LANES)), LANES - RANKS * c, 1)[0:1]
        lines.append(line)
    goal = lines[3].astype(jnp.int32)
    goal_row, goal_lane = goal >> 7, goal & 127
    rows32 = iota((32, LANES), 0)
    spots = jnp.concatenate(
        [jnp.where(rows32 == goal_row, lines[c], F32(0.0)) for c in range(3)], axis=0
    )
    high, low = halves(spots)
    on_lane = (iota((LANES, LANES), 0) == goal_lane).astype(F32).astype(BF16)
    force = dot_rows(
        jnp.concatenate([high, low], axis=1), jnp.concatenate([on_lane, on_lane], axis=1)
    )
    force_out[...] = force
    for x in range(4):
        scale = slab_factor * mass_ref[8 * x : 8 * x + 8, :]
        for c in range(3):
            at = 32 * c + 8 * x
            step_ref[at : at + 8, :] = base_ref[at : at + 8, :] + scale * force[at : at + 8]

    step_copies = face_values(2, step_ref)
    inside = inner_stiffness(step_ref)
    around = outer_stiffness(2, step_copies, inside)
    for x in range(4):
        scale = slab_factor * mass_ref[8 * x : 8 * x + 8, :]
        for c in range(3):
            at = 32 * c + 8 * x
            slab_out[at : at + 8, :] = (
                2.0 * step_ref[at : at + 8, :]
                - slab_ref[at : at + 8, :]
                + scale * (force_out[at : at + 8, :] - around[x][c])
            )
    for copy in sent:
        copy.wait_send()
    owner_in.wait_send()


def copy_out(*refs):
    sems = refs[6]
    copies = [pltpu.make_async_copy(refs[i], refs[3 + i], sems.at[i]) for i in range(3)]
    for copy in copies:
        copy.start()
    for copy in copies:
        copy.wait()


def solution(mesh):
    n_gx, n_gy, n_gz = (mesh.shape[name] for name in ("gx", "gy", "gz"))

    def on_device(
        global_now,
        global_prev,
        cycle_modes,
        wave_speed,
        inv_radius,
        theta_second,
        theta_first,
        point_dest,
        point_target,
        point_source,
        point_azimuth,
        regional_now,
        regional_prev,
        moduli,
        inv_mass,
    ):
        points = point_target.shape[1]
        big = [((192, LANES), F32)] * 2 + [((8, LANES), F32)] * 2 + [((LANES, LANES), F32)] * 2
        big += [((1, points), jnp.int32)] * 3 + [((1, points), F32)]
        big += [((96, LANES), F32)] * 2 + [((32, LANES), F32)] * 2
        scratch = [pltpu.SMEM(cycle_modes.shape, jnp.int32)]
        scratch += [pltpu.VMEM(shape, dtype) for shape, dtype in big]
        scratch += [
            pltpu.VMEM((192, LANES), F32),
            pltpu.VMEM((192, LANES), F32),
            pltpu.VMEM((2 * LANES, 2 * LANES), BF16),
            pltpu.VMEM((2 * LANES, 2 * LANES), BF16),
            pltpu.VMEM((2 * LANES, points), BF16),
            pltpu.VMEM((8, 8, points), F32),
            pltpu.VMEM((LANES, points), BF16),
            pltpu.VMEM((8, LANES), F32),
            pltpu.VMEM((96, LANES), F32),
            pltpu.VMEM((96, LANES), F32),
            pltpu.VMEM((9, 4, 8, LANES), F32),
            pltpu.VMEM((9, 4, 8, LANES), F32),
            pltpu.VMEM((20, 8, LANES), F32),
            pltpu.VMEM((4, 8, LANES), F32),
            pltpu.VMEM((4, 8, LANES), F32),
            pltpu.VMEM((96, LANES), F32),
            pltpu.VMEM((96, LANES), F32),
            pltpu.VMEM((2, 56, LANES), F32),
            pltpu.VMEM((2, 56, LANES), F32),
            pltpu.VMEM((3, 2, 3, 8, LANES), F32),
            pltpu.VMEM((3, 2, 3, 8, LANES), F32),
            pltpu.VMEM((3, 2, 16, LANES), F32),
            pltpu.VMEM((3, 2, 16, LANES), F32),
            pltpu.VMEM((3, 2, 8, LANES), F32),
            pltpu.VMEM((3, 2, 8, LANES), F32),
            pltpu.VMEM((2, 8 * max(1, n_gy // 4), LANES), F32),
            pltpu.VMEM((8 * max(1, n_gy // 4), LANES), F32),
            pltpu.VMEM((n_gy // 2, n_gx, 1, LANES), F32),
            pltpu.VMEM((n_gy // 2 * n_gx, 1, LANES), F32),
            pltpu.SemaphoreType.DMA((15,)),
            pltpu.SemaphoreType.DMA((2, 2)),
            pltpu.SemaphoreType.DMA((2, 3, 6)),
            pltpu.SemaphoreType.DMA((2,)),
            pltpu.SemaphoreType.DMA((2,)),
            pltpu.SemaphoreType.REGULAR((5,)),
        ]
        hbm = pl.BlockSpec(memory_space=pl.ANY)
        two, slab, force = pl.pallas_call(
            functools.partial(kernel, (n_gx, n_gy, n_gz)),
            out_shape=[
                pltpu.VMEM((192, LANES), F32),
                pltpu.VMEM((96, LANES), F32),
                pltpu.VMEM((96, LANES), F32),
            ],
            in_specs=[hbm] * 15,
            out_specs=[pl.BlockSpec(memory_space=pltpu.VMEM)] * 3,
            scratch_shapes=scratch,
            compiler_params=pltpu.CompilerParams(
                collective_id=0, has_side_effects=True, vmem_limit_bytes=48 * 2**20
            ),
        )(
            *[
                pltpu.with_memory_space_constraint(x, pltpu.HBM)
                for x in (
            cycle_modes,
            global_now.reshape(192, LANES),
            global_prev.reshape(192, LANES),
            wave_speed,
            inv_radius,
            theta_second,
            theta_first,
            point_dest.reshape(1, points),
            point_target,
            point_source,
            point_azimuth,
            regional_now.reshape(96, LANES),
            regional_prev.reshape(96, LANES),
            moduli.reshape(32, LANES),
            inv_mass.reshape(32, LANES),
            )]
        )
        two, slab, force = pl.pallas_call(
            copy_out,
            out_shape=[
                pltpu.HBM((192, LANES), F32),
                pltpu.HBM((96, LANES), F32),
                pltpu.HBM((96, LANES), F32),
            ],
            in_specs=[hbm] * 3,
            out_specs=[hbm] * 3,
            scratch_shapes=[pltpu.SemaphoreType.DMA((3,))],
        )(*[pltpu.with_memory_space_constraint(x, pltpu.VMEM) for x in (two, slab, force)])
        return (
            two.reshape(global_now.shape),
            slab.reshape(regional_now.shape),
            force.reshape(regional_now.shape),
        )

    return jax.shard_map(
        on_device,
        mesh=mesh,
        in_specs=(
            P("gy", None, "gx", None),
            P("gy", None, "gx", None),
            P("gx"),
            P("gx", None),
            P("gx", None),
            P(),
            P(),
            P("gz", "gx", None),
            P("gz", "gx"),
            P("gz", "gx"),
            P("gz", "gx"),
            P(None, "gx", "gy", "gz"),
            P(None, "gx", "gy", "gz"),
            P("gx", "gy", "gz"),
            P("gx", "gy", "gz"),
        ),
        out_specs=(P("gy", None, "gx", None), P(None, "gx", "gy", "gz"), P(None, "gx", "gy", "gz")),
        check_vma=False,
    )
```
